32 devices in a mesh: blk: 8 (over z, y), grp: 4 (over x, core).
Axes of the slice: x: 2, y: 2, z: 4, core: 2. Of those that a mesh axis runs over, the one named last changes fastest.
Arguments:
- points: bfloat16 [32768, 768], P(('blk', 'grp')), may hold values from -6 to 6, as said below
- counts: int32 [64], P(('blk', 'grp')), may hold values from 256 to 512, as said below
- pair_rows: int32 [512], P('blk'), may hold values from 0 to 7, as said below
- pair_cols: int32 [512], P('blk'), may hold values from 0 to 15, as said below
- pair_live: int32 [8], P('blk'), may hold values from 1 to 64, as said below
- start: float32 [64, 32768], P(None, ('blk', 'grp')), may hold values from -6 to 6
Outputs:
- embed: float32 [64, 32768], P(None, ('blk', 'grp'))
The draws below stay inside these ranges and needn't reach their ends.
Inputs may be any that keep to these rules, and one draw needn't show every extreme that they name: Padding points are drawn like the others. `counts`: points of a block beyond its count are padding; block 0 is full. `pair_rows`: the live slots of a slab list distinct pairs. `pair_cols`: in a live slot, a value under 8 is above the slot's pair_rows; larger values, naming a block of the next slab, stand in live slots only of slabs below the last. Slots 0 to pair_live - 1 of a slab are live; slab 0 has all 64.
All inputs are finite; a program needn't handle non-finite values.
Results may differ from the reference program's by a relative error of at most 0.0042.
Values may be sent and summed in bfloat16 or wider, within the bound.
No kernel may reach another device: no remote copies, remote signals or barrier semaphores. Data moves between devices by JAX's collectives and lax.ppermute only.
A program may use at most 64 MiB of HBM per device.

```python
import jax
import jax.numpy as jnp
from jax import lax

F = 768
K = 64
PTS = 512
BPD = 2
PAIRS_SLAB = 64
ITERS = 2
NBLOCKS = 64
NPTS = 32768
N_BLK = 8
N_GRP = 4


def pair_tables(key):
    slab = BPD * N_GRP
    width = 2 * slab
    total = slab * width

    def one_slab(index):
        sub = jax.random.fold_in(key, index)
        order = jax.random.permutation(sub, total)
        cand = jnp.arange(total, dtype=jnp.int32)
        rows = cand // width
        cols = cand % width
        valid = jnp.where(cols < slab, rows < cols, index + 1 < N_BLK)
        scores = order + jnp.where(valid, 0, total)
        picked = jnp.argsort(scores)[:PAIRS_SLAB]
        valid_count = jnp.sum(valid.astype(jnp.int32))
        power = jax.random.randint(jax.random.fold_in(sub, 7), (), 0, 4)
        wanted = jnp.right_shift(jnp.int32(PAIRS_SLAB), power)
        wanted = jnp.where(index == 0, PAIRS_SLAB, wanted)
        return (rows[picked], cols[picked], jnp.minimum(wanted, valid_count))
    rows, cols, lives = jax.vmap(one_slab)(jnp.arange(N_BLK, dtype=jnp.int32))
    return (rows.reshape(-1).astype(jnp.int32), cols.reshape(-1).astype(jnp.int32), lives.astype(jnp.int32))


def draw_points(key, part):
    key = jax.random.fold_in(key, 23)
    noise_key, along_key, second_key = jax.random.split(key, 3)
    along = jax.random.uniform(along_key, (NPTS, 1), jnp.float32, -1.5, 1.5)
    second = jnp.where(jax.random.bernoulli(second_key, 0.5, (1, F)), 1.0, -1.0).astype(jnp.float32)
    noise = 0.95 * jax.random.normal(noise_key, (NPTS, F), jnp.float32)
    values = noise + 0.4 * along * second
    return jnp.clip(values, -6.0, 6.0).astype(jnp.bfloat16)


def draw_counts(key, part):
    key = jax.random.fold_in(key, 11)
    values = jax.random.randint(key, (NBLOCKS,), PTS // 2, PTS + 1)
    return values.at[0].set(PTS).astype(jnp.int32)


def draw_pair_rows(key, part):
    return pair_tables(key)[0]


def draw_pair_cols(key, part):
    return pair_tables(key)[1]


def draw_pair_live(key, part):
    return pair_tables(key)[2]


def steps_of(rng, extent, cuts, smallest, top_value):
    def one(position, blocks):
        draws = jax.random.uniform(jax.random.fold_in(jax.random.fold_in(rng, 6), position), (blocks,), jnp.float32, smallest / len(cuts), top_value / len(cuts))
        return jnp.repeat(jnp.exp(draws), extent[position] // blocks).reshape((-1,) + (1,) * (len(extent) - position - 1))

    gain = one(*cuts[0])
    for cut in cuts[1:]:
        gain = gain * one(*cut)
    return gain


def scatter_about(stream_key, dims, deviation, limit, cuts=(), held_as=jnp.bfloat16):
    loudness = steps_of(stream_key, dims, cuts, -0.22, 0.18) if cuts else 1.0
    drawn = jax.random.normal(stream_key, dims, jnp.float32) * deviation * loudness
    return jnp.minimum(jnp.maximum(drawn, -limit), limit).astype(held_as)


def setup_inputs(seed: int = 0) -> dict:
    keys = jax.random.split(jax.random.key(seed), 7)
    points = draw_points(jax.random.fold_in(keys[6], 71), 0)
    counts = draw_counts(jax.random.fold_in(keys[6], 71), 0)
    pair_rows = draw_pair_rows(jax.random.fold_in(keys[6], 71), 0)
    pair_cols = draw_pair_cols(jax.random.fold_in(keys[6], 71), 0)
    pair_live = draw_pair_live(jax.random.fold_in(keys[6], 71), 0)
    start = scatter_about(keys[5], (K, NPTS), 1.0, 6.0, ((1, 32),), jnp.float32)
    return dict(points=points, counts=counts, pair_rows=pair_rows, pair_cols=pair_cols, pair_live=pair_live, start=start)


def score(points, live, row_blk, col_blk):
    left = lax.dynamic_slice_in_dim(points, row_blk * PTS, PTS, 0)
    right = lax.dynamic_slice_in_dim(points, col_blk * PTS, PTS, 0)
    left_live = lax.dynamic_slice_in_dim(live, row_blk * PTS, PTS, 0)
    right_live = lax.dynamic_slice_in_dim(live, col_blk * PTS, PTS, 0)
    left_wide = left.astype(jnp.float32)
    right_wide = right.astype(jnp.float32)
    left_norm = jnp.sum(left_wide * left_wide, 1)
    right_norm = jnp.sum(right_wide * right_wide, 1)
    cross = lax.dot_general(left.astype(jnp.float32), right.astype(jnp.float32), (((1,), (1,)), ((), ())), preferred_element_type=jnp.float32)
    dist = left_norm[:, None] + right_norm[None, :] - 2.0 * cross
    width = left.shape[1]
    tile = jnp.exp(-3.0 / width * dist) * left_live[:, None] * right_live[None, :]
    return tile.astype(jnp.bfloat16)

def bump(total, start_at, addend):
    old = lax.dynamic_slice_in_dim(total, start_at, addend.shape[-1], total.ndim - 1)
    return lax.dynamic_update_slice_in_dim(total, old + addend, start_at, total.ndim - 1)

def reference(points, counts, pair_rows, pair_cols, pair_live, start):
    live = (jnp.arange(PTS)[None, :] < counts[:, None]).reshape(-1).astype(jnp.float32)
    slab = BPD * N_GRP
    pair_ids = jnp.arange(N_BLK * PAIRS_SLAB, dtype=jnp.int32)
    slab_of = pair_ids // PAIRS_SLAB
    used = pair_ids % PAIRS_SLAB < pair_live[slab_of]
    row_glob = (slab_of * slab + pair_rows).astype(jnp.int32)
    col_glob = (slab_of * slab + pair_cols).astype(jnp.int32)
    total_pts = points.shape[0]
    vecs = start
    for turn in range(ITERS):
        vec_half = vecs.astype(jnp.bfloat16)

        def step(carry, item):
            row_blk, col_blk, flag = item

            def add(state):
                acc, dacc = state
                tile = score(points, live, row_blk, col_blk)
                upper = lax.dynamic_slice_in_dim(vec_half, col_blk * PTS, PTS, 1)
                lower_part = lax.dynamic_slice_in_dim(vec_half, row_blk * PTS, PTS, 1)
                to_row = lax.dot_general(upper.astype(jnp.float32), tile.astype(jnp.float32), (((1,), (1,)), ((), ())), preferred_element_type=jnp.float32)
                to_col = jnp.dot(lower_part.astype(jnp.float32), tile.astype(jnp.float32), preferred_element_type=jnp.float32)
                acc = bump(bump(acc, row_blk * PTS, to_row), col_blk * PTS, to_col)
                tile_wide = tile.astype(jnp.float32)
                dacc = bump(bump(dacc, row_blk * PTS, jnp.sum(tile_wide, 1)), col_blk * PTS, jnp.sum(tile_wide, 0))
                return (acc, dacc)
            return (lax.cond(flag, add, lambda state: state, carry), None)
        init = (jnp.zeros((K, total_pts), jnp.float32), jnp.zeros((total_pts,), jnp.float32))
        (acc, dacc), unused = lax.scan(step, init, (row_glob, col_glob, used))
        outcome = live[None, :] * vec_half.astype(jnp.float32) + acc
        degree = 1.0 + dacc
        scaled = outcome / degree[None, :]
        gram = lax.dot_general(scaled, scaled, (((1,), (1,)), ((), ())), precision=lax.Precision.HIGHEST)
        lower = jnp.linalg.cholesky(gram)
        vecs = lax.linalg.triangular_solve(lower, scaled, left_side=True, lower=True)
    return vecs
```

```python
import functools

import jax
import jax.numpy as jnp
from jax import lax
from jax.experimental import pallas as pl
from jax.experimental.pallas import tpu as pltpu
from jax.sharding import PartitionSpec as P

PTS = 512
ITERS = 2
LOG2E = 1.4426950408889634
DEAD = 65536.0
EXTRA = 16
VMEM = pltpu.VMEM
SMEM = pltpu.SMEM
HIGHEST = lax.Precision.HIGHEST


def spec(space):
    return pl.BlockSpec(memory_space=space)


def swap(value, axis, bit):
    count = lax.axis_size(axis)
    return lax.ppermute(value, axis, [(source, source ^ bit) for source in range(count)])


def from_behind(value, axis, steps):
    count = lax.axis_size(axis)
    initial, last = (max(0, -steps), min(count, count - steps))
    return lax.ppermute(value, axis, [(source, source + steps) for source in range(initial, last)])


def bits_of(count):
    bits = []
    bit = 1
    while bit < count:
        bits.append(bit)
        bit *= 2
    return bits


def gather_near(value, axis):
    held = {0: value}
    for bit in reversed(bits_of(lax.axis_size(axis))):
        for rel in list(held):
            held[rel ^ bit] = swap(held[rel], axis, bit)
    return [held[rel] for rel in range(len(held))]


def prepare_kernel(group, cap, pts, counts, rows, cols, live, start, aug, out_rows, out_cols, out_n):
    columns, total = start.shape
    width = pts.shape[1]
    blocks_dev = total // PTS
    slab = blocks_dev * group
    slots = rows.shape[0]
    member = lax.axis_index("grp")

    def local_near(block):
        return (lax.div(block, blocks_dev) ^ member) * blocks_dev + lax.rem(block, blocks_dev)

    def count_far(slot, carry):
        col = cols[slot]
        far = jnp.logical_and(slot < live[0], col >= slab)
        owner = lax.div(col - slab, blocks_dev)
        return tuple(
            old + jnp.where(jnp.logical_and(far, owner == device), 1, 0)
            for device, old in enumerate(carry)
        )

    far_counts = lax.fori_loop(0, slots, count_far, (jnp.int32(0),) * group)
    low = jnp.int32(0)
    room = jnp.int32(0)
    for device in range(group):
        low = low + jnp.where(device < member, cap - far_counts[device], 0)
        room = room + jnp.where(device == member, cap - far_counts[device], 0)

    def place(slot, carry):
        near_rank, filled = carry
        row, col = rows[slot], cols[slot]
        used = slot < live[0]
        far = col >= slab
        mine_far = jnp.logical_and(far, lax.div(col - slab, blocks_dev) == member)
        mine_near = jnp.logical_and(
            jnp.logical_not(far), jnp.logical_and(near_rank >= low, near_rank < low + room)
        )
        mine = jnp.logical_and(used, jnp.logical_or(mine_far, mine_near))

        @pl.when(mine)
        def _():
            out_rows[filled] = local_near(row)
            out_cols[filled] = jnp.where(far, slab + lax.rem(col - slab, blocks_dev), local_near(col))

        near_rank = near_rank + jnp.where(jnp.logical_and(used, jnp.logical_not(far)), 1, 0)
        return (near_rank, filled + jnp.where(mine, 1, 0))

    out_n[0] = lax.fori_loop(0, slots, place, (jnp.int32(0), jnp.int32(0)))[1]

    for block in range(blocks_dev):
        lanes = slice(block * PTS, (block + 1) * PTS)
        wide = pts[lanes, :].astype(jnp.float32)
        norm = lax.dot_general(
            jnp.ones((8, width), jnp.float32),
            wide * wide,
            (((1,), (1,)), ((), ())),
            precision=HIGHEST,
            preferred_element_type=jnp.float32,
        )[0:1, :]
        place_in = lax.broadcasted_iota(jnp.int32, (1, PTS), 1)
        level = norm * (3.0 / width * LOG2E) + jnp.where(place_in < counts[block], 0.0, DEAD)
        high = level.astype(jnp.bfloat16).astype(jnp.float32)
        rest = level - high
        middle = rest.astype(jnp.bfloat16).astype(jnp.float32)
        small = rest - middle
        which = lax.broadcasted_iota(jnp.int32, (EXTRA, PTS), 0)
        tail = jnp.where(which == 0, 1.0, 0.0)
        tail = tail + jnp.where(which == 1, high, 0.0)
        tail = tail + jnp.where(which == 2, middle, 0.0)
        tail = tail + jnp.where(which == 3, small, 0.0)
        aug[0:columns, lanes] = start[:, lanes].astype(jnp.bfloat16)
        aug[columns : columns + EXTRA, lanes] = tail.astype(jnp.bfloat16)


def prepare(points, counts, rows, cols, live, start, group, cap):
    columns, total = start.shape
    return pl.pallas_call(
        functools.partial(prepare_kernel, group, cap),
        out_shape=(
            jax.ShapeDtypeStruct((columns + EXTRA, total), jnp.bfloat16),
            jax.ShapeDtypeStruct((cap,), jnp.int32),
            jax.ShapeDtypeStruct((cap,), jnp.int32),
            jax.ShapeDtypeStruct((1,), jnp.int32),
        ),
        in_specs=[spec(VMEM), spec(SMEM), spec(SMEM), spec(SMEM), spec(SMEM), spec(VMEM)],
        out_specs=(spec(VMEM), spec(SMEM), spec(SMEM), spec(SMEM)),
        compiler_params=pltpu.CompilerParams(vmem_limit_bytes=32 * 2**20),
        name="prepare",
    )(points, counts, rows, cols, live, start)


def message_rels(group):
    groups = [[0]]
    for bit in bits_of(group):
        groups.append([rel for rel in range(group) if rel & bit and rel % bit == 0])
    return groups


def product_shapes(group, blocks_dev, height):
    shapes = [
        jax.ShapeDtypeStruct((len(rels) * blocks_dev, height, PTS), jnp.float32)
        for rels in message_rels(group)
    ]
    shapes.append(jax.ShapeDtypeStruct((blocks_dev, height, PTS), jnp.float32))
    return shapes


def write_products(group, blocks_dev, acc, outs):
    for rels, out in zip(message_rels(group), outs[:-1]):
        for index, rel in enumerate(rels):
            for block in range(blocks_dev):
                out[index * blocks_dev + block] = acc[rel * blocks_dev + block]
    for block in range(blocks_dev):
        outs[-1][block] = acc[group * blocks_dev + block]


def add_products(acc, tile, u_row, u_col, row, col):
    height = acc.shape[1]
    to_row = lax.dot_general(
        u_col, tile, (((1,), (1,)), ((), ())), preferred_element_type=jnp.float32
    )
    acc[row] += to_row[:height]
    to_col = jnp.dot(u_row, tile, preferred_element_type=jnp.float32)
    acc[col] += to_col[:height]


def first_kernel(group, refs):
    pieces = group + 1
    n_ref, rows, cols, counts = refs[:4]
    pts = refs[4 : 4 + pieces]
    augs = refs[4 + pieces : 4 + 2 * pieces]
    tiles_out = refs[4 + 2 * pieces]
    messages = len(message_rels(group)) + 1
    outs = refs[5 + 2 * pieces : 5 + 2 * pieces + messages]
    window, kept, u_win, level_row, level_col, acc, in_sems, out_sems = refs[5 + 2 * pieces + messages :]
    held = pts[0].shape[0]
    width = pts[0].shape[1]
    blocks_dev = held // PTS
    columns = augs[0].shape[0] - EXTRA
    height = acc.shape[1]
    copies = [
        pltpu.make_async_copy(
            pts[piece], window.at[pl.ds(piece * held, held), :], in_sems.at[piece]
        )
        for piece in range(pieces)
    ]
    for copy in copies:
        copy.start()

    pick = lax.broadcasted_iota(jnp.int32, (EXTRA, 128), 0)
    pick = jnp.where(jnp.logical_and(pick >= 1, pick <= 3), 1.0, 0.0).astype(jnp.bfloat16)
    for piece in range(pieces):
        for block in range(blocks_dev):
            place = piece * blocks_dev + block
            lanes = slice(block * PTS, (block + 1) * PTS)
            u_win[place] = augs[piece][:, lanes]
            tail = augs[piece][columns : columns + EXTRA, lanes]
            if piece < group:
                level_col[place] = lax.dot_general(
                    tail, pick, (((0,), (0,)), ((), ())), preferred_element_type=jnp.float32
                )
            tail = tail.astype(jnp.float32)
            level_row[place] = jnp.broadcast_to(tail[1:2] + tail[2:3] + tail[3:4], (8, PTS))
            acc[place] = jnp.zeros((height, PTS), jnp.float32)
    for block in range(blocks_dev):
        lanes = slice(block * PTS, (block + 1) * PTS)
        place_in = lax.broadcasted_iota(jnp.int32, (columns, PTS), 1)
        own = augs[0][0:columns, lanes].astype(jnp.float32)
        acc[block, 0:columns] = jnp.where(place_in < counts[block], own, 0.0)
        acc[block, columns:height] = jnp.ones((height - columns, PTS), jnp.float32)
    for copy in copies:
        copy.wait()

    n = n_ref[0]
    step = 256
    scale = 6.0 / width * LOG2E

    def body(index, carry):
        row, col = rows[index], cols[index]
        right = window[pl.ds(pl.multiple_of(col * PTS, PTS), PTS), :]
        right_level = level_row[col][0:1, :]
        for part in range(PTS // step):
            left = window[pl.ds(pl.multiple_of(row * PTS + part * step, step), step), :]
            cross = lax.dot_general(
                left, right, (((1,), (1,)), ((), ())), preferred_element_type=jnp.float32
            )
            left_level = level_col[row, part * step : (part + 1) * step, :]
            left_level = jnp.concatenate([left_level] * (PTS // 128), axis=1)
            value = jnp.exp2(cross * scale - left_level - right_level)
            kept[index, part * step : (part + 1) * step, :] = value.astype(jnp.bfloat16)
        pltpu.make_async_copy(kept.at[index], tiles_out.at[index], out_sems.at[index]).start()
        add_products(acc, kept[index], u_win[row], u_win[col], row, col)
        return carry

    lax.fori_loop(0, n, body, 0)
    write_products(group, blocks_dev, acc, outs)

    def finish(index, carry):
        pltpu.make_async_copy(kept.at[index], tiles_out.at[index], out_sems.at[index]).wait()
        return carry

    lax.fori_loop(0, n, finish, 0)


def first_turn(n, rows, cols, counts, pts, augs, group, cap):
    held, width = pts[0].shape
    blocks_dev = held // PTS
    places = (group + 1) * blocks_dev
    tall = augs[0].shape[0]
    height = tall - EXTRA + 8
    pieces = group + 1
    shapes = [jax.ShapeDtypeStruct((cap, PTS, PTS), jnp.bfloat16)]
    shapes += product_shapes(group, blocks_dev, height)

    def kernel(*refs):
        first_kernel(group, refs)

    return pl.pallas_call(
        kernel,
        out_shape=tuple(shapes),
        in_specs=[spec(SMEM)] * 4 + [spec(pl.ANY)] * pieces + [spec(VMEM)] * pieces,
        out_specs=(spec(pl.ANY),) + (spec(VMEM),) * (len(shapes) - 1),
        scratch_shapes=[
            VMEM((pieces * held, width), jnp.bfloat16),
            VMEM((cap, PTS, PTS), jnp.bfloat16),
            VMEM((places, tall, PTS), jnp.bfloat16),
            VMEM((places, 8, PTS), jnp.float32),
            VMEM((group * blocks_dev, PTS, 128), jnp.float32),
            VMEM((places, height, PTS), jnp.float32),
            pltpu.SemaphoreType.DMA((pieces,)),
            pltpu.SemaphoreType.DMA((cap,)),
        ],
        compiler_params=pltpu.CompilerParams(vmem_limit_bytes=48 * 2**20),
        name="first_turn",
    )(n, rows, cols, counts, *pts, *augs)


def scale_kernel(blocks_dev, has_degree, refs):
    degree_in = None if has_degree else refs[0]
    parts = refs[:-3] if has_degree else refs[1:-2]
    if has_degree:
        z_out, gram_out, degree_out = refs[-3:]
    else:
        z_out, gram_out = refs[-2:]
    columns = z_out.shape[0]
    gram = jnp.zeros((columns, columns), jnp.float32)
    for block in range(blocks_dev):
        lanes = slice(block * PTS, (block + 1) * PTS)
        total = parts[0][block]
        for part in parts[1:]:
            total = total + part[block]
        if has_degree:
            degree = total[columns : columns + 1, :]
            degree_out[:, lanes] = jnp.broadcast_to(degree, (8, PTS))
        else:
            degree = degree_in[0:1, lanes]
        z = total[0:columns] / degree
        z_out[:, lanes] = z
        gram = gram + lax.dot_general(
            z, z, (((1,), (1,)), ((), ())), precision=HIGHEST, preferred_element_type=jnp.float32
        )
    gram_out[...] = gram


def scaled_gram(parts, degree, columns):
    blocks_dev = parts[0].shape[0]
    for part in parts:
        blocks_dev = min(blocks_dev, part.shape[0])
    total = blocks_dev * PTS
    shapes = [
        jax.ShapeDtypeStruct((columns, total), jnp.float32),
        jax.ShapeDtypeStruct((columns, columns), jnp.float32),
    ]
    if degree is None:
        shapes.append(jax.ShapeDtypeStruct((8, total), jnp.float32))
        operands = list(parts)
    else:
        operands = [degree] + list(parts)

    def kernel(*refs):
        scale_kernel(blocks_dev, degree is None, refs)

    return pl.pallas_call(
        kernel,
        out_shape=tuple(shapes),
        in_specs=[spec(VMEM)] * len(operands),
        out_specs=(spec(VMEM),) * len(shapes),
        compiler_params=pltpu.CompilerParams(vmem_limit_bytes=32 * 2**20),
        name="scaled_gram",
    )(*operands)


def inverse_factor(gram):
    size = gram.shape[0]
    row_id = lax.broadcasted_iota(jnp.int32, (size, size), 0)
    col_id = lax.broadcasted_iota(jnp.int32, (size, size), 1)
    eye = jnp.where(row_id == col_id, 1.0, 0.0)
    whole = jnp.concatenate([gram, eye], axis=1)
    groups = [whole[8 * g : 8 * g + 8, :] for g in range(size // 8)]
    within = lax.broadcasted_iota(jnp.int32, (8, 2 * size), 0)
    for j in range(size):
        g, r = divmod(j, 8)
        top = groups[g][r : r + 1, :]
        factor = lax.rsqrt(top[:, j : j + 1])
        top = top * factor
        for other in range(g, size // 8):
            column = groups[other][:, j : j + 1] * factor
            fresh = groups[other] - column * top
            if other == g:
                fresh = jnp.where(within > r, fresh, jnp.where(within == r, top, groups[g]))
            groups[other] = fresh
    return jnp.concatenate(groups, axis=0)[:, size : 2 * size]


def second_kernel(group, refs):
    pieces = group + 1
    n_ref, rows, cols, counts, gram = refs[:5]
    zs = refs[5 : 5 + pieces]
    tiles = refs[5 + pieces]
    messages = len(message_rels(group)) + 1
    outs = refs[6 + pieces : 6 + pieces + messages]
    kept, u_win, acc, sems = refs[6 + pieces + messages :]
    columns, held = zs[0].shape
    blocks_dev = held // PTS
    n = n_ref[0]

    def fetch(index):
        return pltpu.make_async_copy(tiles.at[index], kept.at[index], sems.at[index])

    def begin(index, carry):
        fetch(index).start()
        return carry

    lax.fori_loop(0, n, begin, 0)
    inverse = inverse_factor(gram[...])
    for piece in range(pieces):
        for block in range(blocks_dev):
            place = piece * blocks_dev + block
            vec = jnp.dot(
                inverse,
                zs[piece][:, block * PTS : (block + 1) * PTS],
                precision=HIGHEST,
                preferred_element_type=jnp.float32,
            ).astype(jnp.bfloat16)
            u_win[place] = vec
            if piece == 0:
                place_in = lax.broadcasted_iota(jnp.int32, (columns, PTS), 1)
                acc[place] = jnp.where(place_in < counts[block], vec.astype(jnp.float32), 0.0)
            else:
                acc[place] = jnp.zeros((columns, PTS), jnp.float32)

    def body(index, carry):
        row, col = rows[index], cols[index]
        fetch(index).wait()
        add_products(acc, kept[index], u_win[row], u_win[col], row, col)
        return carry

    lax.fori_loop(0, n, body, 0)
    write_products(group, blocks_dev, acc, outs)


def next_turn(n, rows, cols, counts, gram, zs, tiles, group, cap):
    columns, held = zs[0].shape
    blocks_dev = held // PTS
    pieces = group + 1
    places = pieces * blocks_dev
    shapes = product_shapes(group, blocks_dev, columns)

    def kernel(*refs):
        second_kernel(group, refs)

    return pl.pallas_call(
        kernel,
        out_shape=tuple(shapes),
        in_specs=[spec(SMEM)] * 4 + [spec(VMEM)] * (1 + pieces) + [spec(pl.ANY)],
        out_specs=(spec(VMEM),) * len(shapes),
        scratch_shapes=[
            VMEM((cap, PTS, PTS), jnp.bfloat16),
            VMEM((places, columns, PTS), jnp.bfloat16),
            VMEM((places, columns, PTS), jnp.float32),
            pltpu.SemaphoreType.DMA((cap,)),
        ],
        compiler_params=pltpu.CompilerParams(vmem_limit_bytes=40 * 2**20),
        name="next_turn",
    )(n, rows, cols, counts, gram, *zs, tiles)


def embed_kernel(gram, z, out):
    out[...] = jnp.dot(
        inverse_factor(gram[...]), z[...], precision=HIGHEST, preferred_element_type=jnp.float32
    )


def embedding(gram, z):
    return pl.pallas_call(
        embed_kernel,
        out_shape=jax.ShapeDtypeStruct(z.shape, jnp.float32),
        in_specs=[spec(VMEM)] * 2,
        out_specs=spec(VMEM),
        name="embedding",
    )(gram, z)


def sum_products(messages, group, blocks_dev):
    rels = message_rels(group)
    parts = {}
    for names, message in zip(rels[1:], messages[1:-1]):
        for index, rel in enumerate(names):
            parts[rel] = [message[index * blocks_dev : (index + 1) * blocks_dev]]
    final = [messages[0], from_behind(messages[-1], "blk", 1)]
    for bit, names, message in zip(bits_of(group), rels[1:], messages[1:-1]):
        if bit > 1:
            message = jnp.concatenate([sum(parts[rel][1:], parts[rel][0]) for rel in names], 0)
        got = swap(message, "grp", bit)
        for index, rel in enumerate(names):
            target = rel ^ bit
            if target == 0:
                final.append(got)
            else:
                parts[target].append(got[index * blocks_dev : (index + 1) * blocks_dev])
    return final


def all_sum(value, axes):
    for axis in axes:
        for bit in bits_of(lax.axis_size(axis)):
            value = value + swap(value, axis, bit)
    return value


def per_device(points, counts, pair_rows, pair_cols, pair_live, start):
    group = lax.axis_size("grp")
    blocks_dev = counts.shape[0]
    columns = start.shape[0]
    slots = pair_rows.shape[0]
    cap = max(-(-slots // group), blocks_dev * blocks_dev * group)
    pts = gather_near(points, "grp") + [from_behind(points, "blk", -1)]
    aug, rows, cols, n = prepare(
        points, counts, pair_rows, pair_cols, pair_live, start, group, cap
    )
    augs = gather_near(aug, "grp") + [from_behind(aug, "blk", -1)]
    tiles, *messages = first_turn(n, rows, cols, counts, pts, augs, group, cap)
    z, gram, degree = scaled_gram(sum_products(messages, group, blocks_dev), None, columns)
    for turn in range(1, ITERS):
        zs = gather_near(z, "grp") + [from_behind(z, "blk", -1)]
        gram = all_sum(gram, ("grp", "blk"))
        messages = next_turn(n, rows, cols, counts, gram, zs, tiles, group, cap)
        z, gram = scaled_gram(sum_products(messages, group, blocks_dev), degree, columns)
    return embedding(all_sum(gram, ("grp", "blk")), z)


def solution(mesh):
    in_specs = (
        P(("blk", "grp"), None),
        P(("blk", "grp")),
        P("blk"),
        P("blk"),
        P("blk"),
        P(None, ("blk", "grp")),
    )
    out_specs = P(None, ("blk", "grp"))
    return jax.shard_map(
        per_device, mesh=mesh, in_specs=in_specs, out_specs=out_specs, check_vma=False
    )
```

```python
import functools

import jax
import jax.numpy as jnp
from jax import lax
from jax.experimental import pallas as pl
from jax.experimental.pallas import tpu as pltpu
from jax.sharding import PartitionSpec as P

PTS = 512
ITERS = 2
LOG2E = 1.4426950408889634
DEAD = 65536.0
EXTRA = 16
VMEM = pltpu.VMEM
SMEM = pltpu.SMEM
HIGHEST = lax.Precision.HIGHEST


def cost(flops, moved):
    return pl.CostEstimate(flops=int(flops), bytes_accessed=int(moved), transcendentals=0)


def spec(space):
    return pl.BlockSpec(memory_space=space)


def swap(value, axis, bit):
    count = lax.axis_size(axis)
    return lax.ppermute(value, axis, [(source, source ^ bit) for source in range(count)])


def from_behind(value, axis, steps):
    count = lax.axis_size(axis)
    initial, last = (max(0, -steps), min(count, count - steps))
    return lax.ppermute(value, axis, [(source, source + steps) for source in range(initial, last)])


def bits_of(count):
    bits = []
    bit = 1
    while bit < count:
        bits.append(bit)
        bit *= 2
    return bits


def gather_near(value, axis, before=()):
    held = {0: value}
    for bit in reversed(bits_of(lax.axis_size(axis))):
        source = dict(held)
        for rel in source:
            if rel and before:
                source[rel] = lax.optimization_barrier((source[rel],) + tuple(before))[0]
            held[rel ^ bit] = swap(source[rel], axis, bit)
    return [held[rel] for rel in range(len(held))]


def prepare_kernel(group, cap, pts, counts, rows, cols, live, start, aug, out_rows, out_cols, out_n):
    columns, total = start.shape
    width = pts.shape[1]
    blocks_dev = total // PTS
    slab = blocks_dev * group
    slots = rows.shape[0]
    member = lax.axis_index("grp")

    def local_near(block):
        return (lax.div(block, blocks_dev) ^ member) * blocks_dev + lax.rem(block, blocks_dev)

    def count_far(slot, carry):
        col = cols[slot]
        far = jnp.logical_and(slot < live[0], col >= slab)
        owner = lax.div(col - slab, blocks_dev)
        return tuple(
            old + jnp.where(jnp.logical_and(far, owner == device), 1, 0)
            for device, old in enumerate(carry)
        )

    far_counts = lax.fori_loop(0, slots, count_far, (jnp.int32(0),) * group)
    low = jnp.int32(0)
    room = jnp.int32(0)
    for device in range(group):
        low = low + jnp.where(device < member, cap - far_counts[device], 0)
        room = room + jnp.where(device == member, cap - far_counts[device], 0)

    def place(slot, carry):
        near_rank, filled = carry
        row, col = rows[slot], cols[slot]
        used = slot < live[0]
        far = col >= slab
        mine_far = jnp.logical_and(far, lax.div(col - slab, blocks_dev) == member)
        mine_near = jnp.logical_and(
            jnp.logical_not(far), jnp.logical_and(near_rank >= low, near_rank < low + room)
        )
        mine = jnp.logical_and(used, jnp.logical_or(mine_far, mine_near))

        @pl.when(mine)
        def _():
            out_rows[filled] = local_near(row)
            out_cols[filled] = jnp.where(far, slab + lax.rem(col - slab, blocks_dev), local_near(col))

        near_rank = near_rank + jnp.where(jnp.logical_and(used, jnp.logical_not(far)), 1, 0)
        return (near_rank, filled + jnp.where(mine, 1, 0))

    out_n[0] = lax.fori_loop(0, slots, place, (jnp.int32(0), jnp.int32(0)))[1]

    for block in range(blocks_dev):
        lanes = slice(block * PTS, (block + 1) * PTS)
        wide = pts[lanes, :].astype(jnp.float32)
        norm = lax.dot_general(
            jnp.ones((8, width), jnp.float32),
            wide * wide,
            (((1,), (1,)), ((), ())),
            precision=HIGHEST,
            preferred_element_type=jnp.float32,
        )[0:1, :]
        place_in = lax.broadcasted_iota(jnp.int32, (1, PTS), 1)
        level = norm * (3.0 / width * LOG2E) + jnp.where(place_in < counts[block], 0.0, DEAD)
        high = level.astype(jnp.bfloat16).astype(jnp.float32)
        rest = level - high
        middle = rest.astype(jnp.bfloat16).astype(jnp.float32)
        small = rest - middle
        which = lax.broadcasted_iota(jnp.int32, (EXTRA, PTS), 0)
        tail = jnp.where(which == 0, 1.0, 0.0)
        tail = tail + jnp.where(which == 1, high, 0.0)
        tail = tail + jnp.where(which == 2, middle, 0.0)
        tail = tail + jnp.where(which == 3, small, 0.0)
        aug[0:columns, lanes] = start[:, lanes].astype(jnp.bfloat16)
        aug[columns : columns + EXTRA, lanes] = tail.astype(jnp.bfloat16)


def prepare(points, counts, rows, cols, live, start, group, cap):
    columns, total = start.shape
    return pl.pallas_call(
        functools.partial(prepare_kernel, group, cap),
        out_shape=(
            jax.ShapeDtypeStruct((columns + EXTRA, total), jnp.bfloat16),
            jax.ShapeDtypeStruct((cap,), jnp.int32),
            jax.ShapeDtypeStruct((cap,), jnp.int32),
            jax.ShapeDtypeStruct((1,), jnp.int32),
        ),
        in_specs=[spec(VMEM), spec(SMEM), spec(SMEM), spec(SMEM), spec(SMEM), spec(VMEM)],
        out_specs=(spec(VMEM), spec(SMEM), spec(SMEM), spec(SMEM)),
        compiler_params=pltpu.CompilerParams(vmem_limit_bytes=32 * 2**20),
        cost_estimate=cost(2**30, 2**24),
        name="prepare",
    )(points, counts, rows, cols, live, start)


def message_rels(group):
    groups = [[0]]
    for bit in bits_of(group):
        groups.append([rel for rel in range(group) if rel & bit and rel % bit == 0])
    return groups


def product_shapes(group, blocks_dev, height):
    shapes = [
        jax.ShapeDtypeStruct((len(rels) * blocks_dev, height, PTS), jnp.float32)
        for rels in message_rels(group)
    ]
    shapes.append(jax.ShapeDtypeStruct((blocks_dev, height, PTS), jnp.float32))
    return shapes


def write_products(group, blocks_dev, acc, outs):
    for rels, out in zip(message_rels(group), outs[:-1]):
        for index, rel in enumerate(rels):
            for block in range(blocks_dev):
                out[index * blocks_dev + block] = acc[rel * blocks_dev + block]
    for block in range(blocks_dev):
        outs[-1][block] = acc[group * blocks_dev + block]


def add_products(acc, tile, u_row, u_col, row, col):
    height = acc.shape[1]
    to_row = lax.dot_general(
        u_col, tile, (((1,), (1,)), ((), ())), preferred_element_type=jnp.float32
    )
    acc[row] += to_row[:height]
    to_col = jnp.dot(u_row, tile, preferred_element_type=jnp.float32)
    acc[col] += to_col[:height]


def first_kernel(group, refs):
    pieces = group + 1
    n_ref, rows, cols, counts = refs[:4]
    pts = refs[4 : 4 + pieces]
    augs = refs[4 + pieces : 4 + 2 * pieces]
    tiles_out = refs[4 + 2 * pieces]
    messages = len(message_rels(group)) + 1
    outs = refs[5 + 2 * pieces : 5 + 2 * pieces + messages]
    window, u_win, level_row, level_col, acc = refs[5 + 2 * pieces + messages :]
    kept = tiles_out
    held = pts[0].shape[0]
    width = pts[0].shape[1]
    blocks_dev = held // PTS
    columns = augs[0].shape[0] - EXTRA
    height = acc.shape[1]
    for piece in range(pieces):
        window[piece * held : (piece + 1) * held, :] = pts[piece][...]

    pick = lax.broadcasted_iota(jnp.int32, (EXTRA, 128), 0)
    pick = jnp.where(jnp.logical_and(pick >= 1, pick <= 3), 1.0, 0.0).astype(jnp.bfloat16)
    for piece in range(pieces):
        for block in range(blocks_dev):
            place = piece * blocks_dev + block
            lanes = slice(block * PTS, (block + 1) * PTS)
            u_win[place] = augs[piece][:, lanes]
            tail = augs[piece][columns : columns + EXTRA, lanes]
            if piece < group:
                level_col[place] = lax.dot_general(
                    tail, pick, (((0,), (0,)), ((), ())), preferred_element_type=jnp.float32
                )
            tail = tail.astype(jnp.float32)
            level_row[place] = jnp.broadcast_to(tail[1:2] + tail[2:3] + tail[3:4], (8, PTS))
            acc[place] = jnp.zeros((height, PTS), jnp.float32)
    for block in range(blocks_dev):
        lanes = slice(block * PTS, (block + 1) * PTS)
        place_in = lax.broadcasted_iota(jnp.int32, (columns, PTS), 1)
        own = augs[0][0:columns, lanes].astype(jnp.float32)
        acc[block, 0:columns] = jnp.where(place_in < counts[block], own, 0.0)
        acc[block, columns:height] = jnp.ones((height - columns, PTS), jnp.float32)

    n = n_ref[0]
    step = 256
    scale = 6.0 / width * LOG2E

    def body(index, carry):
        row, col = rows[index], cols[index]
        right = window[pl.ds(pl.multiple_of(col * PTS, PTS), PTS), :]
        right_level = level_row[col][0:1, :]
        for part in range(PTS // step):
            left = window[pl.ds(pl.multiple_of(row * PTS + part * step, step), step), :]
            cross = lax.dot_general(
                left, right, (((1,), (1,)), ((), ())), preferred_element_type=jnp.float32
            )
            left_level = level_col[row, part * step : (part + 1) * step, :]
            left_level = jnp.concatenate([left_level] * (PTS // 128), axis=1)
            value = jnp.exp2(cross * scale - left_level - right_level)
            kept[index, part * step : (part + 1) * step, :] = value.astype(jnp.bfloat16)
        add_products(acc, kept[index], u_win[row], u_win[col], row, col)
        return carry

    lax.fori_loop(0, n, body, 0)
    write_products(group, blocks_dev, acc, outs)


def first_turn(n, rows, cols, counts, pts, augs, group, cap):
    held, width = pts[0].shape
    blocks_dev = held // PTS
    places = (group + 1) * blocks_dev
    tall = augs[0].shape[0]
    height = tall - EXTRA + 8
    pieces = group + 1
    shapes = [jax.ShapeDtypeStruct((cap, PTS, PTS), jnp.bfloat16)]
    shapes += product_shapes(group, blocks_dev, height)

    def kernel(*refs):
        first_kernel(group, refs)

    return pl.pallas_call(
        kernel,
        out_shape=tuple(shapes),
        in_specs=[spec(SMEM)] * 4 + [spec(VMEM)] * (2 * pieces),
        out_specs=(spec(VMEM),) * len(shapes),
        scratch_shapes=[
            VMEM((pieces * held, width), jnp.bfloat16),
            VMEM((places, tall, PTS), jnp.bfloat16),
            VMEM((places, 8, PTS), jnp.float32),
            VMEM((group * blocks_dev, PTS, 128), jnp.float32),
            VMEM((places, height, PTS), jnp.float32),
        ],
        compiler_params=pltpu.CompilerParams(vmem_limit_bytes=36 * 2**20),
        cost_estimate=cost(2**33, 2**25),
        name="first_turn",
    )(n, rows, cols, counts, *pts, *augs)


def scale_kernel(blocks_dev, has_degree, refs):
    degree_in = None if has_degree else refs[0]
    parts = refs[:-3] if has_degree else refs[1:-2]
    if has_degree:
        z_out, gram_out, degree_out = refs[-3:]
    else:
        z_out, gram_out = refs[-2:]
    columns = z_out.shape[0]
    gram = jnp.zeros((columns, columns), jnp.float32)
    for block in range(blocks_dev):
        lanes = slice(block * PTS, (block + 1) * PTS)
        total = parts[0][block]
        for part in parts[1:]:
            total = total + part[block]
        if has_degree:
            degree = total[columns : columns + 1, :]
            degree_out[:, lanes] = jnp.broadcast_to(degree, (8, PTS))
        else:
            degree = degree_in[0:1, lanes]
        z = total[0:columns] / degree
        z_out[:, lanes] = z
        gram = gram + lax.dot_general(
            z, z, (((1,), (1,)), ((), ())), precision=HIGHEST, preferred_element_type=jnp.float32
        )
    gram_out[...] = gram


def scaled_gram(parts, degree, columns):
    blocks_dev = parts[0].shape[0]
    for part in parts:
        blocks_dev = min(blocks_dev, part.shape[0])
    total = blocks_dev * PTS
    shapes = [
        jax.ShapeDtypeStruct((columns, total), jnp.float32),
        jax.ShapeDtypeStruct((columns, columns), jnp.float32),
    ]
    if degree is None:
        shapes.append(jax.ShapeDtypeStruct((8, total), jnp.float32))
        operands = list(parts)
    else:
        operands = [degree] + list(parts)

    def kernel(*refs):
        scale_kernel(blocks_dev, degree is None, refs)

    return pl.pallas_call(
        kernel,
        out_shape=tuple(shapes),
        in_specs=[spec(VMEM)] * len(operands),
        out_specs=(spec(VMEM),) * len(shapes),
        compiler_params=pltpu.CompilerParams(vmem_limit_bytes=32 * 2**20),
        cost_estimate=cost(2**26, 2**21),
        name="scaled_gram",
    )(*operands)


def inverse_factor(gram):
    size = gram.shape[0]
    row_id = lax.broadcasted_iota(jnp.int32, (size, size), 0)
    col_id = lax.broadcasted_iota(jnp.int32, (size, size), 1)
    eye = jnp.where(row_id == col_id, 1.0, 0.0)
    whole = jnp.concatenate([gram, eye], axis=1)
    wide = 2 * size
    count = size // 8
    groups = [whole[8 * g : 8 * g + 8, :] for g in range(count)]
    within = lax.broadcasted_iota(jnp.int32, (8, wide), 0)

    def spread_row(value, row):
        return jnp.broadcast_to(value[row : row + 1, :], (8, wide))

    results = []
    for g in range(count):
        spread = [
            [
                jnp.broadcast_to(groups[other][:, 8 * g + k : 8 * g + k + 1], (8, wide))
                for other in range(g, count)
            ]
            for k in range(8)
        ]
        pivots = jnp.ones((8, wide), jnp.float32)
        for j in range(8):
            column = spread[j]
            pivot = spread_row(column[0], j)
            pivots = jnp.where(within == j, pivot, pivots)
            over = 1.0 / pivot
            below = jnp.where(within > j, column[0], 0.0)
            for k in range(j + 1, 8):
                share = spread_row(column[0], k) * over
                spread[k][0] = spread[k][0] - below * share
                for other in range(1, count - g):
                    spread[k][other] = spread[k][other] - column[other] * share
            top = spread_row(groups[g], j) * over
            groups[g] = groups[g] - below * top
            for other in range(1, count - g):
                groups[g + other] = groups[g + other] - column[other] * top
        results.append(groups[g] * lax.rsqrt(pivots))
    return jnp.concatenate(results, axis=0)[:, size:wide]


def second_kernel(group, refs):
    pieces = group + 1
    n_ref, rows, cols, counts, gram = refs[:5]
    zs = refs[5 : 5 + pieces]
    tiles = refs[5 + pieces]
    messages = len(message_rels(group)) + 1
    outs = refs[6 + pieces : 6 + pieces + messages]
    u_win, acc = refs[6 + pieces + messages :]
    columns, held = zs[0].shape
    blocks_dev = held // PTS
    n = n_ref[0]

    inverse = inverse_factor(gram[...])
    for piece in range(pieces):
        for block in range(blocks_dev):
            place = piece * blocks_dev + block
            vec = jnp.dot(
                inverse,
                zs[piece][:, block * PTS : (block + 1) * PTS],
                precision=HIGHEST,
                preferred_element_type=jnp.float32,
            ).astype(jnp.bfloat16)
            u_win[place] = vec
            if piece == 0:
                place_in = lax.broadcasted_iota(jnp.int32, (columns, PTS), 1)
                acc[place] = jnp.where(place_in < counts[block], vec.astype(jnp.float32), 0.0)
            else:
                acc[place] = jnp.zeros((columns, PTS), jnp.float32)

    def body(index, carry):
        row, col = rows[index], cols[index]
        add_products(acc, tiles[index], u_win[row], u_win[col], row, col)
        return carry

    lax.fori_loop(0, n, body, 0)
    write_products(group, blocks_dev, acc, outs)


def next_turn(n, rows, cols, counts, gram, zs, tiles, group, cap):
    columns, held = zs[0].shape
    blocks_dev = held // PTS
    pieces = group + 1
    places = pieces * blocks_dev
    shapes = product_shapes(group, blocks_dev, columns)

    def kernel(*refs):
        second_kernel(group, refs)

    return pl.pallas_call(
        kernel,
        out_shape=tuple(shapes),
        in_specs=[spec(SMEM)] * 4 + [spec(VMEM)] * (2 + pieces),
        out_specs=(spec(VMEM),) * len(shapes),
        scratch_shapes=[
            VMEM((places, columns, PTS), jnp.bfloat16),
            VMEM((places, columns, PTS), jnp.float32),
        ],
        compiler_params=pltpu.CompilerParams(vmem_limit_bytes=24 * 2**20),
        cost_estimate=cost(2**32, 2**24),
        name="next_turn",
    )(n, rows, cols, counts, gram, *zs, tiles)


def embed_kernel(gram, z, out):
    out[...] = jnp.dot(
        inverse_factor(gram[...]), z[...], precision=HIGHEST, preferred_element_type=jnp.float32
    )


def embedding(gram, z):
    return pl.pallas_call(
        embed_kernel,
        out_shape=jax.ShapeDtypeStruct(z.shape, jnp.float32),
        in_specs=[spec(VMEM)] * 2,
        out_specs=spec(VMEM),
        cost_estimate=cost(2**30, 2**20),
        name="embedding",
    )(gram, z)


def sum_products(messages, group, blocks_dev):
    rels = message_rels(group)
    parts = {}
    for names, message in zip(rels[1:], messages[1:-1]):
        for index, rel in enumerate(names):
            parts[rel] = [message[index * blocks_dev : (index + 1) * blocks_dev]]
    final = [messages[0], from_behind(messages[-1], "blk", 1)]
    for bit, names, message in zip(bits_of(group), rels[1:], messages[1:-1]):
        if bit > 1:
            message = jnp.concatenate([sum(parts[rel][1:], parts[rel][0]) for rel in names], 0)
        got = swap(message, "grp", bit)
        for index, rel in enumerate(names):
            target = rel ^ bit
            if target == 0:
                final.append(got)
            else:
                parts[target].append(got[index * blocks_dev : (index + 1) * blocks_dev])
    return final


def all_sum(value, axes):
    for axis in axes:
        bits = bits_of(lax.axis_size(axis))
        while bits:
            now, bits = bits[:3], bits[3:]
            base = now[0]
            terms = [value] + [swap(value, axis, base * rel) for rel in range(1, 2 ** len(now))]
            while len(terms) > 1:
                terms = [left + right for left, right in zip(terms[::2], terms[1::2])]
            value = terms[0]
    return value


def per_device(points, counts, pair_rows, pair_cols, pair_live, start):
    group = lax.axis_size("grp")
    blocks_dev = counts.shape[0]
    columns = start.shape[0]
    slots = pair_rows.shape[0]
    cap = max(-(-slots // group), blocks_dev * blocks_dev * group)
    aug, rows, cols, n = prepare(
        points, counts, pair_rows, pair_cols, pair_live, start, group, cap
    )
    augs = gather_near(aug, "grp") + [from_behind(aug, "blk", -1)]
    far = from_behind(points, "blk", -1)
    pts = gather_near(points, "grp", augs + [far]) + [far]
    tiles, *messages = first_turn(n, rows, cols, counts, pts, augs, group, cap)
    z, gram, degree = scaled_gram(sum_products(messages, group, blocks_dev), None, columns)
    for turn in range(1, ITERS):
        zs = gather_near(z, "grp") + [from_behind(z, "blk", -1)]
        gram = all_sum(gram, ("grp", "blk"))
        messages = next_turn(n, rows, cols, counts, gram, zs, tiles, group, cap)
        z, gram = scaled_gram(sum_products(messages, group, blocks_dev), degree, columns)
    return embedding(all_sum(gram, ("grp", "blk")), z)


def solution(mesh):
    in_specs = (
        P(("blk", "grp"), None),
        P(("blk", "grp")),
        P("blk"),
        P("blk"),
        P("blk"),
        P(None, ("blk", "grp")),
    )
    out_specs = P(None, ("blk", "grp"))
    return jax.shard_map(
        per_device, mesh=mesh, in_specs=in_specs, out_specs=out_specs, check_vma=False
    )
```

```python
import functools

import jax
import jax.numpy as jnp
from jax import lax
from jax.experimental import pallas as pl
from jax.experimental.pallas import tpu as pltpu
from jax.sharding import PartitionSpec as P

PTS = 512
ITERS = 2
LOG2E = 1.4426950408889634
DEAD = 65536.0
EXTRA = 16
VMEM = pltpu.VMEM
SMEM = pltpu.SMEM
HIGHEST = lax.Precision.HIGHEST


def cost(flops, moved):
    return pl.CostEstimate(flops=int(flops), bytes_accessed=int(moved), transcendentals=0)


def spec(space):
    return pl.BlockSpec(memory_space=space)


def swap(value, axis, bit):
    count = lax.axis_size(axis)
    return lax.ppermute(value, axis, [(source, source ^ bit) for source in range(count)])


def from_behind(value, axis, steps):
    count = lax.axis_size(axis)
    initial, last = (max(0, -steps), min(count, count - steps))
    return lax.ppermute(value, axis, [(source, source + steps) for source in range(initial, last)])


def bits_of(count):
    bits = []
    bit = 1
    while bit < count:
        bits.append(bit)
        bit *= 2
    return bits


def gather_near(value, axis):
    held = {0: value}
    for bit in reversed(bits_of(lax.axis_size(axis))):
        for rel in list(held):
            held[rel ^ bit] = swap(held[rel], axis, bit)
    return [held[rel] for rel in range(len(held))]


def gather_far_bits(value):
    held = {0: value}
    for bit in reversed(bits_of(lax.axis_size("grp"))[1:]):
        for rel in list(held):
            held[rel ^ bit] = swap(held[rel], "grp", bit)
    held.pop(0)
    return held


def augment_kernel(pts, counts, start, aug):
    columns, total = start.shape
    width = pts.shape[1]
    for block in range(total // PTS):
        lanes = slice(block * PTS, (block + 1) * PTS)
        wide = pts[lanes, :].astype(jnp.float32)
        norm = lax.dot_general(
            jnp.ones((8, width), jnp.float32),
            wide * wide,
            (((1,), (1,)), ((), ())),
            precision=HIGHEST,
            preferred_element_type=jnp.float32,
        )[0:1, :]
        place_in = lax.broadcasted_iota(jnp.int32, (1, PTS), 1)
        level = norm * (3.0 / width * LOG2E) + jnp.where(place_in < counts[block], 0.0, DEAD)
        high = level.astype(jnp.bfloat16).astype(jnp.float32)
        rest = level - high
        middle = rest.astype(jnp.bfloat16).astype(jnp.float32)
        small = rest - middle
        which = lax.broadcasted_iota(jnp.int32, (EXTRA, PTS), 0)
        tail = jnp.where(which == 0, 1.0, 0.0)
        tail = tail + jnp.where(which == 1, high, 0.0)
        tail = tail + jnp.where(which == 2, middle, 0.0)
        tail = tail + jnp.where(which == 3, small, 0.0)
        aug[0:columns, lanes] = start[:, lanes].astype(jnp.bfloat16)
        aug[columns : columns + EXTRA, lanes] = tail.astype(jnp.bfloat16)


def augment(points, counts, start):
    columns, total = start.shape
    return pl.pallas_call(
        augment_kernel,
        out_shape=jax.ShapeDtypeStruct((columns + EXTRA, total), jnp.bfloat16),
        in_specs=[spec(VMEM), spec(SMEM), spec(VMEM)],
        out_specs=spec(VMEM),
        cost_estimate=cost(2**30, 2**24),
        compiler_params=pltpu.CompilerParams(vmem_limit_bytes=24 * 2**20),
        name="augment",
    )(points, counts, start)


def is_early(place, group, blocks_dev):
    near_by = jnp.logical_and(place < min(2, group) * blocks_dev, place < group * blocks_dev)
    return jnp.logical_or(near_by, lax.rem(place, blocks_dev) < blocks_dev // 2)


def listing_kernel(group, cap, blocks_dev, rows, cols, live, out_rows, out_cols, out_n):
    slab = blocks_dev * group
    slots = rows.shape[0]
    member = lax.axis_index("grp")

    def local_near(block):
        return (lax.div(block, blocks_dev) ^ member) * blocks_dev + lax.rem(block, blocks_dev)

    def count_far(slot, carry):
        col = cols[slot]
        far = jnp.logical_and(slot < live[0], col >= slab)
        owner = lax.div(col - slab, blocks_dev)
        return tuple(
            old + jnp.where(jnp.logical_and(far, owner == device), 1, 0)
            for device, old in enumerate(carry)
        )

    far_counts = lax.fori_loop(0, slots, count_far, (jnp.int32(0),) * group)
    low = jnp.int32(0)
    room = jnp.int32(0)
    for device in range(group):
        low = low + jnp.where(device < member, cap - far_counts[device], 0)
        room = room + jnp.where(device == member, cap - far_counts[device], 0)

    def place_those(wanted, filled):
        def place(slot, carry):
            near_rank, filled = carry
            row, col = rows[slot], cols[slot]
            used = slot < live[0]
            far = col >= slab
            mine_far = jnp.logical_and(far, lax.div(col - slab, blocks_dev) == member)
            mine_near = jnp.logical_and(
                jnp.logical_not(far), jnp.logical_and(near_rank >= low, near_rank < low + room)
            )
            row_place = local_near(row)
            col_place = jnp.where(far, slab + lax.rem(col - slab, blocks_dev), local_near(col))
            early = jnp.logical_and(
                is_early(row_place, group, blocks_dev), is_early(col_place, group, blocks_dev)
            )
            mine = jnp.logical_and(used, jnp.logical_or(mine_far, mine_near))
            mine = jnp.logical_and(mine, early if wanted else jnp.logical_not(early))

            @pl.when(mine)
            def _():
                out_rows[filled] = row_place
                out_cols[filled] = col_place

            near_rank = near_rank + jnp.where(jnp.logical_and(used, jnp.logical_not(far)), 1, 0)
            return (near_rank, filled + jnp.where(mine, 1, 0))

        return lax.fori_loop(0, slots, place, (jnp.int32(0), filled))[1]

    early_count = place_those(True, jnp.int32(0))
    out_n[0] = jnp.int32(0)
    out_n[1] = early_count
    out_n[2] = place_those(False, early_count)


def listing(rows, cols, live, group, cap, blocks_dev):
    return pl.pallas_call(
        functools.partial(listing_kernel, group, cap, blocks_dev),
        out_shape=(
            jax.ShapeDtypeStruct((cap,), jnp.int32),
            jax.ShapeDtypeStruct((cap,), jnp.int32),
            jax.ShapeDtypeStruct((3,), jnp.int32),
        ),
        in_specs=[spec(SMEM)] * 3,
        out_specs=(spec(SMEM),) * 3,
        cost_estimate=cost(2**20, 2**10),
        name="listing",
    )(rows, cols, live)


def message_rels(group):
    groups = [[0]]
    for bit in bits_of(group):
        groups.append([rel for rel in range(group) if rel & bit and rel % bit == 0])
    return groups


def product_shapes(group, blocks_dev, height):
    shapes = [
        jax.ShapeDtypeStruct((len(rels) * blocks_dev, height, PTS), jnp.float32)
        for rels in message_rels(group)
    ]
    shapes.append(jax.ShapeDtypeStruct((blocks_dev, height, PTS), jnp.float32))
    return shapes


def write_products(group, blocks_dev, acc, outs):
    for rels, out in zip(message_rels(group), outs[:-1]):
        for index, rel in enumerate(rels):
            for block in range(blocks_dev):
                out[index * blocks_dev + block] = acc[rel * blocks_dev + block]
    for block in range(blocks_dev):
        outs[-1][block] = acc[group * blocks_dev + block]


def add_products(acc, tile, u_row, u_col, row, col):
    height = acc.shape[1]
    to_row = lax.dot_general(
        u_col, tile, (((1,), (1,)), ((), ())), preferred_element_type=jnp.float32
    )
    acc[row] += to_row[:height]
    to_col = jnp.dot(u_row, tile, preferred_element_type=jnp.float32)
    acc[col] += to_col[:height]


def setup_first(group, augs, counts, u_win, level_row, level_col, acc):
    columns = augs[0].shape[0] - EXTRA
    height = acc.shape[1]
    blocks_dev = augs[0].shape[1] // PTS
    pick = lax.broadcasted_iota(jnp.int32, (EXTRA, 128), 0)
    pick = jnp.where(jnp.logical_and(pick >= 1, pick <= 3), 1.0, 0.0).astype(jnp.bfloat16)
    for piece in range(group + 1):
        for block in range(blocks_dev):
            place = piece * blocks_dev + block
            lanes = slice(block * PTS, (block + 1) * PTS)
            u_win[place] = augs[piece][:, lanes]
            tail = augs[piece][columns : columns + EXTRA, lanes]
            if piece < group:
                level_col[place] = lax.dot_general(
                    tail, pick, (((0,), (0,)), ((), ())), preferred_element_type=jnp.float32
                )
            tail = tail.astype(jnp.float32)
            level_row[place] = jnp.broadcast_to(tail[1:2] + tail[2:3] + tail[3:4], (8, PTS))
            acc[place] = jnp.zeros((height, PTS), jnp.float32)
    for block in range(blocks_dev):
        lanes = slice(block * PTS, (block + 1) * PTS)
        place_in = lax.broadcasted_iota(jnp.int32, (columns, PTS), 1)
        own = augs[0][0:columns, lanes].astype(jnp.float32)
        acc[block, 0:columns] = jnp.where(place_in < counts[block], own, 0.0)
        acc[block, columns:height] = jnp.ones((height - columns, PTS), jnp.float32)


def make_tiles(low, high, rows, cols, window, u_win, level_row, level_col, kept, acc):
    width = window.shape[1]
    step = 256
    scale = 6.0 / width * LOG2E

    def body(index, carry):
        row, col = rows[index], cols[index]
        right = window[pl.ds(pl.multiple_of(col * PTS, PTS), PTS), :]
        right_level = level_row[col][0:1, :]
        for part in range(PTS // step):
            left = window[pl.ds(pl.multiple_of(row * PTS + part * step, step), step), :]
            cross = lax.dot_general(
                left, right, (((1,), (1,)), ((), ())), preferred_element_type=jnp.float32
            )
            left_level = level_col[row, part * step : (part + 1) * step, :]
            left_level = jnp.concatenate([left_level] * (PTS // 128), axis=1)
            value = jnp.exp2(cross * scale - left_level - right_level)
            kept[index, part * step : (part + 1) * step, :] = value.astype(jnp.bfloat16)
        add_products(acc, kept[index], u_win[row], u_win[col], row, col)
        return carry

    lax.fori_loop(low, high, body, 0)


def early_tiles(places, n, rows, cols, counts, pts, augs, group, cap):
    width = pts[0].shape[1]
    blocks_dev = augs[0].shape[1] // PTS
    total = (group + 1) * blocks_dev
    tall = augs[0].shape[0]
    height = tall - EXTRA + 8
    shapes = (
        jax.ShapeDtypeStruct((total, tall, PTS), jnp.bfloat16),
        jax.ShapeDtypeStruct((total, 8, PTS), jnp.float32),
        jax.ShapeDtypeStruct((group * blocks_dev, PTS, 128), jnp.float32),
        jax.ShapeDtypeStruct((cap, PTS, PTS), jnp.bfloat16),
        jax.ShapeDtypeStruct((total, height, PTS), jnp.float32),
    )

    def kernel(*refs):
        n_ref, row_ref, col_ref, count_ref = refs[:4]
        pt_refs = refs[4 : 4 + len(pts)]
        aug_refs = refs[4 + len(pts) : 4 + len(pts) + len(augs)]
        u_win, level_row, level_col, kept, acc, window = refs[4 + len(pts) + len(augs) :]
        for place, piece in zip(places, pt_refs):
            window[place * PTS : place * PTS + piece.shape[0], :] = piece[...]
        setup_first(group, aug_refs, count_ref, u_win, level_row, level_col, acc)
        make_tiles(
            n_ref[0], n_ref[1], row_ref, col_ref, window, u_win, level_row, level_col, kept, acc
        )

    return pl.pallas_call(
        kernel,
        out_shape=shapes,
        in_specs=[spec(SMEM)] * 4 + [spec(VMEM)] * (len(pts) + len(augs)),
        out_specs=(spec(VMEM),) * len(shapes),
        scratch_shapes=[VMEM((total * PTS, width), jnp.bfloat16)],
        cost_estimate=cost(2**20, 2**20),
        compiler_params=pltpu.CompilerParams(vmem_limit_bytes=20 * 2**20),
        name="early_tiles",
    )(n, rows, cols, counts, *pts, *augs)


def late_tiles(places, n, rows, cols, pts, state, group, blocks_dev):
    u_win, level_row, level_col, kept, acc = state
    total, height = acc.shape[:2]
    width = pts[0].shape[1]
    shapes = [jax.ShapeDtypeStruct(kept.shape, kept.dtype)]
    shapes += product_shapes(group, blocks_dev, height)
    first = 3 + len(pts)

    def kernel(*refs):
        n_ref, row_ref, col_ref = refs[:3]
        pt_refs = refs[3:first]
        u_win, level_row, level_col, acc_in, kept = refs[first : first + 5]
        outs = refs[first + 5 : -2]
        window, acc = refs[-2:]
        for place, piece in zip(places, pt_refs):
            window[place * PTS : place * PTS + piece.shape[0], :] = piece[...]
        acc[...] = acc_in[...]
        make_tiles(
            n_ref[1], n_ref[2], row_ref, col_ref, window, u_win, level_row, level_col, kept, acc
        )
        write_products(group, blocks_dev, acc, outs)

    return pl.pallas_call(
        kernel,
        out_shape=tuple(shapes),
        in_specs=[spec(SMEM)] * 3 + [spec(VMEM)] * (len(pts) + 4),
        out_specs=(spec(VMEM),) * len(shapes),
        scratch_shapes=[
            VMEM((total * PTS, width), jnp.bfloat16),
            VMEM((total, height, PTS), jnp.float32),
        ],
        cost_estimate=cost(2**33, 2**25),
        compiler_params=pltpu.CompilerParams(vmem_limit_bytes=20 * 2**20),
        name="late_tiles",
    )(n, rows, cols, *pts, u_win, level_row, level_col, acc)


def scale_kernel(blocks_dev, has_degree, refs):
    degree_in = None if has_degree else refs[0]
    parts = refs[:-3] if has_degree else refs[1:-2]
    if has_degree:
        z_out, gram_out, degree_out = refs[-3:]
    else:
        z_out, gram_out = refs[-2:]
    columns = z_out.shape[0]
    gram = jnp.zeros((columns, columns), jnp.float32)
    for block in range(blocks_dev):
        lanes = slice(block * PTS, (block + 1) * PTS)
        total = parts[0][block]
        for part in parts[1:]:
            total = total + part[block]
        if has_degree:
            degree = total[columns : columns + 1, :]
            degree_out[:, lanes] = jnp.broadcast_to(degree, (8, PTS))
        else:
            degree = degree_in[0:1, lanes]
        z = total[0:columns] / degree
        z_out[:, lanes] = z
        gram = gram + lax.dot_general(
            z, z, (((1,), (1,)), ((), ())), precision=HIGHEST, preferred_element_type=jnp.float32
        )
    gram_out[...] = gram


def scaled_gram(parts, degree, columns):
    blocks_dev = parts[0].shape[0]
    for part in parts:
        blocks_dev = min(blocks_dev, part.shape[0])
    total = blocks_dev * PTS
    shapes = [
        jax.ShapeDtypeStruct((columns, total), jnp.float32),
        jax.ShapeDtypeStruct((columns, columns), jnp.float32),
    ]
    if degree is None:
        shapes.append(jax.ShapeDtypeStruct((8, total), jnp.float32))
        operands = list(parts)
    else:
        operands = [degree] + list(parts)

    def kernel(*refs):
        scale_kernel(blocks_dev, degree is None, refs)

    return pl.pallas_call(
        kernel,
        out_shape=tuple(shapes),
        in_specs=[spec(VMEM)] * len(operands),
        out_specs=(spec(VMEM),) * len(shapes),
        compiler_params=pltpu.CompilerParams(vmem_limit_bytes=32 * 2**20),
        cost_estimate=cost(2**26, 2**21),
        name="scaled_gram",
    )(*operands)


def inverse_factor(gram):
    size = gram.shape[0]
    row_id = lax.broadcasted_iota(jnp.int32, (size, size), 0)
    col_id = lax.broadcasted_iota(jnp.int32, (size, size), 1)
    eye = jnp.where(row_id == col_id, 1.0, 0.0)
    whole = jnp.concatenate([gram, eye], axis=1)
    wide = 2 * size
    count = size // 8
    groups = [whole[8 * g : 8 * g + 8, :] for g in range(count)]
    within = lax.broadcasted_iota(jnp.int32, (8, wide), 0)

    def spread_row(value, row):
        return jnp.broadcast_to(value[row : row + 1, :], (8, wide))

    results = []
    for g in range(count):
        spread = [
            [
                jnp.broadcast_to(groups[other][:, 8 * g + k : 8 * g + k + 1], (8, wide))
                for other in range(g, count)
            ]
            for k in range(8)
        ]
        pivots = jnp.ones((8, wide), jnp.float32)
        for j in range(8):
            column = spread[j]
            pivot = spread_row(column[0], j)
            pivots = jnp.where(within == j, pivot, pivots)
            over = 1.0 / pivot
            below = jnp.where(within > j, column[0], 0.0)
            for k in range(j + 1, 8):
                share = spread_row(column[0], k) * over
                spread[k][0] = spread[k][0] - below * share
                for other in range(1, count - g):
                    spread[k][other] = spread[k][other] - column[other] * share
            top = spread_row(groups[g], j) * over
            groups[g] = groups[g] - below * top
            for other in range(1, count - g):
                groups[g + other] = groups[g + other] - column[other] * top
        results.append(groups[g] * lax.rsqrt(pivots))
    return jnp.concatenate(results, axis=0)[:, size:wide]


def second_kernel(group, refs):
    pieces = group + 1
    n_ref, rows, cols, counts, gram = refs[:5]
    zs = refs[5 : 5 + pieces]
    tiles = refs[5 + pieces : 7 + pieces]
    messages = len(message_rels(group)) + 1
    outs = refs[7 + pieces : 7 + pieces + messages]
    u_win, acc = refs[7 + pieces + messages :]
    columns, held = zs[0].shape
    blocks_dev = held // PTS
    inverse = inverse_factor(gram[...])
    for piece in range(pieces):
        for block in range(blocks_dev):
            place = piece * blocks_dev + block
            vec = jnp.dot(
                inverse,
                zs[piece][:, block * PTS : (block + 1) * PTS],
                precision=HIGHEST,
                preferred_element_type=jnp.float32,
            ).astype(jnp.bfloat16)
            u_win[place] = vec
            if piece == 0:
                place_in = lax.broadcasted_iota(jnp.int32, (columns, PTS), 1)
                acc[place] = jnp.where(place_in < counts[block], vec.astype(jnp.float32), 0.0)
            else:
                acc[place] = jnp.zeros((columns, PTS), jnp.float32)

    for stage, kept in enumerate(tiles):

        def body(index, carry):
            row, col = rows[index], cols[index]
            add_products(acc, kept[index], u_win[row], u_win[col], row, col)
            return carry

        lax.fori_loop(n_ref[stage], n_ref[stage + 1], body, 0)
    write_products(group, blocks_dev, acc, outs)


def next_turn(n, rows, cols, counts, gram, zs, tiles, group, cap):
    columns, held = zs[0].shape
    blocks_dev = held // PTS
    pieces = group + 1
    places = pieces * blocks_dev
    shapes = product_shapes(group, blocks_dev, columns)

    def kernel(*refs):
        second_kernel(group, refs)

    return pl.pallas_call(
        kernel,
        out_shape=tuple(shapes),
        in_specs=[spec(SMEM)] * 4 + [spec(VMEM)] * (3 + pieces),
        out_specs=(spec(VMEM),) * len(shapes),
        scratch_shapes=[
            VMEM((places, columns, PTS), jnp.bfloat16),
            VMEM((places, columns, PTS), jnp.float32),
        ],
        compiler_params=pltpu.CompilerParams(vmem_limit_bytes=24 * 2**20),
        cost_estimate=cost(2**32, 2**24),
        name="next_turn",
    )(n, rows, cols, counts, gram, *zs, *tiles)


def embed_kernel(gram, z, out):
    out[...] = jnp.dot(
        inverse_factor(gram[...]), z[...], precision=HIGHEST, preferred_element_type=jnp.float32
    )


def embedding(gram, z):
    return pl.pallas_call(
        embed_kernel,
        out_shape=jax.ShapeDtypeStruct(z.shape, jnp.float32),
        in_specs=[spec(VMEM)] * 2,
        out_specs=spec(VMEM),
        cost_estimate=cost(2**30, 2**20),
        name="embedding",
    )(gram, z)


def sum_products(messages, group, blocks_dev):
    rels = message_rels(group)
    parts = {}
    for names, message in zip(rels[1:], messages[1:-1]):
        for index, rel in enumerate(names):
            parts[rel] = [message[index * blocks_dev : (index + 1) * blocks_dev]]
    final = [messages[0], from_behind(messages[-1], "blk", 1)]
    for bit, names, message in zip(bits_of(group), rels[1:], messages[1:-1]):
        if bit > 1:
            message = jnp.concatenate([sum(parts[rel][1:], parts[rel][0]) for rel in names], 0)
        got = swap(message, "grp", bit)
        for index, rel in enumerate(names):
            target = rel ^ bit
            if target == 0:
                final.append(got)
            else:
                parts[target].append(got[index * blocks_dev : (index + 1) * blocks_dev])
    return final


def all_sum(value):
    for bit in bits_of(lax.axis_size("grp")):
        value = value + swap(value, "grp", bit)
    return jnp.sum(lax.all_gather(value, "blk", axis=0, tiled=False), axis=0)


def per_device(points, counts, pair_rows, pair_cols, pair_live, start):
    group = lax.axis_size("grp")
    blocks_dev = counts.shape[0]
    columns = start.shape[0]
    slots = pair_rows.shape[0]
    cap = max(-(-slots // group), blocks_dev * blocks_dev * group)
    half = (blocks_dev // 2) * PTS
    aug = augment(points, counts, start)
    mate_aug = swap(aug, "grp", 1)
    far_aug = from_behind(aug, "blk", -1)
    cross_aug = gather_far_bits(aug)
    chunks = [points[:half], points[half:]]
    chunks[1] = lax.optimization_barrier((chunks[1], mate_aug))[0]
    rows, cols, n = listing(pair_rows, pair_cols, pair_live, group, cap, blocks_dev)
    far = [from_behind(chunk, "blk", -1) for chunk in chunks]
    crossed = [gather_far_bits(chunk) for chunk in chunks]
    there = (mate_aug, far[0], far_aug, *cross_aug.values(), *crossed[0].values())
    tied = lax.optimization_barrier(there)
    mate_aug, far[0], far_aug = tied[:3]
    for index, rel in enumerate(cross_aug):
        cross_aug[rel] = tied[3 + index]
        crossed[0][rel] = tied[3 + len(cross_aug) + index]
    augs = {0: aug, 1: mate_aug}
    for rel, value in cross_aug.items():
        augs[rel] = value
        augs[rel ^ 1] = swap(value, "grp", 1)
    augs = [augs[rel] for rel in range(group)] + [far_aug]
    mate = swap(points, "grp", 1)

    def placed(index):
        offset = index * (blocks_dev // 2)
        found = [(group * blocks_dev + offset, far[index])]
        for rel, value in crossed[index].items():
            found.append((rel * blocks_dev + offset, value))
            found.append(((rel ^ 1) * blocks_dev + offset, swap(value, "grp", 1)))
        return found

    early = [(0, points), (blocks_dev, mate)] + placed(0)
    places, pts = zip(*early)
    state = early_tiles(places, n, rows, cols, counts, pts, augs, group, cap)
    tied = lax.optimization_barrier((far[1], *crossed[1].values(), state[4]))
    far[1] = tied[0]
    crossed[1] = dict(zip(crossed[1], tied[1:-1]))
    state = (*state[:4], tied[-1])
    places, pts = zip(*(early + placed(1)))
    late, *messages = late_tiles(places, n, rows, cols, pts, state, group, blocks_dev)
    tiles = (state[3], late)
    z, gram, degree = scaled_gram(sum_products(messages, group, blocks_dev), None, columns)
    for turn in range(1, ITERS):
        zs = gather_near(z, "grp") + [from_behind(z, "blk", -1)]
        gram = all_sum(gram)
        messages = next_turn(n, rows, cols, counts, gram, zs, tiles, group, cap)
        z, gram = scaled_gram(sum_products(messages, group, blocks_dev), degree, columns)
    return embedding(all_sum(gram), z)


def solution(mesh):
    in_specs = (
        P(("blk", "grp"), None),
        P(("blk", "grp")),
        P("blk"),
        P("blk"),
        P("blk"),
        P(None, ("blk", "grp")),
    )
    out_specs = P(None, ("blk", "grp"))
    return jax.shard_map(
        per_device, mesh=mesh, in_specs=in_specs, out_specs=out_specs, check_vma=False
    )
```

```python
import functools

import jax
import jax.numpy as jnp
from jax import lax
from jax.experimental import pallas as pl
from jax.experimental.pallas import tpu as pltpu
from jax.sharding import PartitionSpec as P

PTS = 512
ITERS = 2
LOG2E = 1.4426950408889634
DEAD = 65536.0
EXTRA = 16
VMEM = pltpu.VMEM
SMEM = pltpu.SMEM
HIGHEST = lax.Precision.HIGHEST


def cost(flops, moved):
    return pl.CostEstimate(flops=int(flops), bytes_accessed=int(moved), transcendentals=0)


def spec(space):
    return pl.BlockSpec(memory_space=space)


def swap(value, axis, bit):
    count = lax.axis_size(axis)
    return lax.ppermute(value, axis, [(source, source ^ bit) for source in range(count)])


def from_behind(value, axis, steps):
    count = lax.axis_size(axis)
    initial, last = (max(0, -steps), min(count, count - steps))
    return lax.ppermute(value, axis, [(source, source + steps) for source in range(initial, last)])


def bits_of(count):
    bits = []
    bit = 1
    while bit < count:
        bits.append(bit)
        bit *= 2
    return bits


def gather_near(value, axis):
    held = {0: value}
    for bit in reversed(bits_of(lax.axis_size(axis))):
        for rel in list(held):
            held[rel ^ bit] = swap(held[rel], axis, bit)
    return [held[rel] for rel in range(len(held))]


def gather_far_bits(value):
    held = {0: value}
    for bit in reversed(bits_of(lax.axis_size("grp"))[1:]):
        for rel in list(held):
            held[rel ^ bit] = swap(held[rel], "grp", bit)
    held.pop(0)
    return held


def augment_kernel(pts, counts, start, aug):
    columns, total = start.shape
    width = pts.shape[1]
    for block in range(total // PTS):
        lanes = slice(block * PTS, (block + 1) * PTS)
        wide = pts[lanes, :].astype(jnp.float32)
        norm = lax.dot_general(
            jnp.ones((8, width), jnp.float32),
            wide * wide,
            (((1,), (1,)), ((), ())),
            precision=HIGHEST,
            preferred_element_type=jnp.float32,
        )[0:1, :]
        place_in = lax.broadcasted_iota(jnp.int32, (1, PTS), 1)
        level = norm * (3.0 / width * LOG2E) + jnp.where(place_in < counts[block], 0.0, DEAD)
        high = level.astype(jnp.bfloat16).astype(jnp.float32)
        rest = level - high
        middle = rest.astype(jnp.bfloat16).astype(jnp.float32)
        small = rest - middle
        which = lax.broadcasted_iota(jnp.int32, (EXTRA, PTS), 0)
        tail = jnp.where(which == 0, 1.0, 0.0)
        tail = tail + jnp.where(which == 1, high, 0.0)
        tail = tail + jnp.where(which == 2, middle, 0.0)
        tail = tail + jnp.where(which == 3, small, 0.0)
        aug[0:columns, lanes] = start[:, lanes].astype(jnp.bfloat16)
        aug[columns : columns + EXTRA, lanes] = tail.astype(jnp.bfloat16)


def augment(points, counts, start):
    columns, total = start.shape
    return pl.pallas_call(
        augment_kernel,
        out_shape=jax.ShapeDtypeStruct((columns + EXTRA, total), jnp.bfloat16),
        in_specs=[spec(VMEM), spec(SMEM), spec(VMEM)],
        out_specs=spec(VMEM),
        cost_estimate=cost(2**30, 2**24),
        compiler_params=pltpu.CompilerParams(vmem_limit_bytes=8 * 2**20),
        name="augment",
    )(points, counts, start)


def is_early(place, group, blocks_dev):
    near_by = jnp.logical_and(place < min(2, group) * blocks_dev, place < group * blocks_dev)
    return jnp.logical_or(near_by, lax.rem(place, blocks_dev) < blocks_dev // 2)


def listing_kernel(group, cap, early_cap, blocks_dev, rows, cols, live, out_rows, out_cols, out_n):
    slab = blocks_dev * group
    slots = rows.shape[0]
    member = lax.axis_index("grp")

    def local_near(block):
        return (lax.div(block, blocks_dev) ^ member) * blocks_dev + lax.rem(block, blocks_dev)

    def count_far(slot, carry):
        col = cols[slot]
        far = jnp.logical_and(slot < live[0], col >= slab)
        owner = lax.div(col - slab, blocks_dev)
        return tuple(
            old + jnp.where(jnp.logical_and(far, owner == device), 1, 0)
            for device, old in enumerate(carry)
        )

    far_counts = lax.fori_loop(0, slots, count_far, (jnp.int32(0),) * group)
    low = jnp.int32(0)
    room = jnp.int32(0)
    for device in range(group):
        low = low + jnp.where(device < member, cap - far_counts[device], 0)
        room = room + jnp.where(device == member, cap - far_counts[device], 0)

    def place_those(wanted, filled):
        def place(slot, carry):
            near_rank, early_rank, filled = carry
            row, col = rows[slot], cols[slot]
            used = slot < live[0]
            far = col >= slab
            mine_far = jnp.logical_and(far, lax.div(col - slab, blocks_dev) == member)
            mine_near = jnp.logical_and(
                jnp.logical_not(far), jnp.logical_and(near_rank >= low, near_rank < low + room)
            )
            row_place = local_near(row)
            col_place = jnp.where(far, slab + lax.rem(col - slab, blocks_dev), local_near(col))
            early = jnp.logical_and(
                is_early(row_place, group, blocks_dev), is_early(col_place, group, blocks_dev)
            )
            mine = jnp.logical_and(used, jnp.logical_or(mine_far, mine_near))
            early = jnp.logical_and(early, mine)
            room_left = early_rank < early_cap
            early_rank = early_rank + jnp.where(early, 1, 0)
            early = jnp.logical_and(early, room_left)
            mine = jnp.logical_and(mine, early if wanted else jnp.logical_not(early))

            @pl.when(mine)
            def _():
                out_rows[filled] = row_place
                out_cols[filled] = col_place

            near_rank = near_rank + jnp.where(jnp.logical_and(used, jnp.logical_not(far)), 1, 0)
            return (near_rank, early_rank, filled + jnp.where(mine, 1, 0))

        return lax.fori_loop(0, slots, place, (jnp.int32(0), jnp.int32(0), filled))[2]

    early_count = place_those(True, jnp.int32(0))
    out_n[0] = jnp.int32(0)
    out_n[1] = early_count
    out_n[2] = place_those(False, early_count)


def listing(rows, cols, live, group, cap, early_cap, blocks_dev):
    return pl.pallas_call(
        functools.partial(listing_kernel, group, cap, early_cap, blocks_dev),
        out_shape=(
            jax.ShapeDtypeStruct((cap,), jnp.int32),
            jax.ShapeDtypeStruct((cap,), jnp.int32),
            jax.ShapeDtypeStruct((3,), jnp.int32),
        ),
        in_specs=[spec(SMEM)] * 3,
        out_specs=(spec(SMEM),) * 3,
        cost_estimate=cost(2**20, 2**10),
        compiler_params=pltpu.CompilerParams(vmem_limit_bytes=2**20),
        name="listing",
    )(rows, cols, live)


def message_rels(group):
    groups = [[0]]
    for bit in bits_of(group):
        groups.append([rel for rel in range(group) if rel & bit and rel % bit == 0])
    return groups


def product_shapes(group, blocks_dev, height):
    shapes = [
        jax.ShapeDtypeStruct((len(rels) * blocks_dev, height, PTS), jnp.float32)
        for rels in message_rels(group)
    ]
    shapes.append(jax.ShapeDtypeStruct((blocks_dev, height, PTS), jnp.float32))
    return shapes


def write_products(group, blocks_dev, acc, outs):
    for rels, out in zip(message_rels(group), outs[:-1]):
        for index, rel in enumerate(rels):
            for block in range(blocks_dev):
                out[index * blocks_dev + block] = acc[rel * blocks_dev + block]
    for block in range(blocks_dev):
        outs[-1][block] = acc[group * blocks_dev + block]


def add_products(acc, tile, u_row, u_col, row, col):
    height = acc.shape[1]
    to_row = lax.dot_general(
        u_col, tile, (((1,), (1,)), ((), ())), preferred_element_type=jnp.float32
    )
    acc[row] += to_row[:height]
    to_col = jnp.dot(u_row, tile, preferred_element_type=jnp.float32)
    acc[col] += to_col[:height]


def setup_first(group, augs, counts, u_win, level_row, level_col, acc):
    columns = augs[0].shape[0] - EXTRA
    height = acc.shape[1]
    blocks_dev = augs[0].shape[1] // PTS
    pick = lax.broadcasted_iota(jnp.int32, (EXTRA, 128), 0)
    pick = jnp.where(jnp.logical_and(pick >= 1, pick <= 3), 1.0, 0.0).astype(jnp.bfloat16)
    for piece in range(group + 1):
        for block in range(blocks_dev):
            place = piece * blocks_dev + block
            lanes = slice(block * PTS, (block + 1) * PTS)
            u_win[place] = augs[piece][:, lanes]
            tail = augs[piece][columns : columns + EXTRA, lanes]
            if piece < group:
                level_col[place] = lax.dot_general(
                    tail, pick, (((0,), (0,)), ((), ())), preferred_element_type=jnp.float32
                )
            tail = tail.astype(jnp.float32)
            level_row[place] = jnp.broadcast_to(tail[1:2] + tail[2:3] + tail[3:4], (8, PTS))
            acc[place] = jnp.zeros((height, PTS), jnp.float32)
    for block in range(blocks_dev):
        lanes = slice(block * PTS, (block + 1) * PTS)
        place_in = lax.broadcasted_iota(jnp.int32, (columns, PTS), 1)
        own = augs[0][0:columns, lanes].astype(jnp.float32)
        acc[block, 0:columns] = jnp.where(place_in < counts[block], own, 0.0)
        acc[block, columns:height] = jnp.ones((height - columns, PTS), jnp.float32)


def make_tiles(low, high, rows, cols, window, u_win, level_row, level_col, kept, acc):
    width = window.shape[1]
    step = 256
    scale = 6.0 / width * LOG2E

    def body(index, carry):
        row, col = rows[index], cols[index]
        right = window[pl.ds(pl.multiple_of(col * PTS, PTS), PTS), :]
        right_level = level_row[col][0:1, :]
        for part in range(PTS // step):
            left = window[pl.ds(pl.multiple_of(row * PTS + part * step, step), step), :]
            cross = lax.dot_general(
                left, right, (((1,), (1,)), ((), ())), preferred_element_type=jnp.float32
            )
            left_level = level_col[row, part * step : (part + 1) * step, :]
            left_level = jnp.concatenate([left_level] * (PTS // 128), axis=1)
            value = jnp.exp2(cross * scale - left_level - right_level)
            kept[index - low, part * step : (part + 1) * step, :] = value.astype(jnp.bfloat16)
        add_products(acc, kept[index - low], u_win[row], u_win[col], row, col)
        return carry

    lax.fori_loop(low, high, body, 0)


def early_tiles(places, n, rows, cols, counts, pts, augs, group, early_cap):
    width = pts[0].shape[1]
    blocks_dev = augs[0].shape[1] // PTS
    total = (group + 1) * blocks_dev
    tall = augs[0].shape[0]
    height = tall - EXTRA + 8
    shapes = (
        jax.ShapeDtypeStruct((total, tall, PTS), jnp.bfloat16),
        jax.ShapeDtypeStruct((total, 8, PTS), jnp.float32),
        jax.ShapeDtypeStruct((group * blocks_dev, PTS, 128), jnp.float32),
        jax.ShapeDtypeStruct((early_cap, PTS, PTS), jnp.bfloat16),
        jax.ShapeDtypeStruct((total, height, PTS), jnp.float32),
    )

    def kernel(*refs):
        n_ref, row_ref, col_ref, count_ref = refs[:4]
        pt_refs = refs[4 : 4 + len(pts)]
        aug_refs = refs[4 + len(pts) : 4 + len(pts) + len(augs)]
        u_win, level_row, level_col, kept, acc, window = refs[4 + len(pts) + len(augs) :]
        for place, piece in zip(places, pt_refs):
            window[place * PTS : place * PTS + piece.shape[0], :] = piece[...]
        setup_first(group, aug_refs, count_ref, u_win, level_row, level_col, acc)
        make_tiles(
            n_ref[0], n_ref[1], row_ref, col_ref, window, u_win, level_row, level_col, kept, acc
        )

    return pl.pallas_call(
        kernel,
        out_shape=shapes,
        in_specs=[spec(SMEM)] * 4 + [spec(VMEM)] * (len(pts) + len(augs)),
        out_specs=(spec(VMEM),) * len(shapes),
        scratch_shapes=[VMEM((total * PTS, width), jnp.bfloat16)],
        cost_estimate=cost(2**20, 2**20),
        compiler_params=pltpu.CompilerParams(vmem_limit_bytes=14 * 2**20),
        name="early_tiles",
    )(n, rows, cols, counts, *pts, *augs)


def late_tiles(places, n, rows, cols, pts, state, group, blocks_dev, cap):
    u_win, level_row, level_col, _, acc = state
    total, height = acc.shape[:2]
    width = pts[0].shape[1]
    shapes = [jax.ShapeDtypeStruct((cap, PTS, PTS), jnp.bfloat16)]
    shapes += product_shapes(group, blocks_dev, height)
    first = 3 + len(pts)

    def kernel(*refs):
        n_ref, row_ref, col_ref = refs[:3]
        pt_refs = refs[3:first]
        u_win, level_row, level_col, acc_in, kept = refs[first : first + 5]
        outs = refs[first + 5 : -2]
        window, acc = refs[-2:]
        for place, piece in zip(places, pt_refs):
            window[place * PTS : place * PTS + piece.shape[0], :] = piece[...]
        acc[...] = acc_in[...]
        make_tiles(
            n_ref[1], n_ref[2], row_ref, col_ref, window, u_win, level_row, level_col, kept, acc
        )
        write_products(group, blocks_dev, acc, outs)

    return pl.pallas_call(
        kernel,
        out_shape=tuple(shapes),
        in_specs=[spec(SMEM)] * 3 + [spec(VMEM)] * (len(pts) + 4),
        out_specs=(spec(VMEM),) * len(shapes),
        scratch_shapes=[
            VMEM((total * PTS, width), jnp.bfloat16),
            VMEM((total, height, PTS), jnp.float32),
        ],
        cost_estimate=cost(2**33, 2**25),
        compiler_params=pltpu.CompilerParams(vmem_limit_bytes=14 * 2**20),
        name="late_tiles",
    )(n, rows, cols, *pts, u_win, level_row, level_col, acc)


def scale_kernel(blocks_dev, has_degree, refs):
    degree_in = None if has_degree else refs[0]
    parts = refs[:-3] if has_degree else refs[1:-2]
    if has_degree:
        z_out, gram_out, degree_out = refs[-3:]
    else:
        z_out, gram_out = refs[-2:]
    columns = z_out.shape[0]
    gram = jnp.zeros((columns, columns), jnp.float32)
    for block in range(blocks_dev):
        lanes = slice(block * PTS, (block + 1) * PTS)
        total = parts[0][block]
        for part in parts[1:]:
            total = total + part[block]
        if has_degree:
            degree = total[columns : columns + 1, :]
            degree_out[:, lanes] = jnp.broadcast_to(degree, (8, PTS))
        else:
            degree = degree_in[0:1, lanes]
        z = total[0:columns] / degree
        z_out[:, lanes] = z
        gram = gram + lax.dot_general(
            z, z, (((1,), (1,)), ((), ())), precision=HIGHEST, preferred_element_type=jnp.float32
        )
    gram_out[...] = gram


def scaled_gram(parts, degree, columns):
    blocks_dev = parts[0].shape[0]
    for part in parts:
        blocks_dev = min(blocks_dev, part.shape[0])
    total = blocks_dev * PTS
    shapes = [
        jax.ShapeDtypeStruct((columns, total), jnp.float32),
        jax.ShapeDtypeStruct((columns, columns), jnp.float32),
    ]
    if degree is None:
        shapes.append(jax.ShapeDtypeStruct((8, total), jnp.float32))
        operands = list(parts)
    else:
        operands = [degree] + list(parts)

    def kernel(*refs):
        scale_kernel(blocks_dev, degree is None, refs)

    return pl.pallas_call(
        kernel,
        out_shape=tuple(shapes),
        in_specs=[spec(VMEM)] * len(operands),
        out_specs=(spec(VMEM),) * len(shapes),
        compiler_params=pltpu.CompilerParams(vmem_limit_bytes=6 * 2**20),
        cost_estimate=cost(2**26, 2**21),
        name="scaled_gram",
    )(*operands)


def inverse_factor(gram):
    size = gram.shape[0]
    row_id = lax.broadcasted_iota(jnp.int32, (size, size), 0)
    col_id = lax.broadcasted_iota(jnp.int32, (size, size), 1)
    eye = jnp.where(row_id == col_id, 1.0, 0.0)
    whole = jnp.concatenate([gram, eye], axis=1)
    wide = 2 * size
    count = size // 8
    groups = [whole[8 * g : 8 * g + 8, :] for g in range(count)]
    within = lax.broadcasted_iota(jnp.int32, (8, wide), 0)

    def spread_row(value, row):
        return jnp.broadcast_to(value[row : row + 1, :], (8, wide))

    results = []
    for g in range(count):
        spread = [
            [
                jnp.broadcast_to(groups[other][:, 8 * g + k : 8 * g + k + 1], (8, wide))
                for other in range(g, count)
            ]
            for k in range(8)
        ]
        pivots = jnp.ones((8, wide), jnp.float32)
        for j in range(8):
            column = spread[j]
            pivot = spread_row(column[0], j)
            pivots = jnp.where(within == j, pivot, pivots)
            over = 1.0 / pivot
            below = jnp.where(within > j, column[0], 0.0)
            for k in range(j + 1, 8):
                share = spread_row(column[0], k) * over
                spread[k][0] = spread[k][0] - below * share
                for other in range(1, count - g):
                    spread[k][other] = spread[k][other] - column[other] * share
            top = spread_row(groups[g], j) * over
            groups[g] = groups[g] - below * top
            for other in range(1, count - g):
                groups[g + other] = groups[g + other] - column[other] * top
        results.append(groups[g] * lax.rsqrt(pivots))
    return jnp.concatenate(results, axis=0)[:, size:wide]


def second_kernel(group, refs):
    pieces = group + 1
    n_ref, rows, cols, counts, gram = refs[:5]
    zs = refs[5 : 5 + pieces]
    tiles = refs[5 + pieces : 7 + pieces]
    messages = len(message_rels(group)) + 1
    outs = refs[7 + pieces : 7 + pieces + messages]
    u_win, acc = refs[7 + pieces + messages :]
    columns, held = zs[0].shape
    blocks_dev = held // PTS
    inverse = inverse_factor(gram[...])
    for piece in range(pieces):
        for block in range(blocks_dev):
            place = piece * blocks_dev + block
            vec = jnp.dot(
                inverse,
                zs[piece][:, block * PTS : (block + 1) * PTS],
                precision=HIGHEST,
                preferred_element_type=jnp.float32,
            ).astype(jnp.bfloat16)
            u_win[place] = vec
            if piece == 0:
                place_in = lax.broadcasted_iota(jnp.int32, (columns, PTS), 1)
                acc[place] = jnp.where(place_in < counts[block], vec.astype(jnp.float32), 0.0)
            else:
                acc[place] = jnp.zeros((columns, PTS), jnp.float32)

    for stage, kept in enumerate(tiles):
        low = n_ref[stage]

        def body(index, carry):
            row, col = rows[index], cols[index]
            add_products(acc, kept[index - low], u_win[row], u_win[col], row, col)
            return carry

        lax.fori_loop(low, n_ref[stage + 1], body, 0)
    write_products(group, blocks_dev, acc, outs)


def next_turn(n, rows, cols, counts, gram, zs, tiles, group, cap):
    columns, held = zs[0].shape
    blocks_dev = held // PTS
    pieces = group + 1
    places = pieces * blocks_dev
    shapes = product_shapes(group, blocks_dev, columns)

    def kernel(*refs):
        second_kernel(group, refs)

    return pl.pallas_call(
        kernel,
        out_shape=tuple(shapes),
        in_specs=[spec(SMEM)] * 4 + [spec(VMEM)] * (3 + pieces),
        out_specs=(spec(VMEM),) * len(shapes),
        scratch_shapes=[
            VMEM((places, columns, PTS), jnp.bfloat16),
            VMEM((places, columns, PTS), jnp.float32),
        ],
        compiler_params=pltpu.CompilerParams(vmem_limit_bytes=10 * 2**20),
        cost_estimate=cost(2**32, 2**24),
        name="next_turn",
    )(n, rows, cols, counts, gram, *zs, *tiles)


def embed_kernel(gram, z, out):
    out[...] = jnp.dot(
        inverse_factor(gram[...]), z[...], precision=HIGHEST, preferred_element_type=jnp.float32
    )


def embedding(gram, z):
    return pl.pallas_call(
        embed_kernel,
        out_shape=jax.ShapeDtypeStruct(z.shape, jnp.float32),
        in_specs=[spec(VMEM)] * 2,
        out_specs=spec(VMEM),
        cost_estimate=cost(2**30, 2**20),
        compiler_params=pltpu.CompilerParams(vmem_limit_bytes=4 * 2**20),
        name="embedding",
    )(gram, z)


def sum_products(messages, group, blocks_dev):
    rels = message_rels(group)
    parts = {}
    for names, message in zip(rels[1:], messages[1:-1]):
        for index, rel in enumerate(names):
            parts[rel] = [message[index * blocks_dev : (index + 1) * blocks_dev]]
    final = [messages[0], from_behind(messages[-1], "blk", 1)]
    for bit, names, message in zip(bits_of(group), rels[1:], messages[1:-1]):
        if bit > 1:
            message = jnp.concatenate([sum(parts[rel][1:], parts[rel][0]) for rel in names], 0)
        got = swap(message, "grp", bit)
        for index, rel in enumerate(names):
            target = rel ^ bit
            if target == 0:
                final.append(got)
            else:
                parts[target].append(got[index * blocks_dev : (index + 1) * blocks_dev])
    return final


def all_sum(value):
    for axis in ("grp", "blk"):
        for bit in bits_of(lax.axis_size(axis)):
            value = value + swap(value, axis, bit)
    return value


def per_device(points, counts, pair_rows, pair_cols, pair_live, start):
    group = lax.axis_size("grp")
    blocks_dev = counts.shape[0]
    columns = start.shape[0]
    slots = pair_rows.shape[0]
    cap = max(-(-slots // group), blocks_dev * blocks_dev * group)
    early_cap = cap // 2
    half = (blocks_dev // 2) * PTS
    rows, cols, n = listing(pair_rows, pair_cols, pair_live, group, cap, early_cap, blocks_dev)
    mate = swap(points, "grp", 1)
    first = points[:half]
    far = [from_behind(first, "blk", -1)]
    crossed = [gather_far_bits(first)]
    ready, mate = lax.optimization_barrier((points, mate))
    aug = augment(ready, counts, start)
    mate_aug = swap(aug, "grp", 1)
    far_aug = from_behind(aug, "blk", -1)
    cross_aug = gather_far_bits(aug)
    second = lax.optimization_barrier((points, aug))[0][half:]
    tied = lax.optimization_barrier(
        (mate_aug, n, rows, cols, second, far[0], *crossed[0].values())
    )
    mate_aug, n, rows, cols, second, far[0] = tied[:6]
    crossed[0] = dict(zip(crossed[0], tied[6:]))
    far.append(from_behind(second, "blk", -1))
    crossed.append(gather_far_bits(second))
    tied = lax.optimization_barrier((far_aug, *cross_aug.values(), *crossed[0].values()))
    far_aug = tied[0]
    cross_aug = dict(zip(cross_aug, tied[1 : 1 + len(cross_aug)]))
    crossed[0] = dict(zip(crossed[0], tied[1 + len(cross_aug) :]))
    augs = {0: aug, 1: mate_aug}
    for rel, value in cross_aug.items():
        augs[rel] = value
        augs[rel ^ 1] = swap(value, "grp", 1)
    augs = [augs[rel] for rel in range(group)] + [far_aug]
    mate = swap(points, "grp", 1)

    def placed(index):
        offset = index * (blocks_dev // 2)
        found = [(group * blocks_dev + offset, far[index])]
        for rel, value in crossed[index].items():
            found.append((rel * blocks_dev + offset, value))
            found.append(((rel ^ 1) * blocks_dev + offset, swap(value, "grp", 1)))
        return found

    early = [(0, points), (blocks_dev, mate)] + placed(0)
    places, pts = zip(*early)
    state = early_tiles(places, n, rows, cols, counts, pts, augs, group, early_cap)
    tied = lax.optimization_barrier((far[1], *crossed[1].values(), state[4]))
    far[1] = tied[0]
    crossed[1] = dict(zip(crossed[1], tied[1:-1]))
    state = (*state[:4], tied[-1])
    places, pts = zip(*(early + placed(1)))
    late, *messages = late_tiles(places, n, rows, cols, pts, state, group, blocks_dev, cap)
    tiles = (state[3], late)
    z, gram, degree = scaled_gram(sum_products(messages, group, blocks_dev), None, columns)
    for turn in range(1, ITERS):
        zs = gather_near(z, "grp") + [from_behind(z, "blk", -1)]
        gram = all_sum(gram)
        messages = next_turn(n, rows, cols, counts, gram, zs, tiles, group, cap)
        z, gram = scaled_gram(sum_products(messages, group, blocks_dev), degree, columns)
    return embedding(all_sum(gram), z)


def solution(mesh):
    in_specs = (
        P(("blk", "grp"), None),
        P(("blk", "grp")),
        P("blk"),
        P("blk"),
        P("blk"),
        P(None, ("blk", "grp")),
    )
    out_specs = P(None, ("blk", "grp"))
    return jax.shard_map(
        per_device, mesh=mesh, in_specs=in_specs, out_specs=out_specs, check_vma=False
    )
```

```python
import functools

import jax
import jax.numpy as jnp
from jax import lax
from jax.experimental import pallas as pl
from jax.experimental.pallas import tpu as pltpu
from jax.sharding import PartitionSpec as P

PTS = 512
ITERS = 2
LOG2E = 1.4426950408889634
DEAD = 65536.0
EXTRA = 16
VMEM = pltpu.VMEM
SMEM = pltpu.SMEM
HIGHEST = lax.Precision.HIGHEST


def cost(flops, moved):
    return pl.CostEstimate(flops=int(flops), bytes_accessed=int(moved), transcendentals=0)


def spec(space):
    return pl.BlockSpec(memory_space=space)


def swap(value, axis, bit):
    count = lax.axis_size(axis)
    return lax.ppermute(value, axis, [(source, source ^ bit) for source in range(count)])


def from_behind(value, axis, steps):
    count = lax.axis_size(axis)
    initial, last = (max(0, -steps), min(count, count - steps))
    return lax.ppermute(value, axis, [(source, source + steps) for source in range(initial, last)])


def bits_of(count):
    bits = []
    bit = 1
    while bit < count:
        bits.append(bit)
        bit *= 2
    return bits


def gather_near(value, axis):
    held = {0: value}
    for bit in reversed(bits_of(lax.axis_size(axis))):
        for rel in list(held):
            held[rel ^ bit] = swap(held[rel], axis, bit)
    return [held[rel] for rel in range(len(held))]


def gather_far_bits(value):
    held = {0: value}
    for bit in reversed(bits_of(lax.axis_size("grp"))[1:]):
        for rel in list(held):
            held[rel ^ bit] = swap(held[rel], "grp", bit)
    held.pop(0)
    return held


def opening_kernel(start, counts, out):
    columns, total = start.shape
    for block in range(total // PTS):
        lanes = slice(block * PTS, (block + 1) * PTS)
        used = lax.broadcasted_iota(jnp.int32, (columns, PTS), 1) < counts[block]
        out[0:columns, lanes] = jnp.where(used, start[:, lanes], 0.0).astype(jnp.bfloat16)
        which = lax.broadcasted_iota(jnp.int32, (EXTRA, PTS), 0)
        place_in = lax.broadcasted_iota(jnp.int32, (EXTRA, PTS), 1)
        ones = jnp.logical_and(which == 0, place_in < counts[block])
        out[columns : columns + EXTRA, lanes] = jnp.where(ones, 1.0, 0.0).astype(jnp.bfloat16)


def opening(start, counts):
    columns, total = start.shape
    return pl.pallas_call(
        opening_kernel,
        out_shape=jax.ShapeDtypeStruct((columns + EXTRA, total), jnp.bfloat16),
        in_specs=[spec(VMEM), spec(SMEM)],
        out_specs=spec(VMEM),
        cost_estimate=cost(2**20, 2**19),
        compiler_params=pltpu.CompilerParams(vmem_limit_bytes=2 * 2**20),
        name="opening",
    )(start, counts)


def is_early(place, group, blocks_dev):
    near_by = jnp.logical_and(place < min(2, group) * blocks_dev, place < group * blocks_dev)
    return jnp.logical_or(near_by, lax.rem(place, blocks_dev) < blocks_dev // 2)


def listing_kernel(group, cap, early_cap, blocks_dev, rows, cols, live, out_rows, out_cols, out_n):
    slab = blocks_dev * group
    slots = rows.shape[0]
    member = lax.axis_index("grp")

    def local_near(block):
        return (lax.div(block, blocks_dev) ^ member) * blocks_dev + lax.rem(block, blocks_dev)

    def count_far(slot, carry):
        col = cols[slot]
        far = jnp.logical_and(slot < live[0], col >= slab)
        owner = lax.div(col - slab, blocks_dev)
        return tuple(
            old + jnp.where(jnp.logical_and(far, owner == device), 1, 0)
            for device, old in enumerate(carry)
        )

    far_counts = lax.fori_loop(0, slots, count_far, (jnp.int32(0),) * group)
    low = jnp.int32(0)
    room = jnp.int32(0)
    for device in range(group):
        low = low + jnp.where(device < member, cap - far_counts[device], 0)
        room = room + jnp.where(device == member, cap - far_counts[device], 0)

    def place_those(wanted, filled):
        def place(slot, carry):
            near_rank, early_rank, filled = carry
            row, col = rows[slot], cols[slot]
            used = slot < live[0]
            far = col >= slab
            mine_far = jnp.logical_and(far, lax.div(col - slab, blocks_dev) == member)
            mine_near = jnp.logical_and(
                jnp.logical_not(far), jnp.logical_and(near_rank >= low, near_rank < low + room)
            )
            row_place = local_near(row)
            col_place = jnp.where(far, slab + lax.rem(col - slab, blocks_dev), local_near(col))
            early = jnp.logical_and(
                is_early(row_place, group, blocks_dev), is_early(col_place, group, blocks_dev)
            )
            mine = jnp.logical_and(used, jnp.logical_or(mine_far, mine_near))
            early = jnp.logical_and(early, mine)
            room_left = early_rank < early_cap
            early_rank = early_rank + jnp.where(early, 1, 0)
            early = jnp.logical_and(early, room_left)
            mine = jnp.logical_and(mine, early if wanted else jnp.logical_not(early))

            @pl.when(mine)
            def _():
                out_rows[filled] = row_place
                out_cols[filled] = col_place

            near_rank = near_rank + jnp.where(jnp.logical_and(used, jnp.logical_not(far)), 1, 0)
            return (near_rank, early_rank, filled + jnp.where(mine, 1, 0))

        return lax.fori_loop(0, slots, place, (jnp.int32(0), jnp.int32(0), filled))[2]

    early_count = place_those(True, jnp.int32(0))
    out_n[0] = jnp.int32(0)
    out_n[1] = early_count
    out_n[2] = place_those(False, early_count)


def listing(rows, cols, live, group, cap, early_cap, blocks_dev):
    return pl.pallas_call(
        functools.partial(listing_kernel, group, cap, early_cap, blocks_dev),
        out_shape=(
            jax.ShapeDtypeStruct((cap,), jnp.int32),
            jax.ShapeDtypeStruct((cap,), jnp.int32),
            jax.ShapeDtypeStruct((3,), jnp.int32),
        ),
        in_specs=[spec(SMEM)] * 3,
        out_specs=(spec(SMEM),) * 3,
        cost_estimate=cost(2**20, 2**10),
        compiler_params=pltpu.CompilerParams(vmem_limit_bytes=2**20),
        name="listing",
    )(rows, cols, live)


def message_rels(group):
    groups = [[0]]
    for bit in bits_of(group):
        groups.append([rel for rel in range(group) if rel & bit and rel % bit == 0])
    return groups


def product_shapes(group, blocks_dev, height):
    shapes = [
        jax.ShapeDtypeStruct((len(rels) * blocks_dev, height, PTS), jnp.float32)
        for rels in message_rels(group)
    ]
    shapes.append(jax.ShapeDtypeStruct((blocks_dev, height, PTS), jnp.float32))
    return shapes


def write_products(group, blocks_dev, acc, outs):
    for rels, out in zip(message_rels(group), outs[:-1]):
        for index, rel in enumerate(rels):
            for block in range(blocks_dev):
                out[index * blocks_dev + block] = acc[rel * blocks_dev + block]
    for block in range(blocks_dev):
        outs[-1][block] = acc[group * blocks_dev + block]


def set_levels(place, window, level_row, level_col, scale):
    block = window[place * PTS : (place + 1) * PTS, :]
    width = block.shape[1]
    part = jnp.zeros((PTS, 128), jnp.float32)
    for lane in range(0, width, 128):
        wide = block[:, lane : lane + 128].astype(jnp.float32)
        part = part + wide * wide
    level_row[place] = scale * lax.dot_general(
        jnp.ones((8, 128), jnp.float32),
        part,
        (((1,), (1,)), ((), ())),
        precision=HIGHEST,
        preferred_element_type=jnp.float32,
    )
    if place < level_col.shape[0]:
        total = jnp.sum(part, axis=1, keepdims=True) * scale
        level_col[place] = jnp.broadcast_to(total, (PTS, 128))


def make_tiles(low, high, rows, cols, window, level_row, level_col, kept):
    width = window.shape[1]
    step = 256
    scale = 6.0 / width * LOG2E

    def body(index, carry):
        row, col = rows[index], cols[index]
        right = window[pl.ds(pl.multiple_of(col * PTS, PTS), PTS), :]
        right_level = level_row[col][0:1, :]
        for part in range(PTS // step):
            left = window[pl.ds(pl.multiple_of(row * PTS + part * step, step), step), :]
            cross = lax.dot_general(
                left, right, (((1,), (1,)), ((), ())), preferred_element_type=jnp.float32
            )
            left_level = level_col[row, part * step : (part + 1) * step, :]
            left_level = jnp.concatenate([left_level] * (PTS // 128), axis=1)
            value = jnp.exp2(cross * scale - left_level - right_level)
            kept[index - low, part * step : (part + 1) * step, :] = value.astype(jnp.bfloat16)
        return carry

    lax.fori_loop(low, high, body, 0)


def build_tiles(stage, fresh, places, n, rows, cols, pts, levels, group, blocks_dev, cap, name):
    width = pts[0].shape[1]
    total = (group + 1) * blocks_dev
    near = group * blocks_dev
    level_shapes = [
        jax.ShapeDtypeStruct((total, 8, PTS), jnp.float32),
        jax.ShapeDtypeStruct((near, PTS, 128), jnp.float32),
    ]
    shapes = [jax.ShapeDtypeStruct((cap, PTS, PTS), jnp.bfloat16)] + level_shapes

    def kernel(*refs):
        n_ref, row_ref, col_ref = refs[:3]
        pt_refs = refs[3 : 3 + len(pts)]
        level_refs = refs[3 + len(pts) : 3 + len(pts) + len(levels)]
        kept, level_row, level_col, window = refs[3 + len(pts) + len(levels) :]
        for place, piece in zip(places, pt_refs):
            window[place * PTS : place * PTS + piece.shape[0], :] = piece[...]
        for index, (place, piece) in enumerate(zip(places, pt_refs)):
            for block in range(place, place + piece.shape[0] // PTS):
                if index < fresh:
                    set_levels(block, window, level_row, level_col, 3.0 / width * LOG2E)
                else:
                    level_row[block] = level_refs[0][block]
                    if block < near:
                        level_col[block] = level_refs[1][block]
        make_tiles(
            n_ref[stage], n_ref[stage + 1], row_ref, col_ref, window, level_row, level_col, kept
        )

    return pl.pallas_call(
        kernel,
        out_shape=tuple(shapes),
        in_specs=[spec(SMEM)] * 3 + [spec(VMEM)] * (len(pts) + len(levels)),
        out_specs=(spec(VMEM),) * len(shapes),
        scratch_shapes=[VMEM((total * PTS, width), jnp.bfloat16)],
        cost_estimate=cost(2**20 if stage == 0 else 2**32, 2**20),
        compiler_params=pltpu.CompilerParams(vmem_limit_bytes=14 * 2**20),
        name=name,
    )(n, rows, cols, *pts, *levels)


def products(n, rows, cols, vecs, tiles, group, blocks_dev, height, folds):
    pieces = group + 1
    places = pieces * blocks_dev
    tall = vecs[0].shape[0]
    shapes = product_shapes(group, blocks_dev, height)

    def fold(value):
        out = value[:height]
        for index in range(1, folds):
            out = out + value[index * height : (index + 1) * height]
        return out

    def kernel(*refs):
        n_ref, row_ref, col_ref = refs[:3]
        vec_refs = refs[3 : 3 + pieces]
        tile_refs = refs[3 + pieces : 3 + pieces + len(tiles)]
        outs = refs[3 + pieces + len(tiles) : -2]
        u_win, acc = refs[-2:]
        for piece in range(pieces):
            for block in range(blocks_dev):
                lanes = slice(block * PTS, (block + 1) * PTS)
                u_win[piece * blocks_dev + block] = vec_refs[piece][:, lanes]
                acc[piece * blocks_dev + block] = jnp.zeros((height, PTS), jnp.float32)
        for stage, kept in enumerate(tile_refs):
            low = n_ref[stage]

            def body(index, carry):
                row, col = row_ref[index], col_ref[index]
                tile = kept[index - low]
                to_row = lax.dot_general(
                    u_win[col], tile, (((1,), (1,)), ((), ())), preferred_element_type=jnp.float32
                )
                acc[row] += fold(to_row)
                to_col = jnp.dot(u_win[row], tile, preferred_element_type=jnp.float32)
                acc[col] += fold(to_col)
                return carry

            lax.fori_loop(low, n_ref[stage + 1], body, 0)
        write_products(group, blocks_dev, acc, outs)

    return pl.pallas_call(
        kernel,
        out_shape=tuple(shapes),
        in_specs=[spec(SMEM)] * 3 + [spec(VMEM)] * (pieces + len(tiles)),
        out_specs=(spec(VMEM),) * len(shapes),
        scratch_shapes=[
            VMEM((places, tall, PTS), jnp.bfloat16),
            VMEM((places, height, PTS), jnp.float32),
        ],
        cost_estimate=cost(2**32, 2**24),
        compiler_params=pltpu.CompilerParams(vmem_limit_bytes=10 * 2**20),
        name="products",
    )(n, rows, cols, *vecs, *tiles)


def scaled_gram(parts, own, counts, degree, inverse, split):
    columns = own.shape[0] if degree is not None else own.shape[0] - EXTRA
    total = own.shape[1]
    first = degree is None
    shapes = [
        jax.ShapeDtypeStruct((columns, total), jnp.float32),
        jax.ShapeDtypeStruct((columns, columns), jnp.float32),
    ]
    if split:
        shapes.append(jax.ShapeDtypeStruct((2 * columns, total), jnp.bfloat16))
    if first:
        shapes.append(jax.ShapeDtypeStruct((8, total), jnp.float32))
    operands = list(parts) + [own]
    operands += [] if first else [degree]
    operands += [] if inverse is None else [inverse]

    def kernel(count_ref, *refs):
        ins = list(refs[: len(operands)])
        outs = list(refs[len(operands) :])
        part_refs = ins[: len(parts)]
        own_ref = ins[len(parts)]
        z_out, gram_out = outs[:2]
        gram = jnp.zeros((columns, columns), jnp.float32)
        for block in range(total // PTS):
            lanes = slice(block * PTS, (block + 1) * PTS)
            sums = part_refs[0][block]
            for part in part_refs[1:]:
                sums = sums + part[block]
            if first:
                level = 1.0 + sums[columns : columns + 1, :]
                outs[-1][:, lanes] = jnp.broadcast_to(level, (8, PTS))
            else:
                level = ins[len(parts) + 1][0:1, lanes]
            used = lax.broadcasted_iota(jnp.int32, (columns, PTS), 1) < count_ref[block]
            held = own_ref[0:columns, lanes].astype(jnp.float32)
            z = (held + jnp.where(used, sums[0:columns], 0.0)) / level
            if inverse is not None:
                z = jnp.dot(
                    ins[-1][...], z, precision=HIGHEST, preferred_element_type=jnp.float32
                )
            z_out[:, lanes] = z
            if split:
                high = z.astype(jnp.bfloat16)
                outs[2][0:columns, lanes] = high
                rest = z - high.astype(jnp.float32)
                outs[2][columns : 2 * columns, lanes] = rest.astype(jnp.bfloat16)
            gram = gram + lax.dot_general(
                z, z, (((1,), (1,)), ((), ())), precision=HIGHEST, preferred_element_type=jnp.float32
            )
        gram_out[...] = gram

    return pl.pallas_call(
        kernel,
        out_shape=tuple(shapes),
        in_specs=[spec(SMEM)] + [spec(VMEM)] * len(operands),
        out_specs=(spec(VMEM),) * len(shapes),
        cost_estimate=cost(2**26, 2**21),
        compiler_params=pltpu.CompilerParams(vmem_limit_bytes=6 * 2**20),
        name="scaled_gram",
    )(counts, *operands)


def inverse_factor(gram):
    size = gram.shape[0]
    row_id = lax.broadcasted_iota(jnp.int32, (size, size), 0)
    col_id = lax.broadcasted_iota(jnp.int32, (size, size), 1)
    eye = jnp.where(row_id == col_id, 1.0, 0.0)
    whole = jnp.concatenate([gram, eye], axis=1)
    wide = 2 * size
    count = size // 8
    groups = [whole[8 * g : 8 * g + 8, :] for g in range(count)]
    within = lax.broadcasted_iota(jnp.int32, (8, wide), 0)

    def spread_row(value, row):
        return jnp.broadcast_to(value[row : row + 1, :], (8, wide))

    results = []
    for g in range(count):
        spread = [
            [
                jnp.broadcast_to(groups[other][:, 8 * g + k : 8 * g + k + 1], (8, wide))
                for other in range(g, count)
            ]
            for k in range(8)
        ]
        pivots = jnp.ones((8, wide), jnp.float32)
        for j in range(8):
            column = spread[j]
            pivot = spread_row(column[0], j)
            pivots = jnp.where(within == j, pivot, pivots)
            over = 1.0 / pivot
            below = jnp.where(within > j, column[0], 0.0)
            for k in range(j + 1, 8):
                share = spread_row(column[0], k) * over
                spread[k][0] = spread[k][0] - below * share
                for other in range(1, count - g):
                    spread[k][other] = spread[k][other] - column[other] * share
            top = spread_row(groups[g], j) * over
            groups[g] = groups[g] - below * top
            for other in range(1, count - g):
                groups[g + other] = groups[g + other] - column[other] * top
        results.append(groups[g] * lax.rsqrt(pivots))
    return jnp.concatenate(results, axis=0)[:, size:wide]


def factor_kernel(gram, out):
    out[...] = inverse_factor(gram[...])


def factor(gram):
    return pl.pallas_call(
        factor_kernel,
        out_shape=jax.ShapeDtypeStruct(gram.shape, jnp.float32),
        in_specs=[spec(VMEM)],
        out_specs=spec(VMEM),
        cost_estimate=cost(2**31, 2**16),
        compiler_params=pltpu.CompilerParams(vmem_limit_bytes=2 * 2**20),
        name="factor",
    )(gram)


def embed_kernel(gram, z, out):
    out[...] = jnp.dot(
        inverse_factor(gram[...]), z[...], precision=HIGHEST, preferred_element_type=jnp.float32
    )


def embedding(gram, z):
    return pl.pallas_call(
        embed_kernel,
        out_shape=jax.ShapeDtypeStruct(z.shape, jnp.float32),
        in_specs=[spec(VMEM)] * 2,
        out_specs=spec(VMEM),
        cost_estimate=cost(2**30, 2**20),
        compiler_params=pltpu.CompilerParams(vmem_limit_bytes=4 * 2**20),
        name="embedding",
    )(gram, z)


def sum_products(messages, group, blocks_dev):
    rels = message_rels(group)
    parts = {}
    for names, message in zip(rels[1:], messages[1:-1]):
        for index, rel in enumerate(names):
            parts[rel] = [message[index * blocks_dev : (index + 1) * blocks_dev]]
    final = [messages[0], from_behind(messages[-1], "blk", 1)]
    for bit, names, message in zip(bits_of(group), rels[1:], messages[1:-1]):
        if bit > 1:
            message = jnp.concatenate([sum(parts[rel][1:], parts[rel][0]) for rel in names], 0)
        got = swap(message, "grp", bit)
        for index, rel in enumerate(names):
            target = rel ^ bit
            if target == 0:
                final.append(got)
            else:
                parts[target].append(got[index * blocks_dev : (index + 1) * blocks_dev])
    return final


def sum_stages():
    return [(axis, bit) for axis in ("grp", "blk") for bit in bits_of(lax.axis_size(axis))]


def all_sum(value, stages):
    for axis, bit in stages:
        value = value + swap(value, axis, bit)
    return value


def per_device(points, counts, pair_rows, pair_cols, pair_live, start):
    group = lax.axis_size("grp")
    blocks_dev = counts.shape[0]
    columns = start.shape[0]
    slots = pair_rows.shape[0]
    cap = max(-(-slots // group), blocks_dev * blocks_dev * group)
    early_cap = cap // 2
    half = (blocks_dev // 2) * PTS

    rows, cols, n = listing(pair_rows, pair_cols, pair_live, group, cap, early_cap, blocks_dev)
    mate = swap(points, "grp", 1)
    chunks = [points[:half], points[half:]]
    far = [from_behind(chunk, "blk", -1) for chunk in chunks]
    crossed = [gather_far_bits(chunk) for chunk in chunks]
    begin, mate = lax.optimization_barrier((start, mate))
    vec = opening(begin, counts)
    tied = lax.optimization_barrier((vec, n, rows, cols, far[0], *crossed[0].values()))
    vec, n, rows, cols, far[0] = tied[:5]
    crossed[0] = dict(zip(crossed[0], tied[5:]))
    cross_vec = gather_far_bits(vec)
    far_vec = from_behind(vec, "blk", -1)
    mate_vec = swap(vec, "grp", 1)

    def placed(index):
        offset = index * (blocks_dev // 2)
        found = [(group * blocks_dev + offset, far[index])]
        for rel, value in crossed[index].items():
            found.append((rel * blocks_dev + offset, value))
            found.append(((rel ^ 1) * blocks_dev + offset, swap(value, "grp", 1)))
        return found

    def tiles_of(stage, fresh, pieces, levels, size, name):
        places, pts = zip(*pieces)
        return build_tiles(
            stage, fresh, places, n, rows, cols, pts, levels, group, blocks_dev, size, name
        )

    early = [(0, points), (blocks_dev, mate)] + placed(0)
    early_kept, *levels = tiles_of(0, len(early), early, (), early_cap, "early_tiles")
    tied = lax.optimization_barrier((far[1], levels[0], *crossed[1].values()))
    far[1], levels[0] = tied[:2]
    crossed[1] = dict(zip(crossed[1], tied[2:]))
    late = placed(1)
    late_kept, _, _ = tiles_of(1, len(late), late + early, levels, cap, "late_tiles")
    tied = lax.optimization_barrier((late_kept, *cross_vec.values()))
    kept = (early_kept, tied[0])
    cross_vec = dict(zip(cross_vec, tied[1:]))

    vecs = {0: vec, 1: mate_vec}
    for rel, value in cross_vec.items():
        vecs[rel] = value
        vecs[rel ^ 1] = swap(value, "grp", 1)
    vecs = [vecs[rel] for rel in range(group)] + [far_vec]
    messages = products(n, rows, cols, vecs, kept, group, blocks_dev, columns + 8, 1)
    z, gram, parts, degree = scaled_gram(
        sum_products(messages, group, blocks_dev), vec, counts, None, None, True
    )
    for turn in range(1, ITERS):
        stages = sum_stages()
        far_part = from_behind(parts, "blk", -1)
        crossed = gather_far_bits(parts)
        gram = all_sum(gram, stages[:1])
        gram, *tied = lax.optimization_barrier((gram, *crossed.values()))
        vecs = {0: parts, 1: swap(parts, "grp", 1)}
        for rel, value in zip(crossed, tied):
            vecs[rel] = value
            vecs[rel ^ 1] = swap(value, "grp", 1)
        vecs = [vecs[rel] for rel in range(group)] + [far_part]
        gram = all_sum(gram, stages[1:2])
        gram, *vecs = lax.optimization_barrier((gram, *vecs))
        messages = products(n, rows, cols, vecs, kept, group, blocks_dev, columns, 2)
        sums = sum_products(messages, group, blocks_dev)
        inverse = factor(all_sum(gram, stages[2:]))
        z, gram, *parts = scaled_gram(sums, z, counts, degree, inverse, turn + 1 < ITERS)
        parts = parts[0] if parts else None
    return embedding(all_sum(gram, sum_stages()), z)


def solution(mesh):
    in_specs = (
        P(("blk", "grp"), None),
        P(("blk", "grp")),
        P("blk"),
        P("blk"),
        P("blk"),
        P(None, ("blk", "grp")),
    )
    out_specs = P(None, ("blk", "grp"))
    return jax.shard_map(
        per_device, mesh=mesh, in_specs=in_specs, out_specs=out_specs, check_vma=False
    )
```

```python
import functools

import jax
import jax.numpy as jnp
from jax import lax
from jax.experimental import pallas as pl
from jax.experimental.pallas import tpu as pltpu
from jax.sharding import PartitionSpec as P

PTS = 512
ITERS = 2
LOG2E = 1.4426950408889634
DEAD = 65536.0
EXTRA = 16
VMEM = pltpu.VMEM
SMEM = pltpu.SMEM
HIGHEST = lax.Precision.HIGHEST


def cost(flops, moved):
    return pl.CostEstimate(flops=int(flops), bytes_accessed=int(moved), transcendentals=0)


def spec(space):
    return pl.BlockSpec(memory_space=space)


def swap(value, axis, bit):
    count = lax.axis_size(axis)
    return lax.ppermute(value, axis, [(source, source ^ bit) for source in range(count)])


def from_behind(value, axis, steps):
    count = lax.axis_size(axis)
    initial, last = (max(0, -steps), min(count, count - steps))
    return lax.ppermute(value, axis, [(source, source + steps) for source in range(initial, last)])


def bits_of(count):
    bits = []
    bit = 1
    while bit < count:
        bits.append(bit)
        bit *= 2
    return bits


def gather_near(value, axis):
    held = {0: value}
    for bit in reversed(bits_of(lax.axis_size(axis))):
        for rel in list(held):
            held[rel ^ bit] = swap(held[rel], axis, bit)
    return [held[rel] for rel in range(len(held))]


def gather_far_bits(value):
    held = {0: value}
    for bit in reversed(bits_of(lax.axis_size("grp"))[1:]):
        for rel in list(held):
            held[rel ^ bit] = swap(held[rel], "grp", bit)
    held.pop(0)
    return held


def opening_kernel(start, counts, out):
    columns, total = start.shape
    for block in range(total // PTS):
        lanes = slice(block * PTS, (block + 1) * PTS)
        used = lax.broadcasted_iota(jnp.int32, (columns, PTS), 1) < counts[block]
        out[0:columns, lanes] = jnp.where(used, start[:, lanes], 0.0).astype(jnp.bfloat16)
        which = lax.broadcasted_iota(jnp.int32, (EXTRA, PTS), 0)
        place_in = lax.broadcasted_iota(jnp.int32, (EXTRA, PTS), 1)
        ones = jnp.logical_and(which == 0, place_in < counts[block])
        out[columns : columns + EXTRA, lanes] = jnp.where(ones, 1.0, 0.0).astype(jnp.bfloat16)


def opening(start, counts):
    columns, total = start.shape
    return pl.pallas_call(
        opening_kernel,
        out_shape=jax.ShapeDtypeStruct((columns + EXTRA, total), jnp.bfloat16),
        in_specs=[spec(VMEM), spec(SMEM)],
        out_specs=spec(VMEM),
        cost_estimate=cost(2**20, 2**19),
        compiler_params=pltpu.CompilerParams(vmem_limit_bytes=2 * 2**20),
        name="opening",
    )(start, counts)


def is_early(place, group, blocks_dev):
    near_by = place < min(2, group) * blocks_dev
    direct = lax.rem(lax.div(place, blocks_dev), 2) == 0
    first_half = lax.rem(place, blocks_dev) < blocks_dev // 2
    return jnp.logical_or(near_by, jnp.logical_and(direct, first_half))


def listing_kernel(group, cap, early_cap, blocks_dev, rows, cols, live, out_rows, out_cols, out_n):
    slab = blocks_dev * group
    slots = rows.shape[0]
    member = lax.axis_index("grp")

    def local_near(block):
        return (lax.div(block, blocks_dev) ^ member) * blocks_dev + lax.rem(block, blocks_dev)

    def count_far(slot, carry):
        col = cols[slot]
        far = jnp.logical_and(slot < live[0], col >= slab)
        owner = lax.div(col - slab, blocks_dev)
        return tuple(
            old + jnp.where(jnp.logical_and(far, owner == device), 1, 0)
            for device, old in enumerate(carry)
        )

    far_counts = lax.fori_loop(0, slots, count_far, (jnp.int32(0),) * group)
    low = jnp.int32(0)
    room = jnp.int32(0)
    for device in range(group):
        low = low + jnp.where(device < member, cap - far_counts[device], 0)
        room = room + jnp.where(device == member, cap - far_counts[device], 0)

    def place_those(wanted, filled):
        def place(slot, carry):
            near_rank, early_rank, filled = carry
            row, col = rows[slot], cols[slot]
            used = slot < live[0]
            far = col >= slab
            mine_far = jnp.logical_and(far, lax.div(col - slab, blocks_dev) == member)
            mine_near = jnp.logical_and(
                jnp.logical_not(far), jnp.logical_and(near_rank >= low, near_rank < low + room)
            )
            row_place = local_near(row)
            col_place = jnp.where(far, slab + lax.rem(col - slab, blocks_dev), local_near(col))
            early = jnp.logical_and(
                is_early(row_place, group, blocks_dev), is_early(col_place, group, blocks_dev)
            )
            mine = jnp.logical_and(used, jnp.logical_or(mine_far, mine_near))
            early = jnp.logical_and(early, mine)
            room_left = early_rank < early_cap
            early_rank = early_rank + jnp.where(early, 1, 0)
            early = jnp.logical_and(early, room_left)
            mine = jnp.logical_and(mine, early if wanted else jnp.logical_not(early))

            @pl.when(mine)
            def _():
                out_rows[filled] = row_place
                out_cols[filled] = col_place

            near_rank = near_rank + jnp.where(jnp.logical_and(used, jnp.logical_not(far)), 1, 0)
            return (near_rank, early_rank, filled + jnp.where(mine, 1, 0))

        return lax.fori_loop(0, slots, place, (jnp.int32(0), jnp.int32(0), filled))[2]

    early_count = place_those(True, jnp.int32(0))
    out_n[0] = jnp.int32(0)
    out_n[1] = early_count
    out_n[2] = place_those(False, early_count)


def listing(rows, cols, live, group, cap, early_cap, blocks_dev):
    return pl.pallas_call(
        functools.partial(listing_kernel, group, cap, early_cap, blocks_dev),
        out_shape=(
            jax.ShapeDtypeStruct((cap,), jnp.int32),
            jax.ShapeDtypeStruct((cap,), jnp.int32),
            jax.ShapeDtypeStruct((3,), jnp.int32),
        ),
        in_specs=[spec(SMEM)] * 3,
        out_specs=(spec(SMEM),) * 3,
        cost_estimate=cost(2**20, 2**10),
        compiler_params=pltpu.CompilerParams(vmem_limit_bytes=2**20),
        name="listing",
    )(rows, cols, live)


def message_rels(group):
    groups = [[0]]
    for bit in bits_of(group):
        groups.append([rel for rel in range(group) if rel & bit and rel % bit == 0])
    return groups


def product_shapes(group, blocks_dev, height):
    shapes = [
        jax.ShapeDtypeStruct((len(rels) * blocks_dev, height, PTS), jnp.float32)
        for rels in message_rels(group)
    ]
    shapes.append(jax.ShapeDtypeStruct((blocks_dev, height, PTS), jnp.float32))
    return shapes


def write_products(group, blocks_dev, acc, outs):
    for rels, out in zip(message_rels(group), outs[:-1]):
        for index, rel in enumerate(rels):
            for block in range(blocks_dev):
                out[index * blocks_dev + block] = acc[rel * blocks_dev + block]
    for block in range(blocks_dev):
        outs[-1][block] = acc[group * blocks_dev + block]


def set_levels(place, window, level_row, level_col, scale):
    block = window[place * PTS : (place + 1) * PTS, :]
    width = block.shape[1]
    part = jnp.zeros((PTS, 128), jnp.float32)
    for lane in range(0, width, 128):
        wide = block[:, lane : lane + 128].astype(jnp.float32)
        part = part + wide * wide
    level_row[place] = scale * lax.dot_general(
        jnp.ones((8, 128), jnp.float32),
        part,
        (((1,), (1,)), ((), ())),
        precision=HIGHEST,
        preferred_element_type=jnp.float32,
    )
    if place < level_col.shape[0]:
        total = jnp.sum(part, axis=1, keepdims=True) * scale
        level_col[place] = jnp.broadcast_to(total, (PTS, 128))


def make_tiles(low, high, rows, cols, window, level_row, level_col, kept, buffers):
    width = window.shape[1]
    scale = 6.0 / width * LOG2E
    count = high - low
    spare = kept.shape[0] - 1

    def cross(tile, buffer):
        index = low + jnp.minimum(tile, count - 1)
        left = window[pl.ds(pl.multiple_of(rows[index] * PTS, PTS), PTS), :]
        right = window[pl.ds(pl.multiple_of(cols[index] * PTS, PTS), PTS), :]
        buffer[...] = lax.dot_general(
            left, right, (((1,), (1,)), ((), ())), preferred_element_type=jnp.float32
        )

    def finish(tile, buffer):
        valid = jnp.logical_and(tile >= 0, tile < count)
        index = low + jnp.clip(tile, 0, count - 1)
        row, col = rows[index], cols[index]
        right_level = level_row[col][0:1, :]
        left_level = jnp.concatenate([level_col[row]] * (PTS // 128), axis=1)
        value = jnp.exp2(buffer[...] * scale - left_level - right_level)
        kept[jnp.where(valid, tile, spare)] = value.astype(jnp.bfloat16)

    def body(pair, carry):
        cross(2 * pair, buffers[0])
        finish(2 * pair - 1, buffers[1])
        cross(2 * pair + 1, buffers[1])
        finish(2 * pair, buffers[0])
        return carry

    lax.fori_loop(0, jnp.where(count > 0, lax.div(count, 2) + 1, 0), body, 0)


def build_tiles(stage, fresh, places, n, rows, cols, pts, levels, group, blocks_dev, cap, name):
    width = pts[0].shape[1]
    total = (group + 1) * blocks_dev
    near = group * blocks_dev
    level_shapes = [
        jax.ShapeDtypeStruct((total, 8, PTS), jnp.float32),
        jax.ShapeDtypeStruct((near, PTS, 128), jnp.float32),
    ]
    shapes = [jax.ShapeDtypeStruct((cap + 1, PTS, PTS), jnp.bfloat16)] + level_shapes

    def kernel(*refs):
        n_ref, row_ref, col_ref = refs[:3]
        pt_refs = refs[3 : 3 + len(pts)]
        level_refs = refs[3 + len(pts) : 3 + len(pts) + len(levels)]
        kept, level_row, level_col, window, *buffers = refs[3 + len(pts) + len(levels) :]
        for place, piece in zip(places, pt_refs):
            window[place * PTS : place * PTS + piece.shape[0], :] = piece[...]
        for index, (place, piece) in enumerate(zip(places, pt_refs)):
            for block in range(place, place + piece.shape[0] // PTS):
                if index < fresh:
                    set_levels(block, window, level_row, level_col, 3.0 / width * LOG2E)
                else:
                    level_row[block] = level_refs[0][block]
                    if block < near:
                        level_col[block] = level_refs[1][block]
        for buffer in buffers:
            buffer[...] = jnp.zeros((PTS, PTS), jnp.float32)
        make_tiles(
            n_ref[stage],
            n_ref[stage + 1],
            row_ref,
            col_ref,
            window,
            level_row,
            level_col,
            kept,
            buffers,
        )

    return pl.pallas_call(
        kernel,
        out_shape=tuple(shapes),
        in_specs=[spec(SMEM)] * 3 + [spec(VMEM)] * (len(pts) + len(levels)),
        out_specs=(spec(VMEM),) * len(shapes),
        scratch_shapes=[VMEM((total * PTS, width), jnp.bfloat16)]
        + [VMEM((PTS, PTS), jnp.float32)] * 2,
        cost_estimate=cost(2**20 if stage == 0 else 2**32, 2**20),
        compiler_params=pltpu.CompilerParams(vmem_limit_bytes=14 * 2**20),
        name=name,
    )(n, rows, cols, *pts, *levels)


def products(n, rows, cols, vecs, tiles, group, blocks_dev, height, folds):
    pieces = group + 1
    places = pieces * blocks_dev
    tall = vecs[0].shape[0]
    shapes = product_shapes(group, blocks_dev, height)

    def fold(value):
        out = value[:height]
        for index in range(1, folds):
            out = out + value[index * height : (index + 1) * height]
        return out

    def kernel(*refs):
        n_ref, row_ref, col_ref = refs[:3]
        vec_refs = refs[3 : 3 + pieces]
        tile_refs = refs[3 + pieces : 3 + pieces + len(tiles)]
        outs = refs[3 + pieces + len(tiles) : -2]
        u_win, acc = refs[-2:]
        for piece in range(pieces):
            for block in range(blocks_dev):
                lanes = slice(block * PTS, (block + 1) * PTS)
                u_win[piece * blocks_dev + block] = vec_refs[piece][:, lanes]
                acc[piece * blocks_dev + block] = jnp.zeros((height, PTS), jnp.float32)
        for stage, kept in enumerate(tile_refs):
            low = n_ref[stage]

            def body(index, carry):
                row, col = row_ref[index], col_ref[index]
                tile = kept[index - low]
                to_row = lax.dot_general(
                    u_win[col], tile, (((1,), (1,)), ((), ())), preferred_element_type=jnp.float32
                )
                acc[row] += fold(to_row)
                to_col = jnp.dot(u_win[row], tile, preferred_element_type=jnp.float32)
                acc[col] += fold(to_col)
                return carry

            lax.fori_loop(low, n_ref[stage + 1], body, 0)
        write_products(group, blocks_dev, acc, outs)

    return pl.pallas_call(
        kernel,
        out_shape=tuple(shapes),
        in_specs=[spec(SMEM)] * 3 + [spec(VMEM)] * (pieces + len(tiles)),
        out_specs=(spec(VMEM),) * len(shapes),
        scratch_shapes=[
            VMEM((places, tall, PTS), jnp.bfloat16),
            VMEM((places, height, PTS), jnp.float32),
        ],
        cost_estimate=cost(2**32, 2**24),
        compiler_params=pltpu.CompilerParams(vmem_limit_bytes=10 * 2**20),
        name="products",
    )(n, rows, cols, *vecs, *tiles)


def scaled_gram(parts, own, counts, degree, inverse, split):
    columns = own.shape[0] if degree is not None else own.shape[0] - EXTRA
    total = own.shape[1]
    first = degree is None
    shapes = [
        jax.ShapeDtypeStruct((columns, total), jnp.float32),
        jax.ShapeDtypeStruct((columns, columns), jnp.float32),
    ]
    if split:
        shapes.append(jax.ShapeDtypeStruct((2 * columns, total), jnp.bfloat16))
    if first:
        shapes.append(jax.ShapeDtypeStruct((8, total), jnp.float32))
    operands = list(parts) + [own]
    operands += [] if first else [degree]
    operands += [] if inverse is None else [inverse]

    def kernel(count_ref, *refs):
        ins = list(refs[: len(operands)])
        outs = list(refs[len(operands) :])
        part_refs = ins[: len(parts)]
        own_ref = ins[len(parts)]
        z_out, gram_out = outs[:2]
        gram = jnp.zeros((columns, columns), jnp.float32)
        for block in range(total // PTS):
            lanes = slice(block * PTS, (block + 1) * PTS)
            sums = part_refs[0][block]
            for part in part_refs[1:]:
                sums = sums + part[block]
            if first:
                level = 1.0 + sums[columns : columns + 1, :]
                outs[-1][:, lanes] = jnp.broadcast_to(level, (8, PTS))
            else:
                level = ins[len(parts) + 1][0:1, lanes]
            used = lax.broadcasted_iota(jnp.int32, (columns, PTS), 1) < count_ref[block]
            held = own_ref[0:columns, lanes].astype(jnp.float32)
            z = (held + jnp.where(used, sums[0:columns], 0.0)) / level
            if inverse is not None:
                z = jnp.dot(
                    ins[-1][...], z, precision=HIGHEST, preferred_element_type=jnp.float32
                )
            z_out[:, lanes] = z
            if split:
                high = z.astype(jnp.bfloat16)
                outs[2][0:columns, lanes] = high
                rest = z - high.astype(jnp.float32)
                outs[2][columns : 2 * columns, lanes] = rest.astype(jnp.bfloat16)
            gram = gram + lax.dot_general(
                z, z, (((1,), (1,)), ((), ())), precision=HIGHEST, preferred_element_type=jnp.float32
            )
        gram_out[...] = gram

    return pl.pallas_call(
        kernel,
        out_shape=tuple(shapes),
        in_specs=[spec(SMEM)] + [spec(VMEM)] * len(operands),
        out_specs=(spec(VMEM),) * len(shapes),
        cost_estimate=cost(2**26, 2**21),
        compiler_params=pltpu.CompilerParams(vmem_limit_bytes=6 * 2**20),
        name="scaled_gram",
    )(counts, *operands)


def inverse_factor(gram):
    size = gram.shape[0]
    row_id = lax.broadcasted_iota(jnp.int32, (size, size), 0)
    col_id = lax.broadcasted_iota(jnp.int32, (size, size), 1)
    eye = jnp.where(row_id == col_id, 1.0, 0.0)
    whole = jnp.concatenate([gram, eye], axis=1)
    wide = 2 * size
    count = size // 8
    groups = [whole[8 * g : 8 * g + 8, :] for g in range(count)]
    within = lax.broadcasted_iota(jnp.int32, (8, wide), 0)

    def spread_row(value, row):
        return jnp.broadcast_to(value[row : row + 1, :], (8, wide))

    results = []
    for g in range(count):
        spread = [
            [
                jnp.broadcast_to(groups[other][:, 8 * g + k : 8 * g + k + 1], (8, wide))
                for other in range(g, count)
            ]
            for k in range(8)
        ]
        pivots = jnp.ones((8, wide), jnp.float32)
        for j in range(8):
            column = spread[j]
            pivot = spread_row(column[0], j)
            pivots = jnp.where(within == j, pivot, pivots)
            over = 1.0 / pivot
            below = jnp.where(within > j, column[0], 0.0)
            for k in range(j + 1, 8):
                share = spread_row(column[0], k) * over
                spread[k][0] = spread[k][0] - below * share
                for other in range(1, count - g):
                    spread[k][other] = spread[k][other] - column[other] * share
            top = spread_row(groups[g], j) * over
            groups[g] = groups[g] - below * top
            for other in range(1, count - g):
                groups[g + other] = groups[g + other] - column[other] * top
        results.append(groups[g] * lax.rsqrt(pivots))
    return jnp.concatenate(results, axis=0)[:, size:wide]


def factor_kernel(gram, out):
    out[...] = inverse_factor(gram[...])


def factor(gram):
    return pl.pallas_call(
        factor_kernel,
        out_shape=jax.ShapeDtypeStruct(gram.shape, jnp.float32),
        in_specs=[spec(VMEM)],
        out_specs=spec(VMEM),
        cost_estimate=cost(2**31, 2**16),
        compiler_params=pltpu.CompilerParams(vmem_limit_bytes=2 * 2**20),
        name="factor",
    )(gram)


def embed_kernel(gram, z, out):
    out[...] = jnp.dot(
        inverse_factor(gram[...]), z[...], precision=HIGHEST, preferred_element_type=jnp.float32
    )


def embedding(gram, z):
    return pl.pallas_call(
        embed_kernel,
        out_shape=jax.ShapeDtypeStruct(z.shape, jnp.float32),
        in_specs=[spec(VMEM)] * 2,
        out_specs=spec(VMEM),
        cost_estimate=cost(2**30, 2**20),
        compiler_params=pltpu.CompilerParams(vmem_limit_bytes=4 * 2**20),
        name="embedding",
    )(gram, z)


def sum_products(messages, group, blocks_dev):
    rels = message_rels(group)
    parts = {}
    for names, message in zip(rels[1:], messages[1:-1]):
        for index, rel in enumerate(names):
            parts[rel] = [message[index * blocks_dev : (index + 1) * blocks_dev]]
    final = [messages[0], from_behind(messages[-1], "blk", 1)]
    for bit, names, message in zip(bits_of(group), rels[1:], messages[1:-1]):
        if bit > 1:
            message = jnp.concatenate([sum(parts[rel][1:], parts[rel][0]) for rel in names], 0)
        got = swap(message, "grp", bit)
        for index, rel in enumerate(names):
            target = rel ^ bit
            if target == 0:
                final.append(got)
            else:
                parts[target].append(got[index * blocks_dev : (index + 1) * blocks_dev])
    return final


def sum_stages():
    bits = bits_of(lax.axis_size("blk") * lax.axis_size("grp"))
    return [bits[:1]] + [bits[first : first + 2] for first in range(1, len(bits), 2)]


def all_sum(value, stages):
    count = lax.axis_size("blk") * lax.axis_size("grp")
    for bits in stages:
        moves = [0]
        for bit in bits:
            moves += [move ^ bit for move in moves]
        terms = [value] + [
            lax.ppermute(value, ("blk", "grp"), [(source, source ^ move) for source in range(count)])
            for move in moves[1:]
        ]
        while len(terms) > 1:
            terms = [left + right for left, right in zip(terms[::2], terms[1::2])]
        value = terms[0]
    return value


def per_device(points, counts, pair_rows, pair_cols, pair_live, start):
    group = lax.axis_size("grp")
    blocks_dev = counts.shape[0]
    columns = start.shape[0]
    slots = pair_rows.shape[0]
    cap = max(-(-slots // group), blocks_dev * blocks_dev * group)
    early_cap = cap // 2
    half = (blocks_dev // 2) * PTS

    rows, cols, n = listing(pair_rows, pair_cols, pair_live, group, cap, early_cap, blocks_dev)
    mate = swap(points, "grp", 1)
    chunks = [points[:half], points[half:]]
    far = [from_behind(chunk, "blk", -1) for chunk in chunks]
    crossed = [gather_far_bits(chunk) for chunk in chunks]
    begin, mate = lax.optimization_barrier((start, mate))
    vec = opening(begin, counts)
    tied = lax.optimization_barrier((vec, n, rows, cols, far[0], *crossed[0].values()))
    vec, n, rows, cols, far[0] = tied[:5]
    crossed[0] = dict(zip(crossed[0], tied[5:]))
    cross_vec = gather_far_bits(vec)
    far_vec = from_behind(vec, "blk", -1)
    mate_vec = swap(vec, "grp", 1)

    def arrived(index):
        offset = index * (blocks_dev // 2)
        found = [(group * blocks_dev + offset, far[index])]
        return found + [
            (rel * blocks_dev + offset, value) for rel, value in crossed[index].items()
        ]

    def passed_on(index):
        offset = index * (blocks_dev // 2)
        return [
            ((rel ^ 1) * blocks_dev + offset, swap(value, "grp", 1))
            for rel, value in crossed[index].items()
        ]

    def tiles_of(stage, fresh, pieces, levels, size, name):
        places, pts = zip(*pieces)
        return build_tiles(
            stage, fresh, places, n, rows, cols, pts, levels, group, blocks_dev, size, name
        )

    early = [(0, points), (blocks_dev, mate)] + arrived(0)
    early_kept, *levels = tiles_of(0, len(early), early, (), early_cap, "early_tiles")
    tied = lax.optimization_barrier((far[1], levels[0], *crossed[1].values()))
    far[1], levels[0] = tied[:2]
    crossed[1] = dict(zip(crossed[1], tied[2:]))
    late = passed_on(0) + arrived(1) + passed_on(1)
    late_kept, _, _ = tiles_of(1, len(late), late + early, levels, cap, "late_tiles")
    tied = lax.optimization_barrier((late_kept, *cross_vec.values()))
    kept = (early_kept, tied[0])
    cross_vec = dict(zip(cross_vec, tied[1:]))

    vecs = {0: vec, 1: mate_vec}
    for rel, value in cross_vec.items():
        vecs[rel] = value
        vecs[rel ^ 1] = swap(value, "grp", 1)
    vecs = [vecs[rel] for rel in range(group)] + [far_vec]
    messages = products(n, rows, cols, vecs, kept, group, blocks_dev, columns + 8, 1)
    z, gram, parts, degree = scaled_gram(
        sum_products(messages, group, blocks_dev), vec, counts, None, None, True
    )
    for turn in range(1, ITERS):
        stages = sum_stages()
        far_part = from_behind(parts, "blk", -1)
        crossed = gather_far_bits(parts)
        gram = all_sum(gram, stages[:1])
        gram, *tied = lax.optimization_barrier((gram, *crossed.values()))
        vecs = {0: parts, 1: swap(parts, "grp", 1)}
        for rel, value in zip(crossed, tied):
            vecs[rel] = value
            vecs[rel ^ 1] = swap(value, "grp", 1)
        vecs = [vecs[rel] for rel in range(group)] + [far_part]
        gram = all_sum(gram, stages[1:2])
        gram, *vecs = lax.optimization_barrier((gram, *vecs))
        messages = products(n, rows, cols, vecs, kept, group, blocks_dev, columns, 2)
        gram = all_sum(gram, stages[2:])
        gram, *messages = lax.optimization_barrier((gram, *messages))
        sums = sum_products(messages, group, blocks_dev)
        inverse = factor(gram)
        z, gram, *parts = scaled_gram(sums, z, counts, degree, inverse, turn + 1 < ITERS)
        parts = parts[0] if parts else None
    return embedding(all_sum(gram, sum_stages()), z)


def solution(mesh):
    in_specs = (
        P(("blk", "grp"), None),
        P(("blk", "grp")),
        P("blk"),
        P("blk"),
        P("blk"),
        P(None, ("blk", "grp")),
    )
    out_specs = P(None, ("blk", "grp"))
    return jax.shard_map(
        per_device, mesh=mesh, in_specs=in_specs, out_specs=out_specs, check_vma=False
    )
```

```python
import functools

import jax
import jax.numpy as jnp
from jax import lax
from jax.experimental import pallas as pl
from jax.experimental.pallas import tpu as pltpu
from jax.sharding import PartitionSpec as P

PTS = 512
ITERS = 2
LOG2E = 1.4426950408889634
DEAD = 65536.0
EXTRA = 16
VMEM = pltpu.VMEM
SMEM = pltpu.SMEM
HIGHEST = lax.Precision.HIGHEST


def cost(flops, moved):
    return pl.CostEstimate(flops=int(flops), bytes_accessed=int(moved), transcendentals=0)


def spec(space):
    return pl.BlockSpec(memory_space=space)


def swap(value, axis, bit):
    count = lax.axis_size(axis)
    return lax.ppermute(value, axis, [(source, source ^ bit) for source in range(count)])


def from_behind(value, axis, steps):
    count = lax.axis_size(axis)
    initial, last = (max(0, -steps), min(count, count - steps))
    return lax.ppermute(value, axis, [(source, source + steps) for source in range(initial, last)])


def bits_of(count):
    bits = []
    bit = 1
    while bit < count:
        bits.append(bit)
        bit *= 2
    return bits


def gather_near(value, axis):
    held = {0: value}
    for bit in reversed(bits_of(lax.axis_size(axis))):
        for rel in list(held):
            held[rel ^ bit] = swap(held[rel], axis, bit)
    return [held[rel] for rel in range(len(held))]


def gather_far_bits(value):
    held = {0: value}
    for bit in reversed(bits_of(lax.axis_size("grp"))[1:]):
        for rel in list(held):
            held[rel ^ bit] = swap(held[rel], "grp", bit)
    held.pop(0)
    return held


def opening_kernel(start, counts, out):
    columns, total = start.shape
    for block in range(total // PTS):
        lanes = slice(block * PTS, (block + 1) * PTS)
        used = lax.broadcasted_iota(jnp.int32, (columns, PTS), 1) < counts[block]
        out[0:columns, lanes] = jnp.where(used, start[:, lanes], 0.0).astype(jnp.bfloat16)
        which = lax.broadcasted_iota(jnp.int32, (EXTRA, PTS), 0)
        place_in = lax.broadcasted_iota(jnp.int32, (EXTRA, PTS), 1)
        ones = jnp.logical_and(which == 0, place_in < counts[block])
        out[columns : columns + EXTRA, lanes] = jnp.where(ones, 1.0, 0.0).astype(jnp.bfloat16)


def opening(start, counts):
    columns, total = start.shape
    return pl.pallas_call(
        opening_kernel,
        out_shape=jax.ShapeDtypeStruct((columns + EXTRA, total), jnp.bfloat16),
        in_specs=[spec(VMEM), spec(SMEM)],
        out_specs=spec(VMEM),
        cost_estimate=cost(2**20, 2**19),
        compiler_params=pltpu.CompilerParams(vmem_limit_bytes=2 * 2**20),
        name="opening",
    )(start, counts)


def is_early(place, group, blocks_dev):
    near_by = place < min(2, group) * blocks_dev
    direct = lax.rem(lax.div(place, blocks_dev), 2) == 0
    first_half = lax.rem(place, blocks_dev) < blocks_dev // 2
    return jnp.logical_or(near_by, jnp.logical_and(direct, first_half))


def listing_kernel(
    group, cap, early_cap, blocks_dev, rows, cols, live, out_rows, out_cols, out_n, tiles, sources, targets, bounds
):
    slab = blocks_dev * group
    slots = rows.shape[0]
    member = lax.axis_index("grp")

    def local_near(block):
        return (lax.div(block, blocks_dev) ^ member) * blocks_dev + lax.rem(block, blocks_dev)

    def count_far(slot, carry):
        col = cols[slot]
        far = jnp.logical_and(slot < live[0], col >= slab)
        owner = lax.div(col - slab, blocks_dev)
        return tuple(
            old + jnp.where(jnp.logical_and(far, owner == device), 1, 0)
            for device, old in enumerate(carry)
        )

    far_counts = lax.fori_loop(0, slots, count_far, (jnp.int32(0),) * group)
    low = jnp.int32(0)
    room = jnp.int32(0)
    for device in range(group):
        low = low + jnp.where(device < member, cap - far_counts[device], 0)
        room = room + jnp.where(device == member, cap - far_counts[device], 0)

    def place_those(wanted, filled):
        def place(slot, carry):
            near_rank, early_rank, filled = carry
            row, col = rows[slot], cols[slot]
            used = slot < live[0]
            far = col >= slab
            mine_far = jnp.logical_and(far, lax.div(col - slab, blocks_dev) == member)
            mine_near = jnp.logical_and(
                jnp.logical_not(far), jnp.logical_and(near_rank >= low, near_rank < low + room)
            )
            row_place = local_near(row)
            col_place = jnp.where(far, slab + lax.rem(col - slab, blocks_dev), local_near(col))
            early = jnp.logical_and(
                is_early(row_place, group, blocks_dev), is_early(col_place, group, blocks_dev)
            )
            mine = jnp.logical_and(used, jnp.logical_or(mine_far, mine_near))
            early = jnp.logical_and(early, mine)
            room_left = early_rank < early_cap
            early_rank = early_rank + jnp.where(early, 1, 0)
            early = jnp.logical_and(early, room_left)
            mine = jnp.logical_and(mine, early if wanted else jnp.logical_not(early))

            @pl.when(mine)
            def _():
                out_rows[filled] = row_place
                out_cols[filled] = col_place

            near_rank = near_rank + jnp.where(jnp.logical_and(used, jnp.logical_not(far)), 1, 0)
            return (near_rank, early_rank, filled + jnp.where(mine, 1, 0))

        return lax.fori_loop(0, slots, place, (jnp.int32(0), jnp.int32(0), filled))[2]

    early_count = place_those(True, jnp.int32(0))
    count = place_those(False, early_count)
    out_n[0] = jnp.int32(0)
    out_n[1] = early_count
    out_n[2] = count

    home = min(2, group) * blocks_dev
    bounds[0] = jnp.int32(0)
    filled = jnp.int32(0)
    for kind in range(3):
        for to_row in (True, False):

            def enter(index, filled):
                source = (out_cols if to_row else out_rows)[index]
                target = (out_rows if to_row else out_cols)[index]
                if kind == 0:
                    wanted = source < home
                elif kind == 1:
                    wanted = jnp.logical_and(source >= home, target >= blocks_dev)
                else:
                    wanted = jnp.logical_and(source >= home, target < blocks_dev)

                @pl.when(wanted)
                def _():
                    tiles[filled] = jnp.where(
                        index < early_count, index, early_cap + index - early_count
                    )
                    sources[filled] = source
                    targets[filled] = target

                return filled + jnp.where(wanted, 1, 0)

            filled = lax.fori_loop(0, count, enter, filled)
            bounds[2 * kind + (1 if to_row else 2)] = filled


def listing(rows, cols, live, group, cap, early_cap, blocks_dev):
    return pl.pallas_call(
        functools.partial(listing_kernel, group, cap, early_cap, blocks_dev),
        out_shape=(
            jax.ShapeDtypeStruct((cap,), jnp.int32),
            jax.ShapeDtypeStruct((cap,), jnp.int32),
            jax.ShapeDtypeStruct((3,), jnp.int32),
            jax.ShapeDtypeStruct((2 * cap,), jnp.int32),
            jax.ShapeDtypeStruct((2 * cap,), jnp.int32),
            jax.ShapeDtypeStruct((2 * cap,), jnp.int32),
            jax.ShapeDtypeStruct((7,), jnp.int32),
        ),
        in_specs=[spec(SMEM)] * 3,
        out_specs=(spec(SMEM),) * 7,
        cost_estimate=cost(2**20, 2**10),
        compiler_params=pltpu.CompilerParams(vmem_limit_bytes=2**20),
        name="listing",
    )(rows, cols, live)


def set_levels(place, window, level_row, level_col, scale):
    block = window[place * PTS : (place + 1) * PTS, :]
    width = block.shape[1]
    part = jnp.zeros((PTS, 128), jnp.float32)
    for lane in range(0, width, 128):
        wide = block[:, lane : lane + 128].astype(jnp.float32)
        part = part + wide * wide
    level_row[place] = scale * lax.dot_general(
        jnp.ones((8, 128), jnp.float32),
        part,
        (((1,), (1,)), ((), ())),
        precision=HIGHEST,
        preferred_element_type=jnp.float32,
    )
    if place < level_col.shape[0]:
        total = jnp.sum(part, axis=1, keepdims=True) * scale
        level_col[place] = jnp.broadcast_to(total, (PTS, 128))


def make_tiles(low, high, rows, cols, window, level_row, level_col, kept, skip, buffers):
    width = window.shape[1]
    scale = 6.0 / width * LOG2E
    count = high - low
    spare = kept.shape[0] - 1

    def cross(tile, buffer):
        index = low + jnp.minimum(tile, count - 1)
        left = window[pl.ds(pl.multiple_of(rows[index] * PTS, PTS), PTS), :]
        right = window[pl.ds(pl.multiple_of(cols[index] * PTS, PTS), PTS), :]
        buffer[...] = lax.dot_general(
            left, right, (((1,), (1,)), ((), ())), preferred_element_type=jnp.float32
        )

    def finish(tile, buffer):
        valid = jnp.logical_and(tile >= 0, tile < count)
        index = low + jnp.clip(tile, 0, count - 1)
        row, col = rows[index], cols[index]
        right_level = level_row[col][0:1, :]
        left_level = jnp.concatenate([level_col[row]] * (PTS // 128), axis=1)
        value = jnp.exp2(buffer[...] * scale - left_level - right_level)
        kept[jnp.where(valid, skip + tile, spare)] = value.astype(jnp.bfloat16)

    def body(pair, carry):
        cross(2 * pair, buffers[0])
        finish(2 * pair - 1, buffers[1])
        cross(2 * pair + 1, buffers[1])
        finish(2 * pair, buffers[0])
        return carry

    lax.fori_loop(0, jnp.where(count > 0, lax.div(count, 2) + 1, 0), body, 0)


def build_tiles(
    stage, fresh, places, n, rows, cols, pts, levels, before, group, blocks_dev, cap, name
):
    skip = before[0].shape[0] - 1 if before else 0
    width = pts[0].shape[1]
    total = (group + 1) * blocks_dev
    near = group * blocks_dev
    level_shapes = [
        jax.ShapeDtypeStruct((total, 8, PTS), jnp.float32),
        jax.ShapeDtypeStruct((near, PTS, 128), jnp.float32),
    ]
    shapes = [jax.ShapeDtypeStruct((skip + cap + 1, PTS, PTS), jnp.bfloat16)] + level_shapes

    def kernel(*refs):
        n_ref, row_ref, col_ref = refs[:3]
        pt_refs = refs[3 : 3 + len(pts)]
        level_refs = refs[3 + len(pts) : 3 + len(pts) + len(levels)]
        before_refs = refs[3 + len(pts) + len(levels) : 3 + len(pts) + len(levels) + len(before)]
        own_refs = refs[3 + len(pts) + len(levels) + len(before) :]
        kept, level_row, level_col, window, left_buffer, right_buffer, *sems = own_refs
        buffers = (left_buffer, right_buffer)
        copies = [
            pltpu.make_async_copy(ref.at[pl.ds(0, skip)], kept.at[pl.ds(0, skip)], sem)
            for ref, sem in zip(before_refs, sems)
        ]
        for copy in copies:
            copy.start()
        for place, piece in zip(places, pt_refs):
            window[place * PTS : place * PTS + piece.shape[0], :] = piece[...]
        for index, (place, piece) in enumerate(zip(places, pt_refs)):
            for block in range(place, place + piece.shape[0] // PTS):
                if index < fresh:
                    set_levels(block, window, level_row, level_col, 3.0 / width * LOG2E)
                else:
                    level_row[block] = level_refs[0][block]
                    if block < near:
                        level_col[block] = level_refs[1][block]
        for buffer in buffers:
            buffer[...] = jnp.zeros((PTS, PTS), jnp.float32)
        make_tiles(
            n_ref[stage],
            n_ref[stage + 1],
            row_ref,
            col_ref,
            window,
            level_row,
            level_col,
            kept,
            skip,
            buffers,
        )
        for copy in copies:
            copy.wait()

    return pl.pallas_call(
        kernel,
        out_shape=tuple(shapes),
        in_specs=[spec(SMEM)] * 3 + [spec(VMEM)] * (len(pts) + len(levels) + len(before)),
        out_specs=(spec(VMEM),) * len(shapes),
        scratch_shapes=[VMEM((total * PTS, width), jnp.bfloat16)]
        + [VMEM((PTS, PTS), jnp.float32)] * 2
        + [pltpu.SemaphoreType.DMA] * len(before),
        cost_estimate=cost(2**20 if stage == 0 else 2**32, 2**20),
        compiler_params=pltpu.CompilerParams(vmem_limit_bytes=14 * 2**20),
        name=name,
    )(n, rows, cols, *pts, *levels, *before)


def products(entries, kinds, vecs, tiles, start, targets, height, folds):
    firsts = sorted(vecs)
    tall, held = vecs[firsts[0]].shape
    blocks_dev = held // PTS
    begun = sorted(start)
    source_low, source_high = firsts[0], firsts[-1] + blocks_dev
    low = min(first for first, _ in targets)
    high = max(last for _, last in targets)
    shapes = [
        jax.ShapeDtypeStruct((last - first, height, PTS), jnp.float32) for first, last in targets
    ]

    def fold(value):
        out = value[:height]
        for index in range(1, folds):
            out = out + value[index * height : (index + 1) * height]
        return out

    def kernel(*refs):
        tile_ref, source_ref, target_ref, bounds = refs[:4]
        vec_refs = refs[4 : 4 + len(firsts)]
        kept = refs[4 + len(firsts)]
        start_refs = refs[5 + len(firsts) : 5 + len(firsts) + len(begun)]
        outs = refs[5 + len(firsts) + len(begun) : -2]
        u_win, acc = refs[-2:]
        for first, ref in zip(firsts, vec_refs):
            for block in range(blocks_dev):
                lanes = slice(block * PTS, (block + 1) * PTS)
                u_win[first - source_low + block] = ref[:, lanes]
        if begun:
            for first, ref in zip(begun, start_refs):
                acc[first - low : first - low + ref.shape[0]] = ref[...]
        else:
            for place in range(high - low):
                acc[place] = jnp.zeros((height, PTS), jnp.float32)

        def to_row(index, carry):
            value = lax.dot_general(
                u_win[source_ref[index] - source_low],
                kept[tile_ref[index]],
                (((1,), (1,)), ((), ())),
                preferred_element_type=jnp.float32,
            )
            acc[target_ref[index] - low] += fold(value)
            return carry

        def to_col(index, carry):
            value = jnp.dot(
                u_win[source_ref[index] - source_low],
                kept[tile_ref[index]],
                preferred_element_type=jnp.float32,
            )
            acc[target_ref[index] - low] += fold(value)
            return carry

        for kind in kinds:
            lax.fori_loop(bounds[2 * kind], bounds[2 * kind + 1], to_row, 0)
            lax.fori_loop(bounds[2 * kind + 1], bounds[2 * kind + 2], to_col, 0)
        for (first, last), out in zip(targets, outs):
            out[...] = acc[first - low : last - low]

    return pl.pallas_call(
        kernel,
        out_shape=shapes,
        in_specs=[spec(SMEM)] * 4 + [spec(VMEM)] * (len(firsts) + 1 + len(begun)),
        out_specs=[spec(VMEM)] * len(shapes),
        scratch_shapes=[
            VMEM((source_high - source_low, tall, PTS), jnp.bfloat16),
            VMEM((high - low, height, PTS), jnp.float32),
        ],
        cost_estimate=cost(2**31 if kinds == (1,) else 2**20, 2**20),
        compiler_params=pltpu.CompilerParams(vmem_limit_bytes=10 * 2**20),
        name="products",
    )(*entries, *[vecs[first] for first in firsts], tiles, *[start[first] for first in begun])


def urgent_ranges(group, blocks_dev):
    return [(rel * blocks_dev, (rel + 1) * blocks_dev) for rel in range(1, group + 1)]


def send_urgent(results, at_home, group):
    final = [from_behind(results[-1], "blk", 1)]
    parts = {rel: value for rel, value in zip(range(1, group), results)}
    for bit in bits_of(group):
        for rel in reversed([rel for rel in parts if rel & bit and rel % bit == 0]):
            value = parts.pop(rel)
            if bit > 1:
                value, at_home = lax.optimization_barrier((value, at_home))
            got = swap(value, "grp", bit)
            if rel ^ bit:
                parts[rel ^ bit] = parts[rel ^ bit] + got
            else:
                final.append(got)
    return final, at_home


def finish_home(entries, vecs, tiles, start, blocks_dev, height, folds):
    return list(
        products(entries, (2,), vecs, tiles, start, [(0, blocks_dev)], height, folds)
    )


def scaled_gram(parts, own, counts, degree, inverse, split):
    columns = own.shape[0] if degree is not None else own.shape[0] - EXTRA
    total = own.shape[1]
    first = degree is None
    shapes = [
        jax.ShapeDtypeStruct((columns, total), jnp.float32),
        jax.ShapeDtypeStruct((columns, columns), jnp.float32),
    ]
    if split:
        shapes.append(jax.ShapeDtypeStruct((2 * columns, total), jnp.bfloat16))
    if first:
        shapes.append(jax.ShapeDtypeStruct((8, total), jnp.float32))
    operands = list(parts) + [own]
    operands += [] if first else [degree]
    operands += [] if inverse is None else [inverse]

    def kernel(count_ref, *refs):
        ins = list(refs[: len(operands)])
        outs = list(refs[len(operands) :])
        part_refs = ins[: len(parts)]
        own_ref = ins[len(parts)]
        z_out, gram_out = outs[:2]
        gram = jnp.zeros((columns, columns), jnp.float32)
        for block in range(total // PTS):
            lanes = slice(block * PTS, (block + 1) * PTS)
            sums = part_refs[0][block]
            for part in part_refs[1:]:
                sums = sums + part[block]
            if first:
                level = 1.0 + sums[columns : columns + 1, :]
                outs[-1][:, lanes] = jnp.broadcast_to(level, (8, PTS))
            else:
                level = ins[len(parts) + 1][0:1, lanes]
            used = lax.broadcasted_iota(jnp.int32, (columns, PTS), 1) < count_ref[block]
            held = own_ref[0:columns, lanes].astype(jnp.float32)
            z = (held + jnp.where(used, sums[0:columns], 0.0)) / level
            if inverse is not None:
                z = jnp.dot(
                    ins[-1][...], z, precision=HIGHEST, preferred_element_type=jnp.float32
                )
            z_out[:, lanes] = z
            if split:
                high = z.astype(jnp.bfloat16)
                outs[2][0:columns, lanes] = high
                rest = z - high.astype(jnp.float32)
                outs[2][columns : 2 * columns, lanes] = rest.astype(jnp.bfloat16)
            gram = gram + lax.dot_general(
                z, z, (((1,), (1,)), ((), ())), precision=HIGHEST, preferred_element_type=jnp.float32
            )
        gram_out[...] = gram

    return pl.pallas_call(
        kernel,
        out_shape=tuple(shapes),
        in_specs=[spec(SMEM)] + [spec(VMEM)] * len(operands),
        out_specs=(spec(VMEM),) * len(shapes),
        cost_estimate=cost(2**26, 2**21),
        compiler_params=pltpu.CompilerParams(vmem_limit_bytes=6 * 2**20),
        name="scaled_gram",
    )(counts, *operands)


def inverse_factor(gram):
    size = gram.shape[0]
    row_id = lax.broadcasted_iota(jnp.int32, (size, size), 0)
    col_id = lax.broadcasted_iota(jnp.int32, (size, size), 1)
    eye = jnp.where(row_id == col_id, 1.0, 0.0)
    whole = jnp.concatenate([gram, eye], axis=1)
    wide = 2 * size
    count = size // 8
    groups = [whole[8 * g : 8 * g + 8, :] for g in range(count)]
    within = lax.broadcasted_iota(jnp.int32, (8, wide), 0)

    def spread_row(value, row):
        return jnp.broadcast_to(value[row : row + 1, :], (8, wide))

    results = []
    for g in range(count):
        spread = [
            [
                jnp.broadcast_to(groups[other][:, 8 * g + k : 8 * g + k + 1], (8, wide))
                for other in range(g, count)
            ]
            for k in range(8)
        ]
        pivots = jnp.ones((8, wide), jnp.float32)
        for j in range(8):
            column = spread[j]
            pivot = spread_row(column[0], j)
            pivots = jnp.where(within == j, pivot, pivots)
            over = 1.0 / pivot
            below = jnp.where(within > j, column[0], 0.0)
            for k in range(j + 1, 8):
                share = spread_row(column[0], k) * over
                spread[k][0] = spread[k][0] - below * share
                for other in range(1, count - g):
                    spread[k][other] = spread[k][other] - column[other] * share
            top = spread_row(groups[g], j) * over
            groups[g] = groups[g] - below * top
            for other in range(1, count - g):
                groups[g + other] = groups[g + other] - column[other] * top
        results.append(groups[g] * lax.rsqrt(pivots))
    return jnp.concatenate(results, axis=0)[:, size:wide]


def factor_kernel(gram, out):
    out[...] = inverse_factor(gram[...])


def factor(gram):
    return pl.pallas_call(
        factor_kernel,
        out_shape=jax.ShapeDtypeStruct(gram.shape, jnp.float32),
        in_specs=[spec(VMEM)],
        out_specs=spec(VMEM),
        cost_estimate=cost(2**31, 2**16),
        compiler_params=pltpu.CompilerParams(vmem_limit_bytes=2 * 2**20),
        name="factor",
    )(gram)


def embed_kernel(gram, z, out):
    out[...] = jnp.dot(
        inverse_factor(gram[...]), z[...], precision=HIGHEST, preferred_element_type=jnp.float32
    )


def embedding(gram, z):
    return pl.pallas_call(
        embed_kernel,
        out_shape=jax.ShapeDtypeStruct(z.shape, jnp.float32),
        in_specs=[spec(VMEM)] * 2,
        out_specs=spec(VMEM),
        cost_estimate=cost(2**30, 2**20),
        compiler_params=pltpu.CompilerParams(vmem_limit_bytes=4 * 2**20),
        name="embedding",
    )(gram, z)


def sum_stages():
    return bits_of(lax.axis_size("blk") * lax.axis_size("grp"))


def all_sum(value, stages):
    count = lax.axis_size("blk") * lax.axis_size("grp")
    for bits in stages:
        moves = [0]
        for bit in bits if isinstance(bits, list) else [bits]:
            moves += [move ^ bit for move in moves]
        terms = [value] + [
            lax.ppermute(value, ("blk", "grp"), [(source, source ^ move) for source in range(count)])
            for move in moves[1:]
        ]
        while len(terms) > 1:
            terms = [left + right for left, right in zip(terms[::2], terms[1::2])]
        value = terms[0]
    return value


def per_device(points, counts, pair_rows, pair_cols, pair_live, start):
    group = lax.axis_size("grp")
    blocks_dev = counts.shape[0]
    columns = start.shape[0]
    slots = pair_rows.shape[0]
    cap = max(-(-slots // group), blocks_dev * blocks_dev * group)
    early_cap = cap // 2
    half = (blocks_dev // 2) * PTS

    home = min(2, group) * blocks_dev

    rows, cols, n, *entries = listing(
        pair_rows, pair_cols, pair_live, group, cap, early_cap, blocks_dev
    )
    mate = swap(points, "grp", 1)
    chunks = [points[:half], points[half:]]
    far = [from_behind(chunk, "blk", -1) for chunk in chunks]
    crossed = [gather_far_bits(chunk) for chunk in chunks]
    begin, mate = lax.optimization_barrier((start, mate))
    vec = opening(begin, counts)
    tied = lax.optimization_barrier((vec, n, rows, cols, far[0], *crossed[0].values()))
    vec, n, rows, cols, far[0] = tied[:5]
    crossed[0] = dict(zip(crossed[0], tied[5:]))
    cross_vec = gather_far_bits(vec)
    far_vec = from_behind(vec, "blk", -1)
    mate_vec = swap(vec, "grp", 1)

    def arrived(index):
        offset = index * (blocks_dev // 2)
        found = [(group * blocks_dev + offset, far[index])]
        return found + [
            (rel * blocks_dev + offset, value) for rel, value in crossed[index].items()
        ]

    def passed_on(index):
        offset = index * (blocks_dev // 2)
        return [
            ((rel ^ 1) * blocks_dev + offset, swap(value, "grp", 1))
            for rel, value in crossed[index].items()
        ]

    def tiles_of(stage, fresh, pieces, levels, before, size, name):
        places, pts = zip(*pieces)
        return build_tiles(
            stage, fresh, places, n, rows, cols, pts, levels, before, group, blocks_dev, size, name
        )

    early = [(0, points), (blocks_dev, mate)] + arrived(0)
    early_kept, *levels = tiles_of(0, len(early), early, (), (), early_cap, "early_tiles")
    passed = passed_on(0)
    tied = lax.optimization_barrier(
        (far[1], levels[0], mate_vec, *[value for _, value in passed], *crossed[1].values())
    )
    far[1], levels[0], mate_vec = tied[:3]
    passed = [(place, value) for (place, _), value in zip(passed, tied[3:])]
    crossed[1] = dict(zip(crossed[1], tied[3 + len(passed) :]))
    late = passed_on(1)
    late = passed + arrived(1) + late
    kept, _, _ = tiles_of(1, len(late), late + early, levels, (early_kept,), cap, "late_tiles")

    tied = lax.optimization_barrier((kept, *cross_vec.values()))
    kept = tied[0]
    cross_vec = dict(zip(cross_vec, tied[1:]))

    def window_of(own, mate, crossed, far):
        found = {0: own, blocks_dev: mate, group * blocks_dev: far}
        for rel, value in crossed.items():
            found[rel * blocks_dev] = value
            found[(rel ^ 1) * blocks_dev] = swap(value, "grp", 1)
        return found

    def beyond(vecs):
        return {place: value for place, value in vecs.items() if place >= home}

    vecs = window_of(vec, mate_vec, cross_vec, far_vec)
    urgent = urgent_ranges(group, blocks_dev)
    height = columns + 8
    at_home, *results = products(
        entries,
        (0,),
        {0: vec, blocks_dev: mate_vec},
        kept,
        {},
        [(0, blocks_dev)] + urgent,
        height,
        1,
    )
    begun = {first: value for (first, _), value in zip(urgent, results)}
    results = products(entries, (1,), beyond(vecs), kept, begun, urgent, height, 1)
    sums, at_home = send_urgent(results, at_home, group)
    sums = finish_home(entries, beyond(vecs), kept, {0: at_home}, blocks_dev, height, 1) + sums
    z, gram, parts, degree = scaled_gram(sums, vec, counts, None, None, True)
    for turn in range(1, ITERS):
        stages = sum_stages()
        far_part = from_behind(parts, "blk", -1)
        crossed = gather_far_bits(parts)
        mate_part = swap(parts, "grp", 1)
        at_home, *results = products(
            entries,
            (0,),
            {0: parts, blocks_dev: mate_part},
            kept,
            {},
            [(0, blocks_dev)] + urgent,
            columns,
            2,
        )
        gram = all_sum(gram, stages[:1])
        gram, at_home, *tied = lax.optimization_barrier((gram, at_home, *crossed.values()))
        crossed = dict(zip(crossed, tied))
        vecs = beyond(window_of(parts, mate_part, crossed, far_part))
        gram = all_sum(gram, stages[1:2])
        gram, *tied = lax.optimization_barrier((gram, *vecs.values()))
        vecs = dict(zip(vecs, tied))
        begun = {first: value for (first, _), value in zip(urgent, results)}
        results = products(entries, (1,), vecs, kept, begun, urgent, columns, 2)
        gram = all_sum(gram, stages[2:3])
        gram, *results = lax.optimization_barrier((gram, *results))
        sums, at_home = send_urgent(results, at_home, group)
        sums = finish_home(entries, vecs, kept, {0: at_home}, blocks_dev, columns, 2) + sums
        inverse = factor(all_sum(gram, stages[3:]))
        z, gram, *parts = scaled_gram(sums, z, counts, degree, inverse, turn + 1 < ITERS)
        parts = parts[0] if parts else None
    stages = sum_stages()
    pairs = [stages[:1]] + [stages[first : first + 2] for first in range(1, len(stages), 2)]
    return embedding(all_sum(gram, pairs), z)


def solution(mesh):
    in_specs = (
        P(("blk", "grp"), None),
        P(("blk", "grp")),
        P("blk"),
        P("blk"),
        P("blk"),
        P(None, ("blk", "grp")),
    )
    out_specs = P(None, ("blk", "grp"))
    return jax.shard_map(
        per_device, mesh=mesh, in_specs=in_specs, out_specs=out_specs, check_vma=False
    )
```

```python
import functools

import jax
import jax.numpy as jnp
from jax import lax
from jax.experimental import pallas as pl
from jax.experimental.pallas import tpu as pltpu
from jax.sharding import PartitionSpec as P

PTS = 512
ITERS = 2
LOG2E = 1.4426950408889634
DEAD = 65536.0
EXTRA = 16
VMEM = pltpu.VMEM
SMEM = pltpu.SMEM
HIGHEST = lax.Precision.HIGHEST


def cost(flops, moved):
    return pl.CostEstimate(flops=int(flops), bytes_accessed=int(moved), transcendentals=0)


def spec(space):
    return pl.BlockSpec(memory_space=space)


def swap(value, axis, bit):
    count = lax.axis_size(axis)
    return lax.ppermute(value, axis, [(source, source ^ bit) for source in range(count)])


def from_behind(value, axis, steps):
    count = lax.axis_size(axis)
    initial, last = (max(0, -steps), min(count, count - steps))
    return lax.ppermute(value, axis, [(source, source + steps) for source in range(initial, last)])


def bits_of(count):
    bits = []
    bit = 1
    while bit < count:
        bits.append(bit)
        bit *= 2
    return bits


def gather_near(value, axis):
    held = {0: value}
    for bit in reversed(bits_of(lax.axis_size(axis))):
        for rel in list(held):
            held[rel ^ bit] = swap(held[rel], axis, bit)
    return [held[rel] for rel in range(len(held))]


def gather_far_bits(value):
    held = {0: value}
    for bit in reversed(bits_of(lax.axis_size("grp"))[1:]):
        for rel in list(held):
            held[rel ^ bit] = swap(held[rel], "grp", bit)
    held.pop(0)
    return held


def opening_kernel(start, counts, out):
    columns, total = start.shape
    for block in range(total // PTS):
        lanes = slice(block * PTS, (block + 1) * PTS)
        used = lax.broadcasted_iota(jnp.int32, (columns, PTS), 1) < counts[block]
        out[0:columns, lanes] = jnp.where(used, start[:, lanes], 0.0).astype(jnp.bfloat16)
        which = lax.broadcasted_iota(jnp.int32, (EXTRA, PTS), 0)
        place_in = lax.broadcasted_iota(jnp.int32, (EXTRA, PTS), 1)
        ones = jnp.logical_and(which == 0, place_in < counts[block])
        out[columns : columns + EXTRA, lanes] = jnp.where(ones, 1.0, 0.0).astype(jnp.bfloat16)


def opening(start, counts):
    columns, total = start.shape
    return pl.pallas_call(
        opening_kernel,
        out_shape=jax.ShapeDtypeStruct((columns + EXTRA, total), jnp.bfloat16),
        in_specs=[spec(VMEM), spec(SMEM)],
        out_specs=spec(VMEM),
        cost_estimate=cost(2**20, 2**19),
        compiler_params=pltpu.CompilerParams(vmem_limit_bytes=2 * 2**20),
        name="opening",
    )(start, counts)


def stage_of(place, group, blocks_dev):
    piece = lax.div(place, blocks_dev)
    first_half = lax.rem(place, blocks_dev) < blocks_dev // 2
    later = jnp.where(first_half, jnp.where(lax.rem(piece, 2) == 0, 0, 1), 2)
    return jnp.where(piece < min(2, group), 0, later)


def listing_kernel(
    group,
    cap,
    blocks_dev,
    rows,
    cols,
    live,
    out_rows,
    out_cols,
    out_n,
    tiles,
    sources,
    targets,
    bounds,
    owners,
):
    slab = blocks_dev * group
    slots = rows.shape[0]
    member = lax.axis_index("grp")

    def local_near(block, device):
        return (lax.div(block, blocks_dev) ^ device) * blocks_dev + lax.rem(block, blocks_dev)

    def local_far(block):
        return slab + lax.rem(block - slab, blocks_dev)

    def count_far(slot, carry):
        col = cols[slot]
        far = jnp.logical_and(slot < live[0], col >= slab)
        owner = lax.div(col - slab, blocks_dev)
        owners[slot] = jnp.where(far, owner, -1)
        return tuple(
            old + jnp.where(jnp.logical_and(far, owner == device), 1, 0)
            for device, old in enumerate(carry)
        )

    loads = lax.fori_loop(0, slots, count_far, (jnp.int32(0),) * group)

    def give(slot, loads):
        row, col = rows[slot], cols[slot]
        near = jnp.logical_and(slot < live[0], col < slab)
        best = jnp.int32(2**30)
        owner = jnp.int32(0)
        for device in range(group):
            stage = jnp.maximum(
                stage_of(local_near(row, device), group, blocks_dev),
                stage_of(local_near(col, device), group, blocks_dev),
            )
            score = loads[device] + 64 * stage + jnp.where(loads[device] < cap, 0, 2**20)
            owner = jnp.where(score < best, device, owner)
            best = jnp.minimum(score, best)

        @pl.when(near)
        def _():
            owners[slot] = owner

        return tuple(
            load + jnp.where(jnp.logical_and(near, owner == device), 1, 0)
            for device, load in enumerate(loads)
        )

    lax.fori_loop(0, slots, give, loads)

    def place_those(wanted, filled):
        def place(slot, filled):
            row, col = rows[slot], cols[slot]
            row_place = local_near(row, member)
            col_place = jnp.where(col >= slab, local_far(col), local_near(col, member))
            stage = jnp.maximum(
                stage_of(row_place, group, blocks_dev), stage_of(col_place, group, blocks_dev)
            )
            mine = jnp.logical_and(owners[slot] == member, stage == wanted)

            @pl.when(mine)
            def _():
                out_rows[filled] = row_place
                out_cols[filled] = col_place

            return filled + jnp.where(mine, 1, 0)

        return lax.fori_loop(0, slots, place, filled)

    count = jnp.int32(0)
    out_n[0] = count
    for wanted in range(3):
        count = place_those(wanted, count)
        out_n[wanted + 1] = count

    home = min(2, group) * blocks_dev
    bounds[0] = jnp.int32(0)
    filled = jnp.int32(0)
    for kind in range(3):
        for to_row in (True, False):

            def enter(index, filled):
                source = (out_cols if to_row else out_rows)[index]
                target = (out_rows if to_row else out_cols)[index]
                if kind == 0:
                    wanted = source < home
                elif kind == 1:
                    wanted = jnp.logical_and(source >= home, target >= blocks_dev)
                else:
                    wanted = jnp.logical_and(source >= home, target < blocks_dev)

                @pl.when(wanted)
                def _():
                    tiles[filled] = index
                    sources[filled] = source
                    targets[filled] = target

                return filled + jnp.where(wanted, 1, 0)

            filled = lax.fori_loop(0, count, enter, filled)
            bounds[2 * kind + (1 if to_row else 2)] = filled


def listing(rows, cols, live, group, cap, blocks_dev):
    return pl.pallas_call(
        functools.partial(listing_kernel, group, cap, blocks_dev),
        out_shape=(
            jax.ShapeDtypeStruct((cap,), jnp.int32),
            jax.ShapeDtypeStruct((cap,), jnp.int32),
            jax.ShapeDtypeStruct((4,), jnp.int32),
            jax.ShapeDtypeStruct((2 * cap,), jnp.int32),
            jax.ShapeDtypeStruct((2 * cap,), jnp.int32),
            jax.ShapeDtypeStruct((2 * cap,), jnp.int32),
            jax.ShapeDtypeStruct((7,), jnp.int32),
        ),
        in_specs=[spec(SMEM)] * 3,
        out_specs=(spec(SMEM),) * 7,
        scratch_shapes=[SMEM((rows.shape[0],), jnp.int32)],
        cost_estimate=cost(2**20, 2**10),
        compiler_params=pltpu.CompilerParams(vmem_limit_bytes=2**20),
        name="listing",
    )(rows, cols, live)


def set_levels(place, window, level_row, level_col, scale):
    block = window[place * PTS : (place + 1) * PTS, :]
    width = block.shape[1]
    part = jnp.zeros((PTS, 128), jnp.float32)
    for lane in range(0, width, 128):
        wide = block[:, lane : lane + 128].astype(jnp.float32)
        part = part + wide * wide
    level_row[place] = scale * lax.dot_general(
        jnp.ones((8, 128), jnp.float32),
        part,
        (((1,), (1,)), ((), ())),
        precision=HIGHEST,
        preferred_element_type=jnp.float32,
    )
    if place < level_col.shape[0]:
        total = jnp.sum(part, axis=1, keepdims=True) * scale
        level_col[place] = jnp.broadcast_to(total, (PTS, 128))


def make_tiles(low, high, rows, cols, window, level_row, level_col, kept, buffers):
    width = window.shape[1]
    scale = 6.0 / width * LOG2E
    count = high - low
    spare = kept.shape[0] - 1

    def cross(tile, buffer):
        index = low + jnp.minimum(tile, count - 1)
        left = window[pl.ds(pl.multiple_of(rows[index] * PTS, PTS), PTS), :]
        right = window[pl.ds(pl.multiple_of(cols[index] * PTS, PTS), PTS), :]
        buffer[...] = lax.dot_general(
            left, right, (((1,), (1,)), ((), ())), preferred_element_type=jnp.float32
        )

    def finish(tile, buffer):
        valid = jnp.logical_and(tile >= 0, tile < count)
        index = low + jnp.clip(tile, 0, count - 1)
        row, col = rows[index], cols[index]
        right_level = level_row[col][0:1, :]
        left_level = jnp.concatenate([level_col[row]] * (PTS // 128), axis=1)
        value = jnp.exp2(buffer[...] * scale - left_level - right_level)
        kept[jnp.where(valid, index, spare)] = value.astype(jnp.bfloat16)

    def body(pair, carry):
        cross(2 * pair, buffers[0])
        finish(2 * pair - 1, buffers[1])
        cross(2 * pair + 1, buffers[1])
        finish(2 * pair, buffers[0])
        return carry

    @pl.when(count > 0)
    def _():
        buffers[1][...] = jnp.zeros((PTS, PTS), jnp.float32)

    lax.fori_loop(0, jnp.where(count > 0, lax.div(count, 2) + 1, 0), body, 0)


def build_tiles(stage, fresh, n, rows, cols, state, group, blocks_dev, cap, name):
    places = list(fresh)
    pts = list(fresh.values())
    width = pts[0].shape[1]
    total = (group + 1) * blocks_dev
    near = group * blocks_dev
    shapes = [
        jax.ShapeDtypeStruct((total * PTS, width), jnp.bfloat16),
        jax.ShapeDtypeStruct((total, 8, PTS), jnp.float32),
        jax.ShapeDtypeStruct((near, PTS, 128), jnp.float32),
    ]
    makes = stage is not None
    if makes:
        shapes.append(jax.ShapeDtypeStruct((cap + 1, PTS, PTS), jnp.bfloat16))
    state = state[: len(shapes)]
    scalars = (n, rows, cols) if makes else ()
    first = len(scalars) + len(pts)

    def kernel(*refs):
        pt_refs = refs[len(scalars) : first]
        window, level_row, level_col, *rest = refs[first + len(state) :]
        for place, piece in zip(places, pt_refs):
            blocks = piece.shape[0] // PTS
            window[place * PTS : (place + blocks) * PTS, :] = piece[...]
            for block in range(place, place + blocks):
                set_levels(block, window, level_row, level_col, 3.0 / width * LOG2E)
        if makes:
            n_ref, row_ref, col_ref = refs[:3]
            kept, *buffers = rest
            make_tiles(
                n_ref[stage],
                n_ref[stage + 1],
                row_ref,
                col_ref,
                window,
                level_row,
                level_col,
                kept,
                buffers,
            )

    return pl.pallas_call(
        kernel,
        out_shape=shapes,
        in_specs=[spec(SMEM)] * len(scalars) + [spec(VMEM)] * (len(pts) + len(state)),
        out_specs=[spec(VMEM)] * len(shapes),
        input_output_aliases={first + index: index for index in range(len(state))},
        scratch_shapes=[VMEM((PTS, PTS), jnp.float32)] * (2 if makes else 0),
        cost_estimate=cost(2**32 if stage == 2 else 2**20, 2**20),
        compiler_params=pltpu.CompilerParams(vmem_limit_bytes=6 * 2**20),
        name=name,
    )(*scalars, *pts, *state)


def products(entries, kinds, vecs, tiles, start, targets, height, folds):
    firsts = sorted(vecs)
    tall, held = vecs[firsts[0]].shape
    blocks_dev = held // PTS
    begun = sorted(start)
    source_low, source_high = firsts[0], firsts[-1] + blocks_dev
    low = min(first for first, _ in targets)
    high = max(last for _, last in targets)
    shapes = [
        jax.ShapeDtypeStruct((last - first, height, PTS), jnp.float32) for first, last in targets
    ]

    def fold(value):
        out = value[:height]
        for index in range(1, folds):
            out = out + value[index * height : (index + 1) * height]
        return out

    def kernel(*refs):
        tile_ref, source_ref, target_ref, bounds = refs[:4]
        vec_refs = refs[4 : 4 + len(firsts)]
        kept = refs[4 + len(firsts)]
        start_refs = refs[5 + len(firsts) : 5 + len(firsts) + len(begun)]
        outs = refs[5 + len(firsts) + len(begun) : -2]
        u_win, acc = refs[-2:]
        for first, ref in zip(firsts, vec_refs):
            for block in range(blocks_dev):
                lanes = slice(block * PTS, (block + 1) * PTS)
                u_win[first - source_low + block] = ref[:, lanes]
        if begun:
            for first, ref in zip(begun, start_refs):
                acc[first - low : first - low + ref.shape[0]] = ref[...]
        else:
            for place in range(high - low + 1):
                acc[place] = jnp.zeros((height, PTS), jnp.float32)

        spare = high - low
        unroll = 4

        def several(begin, end, transposed):
            def body(step, carry):
                done = []
                for lane in range(unroll):
                    index = begin + step * unroll + lane
                    valid = index < end
                    index = jnp.minimum(index, end - 1)
                    vec = u_win[source_ref[index] - source_low]
                    tile = kept[tile_ref[index]]
                    if transposed:
                        value = lax.dot_general(
                            vec,
                            tile,
                            (((1,), (1,)), ((), ())),
                            preferred_element_type=jnp.float32,
                        )
                    else:
                        value = jnp.dot(vec, tile, preferred_element_type=jnp.float32)
                    done.append((jnp.where(valid, target_ref[index] - low, spare), fold(value)))
                for target, value in done:
                    acc[target] += value
                return carry

            lax.fori_loop(0, lax.div(end - begin + unroll - 1, unroll), body, 0)

        for kind in kinds:
            several(bounds[2 * kind], bounds[2 * kind + 1], True)
            several(bounds[2 * kind + 1], bounds[2 * kind + 2], False)
        for (first, last), out in zip(targets, outs):
            out[...] = acc[first - low : last - low]

    return pl.pallas_call(
        kernel,
        out_shape=shapes,
        in_specs=[spec(SMEM)] * 4 + [spec(VMEM)] * (len(firsts) + 1 + len(begun)),
        out_specs=[spec(VMEM)] * len(shapes),
        scratch_shapes=[
            VMEM((source_high - source_low, tall, PTS), jnp.bfloat16),
            VMEM((high - low + 1, height, PTS), jnp.float32),
        ],
        cost_estimate=cost(2**31 if kinds == (1,) else 2**20, 2**20),
        compiler_params=pltpu.CompilerParams(vmem_limit_bytes=10 * 2**20),
        name="products",
    )(*entries, *[vecs[first] for first in firsts], tiles, *[start[first] for first in begun])


def urgent_ranges(group, blocks_dev):
    return [(rel * blocks_dev, (rel + 1) * blocks_dev) for rel in range(1, group + 1)]


def send_urgent(results, at_home, group):
    final = [from_behind(results[-1], "blk", 1)]
    parts = {rel: value for rel, value in zip(range(1, group), results)}
    for bit in bits_of(group):
        for rel in reversed([rel for rel in parts if rel & bit and rel % bit == 0]):
            value = parts.pop(rel)
            if bit > 1:
                value, at_home = lax.optimization_barrier((value, at_home))
            got = swap(value, "grp", bit)
            if rel ^ bit:
                parts[rel ^ bit] = parts[rel ^ bit] + got
            else:
                final.append(got)
    return final, at_home


def finish_home(entries, vecs, tiles, start, blocks_dev, height, folds):
    return list(
        products(entries, (2,), vecs, tiles, start, [(0, blocks_dev)], height, folds)
    )


def scaled_gram(parts, own, counts, degree, inverse, split):
    columns = own.shape[0] if degree is not None else own.shape[0] - EXTRA
    total = own.shape[1]
    first = degree is None
    shapes = [
        jax.ShapeDtypeStruct((columns, total), jnp.float32),
        jax.ShapeDtypeStruct((columns, columns), jnp.float32),
    ]
    if split:
        shapes.append(jax.ShapeDtypeStruct((2 * columns, total), jnp.bfloat16))
    if first:
        shapes.append(jax.ShapeDtypeStruct((8, total), jnp.float32))
    operands = list(parts) + [own]
    operands += [] if first else [degree]
    operands += [] if inverse is None else [inverse]

    def kernel(count_ref, *refs):
        ins = list(refs[: len(operands)])
        outs = list(refs[len(operands) :])
        part_refs = ins[: len(parts)]
        own_ref = ins[len(parts)]
        z_out, gram_out = outs[:2]
        gram = jnp.zeros((columns, columns), jnp.float32)
        for block in range(total // PTS):
            lanes = slice(block * PTS, (block + 1) * PTS)
            sums = part_refs[0][block]
            for part in part_refs[1:]:
                sums = sums + part[block]
            if first:
                level = 1.0 + sums[columns : columns + 1, :]
                outs[-1][:, lanes] = jnp.broadcast_to(level, (8, PTS))
            else:
                level = ins[len(parts) + 1][0:1, lanes]
            used = lax.broadcasted_iota(jnp.int32, (columns, PTS), 1) < count_ref[block]
            held = own_ref[0:columns, lanes].astype(jnp.float32)
            z = (held + jnp.where(used, sums[0:columns], 0.0)) / level
            if inverse is not None:
                z = jnp.dot(
                    ins[-1][...], z, precision=HIGHEST, preferred_element_type=jnp.float32
                )
            z_out[:, lanes] = z
            if split:
                high = z.astype(jnp.bfloat16)
                outs[2][0:columns, lanes] = high
                rest = z - high.astype(jnp.float32)
                outs[2][columns : 2 * columns, lanes] = rest.astype(jnp.bfloat16)
            gram = gram + lax.dot_general(
                z, z, (((1,), (1,)), ((), ())), precision=HIGHEST, preferred_element_type=jnp.float32
            )
        gram_out[...] = gram

    return pl.pallas_call(
        kernel,
        out_shape=tuple(shapes),
        in_specs=[spec(SMEM)] + [spec(VMEM)] * len(operands),
        out_specs=(spec(VMEM),) * len(shapes),
        cost_estimate=cost(2**26, 2**21),
        compiler_params=pltpu.CompilerParams(vmem_limit_bytes=6 * 2**20),
        name="scaled_gram",
    )(counts, *operands)


def inverse_factor(gram):
    size = gram.shape[0]
    row_id = lax.broadcasted_iota(jnp.int32, (size, size), 0)
    col_id = lax.broadcasted_iota(jnp.int32, (size, size), 1)
    eye = jnp.where(row_id == col_id, 1.0, 0.0)
    whole = jnp.concatenate([gram, eye], axis=1)
    wide = 2 * size
    count = size // 8
    groups = [whole[8 * g : 8 * g + 8, :] for g in range(count)]
    within = lax.broadcasted_iota(jnp.int32, (8, wide), 0)

    def spread_row(value, row):
        return jnp.broadcast_to(value[row : row + 1, :], (8, wide))

    results = []
    for g in range(count):
        spread = [
            [
                jnp.broadcast_to(groups[other][:, 8 * g + k : 8 * g + k + 1], (8, wide))
                for other in range(g, count)
            ]
            for k in range(8)
        ]
        pivots = jnp.ones((8, wide), jnp.float32)
        for j in range(8):
            column = spread[j]
            pivot = spread_row(column[0], j)
            pivots = jnp.where(within == j, pivot, pivots)
            over = 1.0 / pivot
            below = jnp.where(within > j, column[0], 0.0)
            for k in range(j + 1, 8):
                share = spread_row(column[0], k) * over
                spread[k][0] = spread[k][0] - below * share
                for other in range(1, count - g):
                    spread[k][other] = spread[k][other] - column[other] * share
            top = spread_row(groups[g], j) * over
            groups[g] = groups[g] - below * top
            for other in range(1, count - g):
                groups[g + other] = groups[g + other] - column[other] * top
        results.append(groups[g] * lax.rsqrt(pivots))
    return jnp.concatenate(results, axis=0)[:, size:wide]


def factor_kernel(gram, out):
    out[...] = inverse_factor(gram[...])


def factor(gram):
    return pl.pallas_call(
        factor_kernel,
        out_shape=jax.ShapeDtypeStruct(gram.shape, jnp.float32),
        in_specs=[spec(VMEM)],
        out_specs=spec(VMEM),
        cost_estimate=cost(2**31, 2**16),
        compiler_params=pltpu.CompilerParams(vmem_limit_bytes=2 * 2**20),
        name="factor",
    )(gram)


def embed_kernel(gram, z, out):
    out[...] = jnp.dot(
        inverse_factor(gram[...]), z[...], precision=HIGHEST, preferred_element_type=jnp.float32
    )


def embedding(gram, z):
    return pl.pallas_call(
        embed_kernel,
        out_shape=jax.ShapeDtypeStruct(z.shape, jnp.float32),
        in_specs=[spec(VMEM)] * 2,
        out_specs=spec(VMEM),
        cost_estimate=cost(2**30, 2**20),
        compiler_params=pltpu.CompilerParams(vmem_limit_bytes=4 * 2**20),
        name="embedding",
    )(gram, z)


def sum_stages():
    return bits_of(lax.axis_size("blk") * lax.axis_size("grp"))


def pairs_of(bits):
    return [bits[first : first + 2] for first in range(0, len(bits), 2)]


def all_sum(value, stages):
    count = lax.axis_size("blk") * lax.axis_size("grp")
    for bits in stages:
        moves = [0]
        for bit in bits if isinstance(bits, list) else [bits]:
            moves += [move ^ bit for move in moves]
        terms = [value] + [
            lax.ppermute(value, ("blk", "grp"), [(source, source ^ move) for source in range(count)])
            for move in moves[1:]
        ]
        while len(terms) > 1:
            terms = [left + right for left, right in zip(terms[::2], terms[1::2])]
        value = terms[0]
    return value


def per_device(points, counts, pair_rows, pair_cols, pair_live, start):
    group = lax.axis_size("grp")
    blocks_dev = counts.shape[0]
    columns = start.shape[0]
    slots = pair_rows.shape[0]
    cap = max(-(-slots // group), blocks_dev * blocks_dev * group)
    half = (blocks_dev // 2) * PTS

    home = min(2, group) * blocks_dev

    rows, cols, n, *entries = listing(
        pair_rows, pair_cols, pair_live, group, cap, blocks_dev
    )
    mate = swap(points, "grp", 1)
    chunks = [points[:half], points[half:]]
    far = [from_behind(chunk, "blk", -1) for chunk in chunks]
    crossed = [gather_far_bits(chunk) for chunk in chunks]
    begin, mate = lax.optimization_barrier((start, mate))
    vec = opening(begin, counts)
    tied = lax.optimization_barrier((vec, n, rows, cols, far[0], *crossed[0].values()))
    vec, n, rows, cols, far[0] = tied[:5]
    crossed[0] = dict(zip(crossed[0], tied[5:]))
    cross_vec = gather_far_bits(vec)
    far_vec = from_behind(vec, "blk", -1)
    mate_vec = swap(vec, "grp", 1)

    def direct(index):
        offset = index * (blocks_dev // 2)
        found = {group * blocks_dev + offset: far[index]}
        for rel, value in crossed[index].items():
            found[rel * blocks_dev + offset] = value
        return found

    def passed_on(index):
        offset = index * (blocks_dev // 2)
        return {
            (rel ^ 1) * blocks_dev + offset: swap(value, "grp", 1)
            for rel, value in crossed[index].items()
        }

    def build(stage, fresh, state, name):
        return list(
            build_tiles(stage, fresh, n, rows, cols, state, group, blocks_dev, cap, name)
        )

    state = build(0, {0: points, blocks_dev: mate, **direct(0)}, (), "first_tiles")
    tied = lax.optimization_barrier((far[1], mate_vec, state[1], *crossed[1].values()))
    far[1], mate_vec, state[1] = tied[:3]
    crossed[1] = dict(zip(crossed[1], tied[3:]))
    state = build(1, passed_on(0), state, "second_tiles")
    last = passed_on(1)
    *grown, kept = state
    state = build(None, direct(1), grown, "more_blocks") + [kept]
    state = build(2, last, state, "last_tiles")
    kept = state[-1]
    tied = lax.optimization_barrier((kept, *cross_vec.values()))
    kept = tied[0]
    cross_vec = dict(zip(cross_vec, tied[1:]))

    def window_of(own, mate, crossed, far):
        found = {0: own, blocks_dev: mate, group * blocks_dev: far}
        for rel, value in crossed.items():
            found[rel * blocks_dev] = value
            found[(rel ^ 1) * blocks_dev] = swap(value, "grp", 1)
        return found

    def beyond(vecs):
        return {place: value for place, value in vecs.items() if place >= home}

    vecs = window_of(vec, mate_vec, cross_vec, far_vec)
    urgent = urgent_ranges(group, blocks_dev)
    height = columns + 8
    at_home, *results = products(
        entries,
        (0,),
        {0: vec, blocks_dev: mate_vec},
        kept,
        {},
        [(0, blocks_dev)] + urgent,
        height,
        1,
    )
    begun = {first: value for (first, _), value in zip(urgent, results)}
    results = products(entries, (1,), beyond(vecs), kept, begun, urgent, height, 1)
    sums, at_home = send_urgent(results, at_home, group)
    sums = finish_home(entries, beyond(vecs), kept, {0: at_home}, blocks_dev, height, 1) + sums
    z, gram, parts, degree = scaled_gram(sums, vec, counts, None, None, True)
    for turn in range(1, ITERS):
        stages = sum_stages()
        far_part = from_behind(parts, "blk", -1)
        crossed = gather_far_bits(parts)
        mate_part = swap(parts, "grp", 1)
        at_home, *results = products(
            entries,
            (0,),
            {0: parts, blocks_dev: mate_part},
            kept,
            {},
            [(0, blocks_dev)] + urgent,
            columns,
            2,
        )
        gram = all_sum(gram, stages[:1])
        gram, at_home, *tied = lax.optimization_barrier((gram, at_home, *crossed.values()))
        crossed = dict(zip(crossed, tied))
        vecs = beyond(window_of(parts, mate_part, crossed, far_part))
        gram = all_sum(gram, stages[1:2])
        gram, *tied = lax.optimization_barrier((gram, *vecs.values()))
        vecs = dict(zip(vecs, tied))
        begun = {first: value for (first, _), value in zip(urgent, results)}
        results = products(entries, (1,), vecs, kept, begun, urgent, columns, 2)
        gram = all_sum(gram, stages[2:3])
        gram, *results = lax.optimization_barrier((gram, *results))
        sums, at_home = send_urgent(results, at_home, group)
        sums = finish_home(entries, vecs, kept, {0: at_home}, blocks_dev, columns, 2) + sums
        inverse = factor(all_sum(gram, pairs_of(stages[3:])))
        z, gram, *parts = scaled_gram(sums, z, counts, degree, inverse, turn + 1 < ITERS)
        parts = parts[0] if parts else None
    stages = sum_stages()
    return embedding(all_sum(gram, stages[:1] + pairs_of(stages[1:])), z)


def solution(mesh):
    in_specs = (
        P(("blk", "grp"), None),
        P(("blk", "grp")),
        P("blk"),
        P("blk"),
        P("blk"),
        P(None, ("blk", "grp")),
    )
    out_specs = P(None, ("blk", "grp"))
    return jax.shard_map(
        per_device, mesh=mesh, in_specs=in_specs, out_specs=out_specs, check_vma=False
    )
```

```python
import functools

import jax
import jax.numpy as jnp
from jax import lax
from jax.experimental import pallas as pl
from jax.experimental.pallas import tpu as pltpu
from jax.sharding import PartitionSpec as P

PTS = 512
ITERS = 2
LOG2E = 1.4426950408889634
DEAD = 65536.0
EXTRA = 16
VMEM = pltpu.VMEM
SMEM = pltpu.SMEM
HIGHEST = lax.Precision.HIGHEST


def cost(flops, moved):
    return pl.CostEstimate(flops=int(flops), bytes_accessed=int(moved), transcendentals=0)


def spec(space):
    return pl.BlockSpec(memory_space=space)


def swap(value, axis, bit):
    count = lax.axis_size(axis)
    return lax.ppermute(value, axis, [(source, source ^ bit) for source in range(count)])


def from_behind(value, axis, steps):
    count = lax.axis_size(axis)
    initial, last = (max(0, -steps), min(count, count - steps))
    return lax.ppermute(value, axis, [(source, source + steps) for source in range(initial, last)])


def bits_of(count):
    bits = []
    bit = 1
    while bit < count:
        bits.append(bit)
        bit *= 2
    return bits


def gather_near(value, axis):
    held = {0: value}
    for bit in reversed(bits_of(lax.axis_size(axis))):
        for rel in list(held):
            held[rel ^ bit] = swap(held[rel], axis, bit)
    return [held[rel] for rel in range(len(held))]


def gather_far_bits(value):
    held = {0: value}
    for bit in reversed(bits_of(lax.axis_size("grp"))[1:]):
        for rel in list(held):
            held[rel ^ bit] = swap(held[rel], "grp", bit)
    held.pop(0)
    return held


def opening_kernel(start, counts, out):
    columns, total = start.shape
    for block in range(total // PTS):
        lanes = slice(block * PTS, (block + 1) * PTS)
        used = lax.broadcasted_iota(jnp.int32, (columns, PTS), 1) < counts[block]
        out[0:columns, lanes] = jnp.where(used, start[:, lanes], 0.0).astype(jnp.bfloat16)
        which = lax.broadcasted_iota(jnp.int32, (EXTRA, PTS), 0)
        place_in = lax.broadcasted_iota(jnp.int32, (EXTRA, PTS), 1)
        ones = jnp.logical_and(which == 0, place_in < counts[block])
        out[columns : columns + EXTRA, lanes] = jnp.where(ones, 1.0, 0.0).astype(jnp.bfloat16)


def opening(start, counts):
    columns, total = start.shape
    return pl.pallas_call(
        opening_kernel,
        out_shape=jax.ShapeDtypeStruct((columns + EXTRA, total), jnp.bfloat16),
        in_specs=[spec(VMEM), spec(SMEM)],
        out_specs=spec(VMEM),
        cost_estimate=cost(2**20, 2**19),
        compiler_params=pltpu.CompilerParams(vmem_limit_bytes=2 * 2**20),
        name="opening",
    )(start, counts)


def stage_of(place, group, blocks_dev):
    piece = lax.div(place, blocks_dev)
    first_half = lax.rem(place, blocks_dev) < blocks_dev // 2
    later = jnp.where(first_half, jnp.where(lax.rem(piece, 2) == 0, 0, 1), 2)
    return jnp.where(piece < min(2, group), 0, later)


def listing_kernel(
    group,
    cap,
    blocks_dev,
    rows,
    cols,
    live,
    out_rows,
    out_cols,
    out_n,
    tiles,
    sources,
    targets,
    bounds,
    owners,
):
    slab = blocks_dev * group
    slots = rows.shape[0]
    member = lax.axis_index("grp")

    def local_near(block, device):
        return (lax.div(block, blocks_dev) ^ device) * blocks_dev + lax.rem(block, blocks_dev)

    def local_far(block):
        return slab + lax.rem(block - slab, blocks_dev)

    def count_far(slot, carry):
        col = cols[slot]
        far = jnp.logical_and(slot < live[0], col >= slab)
        owner = lax.div(col - slab, blocks_dev)
        owners[slot] = jnp.where(far, owner, -1)
        return tuple(
            old + jnp.where(jnp.logical_and(far, owner == device), 1, 0)
            for device, old in enumerate(carry)
        )

    loads = lax.fori_loop(0, slots, count_far, (jnp.int32(0),) * group)

    def give(slot, loads):
        row, col = rows[slot], cols[slot]
        near = jnp.logical_and(slot < live[0], col < slab)
        best = jnp.int32(2**30)
        owner = jnp.int32(0)
        for device in range(group):
            stage = jnp.maximum(
                stage_of(local_near(row, device), group, blocks_dev),
                stage_of(local_near(col, device), group, blocks_dev),
            )
            score = loads[device] + 64 * stage + jnp.where(loads[device] < cap, 0, 2**20)
            owner = jnp.where(score < best, device, owner)
            best = jnp.minimum(score, best)

        @pl.when(near)
        def _():
            owners[slot] = owner

        return tuple(
            load + jnp.where(jnp.logical_and(near, owner == device), 1, 0)
            for device, load in enumerate(loads)
        )

    lax.fori_loop(0, slots, give, loads)

    def place_those(wanted, filled):
        def place(slot, filled):
            row, col = rows[slot], cols[slot]
            row_place = local_near(row, member)
            col_place = jnp.where(col >= slab, local_far(col), local_near(col, member))
            stage = jnp.maximum(
                stage_of(row_place, group, blocks_dev), stage_of(col_place, group, blocks_dev)
            )
            mine = jnp.logical_and(owners[slot] == member, stage == wanted)

            @pl.when(mine)
            def _():
                out_rows[filled] = row_place
                out_cols[filled] = col_place

            return filled + jnp.where(mine, 1, 0)

        return lax.fori_loop(0, slots, place, filled)

    count = jnp.int32(0)
    out_n[0] = count
    for wanted in range(3):
        count = place_those(wanted, count)
        out_n[wanted + 1] = count

    home = min(2, group) * blocks_dev
    bounds[0] = jnp.int32(0)
    filled = jnp.int32(0)
    for kind in range(3):
        for to_row in (True, False):

            def enter(index, filled):
                source = (out_cols if to_row else out_rows)[index]
                target = (out_rows if to_row else out_cols)[index]
                if kind == 0:
                    wanted = source < home
                elif kind == 1:
                    wanted = jnp.logical_and(source >= home, target >= blocks_dev)
                else:
                    wanted = jnp.logical_and(source >= home, target < blocks_dev)

                @pl.when(wanted)
                def _():
                    tiles[filled] = index
                    sources[filled] = source
                    targets[filled] = target

                return filled + jnp.where(wanted, 1, 0)

            filled = lax.fori_loop(0, count, enter, filled)
            bounds[2 * kind + (1 if to_row else 2)] = filled


def listing(rows, cols, live, group, cap, blocks_dev):
    return pl.pallas_call(
        functools.partial(listing_kernel, group, cap, blocks_dev),
        out_shape=(
            jax.ShapeDtypeStruct((cap,), jnp.int32),
            jax.ShapeDtypeStruct((cap,), jnp.int32),
            jax.ShapeDtypeStruct((4,), jnp.int32),
            jax.ShapeDtypeStruct((2 * cap,), jnp.int32),
            jax.ShapeDtypeStruct((2 * cap,), jnp.int32),
            jax.ShapeDtypeStruct((2 * cap,), jnp.int32),
            jax.ShapeDtypeStruct((7,), jnp.int32),
        ),
        in_specs=[spec(SMEM)] * 3,
        out_specs=(spec(SMEM),) * 7,
        scratch_shapes=[SMEM((rows.shape[0],), jnp.int32)],
        cost_estimate=cost(2**20, 2**10),
        compiler_params=pltpu.CompilerParams(vmem_limit_bytes=2**20),
        name="listing",
    )(rows, cols, live)


def set_levels(place, window, level_row, level_col, scale):
    block = window[place * PTS : (place + 1) * PTS, :]
    width = block.shape[1]
    part = jnp.zeros((PTS, 128), jnp.float32)
    for lane in range(0, width, 128):
        wide = block[:, lane : lane + 128].astype(jnp.float32)
        part = part + wide * wide
    level_row[place] = scale * lax.dot_general(
        jnp.ones((8, 128), jnp.float32),
        part,
        (((1,), (1,)), ((), ())),
        precision=HIGHEST,
        preferred_element_type=jnp.float32,
    )
    if place < level_col.shape[0]:
        total = jnp.sum(part, axis=1, keepdims=True) * scale
        level_col[place] = jnp.broadcast_to(total, (PTS, 128))


def make_tiles(low, high, rows, cols, window, level_row, level_col, kept, buffers):
    width = window.shape[1]
    scale = 6.0 / width * LOG2E
    count = high - low
    spare = kept.shape[0] - 1

    def cross(tile, buffer):
        index = low + jnp.minimum(tile, count - 1)
        left = window[pl.ds(pl.multiple_of(rows[index] * PTS, PTS), PTS), :]
        right = window[pl.ds(pl.multiple_of(cols[index] * PTS, PTS), PTS), :]
        buffer[...] = lax.dot_general(
            left, right, (((1,), (1,)), ((), ())), preferred_element_type=jnp.float32
        )

    def finish(tile, buffer):
        valid = jnp.logical_and(tile >= 0, tile < count)
        index = low + jnp.clip(tile, 0, count - 1)
        row, col = rows[index], cols[index]
        right_level = level_row[col][0:1, :]
        left_level = jnp.concatenate([level_col[row]] * (PTS // 128), axis=1)
        value = jnp.exp2(buffer[...] * scale - left_level - right_level)
        kept[jnp.where(valid, index, spare)] = value.astype(jnp.bfloat16)

    def body(pair, carry):
        cross(2 * pair, buffers[0])
        finish(2 * pair - 1, buffers[1])
        cross(2 * pair + 1, buffers[1])
        finish(2 * pair, buffers[0])
        return carry

    @pl.when(count > 0)
    def _():
        buffers[1][...] = jnp.zeros((PTS, PTS), jnp.float32)

    lax.fori_loop(0, jnp.where(count > 0, lax.div(count, 2) + 1, 0), body, 0)


def build_tiles(stage, fresh, n, rows, cols, state, group, blocks_dev, cap, name):
    places = list(fresh)
    pts = list(fresh.values())
    width = pts[0].shape[1]
    total = (group + 1) * blocks_dev
    near = group * blocks_dev
    shapes = [
        jax.ShapeDtypeStruct((total * PTS, width), jnp.bfloat16),
        jax.ShapeDtypeStruct((total, 8, PTS), jnp.float32),
        jax.ShapeDtypeStruct((near, PTS, 128), jnp.float32),
    ]
    makes = stage is not None
    if makes:
        shapes.append(jax.ShapeDtypeStruct((cap + 1, PTS, PTS), jnp.bfloat16))
    state = state[: len(shapes)]
    scalars = (n, rows, cols) if makes else ()
    first = len(scalars) + len(pts)

    def kernel(*refs):
        pt_refs = refs[len(scalars) : first]
        window, level_row, level_col, *rest = refs[first + len(state) :]
        for place, piece in zip(places, pt_refs):
            blocks = piece.shape[0] // PTS
            window[place * PTS : (place + blocks) * PTS, :] = piece[...]
            for block in range(place, place + blocks):
                set_levels(block, window, level_row, level_col, 3.0 / width * LOG2E)
        if makes:
            n_ref, row_ref, col_ref = refs[:3]
            kept, *buffers = rest
            make_tiles(
                n_ref[stage],
                n_ref[stage + 1],
                row_ref,
                col_ref,
                window,
                level_row,
                level_col,
                kept,
                buffers,
            )

    return pl.pallas_call(
        kernel,
        out_shape=shapes,
        in_specs=[spec(SMEM)] * len(scalars) + [spec(VMEM)] * (len(pts) + len(state)),
        out_specs=[spec(VMEM)] * len(shapes),
        input_output_aliases={first + index: index for index in range(len(state))},
        scratch_shapes=[VMEM((PTS, PTS), jnp.float32)] * (2 if makes else 0),
        cost_estimate=cost(2**32 if stage == 2 else 2**20, 2**20),
        compiler_params=pltpu.CompilerParams(vmem_limit_bytes=6 * 2**20),
        name=name,
    )(*scalars, *pts, *state)


def products(entries, kinds, vecs, tiles, start, targets, height, folds):
    firsts = sorted(vecs)
    tall, held = vecs[firsts[0]].shape
    blocks_dev = held // PTS
    begun = sorted(start)
    source_low, source_high = firsts[0], firsts[-1] + blocks_dev
    low = min(first for first, _ in targets)
    high = max(last for _, last in targets)
    shapes = [
        jax.ShapeDtypeStruct((last - first, height, PTS), jnp.float32) for first, last in targets
    ]

    def fold(value):
        out = value[:height]
        for index in range(1, folds):
            out = out + value[index * height : (index + 1) * height]
        return out

    def kernel(*refs):
        tile_ref, source_ref, target_ref, bounds = refs[:4]
        vec_refs = refs[4 : 4 + len(firsts)]
        kept = refs[4 + len(firsts)]
        start_refs = refs[5 + len(firsts) : 5 + len(firsts) + len(begun)]
        outs = refs[5 + len(firsts) + len(begun) : -2]
        u_win, acc = refs[-2:]
        for first, ref in zip(firsts, vec_refs):
            for block in range(blocks_dev):
                lanes = slice(block * PTS, (block + 1) * PTS)
                u_win[first - source_low + block] = ref[:, lanes]
        if begun:
            for first, ref in zip(begun, start_refs):
                acc[first - low : first - low + ref.shape[0]] = ref[...]
        else:
            for place in range(high - low + 1):
                acc[place] = jnp.zeros((height, PTS), jnp.float32)

        spare = high - low
        unroll = 4

        def several(begin, end, transposed):
            def body(step, carry):
                done = []
                for lane in range(unroll):
                    index = begin + step * unroll + lane
                    valid = index < end
                    index = jnp.minimum(index, end - 1)
                    vec = u_win[source_ref[index] - source_low]
                    tile = kept[tile_ref[index]]
                    if transposed:
                        value = lax.dot_general(
                            vec,
                            tile,
                            (((1,), (1,)), ((), ())),
                            preferred_element_type=jnp.float32,
                        )
                    else:
                        value = jnp.dot(vec, tile, preferred_element_type=jnp.float32)
                    done.append((jnp.where(valid, target_ref[index] - low, spare), fold(value)))
                for target, value in done:
                    acc[target] += value
                return carry

            lax.fori_loop(0, lax.div(end - begin + unroll - 1, unroll), body, 0)

        for kind in kinds:
            several(bounds[2 * kind], bounds[2 * kind + 1], True)
            several(bounds[2 * kind + 1], bounds[2 * kind + 2], False)
        for (first, last), out in zip(targets, outs):
            out[...] = acc[first - low : last - low]

    return pl.pallas_call(
        kernel,
        out_shape=shapes,
        in_specs=[spec(SMEM)] * 4 + [spec(VMEM)] * (len(firsts) + 1 + len(begun)),
        out_specs=[spec(VMEM)] * len(shapes),
        scratch_shapes=[
            VMEM((source_high - source_low, tall, PTS), jnp.bfloat16),
            VMEM((high - low + 1, height, PTS), jnp.float32),
        ],
        cost_estimate=cost(2**31 if kinds == (1,) else 2**20, 2**20),
        compiler_params=pltpu.CompilerParams(vmem_limit_bytes=10 * 2**20),
        name="products",
    )(*entries, *[vecs[first] for first in firsts], tiles, *[start[first] for first in begun])


def urgent_ranges(group, blocks_dev):
    return [(rel * blocks_dev, (rel + 1) * blocks_dev) for rel in range(1, group + 1)]


def send_urgent(results, at_home, group):
    final = []
    *near, far = results
    parts = {rel: value for rel, value in zip(range(1, group), near)}
    for bit in bits_of(group):
        for rel in reversed([rel for rel in parts if rel & bit and rel % bit == 0]):
            value = parts.pop(rel)
            if bit > 1:
                value, far, at_home = lax.optimization_barrier((value, far, at_home))
            got = swap(value, "grp", bit)
            if rel ^ bit:
                parts[rel ^ bit] = parts[rel ^ bit] + got
            else:
                final.append(got)
    return final + [from_behind(far, "blk", 1)], at_home


def finish_home(entries, vecs, tiles, start, blocks_dev, height, folds):
    return list(
        products(entries, (2,), vecs, tiles, start, [(0, blocks_dev)], height, folds)
    )


def scaled_gram(parts, own, counts, degree, inverse, split):
    columns = own.shape[0] if degree is not None else own.shape[0] - EXTRA
    total = own.shape[1]
    first = degree is None
    shapes = [
        jax.ShapeDtypeStruct((columns, total), jnp.float32),
        jax.ShapeDtypeStruct((columns, columns), jnp.float32),
    ]
    if split:
        shapes.append(jax.ShapeDtypeStruct((2 * columns, total), jnp.bfloat16))
    if first:
        shapes.append(jax.ShapeDtypeStruct((8, total), jnp.float32))
    operands = list(parts) + [own]
    operands += [] if first else [degree]
    operands += [] if inverse is None else [inverse]

    def kernel(count_ref, *refs):
        ins = list(refs[: len(operands)])
        outs = list(refs[len(operands) :])
        part_refs = ins[: len(parts)]
        own_ref = ins[len(parts)]
        z_out, gram_out = outs[:2]
        gram = jnp.zeros((columns, columns), jnp.float32)
        for block in range(total // PTS):
            lanes = slice(block * PTS, (block + 1) * PTS)
            sums = part_refs[0][block]
            for part in part_refs[1:]:
                sums = sums + part[block]
            if first:
                level = 1.0 + sums[columns : columns + 1, :]
                outs[-1][:, lanes] = jnp.broadcast_to(level, (8, PTS))
            else:
                level = ins[len(parts) + 1][0:1, lanes]
            used = lax.broadcasted_iota(jnp.int32, (columns, PTS), 1) < count_ref[block]
            held = own_ref[0:columns, lanes].astype(jnp.float32)
            z = (held + jnp.where(used, sums[0:columns], 0.0)) / level
            if inverse is not None:
                z = jnp.dot(
                    ins[-1][...], z, precision=HIGHEST, preferred_element_type=jnp.float32
                )
            z_out[:, lanes] = z
            if split:
                high = z.astype(jnp.bfloat16)
                outs[2][0:columns, lanes] = high
                rest = z - high.astype(jnp.float32)
                outs[2][columns : 2 * columns, lanes] = rest.astype(jnp.bfloat16)
            gram = gram + lax.dot_general(
                z, z, (((1,), (1,)), ((), ())), precision=HIGHEST, preferred_element_type=jnp.float32
            )
        gram_out[...] = gram

    return pl.pallas_call(
        kernel,
        out_shape=tuple(shapes),
        in_specs=[spec(SMEM)] + [spec(VMEM)] * len(operands),
        out_specs=(spec(VMEM),) * len(shapes),
        cost_estimate=cost(2**26, 2**21),
        compiler_params=pltpu.CompilerParams(vmem_limit_bytes=6 * 2**20),
        name="scaled_gram",
    )(counts, *operands)


def inverse_factor(gram):
    size = gram.shape[0]
    row_id = lax.broadcasted_iota(jnp.int32, (size, size), 0)
    col_id = lax.broadcasted_iota(jnp.int32, (size, size), 1)
    eye = jnp.where(row_id == col_id, 1.0, 0.0)
    whole = jnp.concatenate([gram, eye], axis=1)
    wide = 2 * size
    count = size // 8
    groups = [whole[8 * g : 8 * g + 8, :] for g in range(count)]
    within = lax.broadcasted_iota(jnp.int32, (8, wide), 0)

    def spread_row(value, row):
        return jnp.broadcast_to(value[row : row + 1, :], (8, wide))

    results = []
    for g in range(count):
        spread = [
            [
                jnp.broadcast_to(groups[other][:, 8 * g + k : 8 * g + k + 1], (8, wide))
                for other in range(g, count)
            ]
            for k in range(8)
        ]
        pivots = jnp.ones((8, wide), jnp.float32)
        for j in range(8):
            column = spread[j]
            pivot = spread_row(column[0], j)
            pivots = jnp.where(within == j, pivot, pivots)
            over = 1.0 / pivot
            below = jnp.where(within > j, column[0], 0.0)
            for k in range(j + 1, 8):
                share = spread_row(column[0], k) * over
                spread[k][0] = spread[k][0] - below * share
                for other in range(1, count - g):
                    spread[k][other] = spread[k][other] - column[other] * share
            top = spread_row(groups[g], j) * over
            groups[g] = groups[g] - below * top
            for other in range(1, count - g):
                groups[g + other] = groups[g + other] - column[other] * top
        results.append(groups[g] * lax.rsqrt(pivots))
    return jnp.concatenate(results, axis=0)[:, size:wide]


def factor_kernel(gram, out):
    out[...] = inverse_factor(gram[...])


def factor(gram):
    return pl.pallas_call(
        factor_kernel,
        out_shape=jax.ShapeDtypeStruct(gram.shape, jnp.float32),
        in_specs=[spec(VMEM)],
        out_specs=spec(VMEM),
        cost_estimate=cost(2**31, 2**16),
        compiler_params=pltpu.CompilerParams(vmem_limit_bytes=2 * 2**20),
        name="factor",
    )(gram)


def embed_kernel(gram, z, out):
    out[...] = jnp.dot(
        inverse_factor(gram[...]), z[...], precision=HIGHEST, preferred_element_type=jnp.float32
    )


def embedding(gram, z):
    return pl.pallas_call(
        embed_kernel,
        out_shape=jax.ShapeDtypeStruct(z.shape, jnp.float32),
        in_specs=[spec(VMEM)] * 2,
        out_specs=spec(VMEM),
        cost_estimate=cost(2**30, 2**20),
        compiler_params=pltpu.CompilerParams(vmem_limit_bytes=4 * 2**20),
        name="embedding",
    )(gram, z)


def sum_stages():
    return bits_of(lax.axis_size("blk") * lax.axis_size("grp"))


def pairs_of(bits):
    return [bits[first : first + 2] for first in range(0, len(bits), 2)]


def all_sum(value, stages):
    count = lax.axis_size("blk") * lax.axis_size("grp")
    for bits in stages:
        moves = [0]
        for bit in bits if isinstance(bits, list) else [bits]:
            moves += [move ^ bit for move in moves]
        terms = [value] + [
            lax.ppermute(value, ("blk", "grp"), [(source, source ^ move) for source in range(count)])
            for move in moves[1:]
        ]
        while len(terms) > 1:
            terms = [left + right for left, right in zip(terms[::2], terms[1::2])]
        value = terms[0]
    return value


def per_device(points, counts, pair_rows, pair_cols, pair_live, start):
    group = lax.axis_size("grp")
    blocks_dev = counts.shape[0]
    columns = start.shape[0]
    slots = pair_rows.shape[0]
    cap = max(-(-slots // group), blocks_dev * blocks_dev * group)
    half = (blocks_dev // 2) * PTS

    home = min(2, group) * blocks_dev

    rows, cols, n, *entries = listing(
        pair_rows, pair_cols, pair_live, group, cap, blocks_dev
    )
    mate = swap(points, "grp", 1)
    chunks = [points[:half], points[half:]]
    far = [from_behind(chunk, "blk", -1) for chunk in chunks]
    crossed = [gather_far_bits(chunk) for chunk in chunks]
    begin, mate = lax.optimization_barrier((start, mate))
    vec = opening(begin, counts)
    tied = lax.optimization_barrier((vec, n, rows, cols, far[0], *crossed[0].values()))
    vec, n, rows, cols, far[0] = tied[:5]
    crossed[0] = dict(zip(crossed[0], tied[5:]))
    cross_vec = gather_far_bits(vec)
    far_vec = from_behind(vec, "blk", -1)
    mate_vec = swap(vec, "grp", 1)

    def direct(index):
        offset = index * (blocks_dev // 2)
        found = {group * blocks_dev + offset: far[index]}
        for rel, value in crossed[index].items():
            found[rel * blocks_dev + offset] = value
        return found

    def passed_on(index):
        offset = index * (blocks_dev // 2)
        found = {}
        for rel, value in crossed[index].items():
            cut = value.shape[0] // (1 if index else 2)
            parts = [swap(value[at : at + cut], "grp", 1) for at in range(0, value.shape[0], cut)]
            found[(rel ^ 1) * blocks_dev + offset] = jnp.concatenate(parts, 0)
        return found

    def build(stage, fresh, state, name):
        return list(
            build_tiles(stage, fresh, n, rows, cols, state, group, blocks_dev, cap, name)
        )

    state = build(0, {0: points, blocks_dev: mate, **direct(0)}, (), "first_tiles")
    state = build(1, passed_on(0), state, "second_tiles")
    tied = lax.optimization_barrier((far[1], mate_vec, state[1], *crossed[1].values()))
    far[1], mate_vec, state[1] = tied[:3]
    crossed[1] = dict(zip(crossed[1], tied[3:]))
    last = passed_on(1)
    *grown, kept = state
    state = build(None, direct(1), grown, "more_blocks") + [kept]
    state = build(2, last, state, "last_tiles")
    kept = state[-1]
    tied = lax.optimization_barrier((kept, *cross_vec.values()))
    kept = tied[0]
    cross_vec = dict(zip(cross_vec, tied[1:]))

    def window_of(own, mate, crossed, far):
        found = {0: own, blocks_dev: mate, group * blocks_dev: far}
        for rel, value in crossed.items():
            found[rel * blocks_dev] = value
            found[(rel ^ 1) * blocks_dev] = swap(value, "grp", 1)
        return found

    def beyond(vecs):
        return {place: value for place, value in vecs.items() if place >= home}

    vecs = window_of(vec, mate_vec, cross_vec, far_vec)
    urgent = urgent_ranges(group, blocks_dev)
    height = columns + 8
    at_home, *results = products(
        entries,
        (0,),
        {0: vec, blocks_dev: mate_vec},
        kept,
        {},
        [(0, blocks_dev)] + urgent,
        height,
        1,
    )
    begun = {first: value for (first, _), value in zip(urgent, results)}
    results = products(entries, (1,), beyond(vecs), kept, begun, urgent, height, 1)
    sums, at_home = send_urgent(results, at_home, group)
    sums = finish_home(entries, beyond(vecs), kept, {0: at_home}, blocks_dev, height, 1) + sums
    z, gram, parts, degree = scaled_gram(sums, vec, counts, None, None, True)
    for turn in range(1, ITERS):
        stages = sum_stages()
        far_part = from_behind(parts, "blk", -1)
        crossed = gather_far_bits(parts)
        mate_part = swap(parts, "grp", 1)
        at_home, *results = products(
            entries,
            (0,),
            {0: parts, blocks_dev: mate_part},
            kept,
            {},
            [(0, blocks_dev)] + urgent,
            columns,
            2,
        )
        gram = all_sum(gram, stages[:1])
        gram, at_home = lax.optimization_barrier((gram, at_home))
        gram = all_sum(gram, pairs_of(stages[3:]))
        gram, far_part, *tied = lax.optimization_barrier((gram, far_part, *crossed.values()))
        crossed = dict(zip(crossed, tied))
        vecs = beyond(window_of(parts, mate_part, crossed, far_part))
        gram = all_sum(gram, stages[1:2])
        gram, *tied = lax.optimization_barrier((gram, *vecs.values()))
        vecs = dict(zip(vecs, tied))
        begun = {first: value for (first, _), value in zip(urgent, results)}
        results = products(entries, (1,), vecs, kept, begun, urgent, columns, 2)
        gram = all_sum(gram, stages[2:3])
        gram, *results = lax.optimization_barrier((gram, *results))
        sums, at_home = send_urgent(results, at_home, group)
        sums = finish_home(entries, vecs, kept, {0: at_home}, blocks_dev, columns, 2) + sums
        inverse = factor(gram)
        z, gram, *parts = scaled_gram(sums, z, counts, degree, inverse, turn + 1 < ITERS)
        parts = parts[0] if parts else None
    stages = sum_stages()
    return embedding(all_sum(gram, stages[:1] + pairs_of(stages[1:])), z)


def solution(mesh):
    in_specs = (
        P(("blk", "grp"), None),
        P(("blk", "grp")),
        P("blk"),
        P("blk"),
        P("blk"),
        P(None, ("blk", "grp")),
    )
    out_specs = P(None, ("blk", "grp"))
    return jax.shard_map(
        per_device, mesh=mesh, in_specs=in_specs, out_specs=out_specs, check_vma=False
    )
```

```python
import functools

import jax
import jax.numpy as jnp
from jax import lax
from jax.experimental import pallas as pl
from jax.experimental.pallas import tpu as pltpu
from jax.sharding import PartitionSpec as P

PTS = 512
ITERS = 2
LOG2E = 1.4426950408889634
DEAD = 65536.0
EXTRA = 16
VMEM = pltpu.VMEM
SMEM = pltpu.SMEM
HIGHEST = lax.Precision.HIGHEST


def cost(flops, moved):
    return pl.CostEstimate(flops=int(flops), bytes_accessed=int(moved), transcendentals=0)


def spec(space):
    return pl.BlockSpec(memory_space=space)


def swap(value, axis, bit):
    count = lax.axis_size(axis)
    return lax.ppermute(value, axis, [(source, source ^ bit) for source in range(count)])


def from_behind(value, axis, steps):
    count = lax.axis_size(axis)
    initial, last = (max(0, -steps), min(count, count - steps))
    return lax.ppermute(value, axis, [(source, source + steps) for source in range(initial, last)])


def bits_of(count):
    bits = []
    bit = 1
    while bit < count:
        bits.append(bit)
        bit *= 2
    return bits


def gather_near(value, axis):
    held = {0: value}
    for bit in reversed(bits_of(lax.axis_size(axis))):
        for rel in list(held):
            held[rel ^ bit] = swap(held[rel], axis, bit)
    return [held[rel] for rel in range(len(held))]


def gather_far_bits(value):
    held = {0: value}
    for bit in reversed(bits_of(lax.axis_size("grp"))[1:]):
        for rel in list(held):
            held[rel ^ bit] = swap(held[rel], "grp", bit)
    held.pop(0)
    return held


def opening_kernel(start, counts, out):
    columns, total = start.shape
    for block in range(total // PTS):
        lanes = slice(block * PTS, (block + 1) * PTS)
        used = lax.broadcasted_iota(jnp.int32, (columns, PTS), 1) < counts[block]
        out[0:columns, lanes] = jnp.where(used, start[:, lanes], 0.0).astype(jnp.bfloat16)
        which = lax.broadcasted_iota(jnp.int32, (EXTRA, PTS), 0)
        place_in = lax.broadcasted_iota(jnp.int32, (EXTRA, PTS), 1)
        ones = jnp.logical_and(which == 0, place_in < counts[block])
        out[columns : columns + EXTRA, lanes] = jnp.where(ones, 1.0, 0.0).astype(jnp.bfloat16)


def opening(start, counts):
    columns, total = start.shape
    return pl.pallas_call(
        opening_kernel,
        out_shape=jax.ShapeDtypeStruct((columns + EXTRA, total), jnp.bfloat16),
        in_specs=[spec(VMEM), spec(SMEM)],
        out_specs=spec(VMEM),
        cost_estimate=cost(2**20, 2**19),
        compiler_params=pltpu.CompilerParams(vmem_limit_bytes=2 * 2**20),
        name="opening",
    )(start, counts)


def stage_of(place, group, blocks_dev):
    piece = lax.div(place, blocks_dev)
    first_half = lax.rem(place, blocks_dev) < blocks_dev // 2
    later = jnp.where(first_half, jnp.where(lax.rem(piece, 2) == 0, 0, 1), 2)
    return jnp.where(piece < min(2, group), 0, later)


def listing_kernel(
    group,
    cap,
    blocks_dev,
    rows,
    cols,
    live,
    out_rows,
    out_cols,
    out_n,
    tiles,
    sources,
    targets,
    bounds,
    owners,
):
    slab = blocks_dev * group
    slots = rows.shape[0]
    member = lax.axis_index("grp")

    def local_near(block, device):
        return (lax.div(block, blocks_dev) ^ device) * blocks_dev + lax.rem(block, blocks_dev)

    def local_far(block):
        return slab + lax.rem(block - slab, blocks_dev)

    def count_far(slot, carry):
        col = cols[slot]
        far = jnp.logical_and(slot < live[0], col >= slab)
        owner = lax.div(col - slab, blocks_dev)
        owners[slot] = jnp.where(far, owner, -1)
        return tuple(
            old + jnp.where(jnp.logical_and(far, owner == device), 1, 0)
            for device, old in enumerate(carry)
        )

    loads = lax.fori_loop(0, slots, count_far, (jnp.int32(0),) * group)

    def give(slot, loads):
        row, col = rows[slot], cols[slot]
        near = jnp.logical_and(slot < live[0], col < slab)
        best = jnp.int32(2**30)
        owner = jnp.int32(0)
        for device in range(group):
            stage = jnp.maximum(
                stage_of(local_near(row, device), group, blocks_dev),
                stage_of(local_near(col, device), group, blocks_dev),
            )
            score = loads[device] + 64 * stage + jnp.where(loads[device] < cap, 0, 2**20)
            owner = jnp.where(score < best, device, owner)
            best = jnp.minimum(score, best)

        @pl.when(near)
        def _():
            owners[slot] = owner

        return tuple(
            load + jnp.where(jnp.logical_and(near, owner == device), 1, 0)
            for device, load in enumerate(loads)
        )

    lax.fori_loop(0, slots, give, loads)

    def place_those(wanted, filled):
        def place(slot, filled):
            row, col = rows[slot], cols[slot]
            row_place = local_near(row, member)
            col_place = jnp.where(col >= slab, local_far(col), local_near(col, member))
            stage = jnp.maximum(
                stage_of(row_place, group, blocks_dev), stage_of(col_place, group, blocks_dev)
            )
            mine = jnp.logical_and(owners[slot] == member, stage == wanted)

            @pl.when(mine)
            def _():
                out_rows[filled] = row_place
                out_cols[filled] = col_place

            return filled + jnp.where(mine, 1, 0)

        return lax.fori_loop(0, slots, place, filled)

    count = jnp.int32(0)
    out_n[0] = count
    for wanted in range(3):
        count = place_those(wanted, count)
        out_n[wanted + 1] = count

    home = min(2, group) * blocks_dev
    bounds[0] = jnp.int32(0)
    filled = jnp.int32(0)
    for kind in range(3):
        for to_row in (True, False):

            def enter(index, filled):
                source = (out_cols if to_row else out_rows)[index]
                target = (out_rows if to_row else out_cols)[index]
                if kind == 0:
                    wanted = source < home
                elif kind == 1:
                    wanted = jnp.logical_and(source >= home, target >= blocks_dev)
                else:
                    wanted = jnp.logical_and(source >= home, target < blocks_dev)

                @pl.when(wanted)
                def _():
                    tiles[filled] = index
                    sources[filled] = source
                    targets[filled] = target

                return filled + jnp.where(wanted, 1, 0)

            filled = lax.fori_loop(0, count, enter, filled)
            bounds[2 * kind + (1 if to_row else 2)] = filled


def listing(rows, cols, live, group, cap, blocks_dev):
    return pl.pallas_call(
        functools.partial(listing_kernel, group, cap, blocks_dev),
        out_shape=(
            jax.ShapeDtypeStruct((cap,), jnp.int32),
            jax.ShapeDtypeStruct((cap,), jnp.int32),
            jax.ShapeDtypeStruct((4,), jnp.int32),
            jax.ShapeDtypeStruct((2 * cap,), jnp.int32),
            jax.ShapeDtypeStruct((2 * cap,), jnp.int32),
            jax.ShapeDtypeStruct((2 * cap,), jnp.int32),
            jax.ShapeDtypeStruct((7,), jnp.int32),
        ),
        in_specs=[spec(SMEM)] * 3,
        out_specs=(spec(SMEM),) * 7,
        scratch_shapes=[SMEM((rows.shape[0],), jnp.int32)],
        cost_estimate=cost(2**20, 2**10),
        compiler_params=pltpu.CompilerParams(vmem_limit_bytes=2**20),
        name="listing",
    )(rows, cols, live)


def set_levels(place, window, level_row, level_col, scale):
    block = window[place * PTS : (place + 1) * PTS, :]
    width = block.shape[1]
    part = jnp.zeros((PTS, 128), jnp.float32)
    for lane in range(0, width, 128):
        wide = block[:, lane : lane + 128].astype(jnp.float32)
        part = part + wide * wide
    level_row[place] = scale * lax.dot_general(
        jnp.ones((8, 128), jnp.float32),
        part,
        (((1,), (1,)), ((), ())),
        precision=HIGHEST,
        preferred_element_type=jnp.float32,
    )
    if place < level_col.shape[0]:
        total = jnp.sum(part, axis=1, keepdims=True) * scale
        level_col[place] = jnp.broadcast_to(total, (PTS, 128))


def make_tiles(low, high, rows, cols, window, level_row, level_col, kept, buffers):
    width = window.shape[1]
    scale = 6.0 / width * LOG2E
    count = high - low
    spare = kept.shape[0] - 1

    def cross(tile, buffer):
        index = low + jnp.minimum(tile, count - 1)
        left = window[pl.ds(pl.multiple_of(rows[index] * PTS, PTS), PTS), :]
        right = window[pl.ds(pl.multiple_of(cols[index] * PTS, PTS), PTS), :]
        buffer[...] = lax.dot_general(
            left, right, (((1,), (1,)), ((), ())), preferred_element_type=jnp.float32
        )

    def finish(tile, buffer):
        valid = jnp.logical_and(tile >= 0, tile < count)
        index = low + jnp.clip(tile, 0, count - 1)
        row, col = rows[index], cols[index]
        right_level = level_row[col][0:1, :]
        left_level = jnp.concatenate([level_col[row]] * (PTS // 128), axis=1)
        value = jnp.exp2(buffer[...] * scale - left_level - right_level)
        kept[jnp.where(valid, index, spare)] = value.astype(jnp.bfloat16)

    def body(pair, carry):
        cross(2 * pair, buffers[0])
        finish(2 * pair - 1, buffers[1])
        cross(2 * pair + 1, buffers[1])
        finish(2 * pair, buffers[0])
        return carry

    @pl.when(count > 0)
    def _():
        buffers[1][...] = jnp.zeros((PTS, PTS), jnp.float32)

    lax.fori_loop(0, jnp.where(count > 0, lax.div(count, 2) + 1, 0), body, 0)


def build_tiles(stage, fresh, n, rows, cols, state, group, blocks_dev, cap, name):
    places = list(fresh)
    pts = list(fresh.values())
    width = pts[0].shape[1]
    total = (group + 1) * blocks_dev
    near = group * blocks_dev
    shapes = [
        jax.ShapeDtypeStruct((total * PTS, width), jnp.bfloat16),
        jax.ShapeDtypeStruct((total, 8, PTS), jnp.float32),
        jax.ShapeDtypeStruct((near, PTS, 128), jnp.float32),
    ]
    makes = stage is not None
    if makes:
        shapes.append(jax.ShapeDtypeStruct((cap + 1, PTS, PTS), jnp.bfloat16))
    state = state[: len(shapes)]
    scalars = (n, rows, cols) if makes else ()
    first = len(scalars) + len(pts)

    def kernel(*refs):
        pt_refs = refs[len(scalars) : first]
        window, level_row, level_col, *rest = refs[first + len(state) :]
        for place, piece in zip(places, pt_refs):
            blocks = piece.shape[0] // PTS
            window[place * PTS : (place + blocks) * PTS, :] = piece[...]
            for block in range(place, place + blocks):
                set_levels(block, window, level_row, level_col, 3.0 / width * LOG2E)
        if makes:
            n_ref, row_ref, col_ref = refs[:3]
            kept, *buffers = rest
            make_tiles(
                n_ref[stage],
                n_ref[stage + 1],
                row_ref,
                col_ref,
                window,
                level_row,
                level_col,
                kept,
                buffers,
            )

    return pl.pallas_call(
        kernel,
        out_shape=shapes,
        in_specs=[spec(SMEM)] * len(scalars) + [spec(VMEM)] * (len(pts) + len(state)),
        out_specs=[spec(VMEM)] * len(shapes),
        input_output_aliases={first + index: index for index in range(len(state))},
        scratch_shapes=[VMEM((PTS, PTS), jnp.float32)] * (2 if makes else 0),
        cost_estimate=cost(2**32 if stage == 2 else 2**20, 2**20),
        compiler_params=pltpu.CompilerParams(vmem_limit_bytes=6 * 2**20),
        name=name,
    )(*scalars, *pts, *state)


def products(entries, kinds, vecs, tiles, start, targets, height, folds):
    firsts = sorted(vecs)
    tall, held = vecs[firsts[0]].shape
    blocks_dev = held // PTS
    begun = list(start)
    source_low, source_high = firsts[0], firsts[-1] + blocks_dev
    low = min(first for ranges in targets for first, _ in ranges)
    high = max(last for ranges in targets for _, last in ranges)
    shapes = [
        jax.ShapeDtypeStruct((sum(last - first for first, last in ranges), height, PTS), jnp.float32)
        for ranges in targets
    ]

    def pieces(refs):
        for ranges, ref in zip(targets, refs):
            at = 0
            for first, last in ranges:
                yield ref, slice(at, at + last - first), slice(first - low, last - low)
                at += last - first

    def fold(value):
        out = value[:height]
        for index in range(1, folds):
            out = out + value[index * height : (index + 1) * height]
        return out

    def kernel(*refs):
        tile_ref, source_ref, target_ref, bounds = refs[:4]
        vec_refs = refs[4 : 4 + len(firsts)]
        kept = refs[4 + len(firsts)]
        start_refs = refs[5 + len(firsts) : 5 + len(firsts) + len(begun)]
        outs = refs[5 + len(firsts) + len(begun) : -2]
        u_win, acc = refs[-2:]
        for first, ref in zip(firsts, vec_refs):
            for block in range(blocks_dev):
                lanes = slice(block * PTS, (block + 1) * PTS)
                u_win[first - source_low + block] = ref[:, lanes]
        if begun:
            for ref, inside, places in pieces(start_refs):
                acc[places] = ref[inside]
        else:
            for place in range(high - low + 1):
                acc[place] = jnp.zeros((height, PTS), jnp.float32)

        spare = high - low
        unroll = 4

        def several(begin, end, transposed):
            def body(step, carry):
                done = []
                for lane in range(unroll):
                    index = begin + step * unroll + lane
                    valid = index < end
                    index = jnp.minimum(index, end - 1)
                    vec = u_win[source_ref[index] - source_low]
                    tile = kept[tile_ref[index]]
                    if transposed:
                        value = lax.dot_general(
                            vec,
                            tile,
                            (((1,), (1,)), ((), ())),
                            preferred_element_type=jnp.float32,
                        )
                    else:
                        value = jnp.dot(vec, tile, preferred_element_type=jnp.float32)
                    done.append((jnp.where(valid, target_ref[index] - low, spare), fold(value)))
                for target, value in done:
                    acc[target] += value
                return carry

            lax.fori_loop(0, lax.div(end - begin + unroll - 1, unroll), body, 0)

        for kind in kinds:
            several(bounds[2 * kind], bounds[2 * kind + 1], True)
            several(bounds[2 * kind + 1], bounds[2 * kind + 2], False)
        for out, inside, places in pieces(outs):
            out[inside] = acc[places]

    return pl.pallas_call(
        kernel,
        out_shape=shapes,
        in_specs=[spec(SMEM)] * 4 + [spec(VMEM)] * (len(firsts) + 1 + len(begun)),
        out_specs=[spec(VMEM)] * len(shapes),
        scratch_shapes=[
            VMEM((source_high - source_low, tall, PTS), jnp.bfloat16),
            VMEM((high - low + 1, height, PTS), jnp.float32),
        ],
        cost_estimate=cost(2**31 if kinds == (1,) else 2**20, 2**20),
        compiler_params=pltpu.CompilerParams(vmem_limit_bytes=10 * 2**20),
        name="products",
    )(*entries, *[vecs[first] for first in firsts], tiles, *begun)


def urgent_ranges(group, blocks_dev):
    messages = [
        [rel for rel in range(group) if rel & bit and rel % bit == 0] for bit in bits_of(group)
    ]
    return [
        [(rel * blocks_dev, (rel + 1) * blocks_dev) for rel in rels]
        for rels in messages + [[group]]
    ]


def send_urgent(results, later, group, blocks_dev):
    final = []
    *messages, far = results
    parts = {}
    for bit, message in zip(bits_of(group), messages):
        rels = [rel for rel in range(group) if rel & bit and rel % bit == 0]
        for index, rel in enumerate(rels):
            if rel in parts:
                held = message[index * blocks_dev : (index + 1) * blocks_dev]
                message = held + parts[rel] if len(rels) == 1 else message.at[
                    index * blocks_dev : (index + 1) * blocks_dev
                ].add(parts[rel])
        if bit > 1:
            message, far, *later = lax.optimization_barrier((message, far, *later))
        got = swap(message, "grp", bit)
        final.append(got)
        for index, rel in enumerate(rels):
            if rel ^ bit:
                piece = got[index * blocks_dev : (index + 1) * blocks_dev]
                parts[rel ^ bit] = parts[rel ^ bit] + piece if rel ^ bit in parts else piece
    return final + [from_behind(far, "blk", 1)], later


def finish_home(entries, vecs, tiles, start, blocks_dev, height, folds):
    return list(
        products(entries, (2,), vecs, tiles, [start], [[(0, blocks_dev)]], height, folds)
    )


def scaled_gram(parts, own, counts, degree, inverse, split):
    columns = own.shape[0] if degree is not None else own.shape[0] - EXTRA
    total = own.shape[1]
    first = degree is None
    shapes = [
        jax.ShapeDtypeStruct((columns, total), jnp.float32),
        jax.ShapeDtypeStruct((columns, columns), jnp.float32),
    ]
    if split:
        shapes.append(jax.ShapeDtypeStruct((2 * columns, total), jnp.bfloat16))
    if first:
        shapes.append(jax.ShapeDtypeStruct((8, total), jnp.float32))
    operands = list(parts) + [own]
    operands += [] if first else [degree]
    operands += [] if inverse is None else [inverse]

    def kernel(count_ref, *refs):
        ins = list(refs[: len(operands)])
        outs = list(refs[len(operands) :])
        part_refs = ins[: len(parts)]
        own_ref = ins[len(parts)]
        z_out, gram_out = outs[:2]
        gram = jnp.zeros((columns, columns), jnp.float32)
        for block in range(total // PTS):
            lanes = slice(block * PTS, (block + 1) * PTS)
            sums = part_refs[0][block]
            for part in part_refs[1:]:
                sums = sums + part[block]
            if first:
                level = 1.0 + sums[columns : columns + 1, :]
                outs[-1][:, lanes] = jnp.broadcast_to(level, (8, PTS))
            else:
                level = ins[len(parts) + 1][0:1, lanes]
            used = lax.broadcasted_iota(jnp.int32, (columns, PTS), 1) < count_ref[block]
            held = own_ref[0:columns, lanes].astype(jnp.float32)
            z = (held + jnp.where(used, sums[0:columns], 0.0)) / level
            if inverse is not None:
                z = jnp.dot(
                    ins[-1][...], z, precision=HIGHEST, preferred_element_type=jnp.float32
                )
            z_out[:, lanes] = z
            if split:
                high = z.astype(jnp.bfloat16)
                outs[2][0:columns, lanes] = high
                rest = z - high.astype(jnp.float32)
                outs[2][columns : 2 * columns, lanes] = rest.astype(jnp.bfloat16)
            gram = gram + lax.dot_general(
                z, z, (((1,), (1,)), ((), ())), precision=HIGHEST, preferred_element_type=jnp.float32
            )
        gram_out[...] = gram

    return pl.pallas_call(
        kernel,
        out_shape=tuple(shapes),
        in_specs=[spec(SMEM)] + [spec(VMEM)] * len(operands),
        out_specs=(spec(VMEM),) * len(shapes),
        cost_estimate=cost(2**26, 2**21),
        compiler_params=pltpu.CompilerParams(vmem_limit_bytes=6 * 2**20),
        name="scaled_gram",
    )(counts, *operands)


def inverse_factor(gram):
    size = gram.shape[0]
    row_id = lax.broadcasted_iota(jnp.int32, (size, size), 0)
    col_id = lax.broadcasted_iota(jnp.int32, (size, size), 1)
    eye = jnp.where(row_id == col_id, 1.0, 0.0)
    whole = jnp.concatenate([gram, eye], axis=1)
    wide = 2 * size
    count = size // 8
    groups = [whole[8 * g : 8 * g + 8, :] for g in range(count)]
    within = lax.broadcasted_iota(jnp.int32, (8, wide), 0)

    def spread_row(value, row):
        return jnp.broadcast_to(value[row : row + 1, :], (8, wide))

    results = []
    for g in range(count):
        spread = [
            [
                jnp.broadcast_to(groups[other][:, 8 * g + k : 8 * g + k + 1], (8, wide))
                for other in range(g, count)
            ]
            for k in range(8)
        ]
        pivots = jnp.ones((8, wide), jnp.float32)
        for j in range(8):
            column = spread[j]
            pivot = spread_row(column[0], j)
            pivots = jnp.where(within == j, pivot, pivots)
            over = 1.0 / pivot
            below = jnp.where(within > j, column[0], 0.0)
            for k in range(j + 1, 8):
                share = spread_row(column[0], k) * over
                spread[k][0] = spread[k][0] - below * share
                for other in range(1, count - g):
                    spread[k][other] = spread[k][other] - column[other] * share
            top = spread_row(groups[g], j) * over
            groups[g] = groups[g] - below * top
            for other in range(1, count - g):
                groups[g + other] = groups[g + other] - column[other] * top
        results.append(groups[g] * lax.rsqrt(pivots))
    return jnp.concatenate(results, axis=0)[:, size:wide]


def factor_kernel(gram, out):
    out[...] = inverse_factor(gram[...])


def factor(gram):
    return pl.pallas_call(
        factor_kernel,
        out_shape=jax.ShapeDtypeStruct(gram.shape, jnp.float32),
        in_specs=[spec(VMEM)],
        out_specs=spec(VMEM),
        cost_estimate=cost(2**16, 2**16),
        compiler_params=pltpu.CompilerParams(vmem_limit_bytes=2 * 2**20),
        name="factor",
    )(gram)


def embed_kernel(gram, z, out):
    out[...] = jnp.dot(
        inverse_factor(gram[...]), z[...], precision=HIGHEST, preferred_element_type=jnp.float32
    )


def embedding(gram, z):
    return pl.pallas_call(
        embed_kernel,
        out_shape=jax.ShapeDtypeStruct(z.shape, jnp.float32),
        in_specs=[spec(VMEM)] * 2,
        out_specs=spec(VMEM),
        cost_estimate=cost(2**30, 2**20),
        compiler_params=pltpu.CompilerParams(vmem_limit_bytes=4 * 2**20),
        name="embedding",
    )(gram, z)


def sum_stages():
    return bits_of(lax.axis_size("blk") * lax.axis_size("grp"))


def pairs_of(bits):
    return [bits[first : first + 2] for first in range(0, len(bits), 2)]


def all_sum(value, stages):
    count = lax.axis_size("blk") * lax.axis_size("grp")
    for bits in stages:
        moves = [0]
        for bit in bits if isinstance(bits, list) else [bits]:
            moves += [move ^ bit for move in moves]
        terms = [value] + [
            lax.ppermute(value, ("blk", "grp"), [(source, source ^ move) for source in range(count)])
            for move in moves[1:]
        ]
        while len(terms) > 1:
            terms = [left + right for left, right in zip(terms[::2], terms[1::2])]
        value = terms[0]
    return value


def per_device(points, counts, pair_rows, pair_cols, pair_live, start):
    group = lax.axis_size("grp")
    blocks_dev = counts.shape[0]
    columns = start.shape[0]
    slots = pair_rows.shape[0]
    cap = max(-(-slots // group), blocks_dev * blocks_dev * group)
    half = (blocks_dev // 2) * PTS

    home = min(2, group) * blocks_dev

    rows, cols, n, *entries = listing(
        pair_rows, pair_cols, pair_live, group, cap, blocks_dev
    )
    mate = swap(points, "grp", 1)
    chunks = [points[:half], points[half:]]
    far = [from_behind(chunk, "blk", -1) for chunk in chunks]
    crossed = [gather_far_bits(chunk) for chunk in chunks]
    begin, mate = lax.optimization_barrier((start, mate))
    vec = opening(begin, counts)
    tied = lax.optimization_barrier((vec, n, rows, cols, far[0], *crossed[0].values()))
    vec, n, rows, cols, far[0] = tied[:5]
    crossed[0] = dict(zip(crossed[0], tied[5:]))
    cross_vec = gather_far_bits(vec)
    far_vec = from_behind(vec, "blk", -1)
    mate_vec = swap(vec, "grp", 1)

    def direct(index):
        offset = index * (blocks_dev // 2)
        found = {group * blocks_dev + offset: far[index]}
        for rel, value in crossed[index].items():
            found[rel * blocks_dev + offset] = value
        return found

    def passed_on(index):
        offset = index * (blocks_dev // 2)
        found = {}
        for rel, value in crossed[index].items():
            cut = value.shape[0] // (1 if index else 2)
            parts = [swap(value[at : at + cut], "grp", 1) for at in range(0, value.shape[0], cut)]
            found[(rel ^ 1) * blocks_dev + offset] = jnp.concatenate(parts, 0)
        return found

    def build(stage, fresh, state, name):
        return list(
            build_tiles(stage, fresh, n, rows, cols, state, group, blocks_dev, cap, name)
        )

    state = build(0, {0: points, blocks_dev: mate, **direct(0)}, (), "first_tiles")
    state = build(1, passed_on(0), state, "second_tiles")
    tied = lax.optimization_barrier((far[1], mate_vec, state[1], *crossed[1].values()))
    far[1], mate_vec, state[1] = tied[:3]
    crossed[1] = dict(zip(crossed[1], tied[3:]))
    last = passed_on(1)
    *grown, kept = state
    state = build(None, direct(1), grown, "more_blocks") + [kept]
    state = build(2, last, state, "last_tiles")
    kept = state[-1]
    tied = lax.optimization_barrier((kept, *cross_vec.values()))
    kept = tied[0]
    cross_vec = dict(zip(cross_vec, tied[1:]))

    def window_of(own, mate, crossed, far):
        found = {0: own, blocks_dev: mate, group * blocks_dev: far}
        for rel, value in crossed.items():
            found[rel * blocks_dev] = value
            found[(rel ^ 1) * blocks_dev] = swap(value, "grp", 1)
        return found

    def beyond(vecs):
        return {place: value for place, value in vecs.items() if place >= home}

    vecs = window_of(vec, mate_vec, cross_vec, far_vec)
    urgent = urgent_ranges(group, blocks_dev)
    height = columns + 8
    at_home, *results = products(
        entries,
        (0,),
        {0: vec, blocks_dev: mate_vec},
        kept,
        (),
        [[(0, blocks_dev)]] + urgent,
        height,
        1,
    )
    results = products(entries, (1,), beyond(vecs), kept, results, urgent, height, 1)
    sums, (at_home,) = send_urgent(results, (at_home,), group, blocks_dev)
    sums = finish_home(entries, beyond(vecs), kept, at_home, blocks_dev, height, 1) + sums
    z, gram, parts, degree = scaled_gram(sums, vec, counts, None, None, True)
    for turn in range(1, ITERS):
        stages = sum_stages()
        crossed = gather_far_bits(parts)
        mate_part = swap(parts, "grp", 1)
        gram = all_sum(gram, stages[:1])
        gram, far_part = lax.optimization_barrier((gram, parts))
        far_part = from_behind(far_part, "blk", -1)
        at_home, *results = products(
            entries,
            (0,),
            {0: parts, blocks_dev: mate_part},
            kept,
            (),
            [[(0, blocks_dev)]] + urgent,
            columns,
            2,
        )
        at_home, far_part, *tied = lax.optimization_barrier(
            (at_home, far_part, *crossed.values())
        )
        crossed = dict(zip(crossed, tied))
        vecs = beyond(window_of(parts, mate_part, crossed, far_part))
        gram = all_sum(gram, stages[1:2])
        gram, *tied = lax.optimization_barrier((gram, *vecs.values()))
        vecs = dict(zip(vecs, tied))
        results = products(entries, (1,), vecs, kept, results, urgent, columns, 2)
        gram = all_sum(gram, stages[2:3])
        gram, *results = lax.optimization_barrier((gram, *results))
        sums, (at_home, gram) = send_urgent(results, (at_home, gram), group, blocks_dev)
        gram = all_sum(gram, pairs_of(stages[3:]))
        sums = finish_home(entries, vecs, kept, at_home, blocks_dev, columns, 2) + sums
        inverse = factor(gram)
        z, gram, *parts = scaled_gram(sums, z, counts, degree, inverse, turn + 1 < ITERS)
        parts = parts[0] if parts else None
    stages = sum_stages()
    return embedding(all_sum(gram, stages[:1] + pairs_of(stages[1:])), z)


def solution(mesh):
    in_specs = (
        P(("blk", "grp"), None),
        P(("blk", "grp")),
        P("blk"),
        P("blk"),
        P("blk"),
        P(None, ("blk", "grp")),
    )
    out_specs = P(None, ("blk", "grp"))
    return jax.shard_map(
        per_device, mesh=mesh, in_specs=in_specs, out_specs=out_specs, check_vma=False
    )
```

```python
import functools

import jax
import jax.numpy as jnp
from jax import lax
from jax.experimental import pallas as pl
from jax.experimental.pallas import tpu as pltpu
from jax.sharding import PartitionSpec as P

PTS = 512
ITERS = 2
LOG2E = 1.4426950408889634
DEAD = 65536.0
EXTRA = 16
VMEM = pltpu.VMEM
SMEM = pltpu.SMEM
HIGHEST = lax.Precision.HIGHEST


def cost(flops, moved):
    return pl.CostEstimate(flops=int(flops), bytes_accessed=int(moved), transcendentals=0)


def spec(space):
    return pl.BlockSpec(memory_space=space)


def swap(value, axis, bit):
    count = lax.axis_size(axis)
    return lax.ppermute(value, axis, [(source, source ^ bit) for source in range(count)])


def from_behind(value, axis, steps):
    count = lax.axis_size(axis)
    initial, last = (max(0, -steps), min(count, count - steps))
    return lax.ppermute(value, axis, [(source, source + steps) for source in range(initial, last)])


def bits_of(count):
    bits = []
    bit = 1
    while bit < count:
        bits.append(bit)
        bit *= 2
    return bits


def gather_near(value, axis):
    held = {0: value}
    for bit in reversed(bits_of(lax.axis_size(axis))):
        for rel in list(held):
            held[rel ^ bit] = swap(held[rel], axis, bit)
    return [held[rel] for rel in range(len(held))]


def gather_far_bits(value):
    held = {0: value}
    for bit in reversed(bits_of(lax.axis_size("grp"))[1:]):
        for rel in list(held):
            held[rel ^ bit] = swap(held[rel], "grp", bit)
    held.pop(0)
    return held


def opening_kernel(start, counts, out):
    columns, total = start.shape
    for block in range(total // PTS):
        lanes = slice(block * PTS, (block + 1) * PTS)
        used = lax.broadcasted_iota(jnp.int32, (columns, PTS), 1) < counts[block]
        out[0:columns, lanes] = jnp.where(used, start[:, lanes], 0.0).astype(jnp.bfloat16)
        which = lax.broadcasted_iota(jnp.int32, (EXTRA, PTS), 0)
        place_in = lax.broadcasted_iota(jnp.int32, (EXTRA, PTS), 1)
        ones = jnp.logical_and(which == 0, place_in < counts[block])
        out[columns : columns + EXTRA, lanes] = jnp.where(ones, 1.0, 0.0).astype(jnp.bfloat16)


def opening(start, counts):
    columns, total = start.shape
    return pl.pallas_call(
        opening_kernel,
        out_shape=jax.ShapeDtypeStruct((columns + EXTRA, total), jnp.bfloat16),
        in_specs=[spec(VMEM), spec(SMEM)],
        out_specs=spec(VMEM),
        cost_estimate=cost(2**20, 2**19),
        compiler_params=pltpu.CompilerParams(vmem_limit_bytes=2 * 2**20),
        name="opening",
    )(start, counts)


def stage_of(place, group, blocks_dev):
    piece = lax.div(place, blocks_dev)
    first_half = lax.rem(place, blocks_dev) < blocks_dev // 2
    later = jnp.where(first_half, jnp.where(lax.rem(piece, 2) == 0, 0, 1), 2)
    return jnp.where(piece < min(2, group), 0, later)


def listing_kernel(
    group,
    cap,
    blocks_dev,
    rows,
    cols,
    live,
    out_rows,
    out_cols,
    out_n,
    tiles,
    sources,
    targets,
    bounds,
    owners,
):
    slab = blocks_dev * group
    slots = rows.shape[0]
    member = lax.axis_index("grp")

    def local_near(block, device):
        return (lax.div(block, blocks_dev) ^ device) * blocks_dev + lax.rem(block, blocks_dev)

    def local_far(block):
        return slab + lax.rem(block - slab, blocks_dev)

    def count_far(slot, carry):
        col = cols[slot]
        far = jnp.logical_and(slot < live[0], col >= slab)
        owner = lax.div(col - slab, blocks_dev)
        owners[slot] = jnp.where(far, owner, -1)
        return tuple(
            old + jnp.where(jnp.logical_and(far, owner == device), 1, 0)
            for device, old in enumerate(carry)
        )

    loads = lax.fori_loop(0, slots, count_far, (jnp.int32(0),) * group)

    def give(slot, loads):
        row, col = rows[slot], cols[slot]
        near = jnp.logical_and(slot < live[0], col < slab)
        best = jnp.int32(2**30)
        owner = jnp.int32(0)
        for device in range(group):
            stage = jnp.maximum(
                stage_of(local_near(row, device), group, blocks_dev),
                stage_of(local_near(col, device), group, blocks_dev),
            )
            score = loads[device] + 64 * stage + jnp.where(loads[device] < cap, 0, 2**20)
            owner = jnp.where(score < best, device, owner)
            best = jnp.minimum(score, best)

        @pl.when(near)
        def _():
            owners[slot] = owner

        return tuple(
            load + jnp.where(jnp.logical_and(near, owner == device), 1, 0)
            for device, load in enumerate(loads)
        )

    lax.fori_loop(0, slots, give, loads)

    def place_those(wanted, filled):
        def place(slot, filled):
            row, col = rows[slot], cols[slot]
            row_place = local_near(row, member)
            col_place = jnp.where(col >= slab, local_far(col), local_near(col, member))
            stage = jnp.maximum(
                stage_of(row_place, group, blocks_dev), stage_of(col_place, group, blocks_dev)
            )
            mine = jnp.logical_and(owners[slot] == member, stage == wanted)

            @pl.when(mine)
            def _():
                out_rows[filled] = row_place
                out_cols[filled] = col_place

            return filled + jnp.where(mine, 1, 0)

        return lax.fori_loop(0, slots, place, filled)

    count = jnp.int32(0)
    out_n[0] = count
    for wanted in range(3):
        count = place_those(wanted, count)
        out_n[wanted + 1] = count

    home = min(2, group) * blocks_dev
    bounds[0] = jnp.int32(0)
    filled = jnp.int32(0)
    for kind in range(3):
        for to_row in (True, False):

            def enter(index, filled):
                source = (out_cols if to_row else out_rows)[index]
                target = (out_rows if to_row else out_cols)[index]
                if kind == 0:
                    wanted = source < home
                elif kind == 1:
                    wanted = jnp.logical_and(source >= home, target >= blocks_dev)
                else:
                    wanted = jnp.logical_and(source >= home, target < blocks_dev)

                @pl.when(wanted)
                def _():
                    tiles[filled] = index
                    sources[filled] = source
                    targets[filled] = target

                return filled + jnp.where(wanted, 1, 0)

            filled = lax.fori_loop(0, count, enter, filled)
            bounds[2 * kind + (1 if to_row else 2)] = filled


def listing(rows, cols, live, group, cap, blocks_dev):
    return pl.pallas_call(
        functools.partial(listing_kernel, group, cap, blocks_dev),
        out_shape=(
            jax.ShapeDtypeStruct((cap,), jnp.int32),
            jax.ShapeDtypeStruct((cap,), jnp.int32),
            jax.ShapeDtypeStruct((4,), jnp.int32),
            jax.ShapeDtypeStruct((2 * cap,), jnp.int32),
            jax.ShapeDtypeStruct((2 * cap,), jnp.int32),
            jax.ShapeDtypeStruct((2 * cap,), jnp.int32),
            jax.ShapeDtypeStruct((7,), jnp.int32),
        ),
        in_specs=[spec(SMEM)] * 3,
        out_specs=(spec(SMEM),) * 7,
        scratch_shapes=[SMEM((rows.shape[0],), jnp.int32)],
        cost_estimate=cost(2**20, 2**10),
        compiler_params=pltpu.CompilerParams(vmem_limit_bytes=2**20),
        name="listing",
    )(rows, cols, live)


def set_levels(place, window, level_row, level_col, scale):
    block = window[place * PTS : (place + 1) * PTS, :]
    width = block.shape[1]
    part = jnp.zeros((PTS, 128), jnp.float32)
    for lane in range(0, width, 128):
        wide = block[:, lane : lane + 128].astype(jnp.float32)
        part = part + wide * wide
    level_row[place] = scale * lax.dot_general(
        jnp.ones((8, 128), jnp.float32),
        part,
        (((1,), (1,)), ((), ())),
        precision=HIGHEST,
        preferred_element_type=jnp.float32,
    )
    if place < level_col.shape[0]:
        total = jnp.sum(part, axis=1, keepdims=True) * scale
        level_col[place] = jnp.broadcast_to(total, (PTS, 128))


def make_tiles(low, high, rows, cols, window, level_row, level_col, kept, buffers):
    width = window.shape[1]
    scale = 6.0 / width * LOG2E
    count = high - low
    spare = kept.shape[0] - 1

    def cross(tile, buffer):
        index = low + jnp.minimum(tile, count - 1)
        left = window[pl.ds(pl.multiple_of(rows[index] * PTS, PTS), PTS), :]
        right = window[pl.ds(pl.multiple_of(cols[index] * PTS, PTS), PTS), :]
        buffer[...] = lax.dot_general(
            left, right, (((1,), (1,)), ((), ())), preferred_element_type=jnp.float32
        )

    def finish(tile, buffer):
        valid = jnp.logical_and(tile >= 0, tile < count)
        index = low + jnp.clip(tile, 0, count - 1)
        row, col = rows[index], cols[index]
        right_level = level_row[col][0:1, :]
        left_level = jnp.concatenate([level_col[row]] * (PTS // 128), axis=1)
        value = jnp.exp2(buffer[...] * scale - left_level - right_level)
        kept[jnp.where(valid, index, spare)] = value.astype(jnp.bfloat16)

    def body(pair, carry):
        cross(2 * pair, buffers[0])
        finish(2 * pair - 1, buffers[1])
        cross(2 * pair + 1, buffers[1])
        finish(2 * pair, buffers[0])
        return carry

    @pl.when(count > 0)
    def _():
        buffers[1][...] = jnp.zeros((PTS, PTS), jnp.float32)

    lax.fori_loop(0, jnp.where(count > 0, lax.div(count, 2) + 1, 0), body, 0)


def build_tiles(stage, fresh, n, rows, cols, state, group, blocks_dev, cap, name):
    places = list(fresh)
    pts = list(fresh.values())
    width = pts[0].shape[1]
    total = (group + 1) * blocks_dev
    near = group * blocks_dev
    shapes = [
        jax.ShapeDtypeStruct((total * PTS, width), jnp.bfloat16),
        jax.ShapeDtypeStruct((total, 8, PTS), jnp.float32),
        jax.ShapeDtypeStruct((near, PTS, 128), jnp.float32),
    ]
    makes = stage is not None
    if makes:
        shapes.append(jax.ShapeDtypeStruct((cap + 1, PTS, PTS), jnp.bfloat16))
    state = state[: len(shapes)]
    scalars = (n, rows, cols) if makes else ()
    first = len(scalars) + len(pts)

    def kernel(*refs):
        pt_refs = refs[len(scalars) : first]
        window, level_row, level_col, *rest = refs[first + len(state) :]
        for place, piece in zip(places, pt_refs):
            blocks = piece.shape[0] // PTS
            window[place * PTS : (place + blocks) * PTS, :] = piece[...]
            for block in range(place, place + blocks):
                set_levels(block, window, level_row, level_col, 3.0 / width * LOG2E)
        if makes:
            n_ref, row_ref, col_ref = refs[:3]
            kept, *buffers = rest
            make_tiles(
                n_ref[stage],
                n_ref[stage + 1],
                row_ref,
                col_ref,
                window,
                level_row,
                level_col,
                kept,
                buffers,
            )

    return pl.pallas_call(
        kernel,
        out_shape=shapes,
        in_specs=[spec(SMEM)] * len(scalars) + [spec(VMEM)] * (len(pts) + len(state)),
        out_specs=[spec(VMEM)] * len(shapes),
        input_output_aliases={first + index: index for index in range(len(state))},
        scratch_shapes=[VMEM((PTS, PTS), jnp.float32)] * (2 if makes else 0),
        cost_estimate=cost(2**32 if stage == 2 else 2**20, 2**20),
        compiler_params=pltpu.CompilerParams(vmem_limit_bytes=6 * 2**20),
        name=name,
    )(*scalars, *pts, *state)


def products(entries, kinds, vecs, tiles, start, targets, height, folds):
    firsts = sorted(vecs)
    tall, held = vecs[firsts[0]].shape
    blocks_dev = held // PTS
    begun = list(start)
    source_low, source_high = firsts[0], firsts[-1] + blocks_dev
    low = min(first for ranges in targets for first, _ in ranges)
    high = max(last for ranges in targets for _, last in ranges)
    shapes = [
        jax.ShapeDtypeStruct((sum(last - first for first, last in ranges), height, PTS), jnp.float32)
        for ranges in targets
    ]

    def pieces(refs):
        for ranges, ref in zip(targets, refs):
            at = 0
            for first, last in ranges:
                yield ref, slice(at, at + last - first), slice(first - low, last - low)
                at += last - first

    def fold(value):
        out = value[:height]
        for index in range(1, folds):
            out = out + value[index * height : (index + 1) * height]
        return out

    def kernel(*refs):
        tile_ref, source_ref, target_ref, bounds = refs[:4]
        vec_refs = refs[4 : 4 + len(firsts)]
        kept = refs[4 + len(firsts)]
        start_refs = refs[5 + len(firsts) : 5 + len(firsts) + len(begun)]
        outs = refs[5 + len(firsts) + len(begun) : -2]
        u_win, acc = refs[-2:]
        for first, ref in zip(firsts, vec_refs):
            for block in range(blocks_dev):
                lanes = slice(block * PTS, (block + 1) * PTS)
                u_win[first - source_low + block] = ref[:, lanes]
        if begun:
            for ref, inside, places in pieces(start_refs):
                acc[places] = ref[inside]
        else:
            for place in range(high - low + 1):
                acc[place] = jnp.zeros((height, PTS), jnp.float32)

        spare = high - low
        unroll = 4

        def several(begin, end, transposed):
            def body(step, carry):
                done = []
                for lane in range(unroll):
                    index = begin + step * unroll + lane
                    valid = index < end
                    index = jnp.minimum(index, end - 1)
                    vec = u_win[source_ref[index] - source_low]
                    tile = kept[tile_ref[index]]
                    if transposed:
                        value = lax.dot_general(
                            vec,
                            tile,
                            (((1,), (1,)), ((), ())),
                            preferred_element_type=jnp.float32,
                        )
                    else:
                        value = jnp.dot(vec, tile, preferred_element_type=jnp.float32)
                    done.append((jnp.where(valid, target_ref[index] - low, spare), fold(value)))
                for target, value in done:
                    acc[target] += value
                return carry

            lax.fori_loop(0, lax.div(end - begin + unroll - 1, unroll), body, 0)

        for kind in kinds:
            several(bounds[2 * kind], bounds[2 * kind + 1], True)
            several(bounds[2 * kind + 1], bounds[2 * kind + 2], False)
        for out, inside, places in pieces(outs):
            out[inside] = acc[places]

    return pl.pallas_call(
        kernel,
        out_shape=shapes,
        in_specs=[spec(SMEM)] * 4 + [spec(VMEM)] * (len(firsts) + 1 + len(begun)),
        out_specs=[spec(VMEM)] * len(shapes),
        scratch_shapes=[
            VMEM((source_high - source_low, tall, PTS), jnp.bfloat16),
            VMEM((high - low + 1, height, PTS), jnp.float32),
        ],
        cost_estimate=cost(2**31 if kinds == (1,) else 2**20, 2**20),
        compiler_params=pltpu.CompilerParams(vmem_limit_bytes=10 * 2**20),
        name="products",
    )(*entries, *[vecs[first] for first in firsts], tiles, *begun)


def urgent_ranges(group, blocks_dev):
    messages = [
        [rel for rel in range(group) if rel & bit and rel % bit == 0] for bit in bits_of(group)
    ]
    return [
        [(rel * blocks_dev, (rel + 1) * blocks_dev) for rel in rels]
        for rels in messages + [[group]]
    ]


def send_urgent(results, later, group, blocks_dev):
    final = []
    *messages, far = results
    parts = {}
    for bit, message in zip(bits_of(group), messages):
        rels = [rel for rel in range(group) if rel & bit and rel % bit == 0]
        for index, rel in enumerate(rels):
            if rel in parts:
                held = message[index * blocks_dev : (index + 1) * blocks_dev]
                message = held + parts[rel] if len(rels) == 1 else message.at[
                    index * blocks_dev : (index + 1) * blocks_dev
                ].add(parts[rel])
        if bit > 1:
            message, far, *later = lax.optimization_barrier((message, far, *later))
        got = swap(message, "grp", bit)
        final.append(got)
        for index, rel in enumerate(rels):
            if rel ^ bit:
                piece = got[index * blocks_dev : (index + 1) * blocks_dev]
                parts[rel ^ bit] = parts[rel ^ bit] + piece if rel ^ bit in parts else piece
    return final + [from_behind(far, "blk", 1)], later


def finish_home(entries, vecs, tiles, start, blocks_dev, height, folds):
    return list(
        products(entries, (2,), vecs, tiles, [start], [[(0, blocks_dev)]], height, folds)
    )


def scaled_gram(parts, own, counts, degree, inverse, split):
    columns = own.shape[0] if degree is not None else own.shape[0] - EXTRA
    total = own.shape[1]
    first = degree is None
    shapes = [
        jax.ShapeDtypeStruct((columns, total), jnp.float32),
        jax.ShapeDtypeStruct((columns, columns), jnp.float32),
    ]
    if split:
        shapes.append(jax.ShapeDtypeStruct((2 * columns, total), jnp.bfloat16))
    if first:
        shapes.append(jax.ShapeDtypeStruct((8, total), jnp.float32))
    operands = list(parts) + [own]
    operands += [] if first else [degree]
    operands += [] if inverse is None else [inverse]

    def kernel(count_ref, *refs):
        ins = list(refs[: len(operands)])
        outs = list(refs[len(operands) :])
        part_refs = ins[: len(parts)]
        own_ref = ins[len(parts)]
        z_out, gram_out = outs[:2]
        gram = jnp.zeros((columns, columns), jnp.float32)
        for block in range(total // PTS):
            lanes = slice(block * PTS, (block + 1) * PTS)
            sums = part_refs[0][block]
            for part in part_refs[1:]:
                sums = sums + part[block]
            if first:
                level = 1.0 + sums[columns : columns + 1, :]
                outs[-1][:, lanes] = jnp.broadcast_to(level, (8, PTS))
            else:
                level = ins[len(parts) + 1][0:1, lanes]
            used = lax.broadcasted_iota(jnp.int32, (columns, PTS), 1) < count_ref[block]
            held = own_ref[0:columns, lanes].astype(jnp.float32)
            z = (held + jnp.where(used, sums[0:columns], 0.0)) / level
            if inverse is not None:
                z = jnp.dot(
                    ins[-1][...], z, precision=HIGHEST, preferred_element_type=jnp.float32
                )
            z_out[:, lanes] = z
            if split:
                high = z.astype(jnp.bfloat16)
                outs[2][0:columns, lanes] = high
                rest = z - high.astype(jnp.float32)
                outs[2][columns : 2 * columns, lanes] = rest.astype(jnp.bfloat16)
            gram = gram + lax.dot_general(
                z, z, (((1,), (1,)), ((), ())), precision=HIGHEST, preferred_element_type=jnp.float32
            )
        gram_out[...] = gram

    return pl.pallas_call(
        kernel,
        out_shape=tuple(shapes),
        in_specs=[spec(SMEM)] + [spec(VMEM)] * len(operands),
        out_specs=(spec(VMEM),) * len(shapes),
        cost_estimate=cost(2**26, 2**21),
        compiler_params=pltpu.CompilerParams(vmem_limit_bytes=6 * 2**20),
        name="scaled_gram",
    )(counts, *operands)


def inverse_factor(gram):
    size = gram.shape[0]
    row_id = lax.broadcasted_iota(jnp.int32, (size, size), 0)
    col_id = lax.broadcasted_iota(jnp.int32, (size, size), 1)
    eye = jnp.where(row_id == col_id, 1.0, 0.0)
    whole = jnp.concatenate([gram, eye], axis=1)
    wide = 2 * size
    count = size // 8
    groups = [whole[8 * g : 8 * g + 8, :] for g in range(count)]
    within = lax.broadcasted_iota(jnp.int32, (8, wide), 0)

    def spread_row(value, row):
        return jnp.broadcast_to(value[row : row + 1, :], (8, wide))

    results = []
    for g in range(count):
        spread = [
            [
                jnp.broadcast_to(groups[other][:, 8 * g + k : 8 * g + k + 1], (8, wide))
                for other in range(g, count)
            ]
            for k in range(8)
        ]
        pivots = jnp.ones((8, wide), jnp.float32)
        for j in range(8):
            column = spread[j]
            pivot = spread_row(column[0], j)
            pivots = jnp.where(within == j, pivot, pivots)
            over = 1.0 / pivot
            below = jnp.where(within > j, column[0], 0.0)
            for k in range(j + 1, 8):
                share = spread_row(column[0], k) * over
                spread[k][0] = spread[k][0] - below * share
                for other in range(1, count - g):
                    spread[k][other] = spread[k][other] - column[other] * share
            top = spread_row(groups[g], j) * over
            groups[g] = groups[g] - below * top
            for other in range(1, count - g):
                groups[g + other] = groups[g + other] - column[other] * top
        results.append(groups[g] * lax.rsqrt(pivots))
    return jnp.concatenate(results, axis=0)[:, size:wide]


def factor_kernel(gram, out):
    out[...] = inverse_factor(gram[...])


def factor(gram):
    return pl.pallas_call(
        factor_kernel,
        out_shape=jax.ShapeDtypeStruct(gram.shape, jnp.float32),
        in_specs=[spec(VMEM)],
        out_specs=spec(VMEM),
        cost_estimate=cost(2**16, 2**16),
        compiler_params=pltpu.CompilerParams(vmem_limit_bytes=2 * 2**20),
        name="factor",
    )(gram)


def embed_kernel(gram, z, out):
    out[...] = jnp.dot(
        inverse_factor(gram[...]), z[...], precision=HIGHEST, preferred_element_type=jnp.float32
    )


def embedding(gram, z):
    return pl.pallas_call(
        embed_kernel,
        out_shape=jax.ShapeDtypeStruct(z.shape, jnp.float32),
        in_specs=[spec(VMEM)] * 2,
        out_specs=spec(VMEM),
        cost_estimate=cost(2**30, 2**20),
        compiler_params=pltpu.CompilerParams(vmem_limit_bytes=4 * 2**20),
        name="embedding",
    )(gram, z)


def sum_stages():
    return bits_of(lax.axis_size("blk") * lax.axis_size("grp"))


def pairs_of(bits):
    return [bits[first : first + 2] for first in range(0, len(bits), 2)]


def all_sum(value, stages):
    count = lax.axis_size("blk") * lax.axis_size("grp")
    for bits in stages:
        moves = [0]
        for bit in bits if isinstance(bits, list) else [bits]:
            moves += [move ^ bit for move in moves]
        terms = [value] + [
            lax.ppermute(value, ("blk", "grp"), [(source, source ^ move) for source in range(count)])
            for move in moves[1:]
        ]
        while len(terms) > 1:
            terms = [left + right for left, right in zip(terms[::2], terms[1::2])]
        value = terms[0]
    return value


def per_device(points, counts, pair_rows, pair_cols, pair_live, start):
    group = lax.axis_size("grp")
    blocks_dev = counts.shape[0]
    columns = start.shape[0]
    slots = pair_rows.shape[0]
    cap = max(-(-slots // group), blocks_dev * blocks_dev * group)
    half = (blocks_dev // 2) * PTS

    home = min(2, group) * blocks_dev

    rows, cols, n, *entries = listing(
        pair_rows, pair_cols, pair_live, group, cap, blocks_dev
    )
    mate = swap(points, "grp", 1)
    chunks = [points[:half], points[half:]]
    far = [from_behind(chunk, "blk", -1) for chunk in chunks]
    crossed = [gather_far_bits(chunk) for chunk in chunks]
    begin, mate = lax.optimization_barrier((start, mate))
    vec = opening(begin, counts)
    tied = lax.optimization_barrier((vec, n, rows, cols, far[0], *crossed[0].values()))
    vec, n, rows, cols, far[0] = tied[:5]
    crossed[0] = dict(zip(crossed[0], tied[5:]))
    cross_vec = gather_far_bits(vec)
    far_vec = from_behind(vec, "blk", -1)
    mate_vec = swap(vec, "grp", 1)

    def direct(index):
        offset = index * (blocks_dev // 2)
        found = {group * blocks_dev + offset: far[index]}
        for rel, value in crossed[index].items():
            found[rel * blocks_dev + offset] = value
        return found

    def passed_on(index):
        offset = index * (blocks_dev // 2)
        found = {}
        for rel, value in crossed[index].items():
            cut = value.shape[0] // (1 if index else 2)
            parts = [swap(value[at : at + cut], "grp", 1) for at in range(0, value.shape[0], cut)]
            found[(rel ^ 1) * blocks_dev + offset] = jnp.concatenate(parts, 0)
        return found

    def build(stage, fresh, state, name):
        return list(
            build_tiles(stage, fresh, n, rows, cols, state, group, blocks_dev, cap, name)
        )

    state = build(0, {0: points, blocks_dev: mate, **direct(0)}, (), "first_tiles")
    state = build(1, passed_on(0), state, "second_tiles")
    tied = lax.optimization_barrier((far[1], mate_vec, state[1], *crossed[1].values()))
    far[1], mate_vec, state[1] = tied[:3]
    crossed[1] = dict(zip(crossed[1], tied[3:]))
    last = passed_on(1)
    *grown, kept = state
    state = build(None, direct(1), grown, "more_blocks") + [kept]
    state = build(2, last, state, "last_tiles")
    kept = state[-1]
    tied = lax.optimization_barrier((kept, *cross_vec.values()))
    kept = tied[0]
    cross_vec = dict(zip(cross_vec, tied[1:]))

    def window_of(own, mate, crossed, far):
        found = {0: own, blocks_dev: mate, group * blocks_dev: far}
        for rel, value in crossed.items():
            found[rel * blocks_dev] = value
            found[(rel ^ 1) * blocks_dev] = swap(value, "grp", 1)
        return found

    def beyond(vecs):
        return {place: value for place, value in vecs.items() if place >= home}

    vecs = window_of(vec, mate_vec, cross_vec, far_vec)
    urgent = urgent_ranges(group, blocks_dev)
    height = columns + 8
    at_home, *results = products(
        entries,
        (0,),
        {0: vec, blocks_dev: mate_vec},
        kept,
        (),
        [[(0, blocks_dev)]] + urgent,
        height,
        1,
    )
    results = products(entries, (1,), beyond(vecs), kept, results, urgent, height, 1)
    sums, (at_home,) = send_urgent(results, (at_home,), group, blocks_dev)
    sums = finish_home(entries, beyond(vecs), kept, at_home, blocks_dev, height, 1) + sums
    z, gram, parts, degree = scaled_gram(sums, vec, counts, None, None, True)
    for turn in range(1, ITERS):
        stages = sum_stages()
        far_part = from_behind(parts, "blk", -1)
        crossed = gather_far_bits(parts)
        mate_part = swap(parts, "grp", 1)
        gram = all_sum(gram, stages[:1])
        at_home, *results = products(
            entries,
            (0,),
            {0: parts, blocks_dev: mate_part},
            kept,
            (),
            [[(0, blocks_dev)]] + urgent,
            columns,
            2,
        )
        gram, at_home, far_part, *tied = lax.optimization_barrier(
            (gram, at_home, far_part, *crossed.values())
        )
        crossed = dict(zip(crossed, tied))
        vecs = beyond(window_of(parts, mate_part, crossed, far_part))
        gram = all_sum(gram, stages[1:2])
        gram, *tied = lax.optimization_barrier((gram, *vecs.values()))
        vecs = dict(zip(vecs, tied))
        results = products(entries, (1,), vecs, kept, results, urgent, columns, 2)
        gram = all_sum(gram, stages[2:3])
        gram, *results = lax.optimization_barrier((gram, *results))
        gram = all_sum(gram, stages[3:4])
        sums, (at_home, gram) = send_urgent(results, (at_home, gram), group, blocks_dev)
        gram = all_sum(gram, stages[4:])
        sums = finish_home(entries, vecs, kept, at_home, blocks_dev, columns, 2) + sums
        inverse = factor(gram)
        z, gram, *parts = scaled_gram(sums, z, counts, degree, inverse, turn + 1 < ITERS)
        parts = parts[0] if parts else None
    stages = sum_stages()
    return embedding(all_sum(gram, stages[:1] + pairs_of(stages[1:])), z)


def solution(mesh):
    in_specs = (
        P(("blk", "grp"), None),
        P(("blk", "grp")),
        P("blk"),
        P("blk"),
        P("blk"),
        P(None, ("blk", "grp")),
    )
    out_specs = P(None, ("blk", "grp"))
    return jax.shard_map(
        per_device, mesh=mesh, in_specs=in_specs, out_specs=out_specs, check_vma=False
    )
```

```python
import functools

import jax
import jax.numpy as jnp
from jax import lax
from jax.experimental import pallas as pl
from jax.experimental.pallas import tpu as pltpu
from jax.sharding import PartitionSpec as P

PTS = 512
ITERS = 2
LOG2E = 1.4426950408889634
DEAD = 65536.0
EXTRA = 16
VMEM = pltpu.VMEM
SMEM = pltpu.SMEM
HIGHEST = lax.Precision.HIGHEST


def cost(flops, moved):
    return pl.CostEstimate(flops=int(flops), bytes_accessed=int(moved), transcendentals=0)


def spec(space):
    return pl.BlockSpec(memory_space=space)


def swap(value, axis, bit):
    count = lax.axis_size(axis)
    return lax.ppermute(value, axis, [(source, source ^ bit) for source in range(count)])


def from_behind(value, axis, steps):
    count = lax.axis_size(axis)
    initial, last = (max(0, -steps), min(count, count - steps))
    return lax.ppermute(value, axis, [(source, source + steps) for source in range(initial, last)])


def bits_of(count):
    bits = []
    bit = 1
    while bit < count:
        bits.append(bit)
        bit *= 2
    return bits


def gather_near(value, axis):
    held = {0: value}
    for bit in reversed(bits_of(lax.axis_size(axis))):
        for rel in list(held):
            held[rel ^ bit] = swap(held[rel], axis, bit)
    return [held[rel] for rel in range(len(held))]


def gather_far_bits(value):
    held = {0: value}
    for bit in reversed(bits_of(lax.axis_size("grp"))[1:]):
        for rel in list(held):
            held[rel ^ bit] = swap(held[rel], "grp", bit)
    held.pop(0)
    return held


def opening_kernel(start, counts, out):
    columns, total = start.shape
    for block in range(total // PTS):
        lanes = slice(block * PTS, (block + 1) * PTS)
        used = lax.broadcasted_iota(jnp.int32, (columns, PTS), 1) < counts[block]
        out[0:columns, lanes] = jnp.where(used, start[:, lanes], 0.0).astype(jnp.bfloat16)
        which = lax.broadcasted_iota(jnp.int32, (EXTRA, PTS), 0)
        place_in = lax.broadcasted_iota(jnp.int32, (EXTRA, PTS), 1)
        ones = jnp.logical_and(which == 0, place_in < counts[block])
        out[columns : columns + EXTRA, lanes] = jnp.where(ones, 1.0, 0.0).astype(jnp.bfloat16)


def opening(start, counts):
    columns, total = start.shape
    return pl.pallas_call(
        opening_kernel,
        out_shape=jax.ShapeDtypeStruct((columns + EXTRA, total), jnp.bfloat16),
        in_specs=[spec(VMEM), spec(SMEM)],
        out_specs=spec(VMEM),
        cost_estimate=cost(2**20, 2**19),
        compiler_params=pltpu.CompilerParams(vmem_limit_bytes=2 * 2**20),
        name="opening",
    )(start, counts)


def stage_of(place, group, blocks_dev):
    piece = lax.div(place, blocks_dev)
    first_half = lax.rem(place, blocks_dev) < blocks_dev // 2
    later = jnp.where(first_half, jnp.where(lax.rem(piece, 2) == 0, 0, 1), 2)
    return jnp.where(piece < min(2, group), 0, later)


def listing_kernel(
    group,
    cap,
    blocks_dev,
    rows,
    cols,
    live,
    out_rows,
    out_cols,
    out_n,
    tiles,
    sources,
    targets,
    bounds,
    owners,
):
    slab = blocks_dev * group
    slots = rows.shape[0]
    member = lax.axis_index("grp")

    def local_near(block, device):
        return (lax.div(block, blocks_dev) ^ device) * blocks_dev + lax.rem(block, blocks_dev)

    def local_far(block):
        return slab + lax.rem(block - slab, blocks_dev)

    def count_far(slot, carry):
        col = cols[slot]
        far = jnp.logical_and(slot < live[0], col >= slab)
        owner = lax.div(col - slab, blocks_dev)
        owners[slot] = jnp.where(far, owner, -1)
        return tuple(
            old + jnp.where(jnp.logical_and(far, owner == device), 1, 0)
            for device, old in enumerate(carry)
        )

    loads = lax.fori_loop(0, slots, count_far, (jnp.int32(0),) * group)

    def give(slot, loads):
        row, col = rows[slot], cols[slot]
        near = jnp.logical_and(slot < live[0], col < slab)
        best = jnp.int32(2**30)
        owner = jnp.int32(0)
        for device in range(group):
            stage = jnp.maximum(
                stage_of(local_near(row, device), group, blocks_dev),
                stage_of(local_near(col, device), group, blocks_dev),
            )
            score = loads[device] + 64 * stage + jnp.where(loads[device] < cap, 0, 2**20)
            owner = jnp.where(score < best, device, owner)
            best = jnp.minimum(score, best)

        @pl.when(near)
        def _():
            owners[slot] = owner

        return tuple(
            load + jnp.where(jnp.logical_and(near, owner == device), 1, 0)
            for device, load in enumerate(loads)
        )

    lax.fori_loop(0, slots, give, loads)

    def place_those(wanted, filled):
        def place(slot, filled):
            row, col = rows[slot], cols[slot]
            row_place = local_near(row, member)
            col_place = jnp.where(col >= slab, local_far(col), local_near(col, member))
            stage = jnp.maximum(
                stage_of(row_place, group, blocks_dev), stage_of(col_place, group, blocks_dev)
            )
            mine = jnp.logical_and(owners[slot] == member, stage == wanted)

            @pl.when(mine)
            def _():
                out_rows[filled] = row_place
                out_cols[filled] = col_place

            return filled + jnp.where(mine, 1, 0)

        return lax.fori_loop(0, slots, place, filled)

    count = jnp.int32(0)
    out_n[0] = count
    for wanted in range(3):
        count = place_those(wanted, count)
        out_n[wanted + 1] = count

    home = min(2, group) * blocks_dev
    bounds[0] = jnp.int32(0)
    filled = jnp.int32(0)
    for kind in range(3):
        for to_row in (True, False):

            def enter(index, filled):
                source = (out_cols if to_row else out_rows)[index]
                target = (out_rows if to_row else out_cols)[index]
                if kind == 0:
                    wanted = source < home
                elif kind == 1:
                    wanted = jnp.logical_and(source >= home, target >= blocks_dev)
                else:
                    wanted = jnp.logical_and(source >= home, target < blocks_dev)

                @pl.when(wanted)
                def _():
                    tiles[filled] = index
                    sources[filled] = source
                    targets[filled] = target

                return filled + jnp.where(wanted, 1, 0)

            filled = lax.fori_loop(0, count, enter, filled)
            bounds[2 * kind + (1 if to_row else 2)] = filled


def listing(rows, cols, live, group, cap, blocks_dev):
    return pl.pallas_call(
        functools.partial(listing_kernel, group, cap, blocks_dev),
        out_shape=(
            jax.ShapeDtypeStruct((cap,), jnp.int32),
            jax.ShapeDtypeStruct((cap,), jnp.int32),
            jax.ShapeDtypeStruct((4,), jnp.int32),
            jax.ShapeDtypeStruct((2 * cap,), jnp.int32),
            jax.ShapeDtypeStruct((2 * cap,), jnp.int32),
            jax.ShapeDtypeStruct((2 * cap,), jnp.int32),
            jax.ShapeDtypeStruct((7,), jnp.int32),
        ),
        in_specs=[spec(SMEM)] * 3,
        out_specs=(spec(SMEM),) * 7,
        scratch_shapes=[SMEM((rows.shape[0],), jnp.int32)],
        cost_estimate=cost(2**20, 2**10),
        compiler_params=pltpu.CompilerParams(vmem_limit_bytes=2**20),
        name="listing",
    )(rows, cols, live)


def set_levels(place, window, level_row, level_col, scale):
    block = window[place * PTS : (place + 1) * PTS, :]
    width = block.shape[1]
    part = jnp.zeros((PTS, 128), jnp.float32)
    for lane in range(0, width, 128):
        wide = block[:, lane : lane + 128].astype(jnp.float32)
        part = part + wide * wide
    level_row[place] = scale * lax.dot_general(
        jnp.ones((8, 128), jnp.float32),
        part,
        (((1,), (1,)), ((), ())),
        precision=HIGHEST,
        preferred_element_type=jnp.float32,
    )
    if place < level_col.shape[0]:
        total = jnp.sum(part, axis=1, keepdims=True) * scale
        level_col[place] = jnp.broadcast_to(total, (PTS, 128))


def make_tiles(low, high, rows, cols, window, level_row, level_col, kept, buffers):
    width = window.shape[1]
    scale = 6.0 / width * LOG2E
    count = high - low
    spare = kept.shape[0] - 1

    def cross(tile, buffer):
        index = low + jnp.minimum(tile, count - 1)
        left = window[pl.ds(pl.multiple_of(rows[index] * PTS, PTS), PTS), :]
        right = window[pl.ds(pl.multiple_of(cols[index] * PTS, PTS), PTS), :]
        buffer[...] = lax.dot_general(
            left, right, (((1,), (1,)), ((), ())), preferred_element_type=jnp.float32
        )

    def finish(tile, buffer):
        valid = jnp.logical_and(tile >= 0, tile < count)
        index = low + jnp.clip(tile, 0, count - 1)
        row, col = rows[index], cols[index]
        right_level = level_row[col][0:1, :]
        left_level = jnp.concatenate([level_col[row]] * (PTS // 128), axis=1)
        value = jnp.exp2(buffer[...] * scale - left_level - right_level)
        kept[jnp.where(valid, index, spare)] = value.astype(jnp.bfloat16)

    def body(pair, carry):
        cross(2 * pair, buffers[0])
        finish(2 * pair - 1, buffers[1])
        cross(2 * pair + 1, buffers[1])
        finish(2 * pair, buffers[0])
        return carry

    @pl.when(count > 0)
    def _():
        buffers[1][...] = jnp.zeros((PTS, PTS), jnp.float32)

    lax.fori_loop(0, jnp.where(count > 0, lax.div(count, 2) + 1, 0), body, 0)


def build_tiles(stage, fresh, n, rows, cols, state, group, blocks_dev, cap, name):
    places = list(fresh)
    pts = list(fresh.values())
    width = pts[0].shape[1]
    total = (group + 1) * blocks_dev
    near = group * blocks_dev
    shapes = [
        jax.ShapeDtypeStruct((total * PTS, width), jnp.bfloat16),
        jax.ShapeDtypeStruct((total, 8, PTS), jnp.float32),
        jax.ShapeDtypeStruct((near, PTS, 128), jnp.float32),
    ]
    makes = stage is not None
    if makes:
        shapes.append(jax.ShapeDtypeStruct((cap + 1, PTS, PTS), jnp.bfloat16))
    state = state[: len(shapes)]
    scalars = (n, rows, cols) if makes else ()
    first = len(scalars) + len(pts)

    def kernel(*refs):
        pt_refs = refs[len(scalars) : first]
        window, level_row, level_col, *rest = refs[first + len(state) :]
        for place, piece in zip(places, pt_refs):
            blocks = piece.shape[0] // PTS
            window[place * PTS : (place + blocks) * PTS, :] = piece[...]
            for block in range(place, place + blocks):
                set_levels(block, window, level_row, level_col, 3.0 / width * LOG2E)
        if makes:
            n_ref, row_ref, col_ref = refs[:3]
            kept, *buffers = rest
            make_tiles(
                n_ref[stage],
                n_ref[stage + 1],
                row_ref,
                col_ref,
                window,
                level_row,
                level_col,
                kept,
                buffers,
            )

    return pl.pallas_call(
        kernel,
        out_shape=shapes,
        in_specs=[spec(SMEM)] * len(scalars) + [spec(VMEM)] * (len(pts) + len(state)),
        out_specs=[spec(VMEM)] * len(shapes),
        input_output_aliases={first + index: index for index in range(len(state))},
        scratch_shapes=[VMEM((PTS, PTS), jnp.float32)] * (2 if makes else 0),
        cost_estimate=cost(2**32 if stage == 2 else 2**20, 2**20),
        compiler_params=pltpu.CompilerParams(vmem_limit_bytes=6 * 2**20),
        name=name,
    )(*scalars, *pts, *state)


def products(entries, kinds, vecs, tiles, start, targets, height, folds):
    firsts = sorted(vecs)
    tall, held = vecs[firsts[0]].shape
    blocks_dev = held // PTS
    begun = list(start)
    source_low, source_high = firsts[0], firsts[-1] + blocks_dev
    low = min(first for ranges in targets for first, _ in ranges)
    high = max(last for ranges in targets for _, last in ranges)
    shapes = [
        jax.ShapeDtypeStruct((sum(last - first for first, last in ranges), height, PTS), jnp.float32)
        for ranges in targets
    ]

    def pieces(refs):
        for ranges, ref in zip(targets, refs):
            at = 0
            for first, last in ranges:
                yield ref, slice(at, at + last - first), slice(first - low, last - low)
                at += last - first

    def fold(value):
        out = value[:height]
        for index in range(1, folds):
            out = out + value[index * height : (index + 1) * height]
        return out

    def kernel(*refs):
        tile_ref, source_ref, target_ref, bounds = refs[:4]
        vec_refs = refs[4 : 4 + len(firsts)]
        kept = refs[4 + len(firsts)]
        start_refs = refs[5 + len(firsts) : 5 + len(firsts) + len(begun)]
        outs = refs[5 + len(firsts) + len(begun) : -2]
        u_win, acc = refs[-2:]
        for first, ref in zip(firsts, vec_refs):
            for block in range(blocks_dev):
                lanes = slice(block * PTS, (block + 1) * PTS)
                u_win[first - source_low + block] = ref[:, lanes]
        if begun:
            for ref, inside, places in pieces(start_refs):
                acc[places] = ref[inside]
        else:
            for place in range(high - low + 1):
                acc[place] = jnp.zeros((height, PTS), jnp.float32)

        spare = high - low
        unroll = 4

        def several(begin, end, transposed):
            def body(step, carry):
                done = []
                for lane in range(unroll):
                    index = begin + step * unroll + lane
                    valid = index < end
                    index = jnp.minimum(index, end - 1)
                    vec = u_win[source_ref[index] - source_low]
                    tile = kept[tile_ref[index]]
                    if transposed:
                        value = lax.dot_general(
                            vec,
                            tile,
                            (((1,), (1,)), ((), ())),
                            preferred_element_type=jnp.float32,
                        )
                    else:
                        value = jnp.dot(vec, tile, preferred_element_type=jnp.float32)
                    done.append((jnp.where(valid, target_ref[index] - low, spare), fold(value)))
                for target, value in done:
                    acc[target] += value
                return carry

            lax.fori_loop(0, lax.div(end - begin + unroll - 1, unroll), body, 0)

        for kind in kinds:
            several(bounds[2 * kind], bounds[2 * kind + 1], True)
            several(bounds[2 * kind + 1], bounds[2 * kind + 2], False)
        for out, inside, places in pieces(outs):
            out[inside] = acc[places]

    return pl.pallas_call(
        kernel,
        out_shape=shapes,
        in_specs=[spec(SMEM)] * 4 + [spec(VMEM)] * (len(firsts) + 1 + len(begun)),
        out_specs=[spec(VMEM)] * len(shapes),
        scratch_shapes=[
            VMEM((source_high - source_low, tall, PTS), jnp.bfloat16),
            VMEM((high - low + 1, height, PTS), jnp.float32),
        ],
        cost_estimate=cost(2**31 if kinds == (1,) else 2**20, 2**20),
        compiler_params=pltpu.CompilerParams(vmem_limit_bytes=10 * 2**20),
        name="products",
    )(*entries, *[vecs[first] for first in firsts], tiles, *begun)


def urgent_ranges(group, blocks_dev):
    messages = [
        [rel for rel in range(group) if rel & bit and rel % bit == 0] for bit in bits_of(group)
    ]
    return [
        [(rel * blocks_dev, (rel + 1) * blocks_dev) for rel in rels]
        for rels in messages + [[group]]
    ]


def send_urgent(results, later, group, blocks_dev):
    final = []
    *messages, far = results
    parts = {}
    behind = None
    for bit, message in zip(bits_of(group), messages):
        rels = [rel for rel in range(group) if rel & bit and rel % bit == 0]
        for index, rel in enumerate(rels):
            if rel in parts:
                held = message[index * blocks_dev : (index + 1) * blocks_dev]
                message = held + parts[rel] if len(rels) == 1 else message.at[
                    index * blocks_dev : (index + 1) * blocks_dev
                ].add(parts[rel])
        if bit > 1:
            message, *later = lax.optimization_barrier((message, *later))
        got = swap(message, "grp", bit)
        if behind is None:
            got, far = lax.optimization_barrier((got, far))
            behind = from_behind(far, "blk", 1)
        final.append(got)
        for index, rel in enumerate(rels):
            if rel ^ bit:
                piece = got[index * blocks_dev : (index + 1) * blocks_dev]
                parts[rel ^ bit] = parts[rel ^ bit] + piece if rel ^ bit in parts else piece
    if behind is None:
        behind = from_behind(far, "blk", 1)
    return [behind] + final, later


def finish_home(entries, vecs, tiles, start, blocks_dev, height, folds):
    return list(
        products(entries, (2,), vecs, tiles, [start], [[(0, blocks_dev)]], height, folds)
    )


def scaled_gram(parts, own, counts, degree, inverse, split):
    columns = own.shape[0] if degree is not None else own.shape[0] - EXTRA
    total = own.shape[1]
    first = degree is None
    shapes = [
        jax.ShapeDtypeStruct((columns, total), jnp.float32),
        jax.ShapeDtypeStruct((columns, columns), jnp.float32),
    ]
    if split:
        shapes.append(jax.ShapeDtypeStruct((2 * columns, total), jnp.bfloat16))
    if first:
        shapes.append(jax.ShapeDtypeStruct((8, total), jnp.float32))
    operands = list(parts) + [own]
    operands += [] if first else [degree]
    operands += [] if inverse is None else [inverse]

    def kernel(count_ref, *refs):
        ins = list(refs[: len(operands)])
        outs = list(refs[len(operands) :])
        part_refs = ins[: len(parts)]
        own_ref = ins[len(parts)]
        z_out, gram_out = outs[:2]
        gram = jnp.zeros((columns, columns), jnp.float32)
        for block in range(total // PTS):
            lanes = slice(block * PTS, (block + 1) * PTS)
            sums = part_refs[0][block]
            for part in part_refs[1:]:
                sums = sums + part[block]
            if first:
                level = 1.0 + sums[columns : columns + 1, :]
                outs[-1][:, lanes] = jnp.broadcast_to(level, (8, PTS))
            else:
                level = ins[len(parts) + 1][0:1, lanes]
            used = lax.broadcasted_iota(jnp.int32, (columns, PTS), 1) < count_ref[block]
            held = own_ref[0:columns, lanes].astype(jnp.float32)
            z = (held + jnp.where(used, sums[0:columns], 0.0)) / level
            if inverse is not None:
                z = jnp.dot(
                    ins[-1][...], z, precision=HIGHEST, preferred_element_type=jnp.float32
                )
            z_out[:, lanes] = z
            if split:
                high = z.astype(jnp.bfloat16)
                outs[2][0:columns, lanes] = high
                rest = z - high.astype(jnp.float32)
                outs[2][columns : 2 * columns, lanes] = rest.astype(jnp.bfloat16)
            gram = gram + lax.dot_general(
                z, z, (((1,), (1,)), ((), ())), precision=HIGHEST, preferred_element_type=jnp.float32
            )
        gram_out[...] = gram

    return pl.pallas_call(
        kernel,
        out_shape=tuple(shapes),
        in_specs=[spec(SMEM)] + [spec(VMEM)] * len(operands),
        out_specs=(spec(VMEM),) * len(shapes),
        cost_estimate=cost(2**26, 2**21),
        compiler_params=pltpu.CompilerParams(vmem_limit_bytes=6 * 2**20),
        name="scaled_gram",
    )(counts, *operands)


def inverse_factor(gram):
    size = gram.shape[0]
    row_id = lax.broadcasted_iota(jnp.int32, (size, size), 0)
    col_id = lax.broadcasted_iota(jnp.int32, (size, size), 1)
    eye = jnp.where(row_id == col_id, 1.0, 0.0)
    whole = jnp.concatenate([gram, eye], axis=1)
    wide = 2 * size
    count = size // 8
    groups = [whole[8 * g : 8 * g + 8, :] for g in range(count)]
    within = lax.broadcasted_iota(jnp.int32, (8, wide), 0)

    def spread_row(value, row):
        return jnp.broadcast_to(value[row : row + 1, :], (8, wide))

    results = []
    for g in range(count):
        spread = [
            [
                jnp.broadcast_to(groups[other][:, 8 * g + k : 8 * g + k + 1], (8, wide))
                for other in range(g, count)
            ]
            for k in range(8)
        ]
        pivots = jnp.ones((8, wide), jnp.float32)
        for j in range(8):
            column = spread[j]
            pivot = spread_row(column[0], j)
            pivots = jnp.where(within == j, pivot, pivots)
            over = 1.0 / pivot
            below = jnp.where(within > j, column[0], 0.0)
            for k in range(j + 1, 8):
                share = spread_row(column[0], k) * over
                spread[k][0] = spread[k][0] - below * share
                for other in range(1, count - g):
                    spread[k][other] = spread[k][other] - column[other] * share
            top = spread_row(groups[g], j) * over
            groups[g] = groups[g] - below * top
            for other in range(1, count - g):
                groups[g + other] = groups[g + other] - column[other] * top
        results.append(groups[g] * lax.rsqrt(pivots))
    return jnp.concatenate(results, axis=0)[:, size:wide]


def factor_kernel(gram, out):
    out[...] = inverse_factor(gram[...])


def factor(gram):
    return pl.pallas_call(
        factor_kernel,
        out_shape=jax.ShapeDtypeStruct(gram.shape, jnp.float32),
        in_specs=[spec(VMEM)],
        out_specs=spec(VMEM),
        cost_estimate=cost(2**16, 2**16),
        compiler_params=pltpu.CompilerParams(vmem_limit_bytes=2 * 2**20),
        name="factor",
    )(gram)


def embed_kernel(gram, z, out):
    out[...] = jnp.dot(
        inverse_factor(gram[...]), z[...], precision=HIGHEST, preferred_element_type=jnp.float32
    )


def embedding(gram, z):
    return pl.pallas_call(
        embed_kernel,
        out_shape=jax.ShapeDtypeStruct(z.shape, jnp.float32),
        in_specs=[spec(VMEM)] * 2,
        out_specs=spec(VMEM),
        cost_estimate=cost(2**30, 2**20),
        compiler_params=pltpu.CompilerParams(vmem_limit_bytes=4 * 2**20),
        name="embedding",
    )(gram, z)


def sum_stages():
    return bits_of(lax.axis_size("blk") * lax.axis_size("grp"))


def pairs_of(bits):
    return [bits[first : first + 2] for first in range(0, len(bits), 2)]


def all_sum(value, stages, beside=None):
    count = lax.axis_size("blk") * lax.axis_size("grp")
    for bits in stages:
        moves = [0]
        for bit in bits if isinstance(bits, list) else [bits]:
            moves += [move ^ bit for move in moves]
        terms = [value] + [
            lax.ppermute(value, ("blk", "grp"), [(source, source ^ move) for source in range(count)])
            for move in moves[1:]
        ]
        if beside is not None:
            terms[0], beside = lax.optimization_barrier((terms[0], beside))
        while len(terms) > 1:
            terms = [left + right for left, right in zip(terms[::2], terms[1::2])]
        value = terms[0]
    return value if beside is None else (value, beside)


def per_device(points, counts, pair_rows, pair_cols, pair_live, start):
    group = lax.axis_size("grp")
    blocks_dev = counts.shape[0]
    columns = start.shape[0]
    slots = pair_rows.shape[0]
    cap = max(-(-slots // group), blocks_dev * blocks_dev * group)
    half = (blocks_dev // 2) * PTS

    home = min(2, group) * blocks_dev

    rows, cols, n, *entries = listing(
        pair_rows, pair_cols, pair_live, group, cap, blocks_dev
    )
    mate = swap(points, "grp", 1)
    chunks = [points[:half], points[half:]]
    far = [from_behind(chunk, "blk", -1) for chunk in chunks]
    crossed = [gather_far_bits(chunk) for chunk in chunks]
    begin, mate = lax.optimization_barrier((start, mate))
    vec = opening(begin, counts)
    tied = lax.optimization_barrier((vec, n, rows, cols, far[0], *crossed[0].values()))
    vec, n, rows, cols, far[0] = tied[:5]
    crossed[0] = dict(zip(crossed[0], tied[5:]))
    cross_vec = gather_far_bits(vec)
    far_vec = from_behind(vec, "blk", -1)
    mate_vec = swap(vec, "grp", 1)

    def direct(index):
        offset = index * (blocks_dev // 2)
        found = {group * blocks_dev + offset: far[index]}
        for rel, value in crossed[index].items():
            found[rel * blocks_dev + offset] = value
        return found

    def passed_on(index):
        offset = index * (blocks_dev // 2)
        found = {}
        for rel, value in crossed[index].items():
            cut = value.shape[0] // (1 if index else 2)
            parts = [swap(value[at : at + cut], "grp", 1) for at in range(0, value.shape[0], cut)]
            found[(rel ^ 1) * blocks_dev + offset] = jnp.concatenate(parts, 0)
        return found

    def build(stage, fresh, state, name):
        return list(
            build_tiles(stage, fresh, n, rows, cols, state, group, blocks_dev, cap, name)
        )

    state = build(0, {0: points, blocks_dev: mate, **direct(0)}, (), "first_tiles")
    state = build(1, passed_on(0), state, "second_tiles")
    tied = lax.optimization_barrier((far[1], mate_vec, state[1], *crossed[1].values()))
    far[1], mate_vec, state[1] = tied[:3]
    crossed[1] = dict(zip(crossed[1], tied[3:]))
    last = passed_on(1)
    *grown, kept = state
    state = build(None, direct(1), grown, "more_blocks") + [kept]
    state = build(2, last, state, "last_tiles")
    kept = state[-1]
    tied = lax.optimization_barrier((kept, *cross_vec.values()))
    kept = tied[0]
    cross_vec = dict(zip(cross_vec, tied[1:]))

    def window_of(own, mate, crossed, far):
        found = {0: own, blocks_dev: mate, group * blocks_dev: far}
        for rel, value in crossed.items():
            found[rel * blocks_dev] = value
            found[(rel ^ 1) * blocks_dev] = swap(value, "grp", 1)
        return found

    def beyond(vecs):
        return {place: value for place, value in vecs.items() if place >= home}

    vecs = window_of(vec, mate_vec, cross_vec, far_vec)
    urgent = urgent_ranges(group, blocks_dev)
    height = columns + 8
    at_home, *results = products(
        entries,
        (0,),
        {0: vec, blocks_dev: mate_vec},
        kept,
        (),
        [[(0, blocks_dev)]] + urgent,
        height,
        1,
    )
    results = products(entries, (1,), beyond(vecs), kept, results, urgent, height, 1)
    sums, (at_home,) = send_urgent(results, (at_home,), group, blocks_dev)
    sums = finish_home(entries, beyond(vecs), kept, at_home, blocks_dev, height, 1) + sums
    z, gram, parts, degree = scaled_gram(sums, vec, counts, None, None, True)
    for turn in range(1, ITERS):
        stages = sum_stages()
        far_part = from_behind(parts, "blk", -1)
        crossed = gather_far_bits(parts)
        mate_part = swap(parts, "grp", 1)
        gram = all_sum(gram, stages[:1])
        at_home, *results = products(
            entries,
            (0,),
            {0: parts, blocks_dev: mate_part},
            kept,
            (),
            [[(0, blocks_dev)]] + urgent,
            columns,
            2,
        )
        gram, at_home, *tied = lax.optimization_barrier((gram, at_home, *crossed.values()))
        crossed = dict(zip(crossed, tied))
        vecs = beyond(window_of(parts, mate_part, crossed, far_part))
        gram = all_sum(gram, stages[1:2])
        gram, *tied = lax.optimization_barrier((gram, *vecs.values()))
        vecs = dict(zip(vecs, tied))
        results = products(entries, (1,), vecs, kept, results, urgent, columns, 2)
        gram = all_sum(gram, stages[2:3])
        gram, *results = lax.optimization_barrier((gram, *results))
        gram = all_sum(gram, stages[3:4])
        sums, (at_home, gram) = send_urgent(results, (at_home, gram), group, blocks_dev)
        gram = all_sum(gram, stages[4:-1])
        own = finish_home(entries, vecs, kept, at_home, blocks_dev, columns, 2)
        gram, own[0] = all_sum(gram, stages[4:][-1:], own[0])
        sums = own + sums
        inverse = factor(gram)
        z, gram, *parts = scaled_gram(sums, z, counts, degree, inverse, turn + 1 < ITERS)
        parts = parts[0] if parts else None
    stages = sum_stages()
    return embedding(all_sum(gram, stages[:1] + pairs_of(stages[1:])), z)


def solution(mesh):
    in_specs = (
        P(("blk", "grp"), None),
        P(("blk", "grp")),
        P("blk"),
        P("blk"),
        P("blk"),
        P(None, ("blk", "grp")),
    )
    out_specs = P(None, ("blk", "grp"))
    return jax.shard_map(
        per_device, mesh=mesh, in_specs=in_specs, out_specs=out_specs, check_vma=False
    )
```

```python
import functools

import jax
import jax.numpy as jnp
from jax import lax
from jax.experimental import pallas as pl
from jax.experimental.pallas import tpu as pltpu
from jax.sharding import PartitionSpec as P

PTS = 512
ITERS = 2
LOG2E = 1.4426950408889634
DEAD = 65536.0
EXTRA = 16
VMEM = pltpu.VMEM
SMEM = pltpu.SMEM
HIGHEST = lax.Precision.HIGHEST


def cost(flops, moved):
    return pl.CostEstimate(flops=int(flops), bytes_accessed=int(moved), transcendentals=0)


def spec(space):
    return pl.BlockSpec(memory_space=space)


def swap(value, axis, bit):
    count = lax.axis_size(axis)
    return lax.ppermute(value, axis, [(source, source ^ bit) for source in range(count)])


def from_behind(value, axis, steps):
    count = lax.axis_size(axis)
    initial, last = (max(0, -steps), min(count, count - steps))
    return lax.ppermute(value, axis, [(source, source + steps) for source in range(initial, last)])


def bits_of(count):
    bits = []
    bit = 1
    while bit < count:
        bits.append(bit)
        bit *= 2
    return bits


def gather_near(value, axis):
    held = {0: value}
    for bit in reversed(bits_of(lax.axis_size(axis))):
        for rel in list(held):
            held[rel ^ bit] = swap(held[rel], axis, bit)
    return [held[rel] for rel in range(len(held))]


def gather_far_bits(value):
    held = {0: value}
    for bit in reversed(bits_of(lax.axis_size("grp"))[1:]):
        for rel in list(held):
            held[rel ^ bit] = swap(held[rel], "grp", bit)
    held.pop(0)
    return held


def opening_kernel(start, counts, out):
    columns, total = start.shape
    for block in range(total // PTS):
        lanes = slice(block * PTS, (block + 1) * PTS)
        used = lax.broadcasted_iota(jnp.int32, (columns, PTS), 1) < counts[block]
        out[0:columns, lanes] = jnp.where(used, start[:, lanes], 0.0).astype(jnp.bfloat16)
        which = lax.broadcasted_iota(jnp.int32, (EXTRA, PTS), 0)
        place_in = lax.broadcasted_iota(jnp.int32, (EXTRA, PTS), 1)
        ones = jnp.logical_and(which == 0, place_in < counts[block])
        out[columns : columns + EXTRA, lanes] = jnp.where(ones, 1.0, 0.0).astype(jnp.bfloat16)


def opening(start, counts):
    columns, total = start.shape
    return pl.pallas_call(
        opening_kernel,
        out_shape=jax.ShapeDtypeStruct((columns + EXTRA, total), jnp.bfloat16),
        in_specs=[spec(VMEM), spec(SMEM)],
        out_specs=spec(VMEM),
        cost_estimate=cost(2**20, 2**19),
        compiler_params=pltpu.CompilerParams(vmem_limit_bytes=2 * 2**20),
        name="opening",
    )(start, counts)


def stage_of(place, group, blocks_dev):
    piece = lax.div(place, blocks_dev)
    first_half = lax.rem(place, blocks_dev) < blocks_dev // 2
    later = jnp.where(first_half, jnp.where(lax.rem(piece, 2) == 0, 0, 1), 2)
    return jnp.where(piece < min(2, group), 0, later)


def listing_kernel(
    group,
    cap,
    blocks_dev,
    rows,
    cols,
    live,
    out_rows,
    out_cols,
    out_n,
    tiles,
    sources,
    targets,
    bounds,
    owners,
):
    slab = blocks_dev * group
    slots = rows.shape[0]
    member = lax.axis_index("grp")

    def local_near(block, device):
        return (lax.div(block, blocks_dev) ^ device) * blocks_dev + lax.rem(block, blocks_dev)

    def local_far(block):
        return slab + lax.rem(block - slab, blocks_dev)

    def count_far(slot, carry):
        col = cols[slot]
        far = jnp.logical_and(slot < live[0], col >= slab)
        owner = lax.div(col - slab, blocks_dev)
        owners[slot] = jnp.where(far, owner, -1)
        return tuple(
            old + jnp.where(jnp.logical_and(far, owner == device), 1, 0)
            for device, old in enumerate(carry)
        )

    loads = lax.fori_loop(0, slots, count_far, (jnp.int32(0),) * group)

    def give(slot, loads):
        row, col = rows[slot], cols[slot]
        near = jnp.logical_and(slot < live[0], col < slab)
        best = jnp.int32(2**30)
        owner = jnp.int32(0)
        for device in range(group):
            stage = jnp.maximum(
                stage_of(local_near(row, device), group, blocks_dev),
                stage_of(local_near(col, device), group, blocks_dev),
            )
            score = loads[device] + 64 * stage + jnp.where(loads[device] < cap, 0, 2**20)
            owner = jnp.where(score < best, device, owner)
            best = jnp.minimum(score, best)

        @pl.when(near)
        def _():
            owners[slot] = owner

        return tuple(
            load + jnp.where(jnp.logical_and(near, owner == device), 1, 0)
            for device, load in enumerate(loads)
        )

    lax.fori_loop(0, slots, give, loads)

    def place_those(wanted, filled):
        def place(slot, filled):
            row, col = rows[slot], cols[slot]
            row_place = local_near(row, member)
            col_place = jnp.where(col >= slab, local_far(col), local_near(col, member))
            stage = jnp.maximum(
                stage_of(row_place, group, blocks_dev), stage_of(col_place, group, blocks_dev)
            )
            mine = jnp.logical_and(owners[slot] == member, stage == wanted)

            @pl.when(mine)
            def _():
                out_rows[filled] = row_place
                out_cols[filled] = col_place

            return filled + jnp.where(mine, 1, 0)

        return lax.fori_loop(0, slots, place, filled)

    count = jnp.int32(0)
    out_n[0] = count
    for wanted in range(3):
        count = place_those(wanted, count)
        out_n[wanted + 1] = count

    home = min(2, group) * blocks_dev
    bounds[0] = jnp.int32(0)
    filled = jnp.int32(0)
    for kind in range(3):
        for to_row in (True, False):

            def enter(index, filled):
                source = (out_cols if to_row else out_rows)[index]
                target = (out_rows if to_row else out_cols)[index]
                if kind == 0:
                    wanted = source < home
                elif kind == 1:
                    wanted = jnp.logical_and(source >= home, target >= blocks_dev)
                else:
                    wanted = jnp.logical_and(source >= home, target < blocks_dev)

                @pl.when(wanted)
                def _():
                    tiles[filled] = index
                    sources[filled] = source
                    targets[filled] = target

                return filled + jnp.where(wanted, 1, 0)

            filled = lax.fori_loop(0, count, enter, filled)
            bounds[2 * kind + (1 if to_row else 2)] = filled


def listing(rows, cols, live, group, cap, blocks_dev):
    return pl.pallas_call(
        functools.partial(listing_kernel, group, cap, blocks_dev),
        out_shape=(
            jax.ShapeDtypeStruct((cap,), jnp.int32),
            jax.ShapeDtypeStruct((cap,), jnp.int32),
            jax.ShapeDtypeStruct((4,), jnp.int32),
            jax.ShapeDtypeStruct((2 * cap,), jnp.int32),
            jax.ShapeDtypeStruct((2 * cap,), jnp.int32),
            jax.ShapeDtypeStruct((2 * cap,), jnp.int32),
            jax.ShapeDtypeStruct((7,), jnp.int32),
        ),
        in_specs=[spec(SMEM)] * 3,
        out_specs=(spec(SMEM),) * 7,
        scratch_shapes=[SMEM((rows.shape[0],), jnp.int32)],
        cost_estimate=cost(2**20, 2**10),
        compiler_params=pltpu.CompilerParams(vmem_limit_bytes=2**20),
        name="listing",
    )(rows, cols, live)


def set_levels(place, window, level_row, level_col, scale):
    block = window[place * PTS : (place + 1) * PTS, :]
    width = block.shape[1]
    part = jnp.zeros((PTS, 128), jnp.float32)
    for lane in range(0, width, 128):
        wide = block[:, lane : lane + 128].astype(jnp.float32)
        part = part + wide * wide
    level_row[place] = scale * lax.dot_general(
        jnp.ones((8, 128), jnp.float32),
        part,
        (((1,), (1,)), ((), ())),
        precision=HIGHEST,
        preferred_element_type=jnp.float32,
    )
    if place < level_col.shape[0]:
        total = jnp.sum(part, axis=1, keepdims=True) * scale
        level_col[place] = jnp.broadcast_to(total, (PTS, 128))


def make_tiles(low, high, rows, cols, window, level_row, level_col, kept, buffers):
    width = window.shape[1]
    scale = 6.0 / width * LOG2E
    count = high - low
    spare = kept.shape[0] - 1

    def cross(tile, buffer):
        index = low + jnp.minimum(tile, count - 1)
        left = window[pl.ds(pl.multiple_of(rows[index] * PTS, PTS), PTS), :]
        right = window[pl.ds(pl.multiple_of(cols[index] * PTS, PTS), PTS), :]
        buffer[...] = lax.dot_general(
            left, right, (((1,), (1,)), ((), ())), preferred_element_type=jnp.float32
        )

    def finish(tile, buffer):
        valid = jnp.logical_and(tile >= 0, tile < count)
        index = low + jnp.clip(tile, 0, count - 1)
        row, col = rows[index], cols[index]
        right_level = level_row[col][0:1, :]
        left_level = jnp.concatenate([level_col[row]] * (PTS // 128), axis=1)
        value = jnp.exp2(buffer[...] * scale - left_level - right_level)
        kept[jnp.where(valid, index, spare)] = value.astype(jnp.bfloat16)

    def body(pair, carry):
        cross(2 * pair, buffers[0])
        finish(2 * pair - 1, buffers[1])
        cross(2 * pair + 1, buffers[1])
        finish(2 * pair, buffers[0])
        return carry

    @pl.when(count > 0)
    def _():
        buffers[1][...] = jnp.zeros((PTS, PTS), jnp.float32)

    lax.fori_loop(0, jnp.where(count > 0, lax.div(count, 2) + 1, 0), body, 0)


def build_tiles(stage, fresh, n, rows, cols, state, group, blocks_dev, cap, name):
    places = list(fresh)
    pts = list(fresh.values())
    width = pts[0].shape[1]
    total = (group + 1) * blocks_dev
    near = group * blocks_dev
    shapes = [
        jax.ShapeDtypeStruct((total * PTS, width), jnp.bfloat16),
        jax.ShapeDtypeStruct((total, 8, PTS), jnp.float32),
        jax.ShapeDtypeStruct((near, PTS, 128), jnp.float32),
    ]
    makes = stage is not None
    if makes:
        shapes.append(jax.ShapeDtypeStruct((cap + 1, PTS, PTS), jnp.bfloat16))
    state = state[: len(shapes)]
    scalars = (n, rows, cols) if makes else ()
    first = len(scalars) + len(pts)

    def kernel(*refs):
        pt_refs = refs[len(scalars) : first]
        window, level_row, level_col, *rest = refs[first + len(state) :]
        for place, piece in zip(places, pt_refs):
            blocks = piece.shape[0] // PTS
            window[place * PTS : (place + blocks) * PTS, :] = piece[...]
            for block in range(place, place + blocks):
                set_levels(block, window, level_row, level_col, 3.0 / width * LOG2E)
        if makes:
            n_ref, row_ref, col_ref = refs[:3]
            kept, *buffers = rest
            make_tiles(
                n_ref[stage],
                n_ref[stage + 1],
                row_ref,
                col_ref,
                window,
                level_row,
                level_col,
                kept,
                buffers,
            )

    return pl.pallas_call(
        kernel,
        out_shape=shapes,
        in_specs=[spec(SMEM)] * len(scalars) + [spec(VMEM)] * (len(pts) + len(state)),
        out_specs=[spec(VMEM)] * len(shapes),
        input_output_aliases={first + index: index for index in range(len(state))},
        scratch_shapes=[VMEM((PTS, PTS), jnp.float32)] * (2 if makes else 0),
        cost_estimate=cost(2**32 if stage == 2 else 2**20, 2**20),
        compiler_params=pltpu.CompilerParams(vmem_limit_bytes=6 * 2**20),
        name=name,
    )(*scalars, *pts, *state)


def products(entries, kinds, vecs, tiles, start, targets, height, folds):
    firsts = sorted(vecs)
    tall, held = vecs[firsts[0]].shape
    blocks_dev = held // PTS
    begun = list(start)
    source_low, source_high = firsts[0], firsts[-1] + blocks_dev
    low = min(first for ranges in targets for first, _ in ranges)
    high = max(last for ranges in targets for _, last in ranges)
    shapes = [
        jax.ShapeDtypeStruct((sum(last - first for first, last in ranges), height, PTS), jnp.float32)
        for ranges in targets
    ]

    def pieces(refs):
        for ranges, ref in zip(targets, refs):
            at = 0
            for first, last in ranges:
                yield ref, slice(at, at + last - first), slice(first - low, last - low)
                at += last - first

    def fold(value):
        out = value[:height]
        for index in range(1, folds):
            out = out + value[index * height : (index + 1) * height]
        return out

    def kernel(*refs):
        tile_ref, source_ref, target_ref, bounds = refs[:4]
        vec_refs = refs[4 : 4 + len(firsts)]
        kept = refs[4 + len(firsts)]
        start_refs = refs[5 + len(firsts) : 5 + len(firsts) + len(begun)]
        outs = refs[5 + len(firsts) + len(begun) : -2]
        u_win, acc = refs[-2:]
        for first, ref in zip(firsts, vec_refs):
            for block in range(blocks_dev):
                lanes = slice(block * PTS, (block + 1) * PTS)
                u_win[first - source_low + block] = ref[:, lanes]
        if begun:
            for ref, inside, places in pieces(start_refs):
                acc[places] = ref[inside]
        else:
            for place in range(high - low + 1):
                acc[place] = jnp.zeros((height, PTS), jnp.float32)

        spare = high - low
        unroll = 4

        def several(begin, end, transposed):
            def body(step, carry):
                done = []
                for lane in range(unroll):
                    index = begin + step * unroll + lane
                    valid = index < end
                    index = jnp.minimum(index, end - 1)
                    vec = u_win[source_ref[index] - source_low]
                    tile = kept[tile_ref[index]]
                    if transposed:
                        value = lax.dot_general(
                            vec,
                            tile,
                            (((1,), (1,)), ((), ())),
                            preferred_element_type=jnp.float32,
                        )
                    else:
                        value = jnp.dot(vec, tile, preferred_element_type=jnp.float32)
                    done.append((jnp.where(valid, target_ref[index] - low, spare), fold(value)))
                for target, value in done:
                    acc[target] += value
                return carry

            lax.fori_loop(0, lax.div(end - begin + unroll - 1, unroll), body, 0)

        for kind in kinds:
            several(bounds[2 * kind], bounds[2 * kind + 1], True)
            several(bounds[2 * kind + 1], bounds[2 * kind + 2], False)
        for out, inside, places in pieces(outs):
            out[inside] = acc[places]

    return pl.pallas_call(
        kernel,
        out_shape=shapes,
        in_specs=[spec(SMEM)] * 4 + [spec(VMEM)] * (len(firsts) + 1 + len(begun)),
        out_specs=[spec(VMEM)] * len(shapes),
        scratch_shapes=[
            VMEM((source_high - source_low, tall, PTS), jnp.bfloat16),
            VMEM((high - low + 1, height, PTS), jnp.float32),
        ],
        cost_estimate=cost(2**31 if kinds == (1,) else 2**20, 2**20),
        compiler_params=pltpu.CompilerParams(vmem_limit_bytes=10 * 2**20),
        name="products",
    )(*entries, *[vecs[first] for first in firsts], tiles, *begun)


def urgent_ranges(group, blocks_dev):
    messages = [
        [rel for rel in range(group) if rel & bit and rel % bit == 0] for bit in bits_of(group)
    ]
    return [
        [(rel * blocks_dev, (rel + 1) * blocks_dev) for rel in rels]
        for rels in messages + [[group]]
    ]


def send_urgent(results, later, group, blocks_dev):
    final = []
    *messages, far = results
    parts = {}
    behind = None
    for bit, message in zip(bits_of(group), messages):
        rels = [rel for rel in range(group) if rel & bit and rel % bit == 0]
        for index, rel in enumerate(rels):
            if rel in parts:
                held = message[index * blocks_dev : (index + 1) * blocks_dev]
                message = held + parts[rel] if len(rels) == 1 else message.at[
                    index * blocks_dev : (index + 1) * blocks_dev
                ].add(parts[rel])
        if bit > 1:
            message, *later = lax.optimization_barrier((message, *later))
        got = swap(message, "grp", bit)
        if behind is None:
            got, far = lax.optimization_barrier((got, far))
            behind = from_behind(far, "blk", 1)
        final.append(got)
        for index, rel in enumerate(rels):
            if rel ^ bit:
                piece = got[index * blocks_dev : (index + 1) * blocks_dev]
                parts[rel ^ bit] = parts[rel ^ bit] + piece if rel ^ bit in parts else piece
    if behind is None:
        behind = from_behind(far, "blk", 1)
    return [behind] + final, later


def finish_home(entries, vecs, tiles, start, blocks_dev, height, folds):
    return list(
        products(entries, (2,), vecs, tiles, [start], [[(0, blocks_dev)]], height, folds)
    )


def scaled_gram(parts, own, counts, degree, inverse, split):
    columns = own.shape[0] if degree is not None else own.shape[0] - EXTRA
    total = own.shape[1]
    first = degree is None
    shapes = [
        jax.ShapeDtypeStruct((columns, total), jnp.float32),
        jax.ShapeDtypeStruct((columns, columns), jnp.float32),
    ]
    if split:
        shapes.append(jax.ShapeDtypeStruct((2 * columns, total), jnp.bfloat16))
    if first:
        shapes.append(jax.ShapeDtypeStruct((8, total), jnp.float32))
    operands = list(parts) + [own]
    operands += [] if first else [degree]
    operands += [] if inverse is None else [inverse]

    def kernel(count_ref, *refs):
        ins = list(refs[: len(operands)])
        outs = list(refs[len(operands) :])
        part_refs = ins[: len(parts)]
        own_ref = ins[len(parts)]
        z_out, gram_out = outs[:2]
        gram = jnp.zeros((columns, columns), jnp.float32)
        for block in range(total // PTS):
            lanes = slice(block * PTS, (block + 1) * PTS)
            sums = part_refs[0][block]
            for part in part_refs[1:]:
                sums = sums + part[block]
            if first:
                level = 1.0 + sums[columns : columns + 1, :]
                outs[-1][:, lanes] = jnp.broadcast_to(level, (8, PTS))
            else:
                level = ins[len(parts) + 1][0:1, lanes]
            used = lax.broadcasted_iota(jnp.int32, (columns, PTS), 1) < count_ref[block]
            held = own_ref[0:columns, lanes].astype(jnp.float32)
            z = (held + jnp.where(used, sums[0:columns], 0.0)) / level
            if inverse is not None:
                z = jnp.dot(
                    ins[-1][...], z, precision=HIGHEST, preferred_element_type=jnp.float32
                )
            z_out[:, lanes] = z
            if split:
                high = z.astype(jnp.bfloat16)
                outs[2][0:columns, lanes] = high
                rest = z - high.astype(jnp.float32)
                outs[2][columns : 2 * columns, lanes] = rest.astype(jnp.bfloat16)
            gram = gram + lax.dot_general(
                z, z, (((1,), (1,)), ((), ())), precision=HIGHEST, preferred_element_type=jnp.float32
            )
        gram_out[...] = gram

    return pl.pallas_call(
        kernel,
        out_shape=tuple(shapes),
        in_specs=[spec(SMEM)] + [spec(VMEM)] * len(operands),
        out_specs=(spec(VMEM),) * len(shapes),
        cost_estimate=cost(2**26, 2**21),
        compiler_params=pltpu.CompilerParams(vmem_limit_bytes=6 * 2**20),
        name="scaled_gram",
    )(counts, *operands)


def inverse_factor(gram):
    size = gram.shape[0]
    row_id = lax.broadcasted_iota(jnp.int32, (size, size), 0)
    col_id = lax.broadcasted_iota(jnp.int32, (size, size), 1)
    eye = jnp.where(row_id == col_id, 1.0, 0.0)
    whole = jnp.concatenate([gram, eye], axis=1)
    wide = 2 * size
    count = size // 8
    groups = [whole[8 * g : 8 * g + 8, :] for g in range(count)]
    within = lax.broadcasted_iota(jnp.int32, (8, wide), 0)

    def spread_row(value, row):
        return jnp.broadcast_to(value[row : row + 1, :], (8, wide))

    results = []
    for g in range(count):
        spread = [
            [
                jnp.broadcast_to(groups[other][:, 8 * g + k : 8 * g + k + 1], (8, wide))
                for other in range(g, count)
            ]
            for k in range(8)
        ]
        pivots = jnp.ones((8, wide), jnp.float32)
        for j in range(8):
            column = spread[j]
            pivot = spread_row(column[0], j)
            pivots = jnp.where(within == j, pivot, pivots)
            over = 1.0 / pivot
            below = jnp.where(within > j, column[0], 0.0)
            for k in range(j + 1, 8):
                share = spread_row(column[0], k) * over
                spread[k][0] = spread[k][0] - below * share
                for other in range(1, count - g):
                    spread[k][other] = spread[k][other] - column[other] * share
            top = spread_row(groups[g], j) * over
            groups[g] = groups[g] - below * top
            for other in range(1, count - g):
                groups[g + other] = groups[g + other] - column[other] * top
        results.append(groups[g] * lax.rsqrt(pivots))
    return jnp.concatenate(results, axis=0)[:, size:wide]


def factor_kernel(gram, out):
    out[...] = inverse_factor(gram[...])


def factor(gram):
    return pl.pallas_call(
        factor_kernel,
        out_shape=jax.ShapeDtypeStruct(gram.shape, jnp.float32),
        in_specs=[spec(VMEM)],
        out_specs=spec(VMEM),
        cost_estimate=cost(2**16, 2**16),
        compiler_params=pltpu.CompilerParams(vmem_limit_bytes=2 * 2**20),
        name="factor",
    )(gram)


def embed_kernel(gram, z, out):
    out[...] = jnp.dot(
        inverse_factor(gram[...]), z[...], precision=HIGHEST, preferred_element_type=jnp.float32
    )


def embedding(gram, z):
    return pl.pallas_call(
        embed_kernel,
        out_shape=jax.ShapeDtypeStruct(z.shape, jnp.float32),
        in_specs=[spec(VMEM)] * 2,
        out_specs=spec(VMEM),
        cost_estimate=cost(2**30, 2**20),
        compiler_params=pltpu.CompilerParams(vmem_limit_bytes=4 * 2**20),
        name="embedding",
    )(gram, z)


def sum_stages():
    return bits_of(lax.axis_size("blk") * lax.axis_size("grp"))


def sum_by_shares(value):
    axes = ("blk", "grp")
    count = lax.axis_size("blk") * lax.axis_size("grp")
    shares = value.reshape(count, value.size // count)
    share = jnp.sum(lax.all_to_all(shares, axes, 0, 0, tiled=True), axis=0, keepdims=True)
    shares = jnp.broadcast_to(share, shares.shape)
    return lax.all_to_all(shares, axes, 0, 0, tiled=True).reshape(value.shape)


def pairs_of(bits):
    return [bits[first : first + 2] for first in range(0, len(bits), 2)]


def all_sum(value, stages, beside=None):
    count = lax.axis_size("blk") * lax.axis_size("grp")
    for bits in stages:
        moves = [0]
        for bit in bits if isinstance(bits, list) else [bits]:
            moves += [move ^ bit for move in moves]
        terms = [value] + [
            lax.ppermute(value, ("blk", "grp"), [(source, source ^ move) for source in range(count)])
            for move in moves[1:]
        ]
        if beside is not None:
            terms[0], beside = lax.optimization_barrier((terms[0], beside))
        while len(terms) > 1:
            terms = [left + right for left, right in zip(terms[::2], terms[1::2])]
        value = terms[0]
    return value if beside is None else (value, beside)


def per_device(points, counts, pair_rows, pair_cols, pair_live, start):
    group = lax.axis_size("grp")
    blocks_dev = counts.shape[0]
    columns = start.shape[0]
    slots = pair_rows.shape[0]
    cap = max(-(-slots // group), blocks_dev * blocks_dev * group)
    half = (blocks_dev // 2) * PTS

    home = min(2, group) * blocks_dev

    rows, cols, n, *entries = listing(
        pair_rows, pair_cols, pair_live, group, cap, blocks_dev
    )
    mate = swap(points, "grp", 1)
    chunks = [points[:half], points[half:]]
    far = [from_behind(chunk, "blk", -1) for chunk in chunks]
    crossed = [gather_far_bits(chunk) for chunk in chunks]
    begin, mate = lax.optimization_barrier((start, mate))
    vec = opening(begin, counts)
    tied = lax.optimization_barrier((vec, n, rows, cols, far[0], *crossed[0].values()))
    vec, n, rows, cols, far[0] = tied[:5]
    crossed[0] = dict(zip(crossed[0], tied[5:]))
    cross_vec = gather_far_bits(vec)
    far_vec = from_behind(vec, "blk", -1)
    mate_vec = swap(vec, "grp", 1)

    def direct(index):
        offset = index * (blocks_dev // 2)
        found = {group * blocks_dev + offset: far[index]}
        for rel, value in crossed[index].items():
            found[rel * blocks_dev + offset] = value
        return found

    def passed_on(index):
        offset = index * (blocks_dev // 2)
        found = {}
        for rel, value in crossed[index].items():
            cut = value.shape[0] // (1 if index else 2)
            parts = [swap(value[at : at + cut], "grp", 1) for at in range(0, value.shape[0], cut)]
            found[(rel ^ 1) * blocks_dev + offset] = jnp.concatenate(parts, 0)
        return found

    def build(stage, fresh, state, name):
        return list(
            build_tiles(stage, fresh, n, rows, cols, state, group, blocks_dev, cap, name)
        )

    state = build(0, {0: points, blocks_dev: mate, **direct(0)}, (), "first_tiles")
    state = build(1, passed_on(0), state, "second_tiles")
    tied = lax.optimization_barrier((far[1], mate_vec, state[1], *crossed[1].values()))
    far[1], mate_vec, state[1] = tied[:3]
    crossed[1] = dict(zip(crossed[1], tied[3:]))
    last = passed_on(1)
    *grown, kept = state
    state = build(None, direct(1), grown, "more_blocks") + [kept]
    state = build(2, last, state, "last_tiles")
    kept = state[-1]
    tied = lax.optimization_barrier((kept, *cross_vec.values()))
    kept = tied[0]
    cross_vec = dict(zip(cross_vec, tied[1:]))

    def window_of(own, mate, crossed, far):
        found = {0: own, blocks_dev: mate, group * blocks_dev: far}
        for rel, value in crossed.items():
            found[rel * blocks_dev] = value
            found[(rel ^ 1) * blocks_dev] = swap(value, "grp", 1)
        return found

    def beyond(vecs):
        return {place: value for place, value in vecs.items() if place >= home}

    vecs = window_of(vec, mate_vec, cross_vec, far_vec)
    urgent = urgent_ranges(group, blocks_dev)
    height = columns + 8
    at_home, *results = products(
        entries,
        (0,),
        {0: vec, blocks_dev: mate_vec},
        kept,
        (),
        [[(0, blocks_dev)]] + urgent,
        height,
        1,
    )
    results = products(entries, (1,), beyond(vecs), kept, results, urgent, height, 1)
    sums, (at_home,) = send_urgent(results, (at_home,), group, blocks_dev)
    sums = finish_home(entries, beyond(vecs), kept, at_home, blocks_dev, height, 1) + sums
    z, gram, parts, degree = scaled_gram(sums, vec, counts, None, None, True)
    for turn in range(1, ITERS):
        stages = sum_stages()
        far_part = from_behind(parts, "blk", -1)
        crossed = gather_far_bits(parts)
        mate_part = swap(parts, "grp", 1)
        gram = all_sum(gram, stages[:1])
        at_home, *results = products(
            entries,
            (0,),
            {0: parts, blocks_dev: mate_part},
            kept,
            (),
            [[(0, blocks_dev)]] + urgent,
            columns,
            2,
        )
        gram, at_home, *tied = lax.optimization_barrier((gram, at_home, *crossed.values()))
        crossed = dict(zip(crossed, tied))
        vecs = beyond(window_of(parts, mate_part, crossed, far_part))
        gram = all_sum(gram, stages[1:2])
        gram, *tied = lax.optimization_barrier((gram, *vecs.values()))
        vecs = dict(zip(vecs, tied))
        results = products(entries, (1,), vecs, kept, results, urgent, columns, 2)
        gram = all_sum(gram, stages[2:3])
        gram, *results = lax.optimization_barrier((gram, *results))
        gram = all_sum(gram, stages[3:4])
        sums, (at_home, gram) = send_urgent(results, (at_home, gram), group, blocks_dev)
        gram = all_sum(gram, stages[4:-1])
        own = finish_home(entries, vecs, kept, at_home, blocks_dev, columns, 2)
        gram, own[0] = all_sum(gram, stages[4:][-1:], own[0])
        sums = own + sums
        inverse = factor(gram)
        z, gram, *parts = scaled_gram(sums, z, counts, degree, inverse, turn + 1 < ITERS)
        parts = parts[0] if parts else None
    half = columns // 2
    gram = sum_by_shares(jnp.concatenate([gram[:half], gram[half:]], axis=1))
    return embedding(jnp.concatenate([gram[:, :columns], gram[:, columns:]], axis=0), z)


def solution(mesh):
    in_specs = (
        P(("blk", "grp"), None),
        P(("blk", "grp")),
        P("blk"),
        P("blk"),
        P("blk"),
        P(None, ("blk", "grp")),
    )
    out_specs = P(None, ("blk", "grp"))
    return jax.shard_map(
        per_device, mesh=mesh, in_specs=in_specs, out_specs=out_specs, check_vma=False
    )
```

```python
import functools

import jax
import jax.numpy as jnp
from jax import lax
from jax.experimental import pallas as pl
from jax.experimental.pallas import tpu as pltpu
from jax.sharding import PartitionSpec as P

PTS = 512
ITERS = 2
LOG2E = 1.4426950408889634
DEAD = 65536.0
EXTRA = 16
VMEM = pltpu.VMEM
SMEM = pltpu.SMEM
HIGHEST = lax.Precision.HIGHEST


def cost(flops, moved):
    return pl.CostEstimate(flops=int(flops), bytes_accessed=int(moved), transcendentals=0)


def spec(space):
    return pl.BlockSpec(memory_space=space)


def swap(value, axis, bit):
    count = lax.axis_size(axis)
    return lax.ppermute(value, axis, [(source, source ^ bit) for source in range(count)])


def from_behind(value, axis, steps):
    count = lax.axis_size(axis)
    initial, last = (max(0, -steps), min(count, count - steps))
    return lax.ppermute(value, axis, [(source, source + steps) for source in range(initial, last)])


def bits_of(count):
    bits = []
    bit = 1
    while bit < count:
        bits.append(bit)
        bit *= 2
    return bits


def gather_near(value, axis):
    held = {0: value}
    for bit in reversed(bits_of(lax.axis_size(axis))):
        for rel in list(held):
            held[rel ^ bit] = swap(held[rel], axis, bit)
    return [held[rel] for rel in range(len(held))]


def gather_far_bits(value):
    held = {0: value}
    for bit in reversed(bits_of(lax.axis_size("grp"))[1:]):
        for rel in list(held):
            held[rel ^ bit] = swap(held[rel], "grp", bit)
    held.pop(0)
    return held


def opening_kernel(start, counts, out):
    columns, total = start.shape
    for block in range(total // PTS):
        lanes = slice(block * PTS, (block + 1) * PTS)
        used = lax.broadcasted_iota(jnp.int32, (columns, PTS), 1) < counts[block]
        out[0:columns, lanes] = jnp.where(used, start[:, lanes], 0.0).astype(jnp.bfloat16)
        which = lax.broadcasted_iota(jnp.int32, (EXTRA, PTS), 0)
        place_in = lax.broadcasted_iota(jnp.int32, (EXTRA, PTS), 1)
        ones = jnp.logical_and(which == 0, place_in < counts[block])
        out[columns : columns + EXTRA, lanes] = jnp.where(ones, 1.0, 0.0).astype(jnp.bfloat16)


def opening(start, counts):
    columns, total = start.shape
    return pl.pallas_call(
        opening_kernel,
        out_shape=jax.ShapeDtypeStruct((columns + EXTRA, total), jnp.bfloat16),
        in_specs=[spec(VMEM), spec(SMEM)],
        out_specs=spec(VMEM),
        cost_estimate=cost(2**20, 2**19),
        compiler_params=pltpu.CompilerParams(vmem_limit_bytes=2 * 2**20),
        name="opening",
    )(start, counts)


def stage_of(place, group, blocks_dev):
    piece = lax.div(place, blocks_dev)
    first_half = lax.rem(place, blocks_dev) < blocks_dev // 2
    later = jnp.where(first_half, jnp.where(lax.rem(piece, 2) == 0, 0, 1), 2)
    return jnp.where(piece < min(2, group), 0, later)


def listing_kernel(
    group,
    cap,
    blocks_dev,
    rows,
    cols,
    live,
    out_rows,
    out_cols,
    out_n,
    tiles,
    sources,
    targets,
    bounds,
    owners,
):
    slab = blocks_dev * group
    slots = rows.shape[0]
    member = lax.axis_index("grp")

    def local_near(block, device):
        return (lax.div(block, blocks_dev) ^ device) * blocks_dev + lax.rem(block, blocks_dev)

    def local_far(block):
        return slab + lax.rem(block - slab, blocks_dev)

    def count_far(slot, carry):
        col = cols[slot]
        far = jnp.logical_and(slot < live[0], col >= slab)
        owner = lax.div(col - slab, blocks_dev)
        owners[slot] = jnp.where(far, owner, -1)
        return tuple(
            old + jnp.where(jnp.logical_and(far, owner == device), 1, 0)
            for device, old in enumerate(carry)
        )

    loads = lax.fori_loop(0, slots, count_far, (jnp.int32(0),) * group)

    def give(slot, loads):
        row, col = rows[slot], cols[slot]
        near = jnp.logical_and(slot < live[0], col < slab)
        best = jnp.int32(2**30)
        owner = jnp.int32(0)
        for device in range(group):
            stage = jnp.maximum(
                stage_of(local_near(row, device), group, blocks_dev),
                stage_of(local_near(col, device), group, blocks_dev),
            )
            score = loads[device] + 64 * stage + jnp.where(loads[device] < cap, 0, 2**20)
            owner = jnp.where(score < best, device, owner)
            best = jnp.minimum(score, best)

        @pl.when(near)
        def _():
            owners[slot] = owner

        return tuple(
            load + jnp.where(jnp.logical_and(near, owner == device), 1, 0)
            for device, load in enumerate(loads)
        )

    lax.fori_loop(0, slots, give, loads)

    def place_those(wanted, filled):
        def place(slot, filled):
            row, col = rows[slot], cols[slot]
            row_place = local_near(row, member)
            col_place = jnp.where(col >= slab, local_far(col), local_near(col, member))
            stage = jnp.maximum(
                stage_of(row_place, group, blocks_dev), stage_of(col_place, group, blocks_dev)
            )
            mine = jnp.logical_and(owners[slot] == member, stage == wanted)

            @pl.when(mine)
            def _():
                out_rows[filled] = row_place
                out_cols[filled] = col_place

            return filled + jnp.where(mine, 1, 0)

        return lax.fori_loop(0, slots, place, filled)

    count = jnp.int32(0)
    out_n[0] = count
    for wanted in range(3):
        count = place_those(wanted, count)
        out_n[wanted + 1] = count

    home = min(2, group) * blocks_dev
    bounds[0] = jnp.int32(0)
    filled = jnp.int32(0)
    for kind in range(3):
        for to_row in (True, False):

            def enter(index, filled):
                source = (out_cols if to_row else out_rows)[index]
                target = (out_rows if to_row else out_cols)[index]
                if kind == 0:
                    wanted = source < home
                elif kind == 1:
                    wanted = jnp.logical_and(source >= home, target >= blocks_dev)
                else:
                    wanted = jnp.logical_and(source >= home, target < blocks_dev)

                @pl.when(wanted)
                def _():
                    tiles[filled] = index
                    sources[filled] = source
                    targets[filled] = target

                return filled + jnp.where(wanted, 1, 0)

            filled = lax.fori_loop(0, count, enter, filled)
            bounds[2 * kind + (1 if to_row else 2)] = filled


def listing(rows, cols, live, group, cap, blocks_dev):
    return pl.pallas_call(
        functools.partial(listing_kernel, group, cap, blocks_dev),
        out_shape=(
            jax.ShapeDtypeStruct((cap,), jnp.int32),
            jax.ShapeDtypeStruct((cap,), jnp.int32),
            jax.ShapeDtypeStruct((4,), jnp.int32),
            jax.ShapeDtypeStruct((2 * cap,), jnp.int32),
            jax.ShapeDtypeStruct((2 * cap,), jnp.int32),
            jax.ShapeDtypeStruct((2 * cap,), jnp.int32),
            jax.ShapeDtypeStruct((7,), jnp.int32),
        ),
        in_specs=[spec(SMEM)] * 3,
        out_specs=(spec(SMEM),) * 7,
        scratch_shapes=[SMEM((rows.shape[0],), jnp.int32)],
        cost_estimate=cost(2**20, 2**10),
        compiler_params=pltpu.CompilerParams(vmem_limit_bytes=2**20),
        name="listing",
    )(rows, cols, live)


def set_levels(place, window, level_row, level_col, scale):
    block = window[place * PTS : (place + 1) * PTS, :]
    width = block.shape[1]
    part = jnp.zeros((PTS, 128), jnp.float32)
    for lane in range(0, width, 128):
        wide = block[:, lane : lane + 128].astype(jnp.float32)
        part = part + wide * wide
    level_row[place] = scale * lax.dot_general(
        jnp.ones((8, 128), jnp.float32),
        part,
        (((1,), (1,)), ((), ())),
        precision=HIGHEST,
        preferred_element_type=jnp.float32,
    )
    if place < level_col.shape[0]:
        total = jnp.sum(part, axis=1, keepdims=True) * scale
        level_col[place] = jnp.broadcast_to(total, (PTS, 128))


def make_tiles(low, high, rows, cols, window, level_row, level_col, kept, buffers):
    width = window.shape[1]
    scale = 6.0 / width * LOG2E
    count = high - low
    spare = kept.shape[0] - 1

    def cross(tile, buffer):
        index = low + jnp.minimum(tile, count - 1)
        left = window[pl.ds(pl.multiple_of(rows[index] * PTS, PTS), PTS), :]
        right = window[pl.ds(pl.multiple_of(cols[index] * PTS, PTS), PTS), :]
        buffer[...] = lax.dot_general(
            left, right, (((1,), (1,)), ((), ())), preferred_element_type=jnp.float32
        )

    def finish(tile, buffer):
        valid = jnp.logical_and(tile >= 0, tile < count)
        index = low + jnp.clip(tile, 0, count - 1)
        row, col = rows[index], cols[index]
        right_level = level_row[col][0:1, :]
        left_level = jnp.concatenate([level_col[row]] * (PTS // 128), axis=1)
        value = jnp.exp2(buffer[...] * scale - left_level - right_level)
        kept[jnp.where(valid, index, spare)] = value.astype(jnp.bfloat16)

    def body(pair, carry):
        cross(2 * pair, buffers[0])
        finish(2 * pair - 1, buffers[1])
        cross(2 * pair + 1, buffers[1])
        finish(2 * pair, buffers[0])
        return carry

    @pl.when(count > 0)
    def _():
        buffers[1][...] = jnp.zeros((PTS, PTS), jnp.float32)

    lax.fori_loop(0, jnp.where(count > 0, lax.div(count, 2) + 1, 0), body, 0)


def build_tiles(stage, fresh, n, rows, cols, state, group, blocks_dev, cap, name):
    places = list(fresh)
    pts = list(fresh.values())
    width = pts[0].shape[1]
    total = (group + 1) * blocks_dev
    near = group * blocks_dev
    shapes = [
        jax.ShapeDtypeStruct((total * PTS, width), jnp.bfloat16),
        jax.ShapeDtypeStruct((total, 8, PTS), jnp.float32),
        jax.ShapeDtypeStruct((near, PTS, 128), jnp.float32),
    ]
    makes = stage is not None
    if makes:
        shapes.append(jax.ShapeDtypeStruct((cap + 1, PTS, PTS), jnp.bfloat16))
    state = state[: len(shapes)]
    scalars = (n, rows, cols) if makes else ()
    first = len(scalars) + len(pts)

    def kernel(*refs):
        pt_refs = refs[len(scalars) : first]
        window, level_row, level_col, *rest = refs[first + len(state) :]
        for place, piece in zip(places, pt_refs):
            blocks = piece.shape[0] // PTS
            window[place * PTS : (place + blocks) * PTS, :] = piece[...]
            for block in range(place, place + blocks):
                set_levels(block, window, level_row, level_col, 3.0 / width * LOG2E)
        if makes:
            n_ref, row_ref, col_ref = refs[:3]
            kept, *buffers = rest
            make_tiles(
                n_ref[stage],
                n_ref[stage + 1],
                row_ref,
                col_ref,
                window,
                level_row,
                level_col,
                kept,
                buffers,
            )

    return pl.pallas_call(
        kernel,
        out_shape=shapes,
        in_specs=[spec(SMEM)] * len(scalars) + [spec(VMEM)] * (len(pts) + len(state)),
        out_specs=[spec(VMEM)] * len(shapes),
        input_output_aliases={first + index: index for index in range(len(state))},
        scratch_shapes=[VMEM((PTS, PTS), jnp.float32)] * (2 if makes else 0),
        cost_estimate=cost(2**32 if stage == 2 else 2**20, 2**20),
        compiler_params=pltpu.CompilerParams(vmem_limit_bytes=6 * 2**20),
        name=name,
    )(*scalars, *pts, *state)


def products(entries, kinds, vecs, tiles, start, targets, height, folds):
    firsts = sorted(vecs)
    tall, held = vecs[firsts[0]].shape
    blocks_dev = held // PTS
    begun = list(start)
    source_low, source_high = firsts[0], firsts[-1] + blocks_dev
    low = min(first for ranges in targets for first, _ in ranges)
    high = max(last for ranges in targets for _, last in ranges)
    shapes = [
        jax.ShapeDtypeStruct((sum(last - first for first, last in ranges), height, PTS), jnp.float32)
        for ranges in targets
    ]

    def pieces(refs):
        for ranges, ref in zip(targets, refs):
            at = 0
            for first, last in ranges:
                yield ref, slice(at, at + last - first), slice(first - low, last - low)
                at += last - first

    def fold(value):
        out = value[:height]
        for index in range(1, folds):
            out = out + value[index * height : (index + 1) * height]
        return out

    def kernel(*refs):
        tile_ref, source_ref, target_ref, bounds = refs[:4]
        vec_refs = refs[4 : 4 + len(firsts)]
        kept = refs[4 + len(firsts)]
        start_refs = refs[5 + len(firsts) : 5 + len(firsts) + len(begun)]
        outs = refs[5 + len(firsts) + len(begun) : -2]
        u_win, acc = refs[-2:]
        for first, ref in zip(firsts, vec_refs):
            for block in range(blocks_dev):
                lanes = slice(block * PTS, (block + 1) * PTS)
                u_win[first - source_low + block] = ref[:, lanes]
        if begun:
            for ref, inside, places in pieces(start_refs):
                acc[places] = ref[inside]
        else:
            for place in range(high - low + 1):
                acc[place] = jnp.zeros((height, PTS), jnp.float32)

        spare = high - low
        unroll = 4

        def several(begin, end, transposed):
            def body(step, carry):
                done = []
                for lane in range(unroll):
                    index = begin + step * unroll + lane
                    valid = index < end
                    index = jnp.minimum(index, end - 1)
                    vec = u_win[source_ref[index] - source_low]
                    tile = kept[tile_ref[index]]
                    if transposed:
                        value = lax.dot_general(
                            vec,
                            tile,
                            (((1,), (1,)), ((), ())),
                            preferred_element_type=jnp.float32,
                        )
                    else:
                        value = jnp.dot(vec, tile, preferred_element_type=jnp.float32)
                    done.append((jnp.where(valid, target_ref[index] - low, spare), fold(value)))
                for target, value in done:
                    acc[target] += value
                return carry

            lax.fori_loop(0, lax.div(end - begin + unroll - 1, unroll), body, 0)

        for kind in kinds:
            several(bounds[2 * kind], bounds[2 * kind + 1], True)
            several(bounds[2 * kind + 1], bounds[2 * kind + 2], False)
        for out, inside, places in pieces(outs):
            out[inside] = acc[places]

    return pl.pallas_call(
        kernel,
        out_shape=shapes,
        in_specs=[spec(SMEM)] * 4 + [spec(VMEM)] * (len(firsts) + 1 + len(begun)),
        out_specs=[spec(VMEM)] * len(shapes),
        scratch_shapes=[
            VMEM((source_high - source_low, tall, PTS), jnp.bfloat16),
            VMEM((high - low + 1, height, PTS), jnp.float32),
        ],
        cost_estimate=cost(2**31 if kinds == (1,) else 2**20, 2**20),
        compiler_params=pltpu.CompilerParams(vmem_limit_bytes=10 * 2**20),
        name="products",
    )(*entries, *[vecs[first] for first in firsts], tiles, *begun)


def urgent_ranges(group, blocks_dev):
    messages = [
        [rel for rel in range(group) if rel & bit and rel % bit == 0] for bit in bits_of(group)
    ]
    return [
        [(rel * blocks_dev, (rel + 1) * blocks_dev) for rel in rels]
        for rels in messages + [[group]]
    ]


def send_urgent(results, later, group, blocks_dev):
    final = []
    *messages, far = results
    parts = {}
    behind = None
    for bit, message in zip(bits_of(group), messages):
        rels = [rel for rel in range(group) if rel & bit and rel % bit == 0]
        for index, rel in enumerate(rels):
            if rel in parts:
                held = message[index * blocks_dev : (index + 1) * blocks_dev]
                message = held + parts[rel] if len(rels) == 1 else message.at[
                    index * blocks_dev : (index + 1) * blocks_dev
                ].add(parts[rel])
        if bit > 1:
            message, *later = lax.optimization_barrier((message, *later))
        got = swap(message, "grp", bit)
        if behind is None:
            got, far = lax.optimization_barrier((got, far))
            behind = from_behind(far, "blk", 1)
        final.append(got)
        for index, rel in enumerate(rels):
            if rel ^ bit:
                piece = got[index * blocks_dev : (index + 1) * blocks_dev]
                parts[rel ^ bit] = parts[rel ^ bit] + piece if rel ^ bit in parts else piece
    if behind is None:
        behind = from_behind(far, "blk", 1)
    return [behind] + final, later


def finish_home(entries, vecs, tiles, start, blocks_dev, height, folds):
    return list(
        products(entries, (2,), vecs, tiles, [start], [[(0, blocks_dev)]], height, folds)
    )


def scaled_gram(parts, own, counts, degree, inverse, split):
    columns = own.shape[0] if degree is not None else own.shape[0] - EXTRA
    total = own.shape[1]
    first = degree is None
    shapes = [
        jax.ShapeDtypeStruct((columns, total), jnp.float32),
        jax.ShapeDtypeStruct((columns, columns), jnp.float32),
    ]
    if split:
        shapes.append(jax.ShapeDtypeStruct((2 * columns, total), jnp.bfloat16))
    if first:
        shapes.append(jax.ShapeDtypeStruct((8, total), jnp.float32))
    operands = list(parts) + [own]
    operands += [] if first else [degree]
    operands += [] if inverse is None else [inverse]

    def kernel(count_ref, *refs):
        ins = list(refs[: len(operands)])
        outs = list(refs[len(operands) :])
        part_refs = ins[: len(parts)]
        own_ref = ins[len(parts)]
        z_out, gram_out = outs[:2]
        gram = jnp.zeros((columns, columns), jnp.float32)
        for block in range(total // PTS):
            lanes = slice(block * PTS, (block + 1) * PTS)
            sums = part_refs[0][block]
            for part in part_refs[1:]:
                sums = sums + part[block]
            if first:
                level = 1.0 + sums[columns : columns + 1, :]
                outs[-1][:, lanes] = jnp.broadcast_to(level, (8, PTS))
            else:
                level = ins[len(parts) + 1][0:1, lanes]
            used = lax.broadcasted_iota(jnp.int32, (columns, PTS), 1) < count_ref[block]
            held = own_ref[0:columns, lanes].astype(jnp.float32)
            z = (held + jnp.where(used, sums[0:columns], 0.0)) / level
            if inverse is not None:
                z = jnp.dot(
                    ins[-1][...], z, precision=HIGHEST, preferred_element_type=jnp.float32
                )
            z_out[:, lanes] = z
            if split:
                high = z.astype(jnp.bfloat16)
                outs[2][0:columns, lanes] = high
                rest = z - high.astype(jnp.float32)
                outs[2][columns : 2 * columns, lanes] = rest.astype(jnp.bfloat16)
            gram = gram + lax.dot_general(
                z, z, (((1,), (1,)), ((), ())), precision=HIGHEST, preferred_element_type=jnp.float32
            )
        gram_out[...] = gram

    return pl.pallas_call(
        kernel,
        out_shape=tuple(shapes),
        in_specs=[spec(SMEM)] + [spec(VMEM)] * len(operands),
        out_specs=(spec(VMEM),) * len(shapes),
        cost_estimate=cost(2**26, 2**21),
        compiler_params=pltpu.CompilerParams(vmem_limit_bytes=6 * 2**20),
        name="scaled_gram",
    )(counts, *operands)


def inverse_factor(gram):
    size = gram.shape[0]
    row_id = lax.broadcasted_iota(jnp.int32, (size, size), 0)
    col_id = lax.broadcasted_iota(jnp.int32, (size, size), 1)
    eye = jnp.where(row_id == col_id, 1.0, 0.0)
    whole = jnp.concatenate([gram, eye], axis=1)
    wide = 2 * size
    count = size // 8
    groups = [whole[8 * g : 8 * g + 8, :] for g in range(count)]
    within = lax.broadcasted_iota(jnp.int32, (8, wide), 0)

    def spread_row(value, row):
        return jnp.broadcast_to(value[row : row + 1, :], (8, wide))

    results = []
    for g in range(count):
        spread = [
            [
                jnp.broadcast_to(groups[other][:, 8 * g + k : 8 * g + k + 1], (8, wide))
                for other in range(g, count)
            ]
            for k in range(8)
        ]
        pivots = jnp.ones((8, wide), jnp.float32)
        for j in range(8):
            column = spread[j]
            pivot = spread_row(column[0], j)
            pivots = jnp.where(within == j, pivot, pivots)
            over = 1.0 / pivot
            below = jnp.where(within > j, column[0], 0.0)
            for k in range(j + 1, 8):
                share = spread_row(column[0], k) * over
                spread[k][0] = spread[k][0] - below * share
                for other in range(1, count - g):
                    spread[k][other] = spread[k][other] - column[other] * share
            top = spread_row(groups[g], j) * over
            groups[g] = groups[g] - below * top
            for other in range(1, count - g):
                groups[g + other] = groups[g + other] - column[other] * top
        results.append(groups[g] * lax.rsqrt(pivots))
    return jnp.concatenate(results, axis=0)[:, size:wide]


def factor_kernel(gram, out):
    out[...] = inverse_factor(gram[...])


def factor(gram):
    return pl.pallas_call(
        factor_kernel,
        out_shape=jax.ShapeDtypeStruct(gram.shape, jnp.float32),
        in_specs=[spec(VMEM)],
        out_specs=spec(VMEM),
        cost_estimate=cost(2**16, 2**16),
        compiler_params=pltpu.CompilerParams(vmem_limit_bytes=2 * 2**20),
        name="factor",
    )(gram)


def embed_kernel(gram, z, out):
    out[...] = jnp.dot(
        inverse_factor(gram[...]), z[...], precision=HIGHEST, preferred_element_type=jnp.float32
    )


def embedding(gram, z):
    return pl.pallas_call(
        embed_kernel,
        out_shape=jax.ShapeDtypeStruct(z.shape, jnp.float32),
        in_specs=[spec(VMEM)] * 2,
        out_specs=spec(VMEM),
        cost_estimate=cost(2**30, 2**20),
        compiler_params=pltpu.CompilerParams(vmem_limit_bytes=4 * 2**20),
        name="embedding",
    )(gram, z)


def sum_stages():
    return bits_of(lax.axis_size("blk") * lax.axis_size("grp"))


def sum_over(value, axis):
    count = lax.axis_size(axis)
    copies = jnp.broadcast_to(value[None], (count,) + value.shape)
    return jnp.sum(lax.all_to_all(copies, axis, 0, 0, tiled=True), axis=0)


def pairs_of(bits):
    return [bits[first : first + 2] for first in range(0, len(bits), 2)]


def all_sum(value, stages, beside=None):
    count = lax.axis_size("blk") * lax.axis_size("grp")
    for bits in stages:
        moves = [0]
        for bit in bits if isinstance(bits, list) else [bits]:
            moves += [move ^ bit for move in moves]
        terms = [value] + [
            lax.ppermute(value, ("blk", "grp"), [(source, source ^ move) for source in range(count)])
            for move in moves[1:]
        ]
        if beside is not None:
            terms[0], beside = lax.optimization_barrier((terms[0], beside))
        while len(terms) > 1:
            terms = [left + right for left, right in zip(terms[::2], terms[1::2])]
        value = terms[0]
    return value if beside is None else (value, beside)


def per_device(points, counts, pair_rows, pair_cols, pair_live, start):
    group = lax.axis_size("grp")
    blocks_dev = counts.shape[0]
    columns = start.shape[0]
    slots = pair_rows.shape[0]
    cap = max(-(-slots // group), blocks_dev * blocks_dev * group)
    half = (blocks_dev // 2) * PTS

    home = min(2, group) * blocks_dev

    rows, cols, n, *entries = listing(
        pair_rows, pair_cols, pair_live, group, cap, blocks_dev
    )
    mate = swap(points, "grp", 1)
    chunks = [points[:half], points[half:]]
    far = [from_behind(chunk, "blk", -1) for chunk in chunks]
    crossed = [gather_far_bits(chunk) for chunk in chunks]
    begin, mate = lax.optimization_barrier((start, mate))
    vec = opening(begin, counts)
    tied = lax.optimization_barrier((vec, n, rows, cols, far[0], *crossed[0].values()))
    vec, n, rows, cols, far[0] = tied[:5]
    crossed[0] = dict(zip(crossed[0], tied[5:]))
    cross_vec = gather_far_bits(vec)
    far_vec = from_behind(vec, "blk", -1)
    mate_vec = swap(vec, "grp", 1)

    def direct(index):
        offset = index * (blocks_dev // 2)
        found = {group * blocks_dev + offset: far[index]}
        for rel, value in crossed[index].items():
            found[rel * blocks_dev + offset] = value
        return found

    def passed_on(index):
        offset = index * (blocks_dev // 2)
        found = {}
        for rel, value in crossed[index].items():
            cut = value.shape[0] // (1 if index else 2)
            parts = [swap(value[at : at + cut], "grp", 1) for at in range(0, value.shape[0], cut)]
            found[(rel ^ 1) * blocks_dev + offset] = jnp.concatenate(parts, 0)
        return found

    def build(stage, fresh, state, name):
        return list(
            build_tiles(stage, fresh, n, rows, cols, state, group, blocks_dev, cap, name)
        )

    state = build(0, {0: points, blocks_dev: mate, **direct(0)}, (), "first_tiles")
    state = build(1, passed_on(0), state, "second_tiles")
    tied = lax.optimization_barrier((far[1], mate_vec, state[1], *crossed[1].values()))
    far[1], mate_vec, state[1] = tied[:3]
    crossed[1] = dict(zip(crossed[1], tied[3:]))
    last = passed_on(1)
    *grown, kept = state
    state = build(None, direct(1), grown, "more_blocks") + [kept]
    state = build(2, last, state, "last_tiles")
    kept = state[-1]
    tied = lax.optimization_barrier((kept, *cross_vec.values()))
    kept = tied[0]
    cross_vec = dict(zip(cross_vec, tied[1:]))

    def window_of(own, mate, crossed, far):
        found = {0: own, blocks_dev: mate, group * blocks_dev: far}
        for rel, value in crossed.items():
            found[rel * blocks_dev] = value
            found[(rel ^ 1) * blocks_dev] = swap(value, "grp", 1)
        return found

    def beyond(vecs):
        return {place: value for place, value in vecs.items() if place >= home}

    vecs = window_of(vec, mate_vec, cross_vec, far_vec)
    urgent = urgent_ranges(group, blocks_dev)
    height = columns + 8
    at_home, *results = products(
        entries,
        (0,),
        {0: vec, blocks_dev: mate_vec},
        kept,
        (),
        [[(0, blocks_dev)]] + urgent,
        height,
        1,
    )
    results = products(entries, (1,), beyond(vecs), kept, results, urgent, height, 1)
    sums, (at_home,) = send_urgent(results, (at_home,), group, blocks_dev)
    sums = finish_home(entries, beyond(vecs), kept, at_home, blocks_dev, height, 1) + sums
    z, gram, parts, degree = scaled_gram(sums, vec, counts, None, None, True)
    for turn in range(1, ITERS):
        stages = sum_stages()
        far_part = from_behind(parts, "blk", -1)
        crossed = gather_far_bits(parts)
        mate_part = swap(parts, "grp", 1)
        gram = all_sum(gram, stages[:1])
        at_home, *results = products(
            entries,
            (0,),
            {0: parts, blocks_dev: mate_part},
            kept,
            (),
            [[(0, blocks_dev)]] + urgent,
            columns,
            2,
        )
        gram, at_home, *tied = lax.optimization_barrier((gram, at_home, *crossed.values()))
        crossed = dict(zip(crossed, tied))
        vecs = beyond(window_of(parts, mate_part, crossed, far_part))
        gram = all_sum(gram, stages[1:2])
        gram, *tied = lax.optimization_barrier((gram, *vecs.values()))
        vecs = dict(zip(vecs, tied))
        results = products(entries, (1,), vecs, kept, results, urgent, columns, 2)
        gram = all_sum(gram, stages[2:3])
        gram, *results = lax.optimization_barrier((gram, *results))
        gram = all_sum(gram, stages[3:4])
        sums, (at_home, gram) = send_urgent(results, (at_home, gram), group, blocks_dev)
        gram = all_sum(gram, stages[4:-1])
        own = finish_home(entries, vecs, kept, at_home, blocks_dev, columns, 2)
        gram, own[0] = all_sum(gram, stages[4:][-1:], own[0])
        sums = own + sums
        inverse = factor(gram)
        z, gram, *parts = scaled_gram(sums, z, counts, degree, inverse, turn + 1 < ITERS)
        parts = parts[0] if parts else None
    half = columns // 2
    gram = jnp.concatenate([gram[:half], gram[half:]], axis=1)
    gram = sum_over(sum_over(gram, "grp"), "blk")
    return embedding(jnp.concatenate([gram[:, :columns], gram[:, columns:]], axis=0), z)


def solution(mesh):
    in_specs = (
        P(("blk", "grp"), None),
        P(("blk", "grp")),
        P("blk"),
        P("blk"),
        P("blk"),
        P(None, ("blk", "grp")),
    )
    out_specs = P(None, ("blk", "grp"))
    return jax.shard_map(
        per_device, mesh=mesh, in_specs=in_specs, out_specs=out_specs, check_vma=False
    )
```

```python
import functools

import jax
import jax.numpy as jnp
from jax import lax
from jax.experimental import pallas as pl
from jax.experimental.pallas import tpu as pltpu
from jax.sharding import PartitionSpec as P

PTS = 512
ITERS = 2
LOG2E = 1.4426950408889634
DEAD = 65536.0
EXTRA = 16
VMEM = pltpu.VMEM
SMEM = pltpu.SMEM
HIGHEST = lax.Precision.HIGHEST


def cost(flops, moved):
    return pl.CostEstimate(flops=int(flops), bytes_accessed=int(moved), transcendentals=0)


def spec(space):
    return pl.BlockSpec(memory_space=space)


def swap(value, axis, bit):
    count = lax.axis_size(axis)
    return lax.ppermute(value, axis, [(source, source ^ bit) for source in range(count)])


def from_behind(value, axis, steps):
    count = lax.axis_size(axis)
    initial, last = (max(0, -steps), min(count, count - steps))
    return lax.ppermute(value, axis, [(source, source + steps) for source in range(initial, last)])


def bits_of(count):
    bits = []
    bit = 1
    while bit < count:
        bits.append(bit)
        bit *= 2
    return bits


def gather_near(value, axis):
    held = {0: value}
    for bit in reversed(bits_of(lax.axis_size(axis))):
        for rel in list(held):
            held[rel ^ bit] = swap(held[rel], axis, bit)
    return [held[rel] for rel in range(len(held))]


def gather_far_bits(value):
    held = {0: value}
    for bit in reversed(bits_of(lax.axis_size("grp"))[1:]):
        for rel in list(held):
            held[rel ^ bit] = swap(held[rel], "grp", bit)
    held.pop(0)
    return held


def opening_kernel(start, counts, out):
    columns, total = start.shape
    for block in range(total // PTS):
        lanes = slice(block * PTS, (block + 1) * PTS)
        used = lax.broadcasted_iota(jnp.int32, (columns, PTS), 1) < counts[block]
        out[0:columns, lanes] = jnp.where(used, start[:, lanes], 0.0).astype(jnp.bfloat16)
        which = lax.broadcasted_iota(jnp.int32, (EXTRA, PTS), 0)
        place_in = lax.broadcasted_iota(jnp.int32, (EXTRA, PTS), 1)
        ones = jnp.logical_and(which == 0, place_in < counts[block])
        out[columns : columns + EXTRA, lanes] = jnp.where(ones, 1.0, 0.0).astype(jnp.bfloat16)


def opening(start, counts):
    columns, total = start.shape
    return pl.pallas_call(
        opening_kernel,
        out_shape=jax.ShapeDtypeStruct((columns + EXTRA, total), jnp.bfloat16),
        in_specs=[spec(VMEM), spec(SMEM)],
        out_specs=spec(VMEM),
        cost_estimate=cost(2**20, 2**19),
        compiler_params=pltpu.CompilerParams(vmem_limit_bytes=2 * 2**20),
        name="opening",
    )(start, counts)


def stage_of(place, group, blocks_dev):
    piece = lax.div(place, blocks_dev)
    first_half = lax.rem(place, blocks_dev) < blocks_dev // 2
    later = jnp.where(first_half, jnp.where(lax.rem(piece, 2) == 0, 0, 1), 2)
    return jnp.where(piece < min(2, group), 0, later)


def listing_kernel(
    group,
    cap,
    blocks_dev,
    rows,
    cols,
    live,
    out_rows,
    out_cols,
    out_n,
    tiles,
    sources,
    targets,
    bounds,
    owners,
):
    slab = blocks_dev * group
    slots = rows.shape[0]
    member = lax.axis_index("grp")

    def local_near(block, device):
        return (lax.div(block, blocks_dev) ^ device) * blocks_dev + lax.rem(block, blocks_dev)

    def local_far(block):
        return slab + lax.rem(block - slab, blocks_dev)

    def count_far(slot, carry):
        col = cols[slot]
        far = jnp.logical_and(slot < live[0], col >= slab)
        owner = lax.div(col - slab, blocks_dev)
        owners[slot] = jnp.where(far, owner, -1)
        return tuple(
            old + jnp.where(jnp.logical_and(far, owner == device), 1, 0)
            for device, old in enumerate(carry)
        )

    loads = lax.fori_loop(0, slots, count_far, (jnp.int32(0),) * group)

    def give(slot, loads):
        row, col = rows[slot], cols[slot]
        near = jnp.logical_and(slot < live[0], col < slab)
        best = jnp.int32(2**30)
        owner = jnp.int32(0)
        for device in range(group):
            stage = jnp.maximum(
                stage_of(local_near(row, device), group, blocks_dev),
                stage_of(local_near(col, device), group, blocks_dev),
            )
            score = loads[device] + 64 * stage + jnp.where(loads[device] < cap, 0, 2**20)
            owner = jnp.where(score < best, device, owner)
            best = jnp.minimum(score, best)

        @pl.when(near)
        def _():
            owners[slot] = owner

        return tuple(
            load + jnp.where(jnp.logical_and(near, owner == device), 1, 0)
            for device, load in enumerate(loads)
        )

    lax.fori_loop(0, slots, give, loads)

    def place_those(wanted, filled):
        def place(slot, filled):
            row, col = rows[slot], cols[slot]
            row_place = local_near(row, member)
            col_place = jnp.where(col >= slab, local_far(col), local_near(col, member))
            stage = jnp.maximum(
                stage_of(row_place, group, blocks_dev), stage_of(col_place, group, blocks_dev)
            )
            mine = jnp.logical_and(owners[slot] == member, stage == wanted)

            @pl.when(mine)
            def _():
                out_rows[filled] = row_place
                out_cols[filled] = col_place

            return filled + jnp.where(mine, 1, 0)

        return lax.fori_loop(0, slots, place, filled)

    count = jnp.int32(0)
    out_n[0] = count
    for wanted in range(3):
        count = place_those(wanted, count)
        out_n[wanted + 1] = count

    home = min(2, group) * blocks_dev
    bounds[0] = jnp.int32(0)
    filled = jnp.int32(0)
    for kind in range(3):
        for to_row in (True, False):

            def enter(index, filled):
                source = (out_cols if to_row else out_rows)[index]
                target = (out_rows if to_row else out_cols)[index]
                if kind == 0:
                    wanted = source < home
                elif kind == 1:
                    wanted = jnp.logical_and(source >= home, target >= blocks_dev)
                else:
                    wanted = jnp.logical_and(source >= home, target < blocks_dev)

                @pl.when(wanted)
                def _():
                    tiles[filled] = index
                    sources[filled] = source
                    targets[filled] = target

                return filled + jnp.where(wanted, 1, 0)

            filled = lax.fori_loop(0, count, enter, filled)
            bounds[2 * kind + (1 if to_row else 2)] = filled


def listing(rows, cols, live, group, cap, blocks_dev):
    return pl.pallas_call(
        functools.partial(listing_kernel, group, cap, blocks_dev),
        out_shape=(
            jax.ShapeDtypeStruct((cap,), jnp.int32),
            jax.ShapeDtypeStruct((cap,), jnp.int32),
            jax.ShapeDtypeStruct((4,), jnp.int32),
            jax.ShapeDtypeStruct((2 * cap,), jnp.int32),
            jax.ShapeDtypeStruct((2 * cap,), jnp.int32),
            jax.ShapeDtypeStruct((2 * cap,), jnp.int32),
            jax.ShapeDtypeStruct((7,), jnp.int32),
        ),
        in_specs=[spec(SMEM)] * 3,
        out_specs=(spec(SMEM),) * 7,
        scratch_shapes=[SMEM((rows.shape[0],), jnp.int32)],
        cost_estimate=cost(2**20, 2**10),
        compiler_params=pltpu.CompilerParams(vmem_limit_bytes=2**20),
        name="listing",
    )(rows, cols, live)


def set_levels(place, window, level_row, level_col, scale):
    block = window[place * PTS : (place + 1) * PTS, :]
    width = block.shape[1]
    part = jnp.zeros((PTS, 128), jnp.float32)
    for lane in range(0, width, 128):
        wide = block[:, lane : lane + 128].astype(jnp.float32)
        part = part + wide * wide
    level_row[place] = scale * lax.dot_general(
        jnp.ones((8, 128), jnp.float32),
        part,
        (((1,), (1,)), ((), ())),
        precision=HIGHEST,
        preferred_element_type=jnp.float32,
    )
    if place < level_col.shape[0]:
        total = jnp.sum(part, axis=1, keepdims=True) * scale
        level_col[place] = jnp.broadcast_to(total, (PTS, 128))


def make_tiles(low, high, rows, cols, window, level_row, level_col, kept, buffers):
    width = window.shape[1]
    scale = 6.0 / width * LOG2E
    count = high - low
    spare = kept.shape[0] - 1

    def cross(tile, buffer):
        index = low + jnp.minimum(tile, count - 1)
        left = window[pl.ds(pl.multiple_of(rows[index] * PTS, PTS), PTS), :]
        right = window[pl.ds(pl.multiple_of(cols[index] * PTS, PTS), PTS), :]
        buffer[...] = lax.dot_general(
            left, right, (((1,), (1,)), ((), ())), preferred_element_type=jnp.float32
        )

    def finish(tile, buffer):
        valid = jnp.logical_and(tile >= 0, tile < count)
        index = low + jnp.clip(tile, 0, count - 1)
        row, col = rows[index], cols[index]
        right_level = level_row[col][0:1, :]
        left_level = jnp.concatenate([level_col[row]] * (PTS // 128), axis=1)
        value = jnp.exp2(buffer[...] * scale - left_level - right_level)
        kept[jnp.where(valid, index, spare)] = value.astype(jnp.bfloat16)

    def body(pair, carry):
        cross(2 * pair, buffers[0])
        finish(2 * pair - 1, buffers[1])
        cross(2 * pair + 1, buffers[1])
        finish(2 * pair, buffers[0])
        return carry

    @pl.when(count > 0)
    def _():
        buffers[1][...] = jnp.zeros((PTS, PTS), jnp.float32)

    lax.fori_loop(0, jnp.where(count > 0, lax.div(count, 2) + 1, 0), body, 0)


def build_tiles(stage, fresh, n, rows, cols, state, group, blocks_dev, cap, name):
    places = list(fresh)
    pts = list(fresh.values())
    width = pts[0].shape[1]
    total = (group + 1) * blocks_dev
    near = group * blocks_dev
    shapes = [
        jax.ShapeDtypeStruct((total * PTS, width), jnp.bfloat16),
        jax.ShapeDtypeStruct((total, 8, PTS), jnp.float32),
        jax.ShapeDtypeStruct((near, PTS, 128), jnp.float32),
    ]
    makes = stage is not None
    if makes:
        shapes.append(jax.ShapeDtypeStruct((cap + 1, PTS, PTS), jnp.bfloat16))
    state = state[: len(shapes)]
    scalars = (n, rows, cols) if makes else ()
    first = len(scalars) + len(pts)

    def kernel(*refs):
        pt_refs = refs[len(scalars) : first]
        window, level_row, level_col, *rest = refs[first + len(state) :]
        for place, piece in zip(places, pt_refs):
            blocks = piece.shape[0] // PTS
            window[place * PTS : (place + blocks) * PTS, :] = piece[...]
            for block in range(place, place + blocks):
                set_levels(block, window, level_row, level_col, 3.0 / width * LOG2E)
        if makes:
            n_ref, row_ref, col_ref = refs[:3]
            kept, *buffers = rest
            make_tiles(
                n_ref[stage],
                n_ref[stage + 1],
                row_ref,
                col_ref,
                window,
                level_row,
                level_col,
                kept,
                buffers,
            )

    return pl.pallas_call(
        kernel,
        out_shape=shapes,
        in_specs=[spec(SMEM)] * len(scalars) + [spec(VMEM)] * (len(pts) + len(state)),
        out_specs=[spec(VMEM)] * len(shapes),
        input_output_aliases={first + index: index for index in range(len(state))},
        scratch_shapes=[VMEM((PTS, PTS), jnp.float32)] * (2 if makes else 0),
        cost_estimate=cost(2**32 if stage == 2 else 2**20, 2**20),
        compiler_params=pltpu.CompilerParams(vmem_limit_bytes=6 * 2**20),
        name=name,
    )(*scalars, *pts, *state)


def products(entries, kinds, vecs, tiles, start, targets, height, folds):
    firsts = sorted(vecs)
    tall, held = vecs[firsts[0]].shape
    blocks_dev = held // PTS
    begun = list(start)
    source_low, source_high = firsts[0], firsts[-1] + blocks_dev
    low = min(first for ranges in targets for first, _ in ranges)
    high = max(last for ranges in targets for _, last in ranges)
    shapes = [
        jax.ShapeDtypeStruct((sum(last - first for first, last in ranges), height, PTS), jnp.float32)
        for ranges in targets
    ]

    def pieces(refs):
        for ranges, ref in zip(targets, refs):
            at = 0
            for first, last in ranges:
                yield ref, slice(at, at + last - first), slice(first - low, last - low)
                at += last - first

    def fold(value):
        out = value[:height]
        for index in range(1, folds):
            out = out + value[index * height : (index + 1) * height]
        return out

    def kernel(*refs):
        tile_ref, source_ref, target_ref, bounds = refs[:4]
        vec_refs = refs[4 : 4 + len(firsts)]
        kept = refs[4 + len(firsts)]
        start_refs = refs[5 + len(firsts) : 5 + len(firsts) + len(begun)]
        outs = refs[5 + len(firsts) + len(begun) : -2]
        u_win, acc = refs[-2:]
        for first, ref in zip(firsts, vec_refs):
            for block in range(blocks_dev):
                lanes = slice(block * PTS, (block + 1) * PTS)
                u_win[first - source_low + block] = ref[:, lanes]
        if begun:
            for ref, inside, places in pieces(start_refs):
                acc[places] = ref[inside]
        else:
            for place in range(high - low + 1):
                acc[place] = jnp.zeros((height, PTS), jnp.float32)

        spare = high - low
        unroll = 4

        def several(begin, end, transposed):
            def body(step, carry):
                done = []
                for lane in range(unroll):
                    index = begin + step * unroll + lane
                    valid = index < end
                    index = jnp.minimum(index, end - 1)
                    vec = u_win[source_ref[index] - source_low]
                    tile = kept[tile_ref[index]]
                    if transposed:
                        value = lax.dot_general(
                            vec,
                            tile,
                            (((1,), (1,)), ((), ())),
                            preferred_element_type=jnp.float32,
                        )
                    else:
                        value = jnp.dot(vec, tile, preferred_element_type=jnp.float32)
                    done.append((jnp.where(valid, target_ref[index] - low, spare), fold(value)))
                for target, value in done:
                    acc[target] += value
                return carry

            lax.fori_loop(0, lax.div(end - begin + unroll - 1, unroll), body, 0)

        for kind in kinds:
            several(bounds[2 * kind], bounds[2 * kind + 1], True)
            several(bounds[2 * kind + 1], bounds[2 * kind + 2], False)
        for out, inside, places in pieces(outs):
            out[inside] = acc[places]

    return pl.pallas_call(
        kernel,
        out_shape=shapes,
        in_specs=[spec(SMEM)] * 4 + [spec(VMEM)] * (len(firsts) + 1 + len(begun)),
        out_specs=[spec(VMEM)] * len(shapes),
        scratch_shapes=[
            VMEM((source_high - source_low, tall, PTS), jnp.bfloat16),
            VMEM((high - low + 1, height, PTS), jnp.float32),
        ],
        cost_estimate=cost(2**31 if kinds == (1,) else 2**20, 2**20),
        compiler_params=pltpu.CompilerParams(vmem_limit_bytes=10 * 2**20),
        name="products",
    )(*entries, *[vecs[first] for first in firsts], tiles, *begun)


def urgent_ranges(group, blocks_dev):
    messages = [
        [rel for rel in range(group) if rel & bit and rel % bit == 0] for bit in bits_of(group)
    ]
    return [
        [(rel * blocks_dev, (rel + 1) * blocks_dev) for rel in rels]
        for rels in messages + [[group]]
    ]


def send_urgent(results, later, group, blocks_dev):
    final = []
    *messages, far = results
    parts = {}
    behind = None
    for bit, message in zip(bits_of(group), messages):
        rels = [rel for rel in range(group) if rel & bit and rel % bit == 0]
        for index, rel in enumerate(rels):
            if rel in parts:
                held = message[index * blocks_dev : (index + 1) * blocks_dev]
                message = held + parts[rel] if len(rels) == 1 else message.at[
                    index * blocks_dev : (index + 1) * blocks_dev
                ].add(parts[rel])
        if bit > 1:
            message, *later = lax.optimization_barrier((message, *later))
        got = swap(message, "grp", bit)
        if behind is None:
            got, far = lax.optimization_barrier((got, far))
            behind = from_behind(far, "blk", 1)
        final.append(got)
        for index, rel in enumerate(rels):
            if rel ^ bit:
                piece = got[index * blocks_dev : (index + 1) * blocks_dev]
                parts[rel ^ bit] = parts[rel ^ bit] + piece if rel ^ bit in parts else piece
    if behind is None:
        behind = from_behind(far, "blk", 1)
    return [behind] + final, later


def finish_home(entries, vecs, tiles, start, blocks_dev, height, folds):
    return list(
        products(entries, (2,), vecs, tiles, [start], [[(0, blocks_dev)]], height, folds)
    )


def scaled_gram(parts, own, counts, degree, inverse, split):
    columns = own.shape[0] if degree is not None else own.shape[0] - EXTRA
    total = own.shape[1]
    first = degree is None
    shapes = [
        jax.ShapeDtypeStruct((columns, total), jnp.float32),
        jax.ShapeDtypeStruct((columns, columns), jnp.float32),
    ]
    if split:
        shapes.append(jax.ShapeDtypeStruct((2 * columns, total), jnp.bfloat16))
    if first:
        shapes.append(jax.ShapeDtypeStruct((8, total), jnp.float32))
    operands = list(parts) + [own]
    operands += [] if first else [degree]
    operands += [] if inverse is None else [inverse]

    def kernel(count_ref, *refs):
        ins = list(refs[: len(operands)])
        outs = list(refs[len(operands) :])
        part_refs = ins[: len(parts)]
        own_ref = ins[len(parts)]
        z_out, gram_out = outs[:2]
        gram = jnp.zeros((columns, columns), jnp.float32)
        for block in range(total // PTS):
            lanes = slice(block * PTS, (block + 1) * PTS)
            sums = part_refs[0][block]
            for part in part_refs[1:]:
                sums = sums + part[block]
            if first:
                level = 1.0 + sums[columns : columns + 1, :]
                outs[-1][:, lanes] = jnp.broadcast_to(level, (8, PTS))
            else:
                level = ins[len(parts) + 1][0:1, lanes]
            used = lax.broadcasted_iota(jnp.int32, (columns, PTS), 1) < count_ref[block]
            held = own_ref[0:columns, lanes].astype(jnp.float32)
            z = (held + jnp.where(used, sums[0:columns], 0.0)) / level
            if inverse is not None:
                z = jnp.dot(
                    ins[-1][...], z, precision=HIGHEST, preferred_element_type=jnp.float32
                )
            z_out[:, lanes] = z
            if split:
                high = z.astype(jnp.bfloat16)
                outs[2][0:columns, lanes] = high
                rest = z - high.astype(jnp.float32)
                outs[2][columns : 2 * columns, lanes] = rest.astype(jnp.bfloat16)
            gram = gram + lax.dot_general(
                z, z, (((1,), (1,)), ((), ())), precision=HIGHEST, preferred_element_type=jnp.float32
            )
        gram_out[...] = gram

    return pl.pallas_call(
        kernel,
        out_shape=tuple(shapes),
        in_specs=[spec(SMEM)] + [spec(VMEM)] * len(operands),
        out_specs=(spec(VMEM),) * len(shapes),
        cost_estimate=cost(2**26, 2**21),
        compiler_params=pltpu.CompilerParams(vmem_limit_bytes=6 * 2**20),
        name="scaled_gram",
    )(counts, *operands)


def inverse_factor(gram):
    size = gram.shape[0]
    row_id = lax.broadcasted_iota(jnp.int32, (size, size), 0)
    col_id = lax.broadcasted_iota(jnp.int32, (size, size), 1)
    eye = jnp.where(row_id == col_id, 1.0, 0.0)
    whole = jnp.concatenate([gram, eye], axis=1)
    wide = 2 * size
    count = size // 8
    groups = [whole[8 * g : 8 * g + 8, :] for g in range(count)]
    within = lax.broadcasted_iota(jnp.int32, (8, wide), 0)

    def spread_row(value, row):
        return jnp.broadcast_to(value[row : row + 1, :], (8, wide))

    results = []
    for g in range(count):
        spread = [
            [
                jnp.broadcast_to(groups[other][:, 8 * g + k : 8 * g + k + 1], (8, wide))
                for other in range(g, count)
            ]
            for k in range(8)
        ]
        pivots = jnp.ones((8, wide), jnp.float32)
        for j in range(8):
            column = spread[j]
            pivot = spread_row(column[0], j)
            pivots = jnp.where(within == j, pivot, pivots)
            over = 1.0 / pivot
            below = jnp.where(within > j, column[0], 0.0)
            for k in range(j + 1, 8):
                share = spread_row(column[0], k) * over
                spread[k][0] = spread[k][0] - below * share
                for other in range(1, count - g):
                    spread[k][other] = spread[k][other] - column[other] * share
            top = spread_row(groups[g], j) * over
            groups[g] = groups[g] - below * top
            for other in range(1, count - g):
                groups[g + other] = groups[g + other] - column[other] * top
        results.append(groups[g] * lax.rsqrt(pivots))
    return jnp.concatenate(results, axis=0)[:, size:wide]


def factor_kernel(gram, out):
    out[...] = inverse_factor(gram[...])


def factor(gram):
    return pl.pallas_call(
        factor_kernel,
        out_shape=jax.ShapeDtypeStruct(gram.shape, jnp.float32),
        in_specs=[spec(VMEM)],
        out_specs=spec(VMEM),
        cost_estimate=cost(2**16, 2**16),
        compiler_params=pltpu.CompilerParams(vmem_limit_bytes=2 * 2**20),
        name="factor",
    )(gram)


def embed_kernel(gram, z, out):
    out[...] = jnp.dot(
        inverse_factor(gram[...]), z[...], precision=HIGHEST, preferred_element_type=jnp.float32
    )


def embedding(gram, z):
    return pl.pallas_call(
        embed_kernel,
        out_shape=jax.ShapeDtypeStruct(z.shape, jnp.float32),
        in_specs=[spec(VMEM)] * 2,
        out_specs=spec(VMEM),
        cost_estimate=cost(2**30, 2**20),
        compiler_params=pltpu.CompilerParams(vmem_limit_bytes=4 * 2**20),
        name="embedding",
    )(gram, z)


def sum_stages():
    return bits_of(lax.axis_size("blk") * lax.axis_size("grp"))


def all_sum_split(value):
    axes = ("blk", "grp")
    count = lax.axis_size("blk") * lax.axis_size("grp")
    index = lax.axis_index("blk") * lax.axis_size("grp") + lax.axis_index("grp")
    odd = lax.rem(index, 2) == 1

    def move(value, even_by, odd_by):
        steps = [odd_by if source % 2 else even_by for source in range(count)]
        pairs = [(source, source ^ step) for source, step in enumerate(steps) if step]
        return lax.ppermute(value, axes, pairs)

    bits = bits_of(count)
    value = value + move(value, 1, 1)
    bits = bits[1:]
    while len(bits) > 1:
        one, two, bits = bits[0], bits[1], bits[2:]
        near = move(value, one, two)
        far = move(value, 0, one ^ two)
        part = near + jnp.where(odd, far, value)
        value = part + move(part, 1, 1)
    for bit in bits:
        value = value + move(value, bit, bit)
    return value


def all_sum(value, stages, beside=None):
    count = lax.axis_size("blk") * lax.axis_size("grp")
    for bits in stages:
        moves = [0]
        for bit in bits if isinstance(bits, list) else [bits]:
            moves += [move ^ bit for move in moves]
        terms = [value] + [
            lax.ppermute(value, ("blk", "grp"), [(source, source ^ move) for source in range(count)])
            for move in moves[1:]
        ]
        if beside is not None:
            terms[0], beside = lax.optimization_barrier((terms[0], beside))
        while len(terms) > 1:
            terms = [left + right for left, right in zip(terms[::2], terms[1::2])]
        value = terms[0]
    return value if beside is None else (value, beside)


def per_device(points, counts, pair_rows, pair_cols, pair_live, start):
    group = lax.axis_size("grp")
    blocks_dev = counts.shape[0]
    columns = start.shape[0]
    slots = pair_rows.shape[0]
    cap = max(-(-slots // group), blocks_dev * blocks_dev * group)
    half = (blocks_dev // 2) * PTS

    home = min(2, group) * blocks_dev

    rows, cols, n, *entries = listing(
        pair_rows, pair_cols, pair_live, group, cap, blocks_dev
    )
    first = points[:half]
    rest, first = lax.optimization_barrier((points, first))
    mate = swap(rest, "grp", 1)
    chunks = [first, rest[half:]]
    far = [from_behind(chunk, "blk", -1) for chunk in chunks]
    crossed = [gather_far_bits(chunk) for chunk in chunks]
    begin, mate = lax.optimization_barrier((start, mate))
    vec = opening(begin, counts)
    tied = lax.optimization_barrier((vec, n, rows, cols, far[0], *crossed[0].values()))
    vec, n, rows, cols, far[0] = tied[:5]
    crossed[0] = dict(zip(crossed[0], tied[5:]))
    cross_vec = gather_far_bits(vec)
    far_vec = from_behind(vec, "blk", -1)
    mate_vec = swap(vec, "grp", 1)

    def direct(index):
        offset = index * (blocks_dev // 2)
        found = {group * blocks_dev + offset: far[index]}
        for rel, value in crossed[index].items():
            found[rel * blocks_dev + offset] = value
        return found

    def passed_on(index):
        offset = index * (blocks_dev // 2)
        found = {}
        for rel, value in crossed[index].items():
            cut = value.shape[0] // (1 if index else 2)
            parts = [swap(value[at : at + cut], "grp", 1) for at in range(0, value.shape[0], cut)]
            found[(rel ^ 1) * blocks_dev + offset] = jnp.concatenate(parts, 0)
        return found

    def build(stage, fresh, state, name):
        return list(
            build_tiles(stage, fresh, n, rows, cols, state, group, blocks_dev, cap, name)
        )

    state = build(0, {0: points, blocks_dev: mate, **direct(0)}, (), "first_tiles")
    state = build(1, passed_on(0), state, "second_tiles")
    tied = lax.optimization_barrier((far[1], mate_vec, state[1], *crossed[1].values()))
    far[1], mate_vec, state[1] = tied[:3]
    crossed[1] = dict(zip(crossed[1], tied[3:]))
    last = passed_on(1)
    *grown, kept = state
    state = build(None, direct(1), grown, "more_blocks") + [kept]
    state = build(2, last, state, "last_tiles")
    kept = state[-1]
    tied = lax.optimization_barrier((kept, *cross_vec.values()))
    kept = tied[0]
    cross_vec = dict(zip(cross_vec, tied[1:]))

    def window_of(own, mate, crossed, far):
        found = {0: own, blocks_dev: mate, group * blocks_dev: far}
        for rel, value in crossed.items():
            found[rel * blocks_dev] = value
            found[(rel ^ 1) * blocks_dev] = swap(value, "grp", 1)
        return found

    def beyond(vecs):
        return {place: value for place, value in vecs.items() if place >= home}

    vecs = window_of(vec, mate_vec, cross_vec, far_vec)
    urgent = urgent_ranges(group, blocks_dev)
    height = columns + 8
    at_home, *results = products(
        entries,
        (0,),
        {0: vec, blocks_dev: mate_vec},
        kept,
        (),
        [[(0, blocks_dev)]] + urgent,
        height,
        1,
    )
    results = products(entries, (1,), beyond(vecs), kept, results, urgent, height, 1)
    sums, (at_home,) = send_urgent(results, (at_home,), group, blocks_dev)
    sums = finish_home(entries, beyond(vecs), kept, at_home, blocks_dev, height, 1) + sums
    z, gram, parts, degree = scaled_gram(sums, vec, counts, None, None, True)
    for turn in range(1, ITERS):
        stages = sum_stages()
        far_part = from_behind(parts, "blk", -1)
        crossed = gather_far_bits(parts)
        mate_part = swap(parts, "grp", 1)
        gram = all_sum(gram, stages[:1])
        at_home, *results = products(
            entries,
            (0,),
            {0: parts, blocks_dev: mate_part},
            kept,
            (),
            [[(0, blocks_dev)]] + urgent,
            columns,
            2,
        )
        gram, at_home, *tied = lax.optimization_barrier((gram, at_home, *crossed.values()))
        crossed = dict(zip(crossed, tied))
        vecs = beyond(window_of(parts, mate_part, crossed, far_part))
        gram = all_sum(gram, stages[1:2])
        gram, *tied = lax.optimization_barrier((gram, *vecs.values()))
        vecs = dict(zip(vecs, tied))
        results = products(entries, (1,), vecs, kept, results, urgent, columns, 2)
        gram = all_sum(gram, stages[2:3])
        gram, *results = lax.optimization_barrier((gram, *results))
        gram = all_sum(gram, stages[3:4])
        sums, (at_home, gram) = send_urgent(results, (at_home, gram), group, blocks_dev)
        gram = all_sum(gram, stages[4:-1])
        own = finish_home(entries, vecs, kept, at_home, blocks_dev, columns, 2)
        gram, own[0] = all_sum(gram, stages[4:][-1:], own[0])
        sums = own + sums
        inverse = factor(gram)
        z, gram, *parts = scaled_gram(sums, z, counts, degree, inverse, turn + 1 < ITERS)
        parts = parts[0] if parts else None
    return embedding(all_sum_split(gram), z)


def solution(mesh):
    in_specs = (
        P(("blk", "grp"), None),
        P(("blk", "grp")),
        P("blk"),
        P("blk"),
        P("blk"),
        P(None, ("blk", "grp")),
    )
    out_specs = P(None, ("blk", "grp"))
    return jax.shard_map(
        per_device, mesh=mesh, in_specs=in_specs, out_specs=out_specs, check_vma=False
    )
```

```python
import functools

import jax
import jax.numpy as jnp
from jax import lax
from jax.experimental import pallas as pl
from jax.experimental.pallas import tpu as pltpu
from jax.sharding import PartitionSpec as P

PTS = 512
LOG2E = 1.4426950408889634
DEAD = 65536.0
EXTRA = 16
VMEM = pltpu.VMEM
SMEM = pltpu.SMEM
HIGHEST = lax.Precision.HIGHEST


def cost(flops, moved):
    return pl.CostEstimate(flops=int(flops), bytes_accessed=int(moved), transcendentals=0)


def spec(space):
    return pl.BlockSpec(memory_space=space)


def swap(value, axis, bit):
    count = lax.axis_size(axis)
    return lax.ppermute(value, axis, [(source, source ^ bit) for source in range(count)])


def from_behind(value, axis, steps):
    count = lax.axis_size(axis)
    initial, last = (max(0, -steps), min(count, count - steps))
    return lax.ppermute(value, axis, [(source, source + steps) for source in range(initial, last)])


def bits_of(count):
    bits = []
    bit = 1
    while bit < count:
        bits.append(bit)
        bit *= 2
    return bits


def gather_near(value, axis):
    held = {0: value}
    for bit in reversed(bits_of(lax.axis_size(axis))):
        for rel in list(held):
            held[rel ^ bit] = swap(held[rel], axis, bit)
    return [held[rel] for rel in range(len(held))]


def gather_far_bits(value):
    held = {0: value}
    for bit in reversed(bits_of(lax.axis_size("grp"))[1:]):
        for rel in list(held):
            held[rel ^ bit] = swap(held[rel], "grp", bit)
    held.pop(0)
    return held


def opening_kernel(start, counts, out):
    columns, total = start.shape
    for block in range(total // PTS):
        lanes = slice(block * PTS, (block + 1) * PTS)
        used = lax.broadcasted_iota(jnp.int32, (columns, PTS), 1) < counts[block]
        out[0:columns, lanes] = jnp.where(used, start[:, lanes], 0.0).astype(jnp.bfloat16)
        which = lax.broadcasted_iota(jnp.int32, (EXTRA, PTS), 0)
        place_in = lax.broadcasted_iota(jnp.int32, (EXTRA, PTS), 1)
        ones = jnp.logical_and(which == 0, place_in < counts[block])
        out[columns : columns + EXTRA, lanes] = jnp.where(ones, 1.0, 0.0).astype(jnp.bfloat16)


def opening(start, counts):
    columns, total = start.shape
    return pl.pallas_call(
        opening_kernel,
        out_shape=jax.ShapeDtypeStruct((columns + EXTRA, total), jnp.bfloat16),
        in_specs=[spec(VMEM), spec(SMEM)],
        out_specs=spec(VMEM),
        cost_estimate=cost(2**20, 2**19),
        compiler_params=pltpu.CompilerParams(vmem_limit_bytes=2 * 2**20),
        name="opening",
    )(start, counts)


def stage_of(place, group, blocks_dev):
    piece = lax.div(place, blocks_dev)
    first_half = lax.rem(place, blocks_dev) < blocks_dev // 2
    later = jnp.where(first_half, jnp.where(lax.rem(piece, 2) == 0, 0, 1), 2)
    return jnp.where(piece < min(2, group), 0, later)


def listing_kernel(
    group,
    cap,
    blocks_dev,
    rows,
    cols,
    live,
    out_rows,
    out_cols,
    out_n,
    tiles,
    sources,
    targets,
    bounds,
    owners,
):
    slab = blocks_dev * group
    slots = rows.shape[0]
    member = lax.axis_index("grp")

    def local_near(block, device):
        return (lax.div(block, blocks_dev) ^ device) * blocks_dev + lax.rem(block, blocks_dev)

    def local_far(block):
        return slab + lax.rem(block - slab, blocks_dev)

    def count_far(slot, carry):
        col = cols[slot]
        far = jnp.logical_and(slot < live[0], col >= slab)
        owner = lax.div(col - slab, blocks_dev)
        owners[slot] = jnp.where(far, owner, -1)
        return tuple(
            old + jnp.where(jnp.logical_and(far, owner == device), 1, 0)
            for device, old in enumerate(carry)
        )

    loads = lax.fori_loop(0, slots, count_far, (jnp.int32(0),) * group)

    def give(slot, loads):
        row, col = rows[slot], cols[slot]
        near = jnp.logical_and(slot < live[0], col < slab)
        best = jnp.int32(2**30)
        owner = jnp.int32(0)
        for device in range(group):
            stage = jnp.maximum(
                stage_of(local_near(row, device), group, blocks_dev),
                stage_of(local_near(col, device), group, blocks_dev),
            )
            score = loads[device] + 64 * stage + jnp.where(loads[device] < cap, 0, 2**20)
            owner = jnp.where(score < best, device, owner)
            best = jnp.minimum(score, best)

        @pl.when(near)
        def _():
            owners[slot] = owner

        return tuple(
            load + jnp.where(jnp.logical_and(near, owner == device), 1, 0)
            for device, load in enumerate(loads)
        )

    lax.fori_loop(0, slots, give, loads)

    def place_those(wanted, filled):
        def place(slot, filled):
            row, col = rows[slot], cols[slot]
            row_place = local_near(row, member)
            col_place = jnp.where(col >= slab, local_far(col), local_near(col, member))
            stage = jnp.maximum(
                stage_of(row_place, group, blocks_dev), stage_of(col_place, group, blocks_dev)
            )
            mine = jnp.logical_and(owners[slot] == member, stage == wanted)

            @pl.when(mine)
            def _():
                out_rows[filled] = row_place
                out_cols[filled] = col_place

            return filled + jnp.where(mine, 1, 0)

        return lax.fori_loop(0, slots, place, filled)

    count = jnp.int32(0)
    out_n[0] = count
    for wanted in range(3):
        count = place_those(wanted, count)
        out_n[wanted + 1] = count

    home = min(2, group) * blocks_dev
    bounds[0] = jnp.int32(0)
    filled = jnp.int32(0)
    for kind in range(3):
        for to_row in (True, False):

            def enter(index, filled):
                source = (out_cols if to_row else out_rows)[index]
                target = (out_rows if to_row else out_cols)[index]
                if kind == 0:
                    wanted = source < home
                elif kind == 1:
                    wanted = jnp.logical_and(source >= home, target >= blocks_dev)
                else:
                    wanted = jnp.logical_and(source >= home, target < blocks_dev)

                @pl.when(wanted)
                def _():
                    tiles[filled] = index
                    sources[filled] = source
                    targets[filled] = target

                return filled + jnp.where(wanted, 1, 0)

            filled = lax.fori_loop(0, count, enter, filled)
            bounds[2 * kind + (1 if to_row else 2)] = filled


def listing(rows, cols, live, group, cap, blocks_dev):
    return pl.pallas_call(
        functools.partial(listing_kernel, group, cap, blocks_dev),
        out_shape=(
            jax.ShapeDtypeStruct((cap,), jnp.int32),
            jax.ShapeDtypeStruct((cap,), jnp.int32),
            jax.ShapeDtypeStruct((4,), jnp.int32),
            jax.ShapeDtypeStruct((2 * cap,), jnp.int32),
            jax.ShapeDtypeStruct((2 * cap,), jnp.int32),
            jax.ShapeDtypeStruct((2 * cap,), jnp.int32),
            jax.ShapeDtypeStruct((7,), jnp.int32),
        ),
        in_specs=[spec(SMEM)] * 3,
        out_specs=(spec(SMEM),) * 7,
        scratch_shapes=[SMEM((rows.shape[0],), jnp.int32)],
        cost_estimate=cost(2**20, 2**10),
        compiler_params=pltpu.CompilerParams(vmem_limit_bytes=2**20),
        name="listing",
    )(rows, cols, live)


def set_levels(place, window, level_row, level_col, scale):
    block = window[place * PTS : (place + 1) * PTS, :]
    width = block.shape[1]
    part = jnp.zeros((PTS, 128), jnp.float32)
    for lane in range(0, width, 128):
        wide = block[:, lane : lane + 128].astype(jnp.float32)
        part = part + wide * wide
    level_row[place] = scale * lax.dot_general(
        jnp.ones((8, 128), jnp.float32),
        part,
        (((1,), (1,)), ((), ())),
        precision=HIGHEST,
        preferred_element_type=jnp.float32,
    )
    if place < level_col.shape[0]:
        total = jnp.sum(part, axis=1, keepdims=True) * scale
        level_col[place] = jnp.broadcast_to(total, (PTS, 128))


def make_tiles(low, high, rows, cols, window, level_row, level_col, kept, buffers):
    width = window.shape[1]
    scale = 6.0 / width * LOG2E
    count = high - low
    spare = kept.shape[0] - 1

    def cross(tile, buffer):
        index = low + jnp.minimum(tile, count - 1)
        left = window[pl.ds(pl.multiple_of(rows[index] * PTS, PTS), PTS), :]
        right = window[pl.ds(pl.multiple_of(cols[index] * PTS, PTS), PTS), :]
        buffer[...] = lax.dot_general(
            left, right, (((1,), (1,)), ((), ())), preferred_element_type=jnp.float32
        )

    def finish(tile, buffer):
        valid = jnp.logical_and(tile >= 0, tile < count)
        index = low + jnp.clip(tile, 0, count - 1)
        row, col = rows[index], cols[index]
        right_level = level_row[col][0:1, :]
        left_level = jnp.concatenate([level_col[row]] * (PTS // 128), axis=1)
        value = jnp.exp2(buffer[...] * scale - left_level - right_level)
        kept[jnp.where(valid, index, spare)] = value.astype(jnp.bfloat16)

    def body(pair, carry):
        cross(2 * pair, buffers[0])
        finish(2 * pair - 1, buffers[1])
        cross(2 * pair + 1, buffers[1])
        finish(2 * pair, buffers[0])
        return carry

    @pl.when(count > 0)
    def _():
        buffers[1][...] = jnp.zeros((PTS, PTS), jnp.float32)

    lax.fori_loop(0, jnp.where(count > 0, lax.div(count, 2) + 1, 0), body, 0)


def build_tiles(stage, fresh, n, rows, cols, state, group, blocks_dev, cap, name):
    places = list(fresh)
    pts = list(fresh.values())
    width = pts[0].shape[1]
    total = (group + 1) * blocks_dev
    near = group * blocks_dev
    shapes = [
        jax.ShapeDtypeStruct((total * PTS, width), jnp.bfloat16),
        jax.ShapeDtypeStruct((total, 8, PTS), jnp.float32),
        jax.ShapeDtypeStruct((near, PTS, 128), jnp.float32),
    ]
    makes = stage is not None
    if makes:
        shapes.append(jax.ShapeDtypeStruct((cap + 1, PTS, PTS), jnp.bfloat16))
    state = state[: len(shapes)]
    scalars = (n, rows, cols) if makes else ()
    first = len(scalars) + len(pts)

    def kernel(*refs):
        pt_refs = refs[len(scalars) : first]
        window, level_row, level_col, *rest = refs[first + len(state) :]
        for place, piece in zip(places, pt_refs):
            blocks = piece.shape[0] // PTS
            window[place * PTS : (place + blocks) * PTS, :] = piece[...]
            for block in range(place, place + blocks):
                set_levels(block, window, level_row, level_col, 3.0 / width * LOG2E)
        if makes:
            n_ref, row_ref, col_ref = refs[:3]
            kept, *buffers = rest
            make_tiles(
                n_ref[stage],
                n_ref[stage + 1],
                row_ref,
                col_ref,
                window,
                level_row,
                level_col,
                kept,
                buffers,
            )

    return pl.pallas_call(
        kernel,
        out_shape=shapes,
        in_specs=[spec(SMEM)] * len(scalars) + [spec(VMEM)] * (len(pts) + len(state)),
        out_specs=[spec(VMEM)] * len(shapes),
        input_output_aliases={first + index: index for index in range(len(state))},
        scratch_shapes=[VMEM((PTS, PTS), jnp.float32)] * (2 if makes else 0),
        cost_estimate=cost(2**32 if stage == 2 else 2**20, 2**20),
        compiler_params=pltpu.CompilerParams(vmem_limit_bytes=6 * 2**20),
        name=name,
    )(*scalars, *pts, *state)


def products(entries, kinds, vecs, tiles, start, targets, height, folds):
    firsts = sorted(vecs)
    tall, held = vecs[firsts[0]].shape
    blocks_dev = held // PTS
    begun = list(start)
    source_low, source_high = firsts[0], firsts[-1] + blocks_dev
    low = min(first for ranges in targets for first, _ in ranges)
    high = max(last for ranges in targets for _, last in ranges)
    shapes = [
        jax.ShapeDtypeStruct((sum(last - first for first, last in ranges), height, PTS), jnp.float32)
        for ranges in targets
    ]

    def pieces(refs):
        for ranges, ref in zip(targets, refs):
            at = 0
            for first, last in ranges:
                yield ref, slice(at, at + last - first), slice(first - low, last - low)
                at += last - first

    def fold(value):
        out = value[:height]
        for index in range(1, folds):
            out = out + value[index * height : (index + 1) * height]
        return out

    def kernel(*refs):
        tile_ref, source_ref, target_ref, bounds = refs[:4]
        vec_refs = refs[4 : 4 + len(firsts)]
        kept = refs[4 + len(firsts)]
        start_refs = refs[5 + len(firsts) : 5 + len(firsts) + len(begun)]
        outs = refs[5 + len(firsts) + len(begun) : -2]
        u_win, acc = refs[-2:]
        for first, ref in zip(firsts, vec_refs):
            for block in range(blocks_dev):
                lanes = slice(block * PTS, (block + 1) * PTS)
                u_win[first - source_low + block] = ref[:, lanes]
        if begun:
            for ref, inside, places in pieces(start_refs):
                acc[places] = ref[inside]
        else:
            for place in range(high - low + 1):
                acc[place] = jnp.zeros((height, PTS), jnp.float32)

        spare = high - low
        unroll = 4

        def several(begin, end, transposed):
            def body(step, carry):
                done = []
                for lane in range(unroll):
                    index = begin + step * unroll + lane
                    valid = index < end
                    index = jnp.minimum(index, end - 1)
                    vec = u_win[source_ref[index] - source_low]
                    tile = kept[tile_ref[index]]
                    if transposed:
                        value = lax.dot_general(
                            vec,
                            tile,
                            (((1,), (1,)), ((), ())),
                            preferred_element_type=jnp.float32,
                        )
                    else:
                        value = jnp.dot(vec, tile, preferred_element_type=jnp.float32)
                    done.append((jnp.where(valid, target_ref[index] - low, spare), fold(value)))
                for target, value in done:
                    acc[target] += value
                return carry

            lax.fori_loop(0, lax.div(end - begin + unroll - 1, unroll), body, 0)

        for kind in kinds:
            several(bounds[2 * kind], bounds[2 * kind + 1], True)
            several(bounds[2 * kind + 1], bounds[2 * kind + 2], False)
        for out, inside, places in pieces(outs):
            out[inside] = acc[places]

    return pl.pallas_call(
        kernel,
        out_shape=shapes,
        in_specs=[spec(SMEM)] * 4 + [spec(VMEM)] * (len(firsts) + 1 + len(begun)),
        out_specs=[spec(VMEM)] * len(shapes),
        scratch_shapes=[
            VMEM((source_high - source_low, tall, PTS), jnp.bfloat16),
            VMEM((high - low + 1, height, PTS), jnp.float32),
        ],
        cost_estimate=cost(2**31 if kinds == (1,) else 2**20, 2**20),
        compiler_params=pltpu.CompilerParams(vmem_limit_bytes=10 * 2**20),
        name="products",
    )(*entries, *[vecs[first] for first in firsts], tiles, *begun)


def urgent_ranges(group, blocks_dev):
    messages = [
        [rel for rel in range(group) if rel & bit and rel % bit == 0] for bit in bits_of(group)
    ]
    return [
        [(rel * blocks_dev, (rel + 1) * blocks_dev) for rel in rels]
        for rels in messages + [[group]]
    ]


def send_urgent(results, later, group, blocks_dev):
    final = []
    *messages, far = results
    parts = {}
    behind = None
    for bit, message in zip(bits_of(group), messages):
        rels = [rel for rel in range(group) if rel & bit and rel % bit == 0]
        for index, rel in enumerate(rels):
            if rel in parts:
                held = message[index * blocks_dev : (index + 1) * blocks_dev]
                message = held + parts[rel] if len(rels) == 1 else message.at[
                    index * blocks_dev : (index + 1) * blocks_dev
                ].add(parts[rel])
        if bit > 1:
            message, *later = lax.optimization_barrier((message, *later))
        got = swap(message, "grp", bit)
        if behind is None:
            got, far = lax.optimization_barrier((got, far))
            behind = from_behind(far, "blk", 1)
        final.append(got)
        for index, rel in enumerate(rels):
            if rel ^ bit:
                piece = got[index * blocks_dev : (index + 1) * blocks_dev]
                parts[rel ^ bit] = parts[rel ^ bit] + piece if rel ^ bit in parts else piece
    if behind is None:
        behind = from_behind(far, "blk", 1)
    return [behind] + final, later


def finish_home(entries, vecs, tiles, start, blocks_dev, height, folds):
    return list(
        products(entries, (2,), vecs, tiles, [start], [[(0, blocks_dev)]], height, folds)
    )


def scaled_gram(parts, own, counts, degree, earlier):
    columns = own.shape[0] if degree is not None else own.shape[0] - EXTRA
    total = own.shape[1]
    first = degree is None
    shapes = [
        jax.ShapeDtypeStruct((columns, total), jnp.float32),
        jax.ShapeDtypeStruct((columns, columns * (1 if first else 2)), jnp.float32),
    ]
    if first:
        shapes.append(jax.ShapeDtypeStruct((2 * columns, total), jnp.bfloat16))
        shapes.append(jax.ShapeDtypeStruct((8, total), jnp.float32))
    operands = list(parts) + [own]
    operands += [] if first else [degree, earlier]

    def kernel(count_ref, *refs):
        ins = list(refs[: len(operands)])
        outs = list(refs[len(operands) :])
        part_refs = ins[: len(parts)]
        own_ref = ins[len(parts)]
        z_out, gram_out = outs[:2]
        gram = jnp.zeros((columns, columns), jnp.float32)
        for block in range(total // PTS):
            lanes = slice(block * PTS, (block + 1) * PTS)
            sums = part_refs[0][block]
            for part in part_refs[1:]:
                sums = sums + part[block]
            if first:
                level = 1.0 + sums[columns : columns + 1, :]
                outs[-1][:, lanes] = jnp.broadcast_to(level, (8, PTS))
            else:
                level = ins[len(parts) + 1][0:1, lanes]
            used = lax.broadcasted_iota(jnp.int32, (columns, PTS), 1) < count_ref[block]
            held = own_ref[0:columns, lanes].astype(jnp.float32)
            z = (held + jnp.where(used, sums[0:columns], 0.0)) / level
            z_out[:, lanes] = z
            if first:
                high = z.astype(jnp.bfloat16)
                outs[2][0:columns, lanes] = high
                rest = z - high.astype(jnp.float32)
                outs[2][columns : 2 * columns, lanes] = rest.astype(jnp.bfloat16)
            gram = gram + lax.dot_general(
                z, z, (((1,), (1,)), ((), ())), precision=HIGHEST, preferred_element_type=jnp.float32
            )
        if not first:
            gram = jnp.concatenate([ins[-1][...], gram], axis=1)
        gram_out[...] = gram

    return pl.pallas_call(
        kernel,
        out_shape=tuple(shapes),
        in_specs=[spec(SMEM)] + [spec(VMEM)] * len(operands),
        out_specs=(spec(VMEM),) * len(shapes),
        cost_estimate=cost(2**26, 2**21),
        compiler_params=pltpu.CompilerParams(vmem_limit_bytes=6 * 2**20),
        name="scaled_gram",
    )(counts, *operands)


def inverse_factor(gram):
    size = gram.shape[0]
    row_id = lax.broadcasted_iota(jnp.int32, (size, size), 0)
    col_id = lax.broadcasted_iota(jnp.int32, (size, size), 1)
    eye = jnp.where(row_id == col_id, 1.0, 0.0)
    whole = jnp.concatenate([gram, eye], axis=1)
    wide = 2 * size
    count = size // 8
    groups = [whole[8 * g : 8 * g + 8, :] for g in range(count)]
    within = lax.broadcasted_iota(jnp.int32, (8, wide), 0)

    def spread_row(value, row):
        return jnp.broadcast_to(value[row : row + 1, :], (8, wide))

    results = []
    for g in range(count):
        spread = [
            [
                jnp.broadcast_to(groups[other][:, 8 * g + k : 8 * g + k + 1], (8, wide))
                for other in range(g, count)
            ]
            for k in range(8)
        ]
        pivots = jnp.ones((8, wide), jnp.float32)
        for j in range(8):
            column = spread[j]
            pivot = spread_row(column[0], j)
            pivots = jnp.where(within == j, pivot, pivots)
            over = 1.0 / pivot
            below = jnp.where(within > j, column[0], 0.0)
            for k in range(j + 1, 8):
                share = spread_row(column[0], k) * over
                spread[k][0] = spread[k][0] - below * share
                for other in range(1, count - g):
                    spread[k][other] = spread[k][other] - column[other] * share
            top = spread_row(groups[g], j) * over
            groups[g] = groups[g] - below * top
            for other in range(1, count - g):
                groups[g + other] = groups[g + other] - column[other] * top
        results.append(groups[g] * lax.rsqrt(pivots))
    return jnp.concatenate(results, axis=0)[:, size:wide]


def exact_dot(left, right, contract):
    return lax.dot_general(
        left,
        right,
        (contract, ((), ())),
        precision=HIGHEST,
        preferred_element_type=jnp.float32,
    )


def factors_kernel(grams, both_out, first_out, sound_out):
    columns = grams.shape[0]
    plain = ((1,), (0,))
    turned = ((1,), (1,))
    second = grams[:, columns : 2 * columns]
    first_inverse = inverse_factor(grams[:, 0:columns])
    middle = exact_dot(exact_dot(first_inverse, second, plain), first_inverse, turned)
    both = exact_dot(inverse_factor(middle), first_inverse, plain)
    both_out[...] = both
    first_out[...] = first_inverse
    row_id = lax.broadcasted_iota(jnp.int32, (columns, columns), 0)
    col_id = lax.broadcasted_iota(jnp.int32, (columns, columns), 1)
    trace = jnp.sum(jnp.where(row_id == col_id, second, 0.0))
    spread = jnp.sum(both * both) * trace / (columns * columns)
    sound_out[0] = jnp.where(spread < 64.0, 1, 0)


def factors(grams):
    columns = grams.shape[0]
    square = jax.ShapeDtypeStruct((columns, columns), jnp.float32)
    return pl.pallas_call(
        factors_kernel,
        out_shape=(square, square, jax.ShapeDtypeStruct((1,), jnp.int32)),
        in_specs=[spec(VMEM)],
        out_specs=(spec(VMEM), spec(VMEM), spec(SMEM)),
        cost_estimate=cost(2**30, 2**16),
        compiler_params=pltpu.CompilerParams(vmem_limit_bytes=2 * 2**20),
        name="factors",
    )(grams)


def apply_kernel(factor, z, out, *gram):
    value = exact_dot(factor[...], z[...], ((1,), (0,)))
    out[...] = value
    if gram:
        gram[0][...] = exact_dot(value, value, ((1,), (1,)))


def applied(factor, z, with_gram):
    shapes = [jax.ShapeDtypeStruct(z.shape, jnp.float32)]
    if with_gram:
        shapes.append(jax.ShapeDtypeStruct(factor.shape, jnp.float32))
    return pl.pallas_call(
        apply_kernel,
        out_shape=shapes,
        in_specs=[spec(VMEM)] * 2,
        out_specs=[spec(VMEM)] * len(shapes),
        compiler_params=pltpu.CompilerParams(vmem_limit_bytes=4 * 2**20),
        name="applied",
    )(factor, z)


def embed_kernel(gram, z, out):
    out[...] = exact_dot(inverse_factor(gram[...]), z[...], ((1,), (0,)))


def embedding(gram, z):
    return pl.pallas_call(
        embed_kernel,
        out_shape=jax.ShapeDtypeStruct(z.shape, jnp.float32),
        in_specs=[spec(VMEM)] * 2,
        out_specs=spec(VMEM),
        compiler_params=pltpu.CompilerParams(vmem_limit_bytes=4 * 2**20),
        name="embedding",
    )(gram, z)


def sum_stages():
    return bits_of(lax.axis_size("blk") * lax.axis_size("grp"))


def pairs_of(bits):
    return [bits[first : first + 2] for first in range(0, len(bits), 2)]


def all_sum(value, stages, beside=None):
    count = lax.axis_size("blk") * lax.axis_size("grp")
    for bits in stages:
        moves = [0]
        for bit in bits if isinstance(bits, list) else [bits]:
            moves += [move ^ bit for move in moves]
        terms = [value] + [
            lax.ppermute(value, ("blk", "grp"), [(source, source ^ move) for source in range(count)])
            for move in moves[1:]
        ]
        if beside is not None:
            terms[0], beside = lax.optimization_barrier((terms[0], beside))
        while len(terms) > 1:
            terms = [left + right for left, right in zip(terms[::2], terms[1::2])]
        value = terms[0]
    return value if beside is None else (value, beside)


def per_device(points, counts, pair_rows, pair_cols, pair_live, start):
    group = lax.axis_size("grp")
    blocks_dev = counts.shape[0]
    columns = start.shape[0]
    slots = pair_rows.shape[0]
    cap = max(-(-slots // group), blocks_dev * blocks_dev * group)
    half = (blocks_dev // 2) * PTS

    home = min(2, group) * blocks_dev

    rows, cols, n, *entries = listing(
        pair_rows, pair_cols, pair_live, group, cap, blocks_dev
    )
    mate = swap(points, "grp", 1)
    chunks = [points[:half], points[half:]]
    far = [from_behind(chunk, "blk", -1) for chunk in chunks]
    crossed = [gather_far_bits(chunk) for chunk in chunks]
    begin, mate = lax.optimization_barrier((start, mate))
    vec = opening(begin, counts)
    tied = lax.optimization_barrier((vec, n, rows, cols, far[0], *crossed[0].values()))
    vec, n, rows, cols, far[0] = tied[:5]
    crossed[0] = dict(zip(crossed[0], tied[5:]))
    cross_vec = gather_far_bits(vec)
    far_vec = from_behind(vec, "blk", -1)
    mate_vec = swap(vec, "grp", 1)

    def direct(index):
        offset = index * (blocks_dev // 2)
        found = {group * blocks_dev + offset: far[index]}
        for rel, value in crossed[index].items():
            found[rel * blocks_dev + offset] = value
        return found

    def passed_on(index):
        offset = index * (blocks_dev // 2)
        found = {}
        for rel, value in crossed[index].items():
            cut = value.shape[0] // (1 if index else 2)
            parts = [swap(value[at : at + cut], "grp", 1) for at in range(0, value.shape[0], cut)]
            found[(rel ^ 1) * blocks_dev + offset] = jnp.concatenate(parts, 0)
        return found

    def build(stage, fresh, state, name):
        return list(
            build_tiles(stage, fresh, n, rows, cols, state, group, blocks_dev, cap, name)
        )

    state = build(0, {0: points, blocks_dev: mate, **direct(0)}, (), "first_tiles")
    state = build(1, passed_on(0), state, "second_tiles")
    tied = lax.optimization_barrier((far[1], mate_vec, state[1], *crossed[1].values()))
    far[1], mate_vec, state[1] = tied[:3]
    crossed[1] = dict(zip(crossed[1], tied[3:]))
    last = passed_on(1)
    *grown, kept = state
    state = build(None, direct(1), grown, "more_blocks") + [kept]
    state = build(2, last, state, "last_tiles")
    kept = state[-1]
    tied = lax.optimization_barrier((kept, *cross_vec.values()))
    kept = tied[0]
    cross_vec = dict(zip(cross_vec, tied[1:]))

    def window_of(own, mate, crossed, far):
        found = {0: own, blocks_dev: mate, group * blocks_dev: far}
        for rel, value in crossed.items():
            found[rel * blocks_dev] = value
            found[(rel ^ 1) * blocks_dev] = swap(value, "grp", 1)
        return found

    def beyond(vecs):
        return {place: value for place, value in vecs.items() if place >= home}

    vecs = window_of(vec, mate_vec, cross_vec, far_vec)
    urgent = urgent_ranges(group, blocks_dev)
    height = columns + 8
    at_home, *results = products(
        entries,
        (0,),
        {0: vec, blocks_dev: mate_vec},
        kept,
        (),
        [[(0, blocks_dev)]] + urgent,
        height,
        1,
    )
    results = products(entries, (1,), beyond(vecs), kept, results, urgent, height, 1)
    sums, (at_home,) = send_urgent(results, (at_home,), group, blocks_dev)
    sums = finish_home(entries, beyond(vecs), kept, at_home, blocks_dev, height, 1) + sums
    z, gram, parts, degree = scaled_gram(sums, vec, counts, None, None)

    far_part = from_behind(parts, "blk", -1)
    crossed = gather_far_bits(parts)
    mate_part = swap(parts, "grp", 1)
    at_home, *results = products(
        entries,
        (0,),
        {0: parts, blocks_dev: mate_part},
        kept,
        (),
        [[(0, blocks_dev)]] + urgent,
        columns,
        2,
    )
    at_home, *tied = lax.optimization_barrier((at_home, *crossed.values()))
    crossed = dict(zip(crossed, tied))
    vecs = beyond(window_of(parts, mate_part, crossed, far_part))
    results = products(entries, (1,), vecs, kept, results, urgent, columns, 2)
    sums, (at_home,) = send_urgent(results, (at_home,), group, blocks_dev)
    sums = finish_home(entries, vecs, kept, at_home, blocks_dev, columns, 2) + sums
    z, grams = scaled_gram(sums, z, counts, degree, gram)

    stages = sum_stages()
    stages = stages[:1] + pairs_of(stages[1:])
    both, first, sound = factors(all_sum(grams, stages))

    def at_once(both, first, z):
        return applied(both, z, False)[0]

    def in_two(both, first, z):
        value, gram = applied(first, z, True)
        return embedding(all_sum(gram, stages), value)

    return lax.cond(sound[0] == 1, at_once, in_two, both, first, z)


def solution(mesh):
    in_specs = (
        P(("blk", "grp"), None),
        P(("blk", "grp")),
        P("blk"),
        P("blk"),
        P("blk"),
        P(None, ("blk", "grp")),
    )
    out_specs = P(None, ("blk", "grp"))
    return jax.shard_map(
        per_device, mesh=mesh, in_specs=in_specs, out_specs=out_specs, check_vma=False
    )
```

```python
import functools

import jax
import jax.numpy as jnp
from jax import lax
from jax.experimental import pallas as pl
from jax.experimental.pallas import tpu as pltpu
from jax.sharding import PartitionSpec as P

PTS = 512
LOG2E = 1.4426950408889634
DEAD = 65536.0
EXTRA = 16
VMEM = pltpu.VMEM
SMEM = pltpu.SMEM
HIGHEST = lax.Precision.HIGHEST


def cost(flops, moved):
    return pl.CostEstimate(flops=int(flops), bytes_accessed=int(moved), transcendentals=0)


def spec(space):
    return pl.BlockSpec(memory_space=space)


def swap(value, axis, bit):
    count = lax.axis_size(axis)
    return lax.ppermute(value, axis, [(source, source ^ bit) for source in range(count)])


def from_behind(value, axis, steps):
    count = lax.axis_size(axis)
    initial, last = (max(0, -steps), min(count, count - steps))
    return lax.ppermute(value, axis, [(source, source + steps) for source in range(initial, last)])


def bits_of(count):
    bits = []
    bit = 1
    while bit < count:
        bits.append(bit)
        bit *= 2
    return bits


def gather_near(value, axis):
    held = {0: value}
    for bit in reversed(bits_of(lax.axis_size(axis))):
        for rel in list(held):
            held[rel ^ bit] = swap(held[rel], axis, bit)
    return [held[rel] for rel in range(len(held))]


def gather_far_bits(value):
    held = {0: value}
    for bit in reversed(bits_of(lax.axis_size("grp"))[1:]):
        for rel in list(held):
            held[rel ^ bit] = swap(held[rel], "grp", bit)
    held.pop(0)
    return held


def opening_kernel(start, counts, out):
    columns, total = start.shape
    for block in range(total // PTS):
        lanes = slice(block * PTS, (block + 1) * PTS)
        used = lax.broadcasted_iota(jnp.int32, (columns, PTS), 1) < counts[block]
        out[0:columns, lanes] = jnp.where(used, start[:, lanes], 0.0).astype(jnp.bfloat16)
        which = lax.broadcasted_iota(jnp.int32, (EXTRA, PTS), 0)
        place_in = lax.broadcasted_iota(jnp.int32, (EXTRA, PTS), 1)
        ones = jnp.logical_and(which == 0, place_in < counts[block])
        out[columns : columns + EXTRA, lanes] = jnp.where(ones, 1.0, 0.0).astype(jnp.bfloat16)


def opening(start, counts):
    columns, total = start.shape
    return pl.pallas_call(
        opening_kernel,
        out_shape=jax.ShapeDtypeStruct((columns + EXTRA, total), jnp.bfloat16),
        in_specs=[spec(VMEM), spec(SMEM)],
        out_specs=spec(VMEM),
        cost_estimate=cost(2**20, 2**19),
        compiler_params=pltpu.CompilerParams(vmem_limit_bytes=2 * 2**20),
        name="opening",
    )(start, counts)


def stage_of(place, group, blocks_dev):
    piece = lax.div(place, blocks_dev)
    first_half = lax.rem(place, blocks_dev) < blocks_dev // 2
    later = jnp.where(first_half, jnp.where(lax.rem(piece, 2) == 0, 0, 1), 2)
    return jnp.where(piece < min(2, group), 0, later)


def listing_kernel(
    group,
    cap,
    blocks_dev,
    rows,
    cols,
    live,
    out_rows,
    out_cols,
    out_n,
    tiles,
    sources,
    targets,
    bounds,
    owners,
):
    slab = blocks_dev * group
    slots = rows.shape[0]
    member = lax.axis_index("grp")

    def local_near(block, device):
        return (lax.div(block, blocks_dev) ^ device) * blocks_dev + lax.rem(block, blocks_dev)

    def local_far(block):
        return slab + lax.rem(block - slab, blocks_dev)

    def count_far(slot, carry):
        col = cols[slot]
        far = jnp.logical_and(slot < live[0], col >= slab)
        owner = lax.div(col - slab, blocks_dev)
        owners[slot] = jnp.where(far, owner, -1)
        return tuple(
            old + jnp.where(jnp.logical_and(far, owner == device), 1, 0)
            for device, old in enumerate(carry)
        )

    loads = lax.fori_loop(0, slots, count_far, (jnp.int32(0),) * group)

    def give(slot, loads):
        row, col = rows[slot], cols[slot]
        near = jnp.logical_and(slot < live[0], col < slab)
        best = jnp.int32(2**30)
        owner = jnp.int32(0)
        for device in range(group):
            stage = jnp.maximum(
                stage_of(local_near(row, device), group, blocks_dev),
                stage_of(local_near(col, device), group, blocks_dev),
            )
            score = loads[device] + 64 * stage + jnp.where(loads[device] < cap, 0, 2**20)
            owner = jnp.where(score < best, device, owner)
            best = jnp.minimum(score, best)

        @pl.when(near)
        def _():
            owners[slot] = owner

        return tuple(
            load + jnp.where(jnp.logical_and(near, owner == device), 1, 0)
            for device, load in enumerate(loads)
        )

    lax.fori_loop(0, slots, give, loads)

    def place_those(wanted, filled):
        def place(slot, filled):
            row, col = rows[slot], cols[slot]
            row_place = local_near(row, member)
            col_place = jnp.where(col >= slab, local_far(col), local_near(col, member))
            stage = jnp.maximum(
                stage_of(row_place, group, blocks_dev), stage_of(col_place, group, blocks_dev)
            )
            mine = jnp.logical_and(owners[slot] == member, stage == wanted)

            @pl.when(mine)
            def _():
                out_rows[filled] = row_place
                out_cols[filled] = col_place

            return filled + jnp.where(mine, 1, 0)

        return lax.fori_loop(0, slots, place, filled)

    count = jnp.int32(0)
    out_n[0] = count
    for wanted in range(3):
        count = place_those(wanted, count)
        out_n[wanted + 1] = count

    home = min(2, group) * blocks_dev
    bounds[0] = jnp.int32(0)
    filled = jnp.int32(0)
    for kind in range(3):
        for to_row in (True, False):

            def enter(index, filled):
                source = (out_cols if to_row else out_rows)[index]
                target = (out_rows if to_row else out_cols)[index]
                if kind == 0:
                    wanted = source < home
                elif kind == 1:
                    wanted = jnp.logical_and(source >= home, target >= blocks_dev)
                else:
                    wanted = jnp.logical_and(source >= home, target < blocks_dev)

                @pl.when(wanted)
                def _():
                    tiles[filled] = index
                    sources[filled] = source
                    targets[filled] = target

                return filled + jnp.where(wanted, 1, 0)

            filled = lax.fori_loop(0, count, enter, filled)
            bounds[2 * kind + (1 if to_row else 2)] = filled


def listing(rows, cols, live, group, cap, blocks_dev):
    return pl.pallas_call(
        functools.partial(listing_kernel, group, cap, blocks_dev),
        out_shape=(
            jax.ShapeDtypeStruct((cap,), jnp.int32),
            jax.ShapeDtypeStruct((cap,), jnp.int32),
            jax.ShapeDtypeStruct((4,), jnp.int32),
            jax.ShapeDtypeStruct((2 * cap,), jnp.int32),
            jax.ShapeDtypeStruct((2 * cap,), jnp.int32),
            jax.ShapeDtypeStruct((2 * cap,), jnp.int32),
            jax.ShapeDtypeStruct((7,), jnp.int32),
        ),
        in_specs=[spec(SMEM)] * 3,
        out_specs=(spec(SMEM),) * 7,
        scratch_shapes=[SMEM((rows.shape[0],), jnp.int32)],
        cost_estimate=cost(2**20, 2**10),
        compiler_params=pltpu.CompilerParams(vmem_limit_bytes=2**20),
        name="listing",
    )(rows, cols, live)


def set_levels(place, window, level_row, level_col, scale):
    block = window[place * PTS : (place + 1) * PTS, :]
    width = block.shape[1]
    part = jnp.zeros((PTS, 128), jnp.float32)
    for lane in range(0, width, 128):
        wide = block[:, lane : lane + 128].astype(jnp.float32)
        part = part + wide * wide
    level_row[place] = scale * lax.dot_general(
        jnp.ones((8, 128), jnp.float32),
        part,
        (((1,), (1,)), ((), ())),
        precision=HIGHEST,
        preferred_element_type=jnp.float32,
    )
    if place < level_col.shape[0]:
        total = jnp.sum(part, axis=1, keepdims=True) * scale
        level_col[place] = jnp.broadcast_to(total, (PTS, 128))


def make_tiles(low, high, rows, cols, window, level_row, level_col, kept, buffers):
    width = window.shape[1]
    scale = 6.0 / width * LOG2E
    count = high - low
    spare = kept.shape[0] - 1

    def cross(tile, buffer):
        index = low + jnp.minimum(tile, count - 1)
        left = window[pl.ds(pl.multiple_of(rows[index] * PTS, PTS), PTS), :]
        right = window[pl.ds(pl.multiple_of(cols[index] * PTS, PTS), PTS), :]
        buffer[...] = lax.dot_general(
            left, right, (((1,), (1,)), ((), ())), preferred_element_type=jnp.float32
        )

    def finish(tile, buffer):
        valid = jnp.logical_and(tile >= 0, tile < count)
        index = low + jnp.clip(tile, 0, count - 1)
        row, col = rows[index], cols[index]
        right_level = level_row[col][0:1, :]
        left_level = jnp.concatenate([level_col[row]] * (PTS // 128), axis=1)
        value = jnp.exp2(buffer[...] * scale - left_level - right_level)
        kept[jnp.where(valid, index, spare)] = value.astype(jnp.bfloat16)

    def body(pair, carry):
        cross(2 * pair, buffers[0])
        finish(2 * pair - 1, buffers[1])
        cross(2 * pair + 1, buffers[1])
        finish(2 * pair, buffers[0])
        return carry

    @pl.when(count > 0)
    def _():
        buffers[1][...] = jnp.zeros((PTS, PTS), jnp.float32)

    lax.fori_loop(0, jnp.where(count > 0, lax.div(count, 2) + 1, 0), body, 0)


def build_tiles(stage, fresh, n, rows, cols, state, group, blocks_dev, cap, name):
    places = list(fresh)
    pts = list(fresh.values())
    width = pts[0].shape[1]
    total = (group + 1) * blocks_dev
    near = group * blocks_dev
    shapes = [
        jax.ShapeDtypeStruct((total * PTS, width), jnp.bfloat16),
        jax.ShapeDtypeStruct((total, 8, PTS), jnp.float32),
        jax.ShapeDtypeStruct((near, PTS, 128), jnp.float32),
    ]
    makes = stage is not None
    if makes:
        shapes.append(jax.ShapeDtypeStruct((cap + 1, PTS, PTS), jnp.bfloat16))
    state = state[: len(shapes)]
    scalars = (n, rows, cols) if makes else ()
    first = len(scalars) + len(pts)

    def kernel(*refs):
        pt_refs = refs[len(scalars) : first]
        window, level_row, level_col, *rest = refs[first + len(state) :]
        for place, piece in zip(places, pt_refs):
            blocks = piece.shape[0] // PTS
            window[place * PTS : (place + blocks) * PTS, :] = piece[...]
            for block in range(place, place + blocks):
                set_levels(block, window, level_row, level_col, 3.0 / width * LOG2E)
        if makes:
            n_ref, row_ref, col_ref = refs[:3]
            kept, *buffers = rest
            make_tiles(
                n_ref[stage],
                n_ref[stage + 1],
                row_ref,
                col_ref,
                window,
                level_row,
                level_col,
                kept,
                buffers,
            )

    return pl.pallas_call(
        kernel,
        out_shape=shapes,
        in_specs=[spec(SMEM)] * len(scalars) + [spec(VMEM)] * (len(pts) + len(state)),
        out_specs=[spec(VMEM)] * len(shapes),
        input_output_aliases={first + index: index for index in range(len(state))},
        scratch_shapes=[VMEM((PTS, PTS), jnp.float32)] * (2 if makes else 0),
        cost_estimate=cost(2**32 if stage == 2 else 2**20, 2**20),
        compiler_params=pltpu.CompilerParams(vmem_limit_bytes=6 * 2**20),
        name=name,
    )(*scalars, *pts, *state)


def products(entries, kinds, vecs, tiles, start, targets, height, folds):
    firsts = sorted(vecs)
    tall, held = vecs[firsts[0]].shape
    blocks_dev = held // PTS
    begun = list(start)
    source_low, source_high = firsts[0], firsts[-1] + blocks_dev
    low = min(first for ranges in targets for first, _ in ranges)
    high = max(last for ranges in targets for _, last in ranges)
    shapes = [
        jax.ShapeDtypeStruct((sum(last - first for first, last in ranges), height, PTS), jnp.float32)
        for ranges in targets
    ]

    def pieces(refs):
        for ranges, ref in zip(targets, refs):
            at = 0
            for first, last in ranges:
                yield ref, slice(at, at + last - first), slice(first - low, last - low)
                at += last - first

    def fold(value):
        out = value[:height]
        for index in range(1, folds):
            out = out + value[index * height : (index + 1) * height]
        return out

    def kernel(*refs):
        tile_ref, source_ref, target_ref, bounds = refs[:4]
        vec_refs = refs[4 : 4 + len(firsts)]
        kept = refs[4 + len(firsts)]
        start_refs = refs[5 + len(firsts) : 5 + len(firsts) + len(begun)]
        outs = refs[5 + len(firsts) + len(begun) : -2]
        u_win, acc = refs[-2:]
        for first, ref in zip(firsts, vec_refs):
            for block in range(blocks_dev):
                lanes = slice(block * PTS, (block + 1) * PTS)
                u_win[first - source_low + block] = ref[:, lanes]
        if begun:
            for ref, inside, places in pieces(start_refs):
                acc[places] = ref[inside]
        else:
            for place in range(high - low + 1):
                acc[place] = jnp.zeros((height, PTS), jnp.float32)

        spare = high - low
        unroll = 4

        def several(begin, end, transposed):
            def body(step, carry):
                done = []
                for lane in range(unroll):
                    index = begin + step * unroll + lane
                    valid = index < end
                    index = jnp.minimum(index, end - 1)
                    vec = u_win[source_ref[index] - source_low]
                    tile = kept[tile_ref[index]]
                    if transposed:
                        value = lax.dot_general(
                            vec,
                            tile,
                            (((1,), (1,)), ((), ())),
                            preferred_element_type=jnp.float32,
                        )
                    else:
                        value = jnp.dot(vec, tile, preferred_element_type=jnp.float32)
                    done.append((jnp.where(valid, target_ref[index] - low, spare), fold(value)))
                for target, value in done:
                    acc[target] += value
                return carry

            lax.fori_loop(0, lax.div(end - begin + unroll - 1, unroll), body, 0)

        for kind in kinds:
            several(bounds[2 * kind], bounds[2 * kind + 1], True)
            several(bounds[2 * kind + 1], bounds[2 * kind + 2], False)
        for out, inside, places in pieces(outs):
            out[inside] = acc[places]

    return pl.pallas_call(
        kernel,
        out_shape=shapes,
        in_specs=[spec(SMEM)] * 4 + [spec(VMEM)] * (len(firsts) + 1 + len(begun)),
        out_specs=[spec(VMEM)] * len(shapes),
        scratch_shapes=[
            VMEM((source_high - source_low, tall, PTS), jnp.bfloat16),
            VMEM((high - low + 1, height, PTS), jnp.float32),
        ],
        cost_estimate=cost(2**31 if kinds == (1,) else 2**20, 2**20),
        compiler_params=pltpu.CompilerParams(vmem_limit_bytes=10 * 2**20),
        name="products",
    )(*entries, *[vecs[first] for first in firsts], tiles, *begun)


def urgent_ranges(group, blocks_dev):
    messages = [
        [rel for rel in range(group) if rel & bit and rel % bit == 0] for bit in bits_of(group)
    ]
    return [
        [(rel * blocks_dev, (rel + 1) * blocks_dev) for rel in rels]
        for rels in messages + [[group]]
    ]


def send_urgent(results, later, group, blocks_dev):
    final = []
    *messages, far = results
    parts = {}
    behind = None
    for bit, message in zip(bits_of(group), messages):
        rels = [rel for rel in range(group) if rel & bit and rel % bit == 0]
        for index, rel in enumerate(rels):
            if rel in parts:
                held = message[index * blocks_dev : (index + 1) * blocks_dev]
                message = held + parts[rel] if len(rels) == 1 else message.at[
                    index * blocks_dev : (index + 1) * blocks_dev
                ].add(parts[rel])
        if bit > 1:
            message, *later = lax.optimization_barrier((message, *later))
        got = swap(message, "grp", bit)
        if behind is None:
            got, far = lax.optimization_barrier((got, far))
            behind = from_behind(far, "blk", 1)
        final.append(got)
        for index, rel in enumerate(rels):
            if rel ^ bit:
                piece = got[index * blocks_dev : (index + 1) * blocks_dev]
                parts[rel ^ bit] = parts[rel ^ bit] + piece if rel ^ bit in parts else piece
    if behind is None:
        behind = from_behind(far, "blk", 1)
    return [behind] + final, later


def finish_home(entries, vecs, tiles, start, blocks_dev, height, folds):
    return list(
        products(entries, (2,), vecs, tiles, [start], [[(0, blocks_dev)]], height, folds)
    )


def scaled_gram(parts, own, counts, degree, earlier):
    columns = own.shape[0] if degree is not None else own.shape[0] - EXTRA
    total = own.shape[1]
    first = degree is None
    shapes = [
        jax.ShapeDtypeStruct((columns, total), jnp.float32),
        jax.ShapeDtypeStruct((columns, columns * (1 if first else 2)), jnp.float32),
    ]
    if first:
        shapes.append(jax.ShapeDtypeStruct((2 * columns, total), jnp.bfloat16))
        shapes.append(jax.ShapeDtypeStruct((8, total), jnp.float32))
    operands = list(parts) + [own]
    operands += [] if first else [degree, earlier]

    def kernel(count_ref, *refs):
        ins = list(refs[: len(operands)])
        outs = list(refs[len(operands) :])
        part_refs = ins[: len(parts)]
        own_ref = ins[len(parts)]
        z_out, gram_out = outs[:2]
        gram = jnp.zeros((columns, columns), jnp.float32)
        for block in range(total // PTS):
            lanes = slice(block * PTS, (block + 1) * PTS)
            sums = part_refs[0][block]
            for part in part_refs[1:]:
                sums = sums + part[block]
            if first:
                level = 1.0 + sums[columns : columns + 1, :]
                outs[-1][:, lanes] = jnp.broadcast_to(level, (8, PTS))
            else:
                level = ins[len(parts) + 1][0:1, lanes]
            used = lax.broadcasted_iota(jnp.int32, (columns, PTS), 1) < count_ref[block]
            held = own_ref[0:columns, lanes].astype(jnp.float32)
            z = (held + jnp.where(used, sums[0:columns], 0.0)) / level
            z_out[:, lanes] = z
            if first:
                high = z.astype(jnp.bfloat16)
                outs[2][0:columns, lanes] = high
                rest = z - high.astype(jnp.float32)
                outs[2][columns : 2 * columns, lanes] = rest.astype(jnp.bfloat16)
            gram = gram + lax.dot_general(
                z, z, (((1,), (1,)), ((), ())), precision=HIGHEST, preferred_element_type=jnp.float32
            )
        if not first:
            gram = jnp.concatenate([ins[-1][...], gram], axis=1)
        gram_out[...] = gram

    return pl.pallas_call(
        kernel,
        out_shape=tuple(shapes),
        in_specs=[spec(SMEM)] + [spec(VMEM)] * len(operands),
        out_specs=(spec(VMEM),) * len(shapes),
        cost_estimate=cost(2**26, 2**21),
        compiler_params=pltpu.CompilerParams(vmem_limit_bytes=6 * 2**20),
        name="scaled_gram",
    )(counts, *operands)


def inverse_factor(gram):
    size = gram.shape[0]
    row_id = lax.broadcasted_iota(jnp.int32, (size, size), 0)
    col_id = lax.broadcasted_iota(jnp.int32, (size, size), 1)
    eye = jnp.where(row_id == col_id, 1.0, 0.0)
    whole = jnp.concatenate([gram, eye], axis=1)
    wide = 2 * size
    count = size // 8
    groups = [whole[8 * g : 8 * g + 8, :] for g in range(count)]
    within = lax.broadcasted_iota(jnp.int32, (8, wide), 0)

    def spread_row(value, row):
        return jnp.broadcast_to(value[row : row + 1, :], (8, wide))

    results = []
    for g in range(count):
        spread = [
            [
                jnp.broadcast_to(groups[other][:, 8 * g + k : 8 * g + k + 1], (8, wide))
                for other in range(g, count)
            ]
            for k in range(8)
        ]
        pivots = jnp.ones((8, wide), jnp.float32)
        for j in range(8):
            column = spread[j]
            pivot = spread_row(column[0], j)
            pivots = jnp.where(within == j, pivot, pivots)
            over = 1.0 / pivot
            below = jnp.where(within > j, column[0], 0.0)
            for k in range(j + 1, 8):
                share = spread_row(column[0], k) * over
                spread[k][0] = spread[k][0] - below * share
                for other in range(1, count - g):
                    spread[k][other] = spread[k][other] - column[other] * share
            top = spread_row(groups[g], j) * over
            groups[g] = groups[g] - below * top
            for other in range(1, count - g):
                groups[g + other] = groups[g + other] - column[other] * top
        results.append(groups[g] * lax.rsqrt(pivots))
    return jnp.concatenate(results, axis=0)[:, size:wide]


def exact_dot(left, right, contract):
    return lax.dot_general(
        left,
        right,
        (contract, ((), ())),
        precision=HIGHEST,
        preferred_element_type=jnp.float32,
    )


def factors_kernel(grams, both_out, first_out, sound_out):
    columns = grams.shape[0]
    plain = ((1,), (0,))
    turned = ((1,), (1,))
    second = grams[:, columns : 2 * columns]
    first_inverse = inverse_factor(grams[:, 0:columns])
    middle = exact_dot(exact_dot(first_inverse, second, plain), first_inverse, turned)
    both = exact_dot(inverse_factor(middle), first_inverse, plain)
    both_out[...] = both
    first_out[...] = first_inverse
    row_id = lax.broadcasted_iota(jnp.int32, (columns, columns), 0)
    col_id = lax.broadcasted_iota(jnp.int32, (columns, columns), 1)
    trace = jnp.sum(jnp.where(row_id == col_id, second, 0.0))
    spread = jnp.sum(both * both) * trace / (columns * columns)
    sound_out[0] = jnp.where(spread < 64.0, 1, 0)


def factors(grams):
    columns = grams.shape[0]
    square = jax.ShapeDtypeStruct((columns, columns), jnp.float32)
    return pl.pallas_call(
        factors_kernel,
        out_shape=(square, square, jax.ShapeDtypeStruct((1,), jnp.int32)),
        in_specs=[spec(VMEM)],
        out_specs=(spec(VMEM), spec(VMEM), spec(SMEM)),
        cost_estimate=cost(2**30, 2**16),
        compiler_params=pltpu.CompilerParams(vmem_limit_bytes=2 * 2**20),
        name="factors",
    )(grams)


def apply_kernel(factor, z, out, *gram):
    value = exact_dot(factor[...], z[...], ((1,), (0,)))
    out[...] = value
    if gram:
        gram[0][...] = exact_dot(value, value, ((1,), (1,)))


def applied(factor, z, with_gram):
    shapes = [jax.ShapeDtypeStruct(z.shape, jnp.float32)]
    if with_gram:
        shapes.append(jax.ShapeDtypeStruct(factor.shape, jnp.float32))
    return pl.pallas_call(
        apply_kernel,
        out_shape=shapes,
        in_specs=[spec(VMEM)] * 2,
        out_specs=[spec(VMEM)] * len(shapes),
        compiler_params=pltpu.CompilerParams(vmem_limit_bytes=4 * 2**20),
        name="applied",
    )(factor, z)


def second_kernel(gram, first, out):
    out[...] = exact_dot(inverse_factor(gram[...]), first[...], ((1,), (0,)))


def second_factor(gram, first):
    return pl.pallas_call(
        second_kernel,
        out_shape=jax.ShapeDtypeStruct(gram.shape, jnp.float32),
        in_specs=[spec(VMEM)] * 2,
        out_specs=spec(VMEM),
        compiler_params=pltpu.CompilerParams(vmem_limit_bytes=2 * 2**20),
        name="second_factor",
    )(gram, first)


def sum_stages():
    return bits_of(lax.axis_size("blk") * lax.axis_size("grp"))


def pairs_of(bits):
    return [bits[first : first + 2] for first in range(0, len(bits), 2)]


def all_sum(value, stages, beside=None):
    count = lax.axis_size("blk") * lax.axis_size("grp")
    for bits in stages:
        moves = [0]
        for bit in bits if isinstance(bits, list) else [bits]:
            moves += [move ^ bit for move in moves]
        terms = [value] + [
            lax.ppermute(value, ("blk", "grp"), [(source, source ^ move) for source in range(count)])
            for move in moves[1:]
        ]
        if beside is not None:
            terms[0], beside = lax.optimization_barrier((terms[0], beside))
        while len(terms) > 1:
            terms = [left + right for left, right in zip(terms[::2], terms[1::2])]
        value = terms[0]
    return value if beside is None else (value, beside)


def per_device(points, counts, pair_rows, pair_cols, pair_live, start):
    group = lax.axis_size("grp")
    blocks_dev = counts.shape[0]
    columns = start.shape[0]
    slots = pair_rows.shape[0]
    cap = max(-(-slots // group), blocks_dev * blocks_dev * group)
    half = (blocks_dev // 2) * PTS

    home = min(2, group) * blocks_dev

    rows, cols, n, *entries = listing(
        pair_rows, pair_cols, pair_live, group, cap, blocks_dev
    )
    mate = swap(points, "grp", 1)
    chunks = [points[:half], points[half:]]
    far = [from_behind(chunk, "blk", -1) for chunk in chunks]
    crossed = [gather_far_bits(chunk) for chunk in chunks]
    begin, mate = lax.optimization_barrier((start, mate))
    vec = opening(begin, counts)
    tied = lax.optimization_barrier((vec, n, rows, cols, far[0], *crossed[0].values()))
    vec, n, rows, cols, far[0] = tied[:5]
    crossed[0] = dict(zip(crossed[0], tied[5:]))
    cross_vec = gather_far_bits(vec)
    far_vec = from_behind(vec, "blk", -1)
    mate_vec = swap(vec, "grp", 1)

    def direct(index):
        offset = index * (blocks_dev // 2)
        found = {group * blocks_dev + offset: far[index]}
        for rel, value in crossed[index].items():
            found[rel * blocks_dev + offset] = value
        return found

    def passed_on(index):
        offset = index * (blocks_dev // 2)
        found = {}
        for rel, value in crossed[index].items():
            cut = value.shape[0] // (1 if index else 2)
            parts = [swap(value[at : at + cut], "grp", 1) for at in range(0, value.shape[0], cut)]
            found[(rel ^ 1) * blocks_dev + offset] = jnp.concatenate(parts, 0)
        return found

    def build(stage, fresh, state, name):
        return list(
            build_tiles(stage, fresh, n, rows, cols, state, group, blocks_dev, cap, name)
        )

    state = build(0, {0: points, blocks_dev: mate, **direct(0)}, (), "first_tiles")
    state = build(1, passed_on(0), state, "second_tiles")
    tied = lax.optimization_barrier((far[1], mate_vec, state[1], *crossed[1].values()))
    far[1], mate_vec, state[1] = tied[:3]
    crossed[1] = dict(zip(crossed[1], tied[3:]))
    last = passed_on(1)
    *grown, kept = state
    state = build(None, direct(1), grown, "more_blocks") + [kept]
    state = build(2, last, state, "last_tiles")
    kept = state[-1]
    tied = lax.optimization_barrier((kept, *cross_vec.values()))
    kept = tied[0]
    cross_vec = dict(zip(cross_vec, tied[1:]))

    def window_of(own, mate, crossed, far):
        found = {0: own, blocks_dev: mate, group * blocks_dev: far}
        for rel, value in crossed.items():
            found[rel * blocks_dev] = value
            found[(rel ^ 1) * blocks_dev] = swap(value, "grp", 1)
        return found

    def beyond(vecs):
        return {place: value for place, value in vecs.items() if place >= home}

    vecs = window_of(vec, mate_vec, cross_vec, far_vec)
    urgent = urgent_ranges(group, blocks_dev)
    height = columns + 8
    at_home, *results = products(
        entries,
        (0,),
        {0: vec, blocks_dev: mate_vec},
        kept,
        (),
        [[(0, blocks_dev)]] + urgent,
        height,
        1,
    )
    results = products(entries, (1,), beyond(vecs), kept, results, urgent, height, 1)
    sums, (at_home,) = send_urgent(results, (at_home,), group, blocks_dev)
    sums = finish_home(entries, beyond(vecs), kept, at_home, blocks_dev, height, 1) + sums
    z, gram, parts, degree = scaled_gram(sums, vec, counts, None, None)

    far_part = from_behind(parts, "blk", -1)
    crossed = gather_far_bits(parts)
    mate_part = swap(parts, "grp", 1)
    at_home, *results = products(
        entries,
        (0,),
        {0: parts, blocks_dev: mate_part},
        kept,
        (),
        [[(0, blocks_dev)]] + urgent,
        columns,
        2,
    )
    at_home, *tied = lax.optimization_barrier((at_home, *crossed.values()))
    crossed = dict(zip(crossed, tied))
    vecs = beyond(window_of(parts, mate_part, crossed, far_part))
    results = products(entries, (1,), vecs, kept, results, urgent, columns, 2)
    sums, (at_home,) = send_urgent(results, (at_home,), group, blocks_dev)
    sums = finish_home(entries, vecs, kept, at_home, blocks_dev, columns, 2) + sums
    z, grams = scaled_gram(sums, z, counts, degree, gram)

    stages = sum_stages()
    stages = stages[:1] + pairs_of(stages[1:])
    both, first, sound = factors(all_sum(grams, stages))

    def at_once(both, first, z):
        return both

    def in_two(both, first, z):
        return second_factor(all_sum(applied(first, z, True)[1], stages), first)

    return applied(lax.cond(sound[0] == 1, at_once, in_two, both, first, z), z, False)[0]


def solution(mesh):
    in_specs = (
        P(("blk", "grp"), None),
        P(("blk", "grp")),
        P("blk"),
        P("blk"),
        P("blk"),
        P(None, ("blk", "grp")),
    )
    out_specs = P(None, ("blk", "grp"))
    return jax.shard_map(
        per_device, mesh=mesh, in_specs=in_specs, out_specs=out_specs, check_vma=False
    )
```

```python
import functools

import jax
import jax.numpy as jnp
from jax import lax
from jax.experimental import pallas as pl
from jax.experimental.pallas import tpu as pltpu
from jax.sharding import PartitionSpec as P

PTS = 512
LOG2E = 1.4426950408889634
DEAD = 65536.0
EXTRA = 16
HOME_EARLY, HOME_LAST, FROM_SLAB, FROM_FAR, TO_OWN = range(5)
KINDS = 5
VMEM = pltpu.VMEM
SMEM = pltpu.SMEM
HIGHEST = lax.Precision.HIGHEST


def cost(flops, moved):
    return pl.CostEstimate(flops=int(flops), bytes_accessed=int(moved), transcendentals=0)


def spec(space):
    return pl.BlockSpec(memory_space=space)


def swap(value, axis, bit):
    count = lax.axis_size(axis)
    return lax.ppermute(value, axis, [(source, source ^ bit) for source in range(count)])


def from_behind(value, axis, steps):
    count = lax.axis_size(axis)
    initial, last = (max(0, -steps), min(count, count - steps))
    return lax.ppermute(value, axis, [(source, source + steps) for source in range(initial, last)])


def bits_of(count):
    bits = []
    bit = 1
    while bit < count:
        bits.append(bit)
        bit *= 2
    return bits


def gather_near(value, axis):
    held = {0: value}
    for bit in reversed(bits_of(lax.axis_size(axis))):
        for rel in list(held):
            held[rel ^ bit] = swap(held[rel], axis, bit)
    return [held[rel] for rel in range(len(held))]


def gather_far_bits(value):
    held = {0: value}
    for bit in reversed(bits_of(lax.axis_size("grp"))[1:]):
        for rel in list(held):
            held[rel ^ bit] = swap(held[rel], "grp", bit)
    held.pop(0)
    return held


def opening_kernel(start, counts, out):
    columns, total = start.shape
    for block in range(total // PTS):
        lanes = slice(block * PTS, (block + 1) * PTS)
        used = lax.broadcasted_iota(jnp.int32, (columns, PTS), 1) < counts[block]
        out[0:columns, lanes] = jnp.where(used, start[:, lanes], 0.0).astype(jnp.bfloat16)
        which = lax.broadcasted_iota(jnp.int32, (EXTRA, PTS), 0)
        place_in = lax.broadcasted_iota(jnp.int32, (EXTRA, PTS), 1)
        ones = jnp.logical_and(which == 0, place_in < counts[block])
        out[columns : columns + EXTRA, lanes] = jnp.where(ones, 1.0, 0.0).astype(jnp.bfloat16)


def opening(start, counts):
    columns, total = start.shape
    return pl.pallas_call(
        opening_kernel,
        out_shape=jax.ShapeDtypeStruct((columns + EXTRA, total), jnp.bfloat16),
        in_specs=[spec(VMEM), spec(SMEM)],
        out_specs=spec(VMEM),
        cost_estimate=cost(2**20, 2**19),
        compiler_params=pltpu.CompilerParams(vmem_limit_bytes=2 * 2**20),
        name="opening",
    )(start, counts)


def stage_of(place, group, blocks_dev):
    piece = lax.div(place, blocks_dev)
    first_half = lax.rem(place, blocks_dev) < blocks_dev // 2
    later = jnp.where(first_half, jnp.where(lax.rem(piece, 2) == 0, 0, 1), 2)
    return jnp.where(piece < min(2, group), 0, later)


def listing_kernel(
    group,
    cap,
    blocks_dev,
    rows,
    cols,
    live,
    out_rows,
    out_cols,
    out_n,
    tiles,
    sources,
    targets,
    bounds,
    owners,
):
    slab = blocks_dev * group
    slots = rows.shape[0]
    member = lax.axis_index("grp")

    def local_near(block, device):
        return (lax.div(block, blocks_dev) ^ device) * blocks_dev + lax.rem(block, blocks_dev)

    def local_far(block):
        return slab + lax.rem(block - slab, blocks_dev)

    def count_far(slot, carry):
        col = cols[slot]
        far = jnp.logical_and(slot < live[0], col >= slab)
        owner = lax.div(col - slab, blocks_dev)
        owners[slot] = jnp.where(far, owner, -1)
        return tuple(
            old + jnp.where(jnp.logical_and(far, owner == device), 1, 0)
            for device, old in enumerate(carry)
        )

    loads = lax.fori_loop(0, slots, count_far, (jnp.int32(0),) * group)

    def give(slot, loads):
        row, col = rows[slot], cols[slot]
        near = jnp.logical_and(slot < live[0], col < slab)
        best = jnp.int32(2**30)
        owner = jnp.int32(0)
        for device in range(group):
            stage = jnp.maximum(
                stage_of(local_near(row, device), group, blocks_dev),
                stage_of(local_near(col, device), group, blocks_dev),
            )
            score = loads[device] + 64 * stage + jnp.where(loads[device] < cap, 0, 2**20)
            owner = jnp.where(score < best, device, owner)
            best = jnp.minimum(score, best)

        @pl.when(near)
        def _():
            owners[slot] = owner

        return tuple(
            load + jnp.where(jnp.logical_and(near, owner == device), 1, 0)
            for device, load in enumerate(loads)
        )

    lax.fori_loop(0, slots, give, loads)

    def place_those(wanted, filled):
        def place(slot, filled):
            row, col = rows[slot], cols[slot]
            row_place = local_near(row, member)
            col_place = jnp.where(col >= slab, local_far(col), local_near(col, member))
            stage = jnp.maximum(
                stage_of(row_place, group, blocks_dev), stage_of(col_place, group, blocks_dev)
            )
            mine = jnp.logical_and(owners[slot] == member, stage == wanted)

            @pl.when(mine)
            def _():
                out_rows[filled] = row_place
                out_cols[filled] = col_place

            return filled + jnp.where(mine, 1, 0)

        return lax.fori_loop(0, slots, place, filled)

    count = jnp.int32(0)
    out_n[0] = count
    for wanted in range(3):
        count = place_those(wanted, count)
        out_n[wanted + 1] = count

    home = min(2, group) * blocks_dev
    bounds[0] = jnp.int32(0)
    filled = jnp.int32(0)
    for kind in range(KINDS):
        for to_row in (True, False):

            def enter(index, filled):
                source = (out_cols if to_row else out_rows)[index]
                target = (out_rows if to_row else out_cols)[index]
                own_target = jnp.logical_and(source >= home, target < blocks_dev)
                other_target = jnp.logical_and(source >= home, target >= blocks_dev)
                if kind == HOME_EARLY:
                    wanted = jnp.logical_and(source < home, index < out_n[2])
                elif kind == HOME_LAST:
                    wanted = jnp.logical_and(source < home, index >= out_n[2])
                elif kind == FROM_SLAB:
                    wanted = jnp.logical_and(other_target, source < slab)
                elif kind == FROM_FAR:
                    wanted = jnp.logical_and(other_target, source >= slab)
                else:
                    wanted = own_target

                @pl.when(wanted)
                def _():
                    tiles[filled] = index
                    sources[filled] = source
                    targets[filled] = target

                return filled + jnp.where(wanted, 1, 0)

            filled = lax.fori_loop(0, count, enter, filled)
            bounds[2 * kind + (1 if to_row else 2)] = filled


def listing(rows, cols, live, group, cap, blocks_dev):
    return pl.pallas_call(
        functools.partial(listing_kernel, group, cap, blocks_dev),
        out_shape=(
            jax.ShapeDtypeStruct((cap,), jnp.int32),
            jax.ShapeDtypeStruct((cap,), jnp.int32),
            jax.ShapeDtypeStruct((4,), jnp.int32),
            jax.ShapeDtypeStruct((2 * cap,), jnp.int32),
            jax.ShapeDtypeStruct((2 * cap,), jnp.int32),
            jax.ShapeDtypeStruct((2 * cap,), jnp.int32),
            jax.ShapeDtypeStruct((2 * KINDS + 1,), jnp.int32),
        ),
        in_specs=[spec(SMEM)] * 3,
        out_specs=(spec(SMEM),) * 7,
        scratch_shapes=[SMEM((rows.shape[0],), jnp.int32)],
        cost_estimate=cost(2**20, 2**10),
        compiler_params=pltpu.CompilerParams(vmem_limit_bytes=2**20),
        name="listing",
    )(rows, cols, live)


def set_levels(place, window, level_row, level_col, scale):
    block = window[place * PTS : (place + 1) * PTS, :]
    width = block.shape[1]
    part = jnp.zeros((PTS, 128), jnp.float32)
    for lane in range(0, width, 128):
        wide = block[:, lane : lane + 128].astype(jnp.float32)
        part = part + wide * wide
    level_row[place] = scale * lax.dot_general(
        jnp.ones((8, 128), jnp.float32),
        part,
        (((1,), (1,)), ((), ())),
        precision=HIGHEST,
        preferred_element_type=jnp.float32,
    )
    if place < level_col.shape[0]:
        total = jnp.sum(part, axis=1, keepdims=True) * scale
        level_col[place] = jnp.broadcast_to(total, (PTS, 128))


def make_tiles(low, high, rows, cols, window, level_row, level_col, kept, buffers):
    width = window.shape[1]
    scale = 6.0 / width * LOG2E
    count = high - low
    spare = kept.shape[0] - 1

    def cross(tile, buffer):
        index = low + jnp.minimum(tile, count - 1)
        left = window[pl.ds(pl.multiple_of(rows[index] * PTS, PTS), PTS), :]
        right = window[pl.ds(pl.multiple_of(cols[index] * PTS, PTS), PTS), :]
        buffer[...] = lax.dot_general(
            left, right, (((1,), (1,)), ((), ())), preferred_element_type=jnp.float32
        )

    def finish(tile, buffer):
        valid = jnp.logical_and(tile >= 0, tile < count)
        index = low + jnp.clip(tile, 0, count - 1)
        row, col = rows[index], cols[index]
        right_level = level_row[col][0:1, :]
        left_level = jnp.concatenate([level_col[row]] * (PTS // 128), axis=1)
        value = jnp.exp2(buffer[...] * scale - left_level - right_level)
        kept[jnp.where(valid, index, spare)] = value.astype(jnp.bfloat16)

    def body(pair, carry):
        cross(2 * pair, buffers[0])
        finish(2 * pair - 1, buffers[1])
        cross(2 * pair + 1, buffers[1])
        finish(2 * pair, buffers[0])
        return carry

    @pl.when(count > 0)
    def _():
        buffers[1][...] = jnp.zeros((PTS, PTS), jnp.float32)

    lax.fori_loop(0, jnp.where(count > 0, lax.div(count, 2) + 1, 0), body, 0)


def build_tiles(stage, fresh, n, rows, cols, state, group, blocks_dev, cap, name):
    places = list(fresh)
    pts = list(fresh.values())
    width = pts[0].shape[1]
    total = (group + 1) * blocks_dev
    near = group * blocks_dev
    shapes = [
        jax.ShapeDtypeStruct((total * PTS, width), jnp.bfloat16),
        jax.ShapeDtypeStruct((total, 8, PTS), jnp.float32),
        jax.ShapeDtypeStruct((near, PTS, 128), jnp.float32),
    ]
    makes = stage is not None
    if makes:
        shapes.append(jax.ShapeDtypeStruct((cap + 1, PTS, PTS), jnp.bfloat16))
    state = state[: len(shapes)]
    scalars = (n, rows, cols) if makes else ()
    first = len(scalars) + len(pts)

    def kernel(*refs):
        pt_refs = refs[len(scalars) : first]
        window, level_row, level_col, *rest = refs[first + len(state) :]
        for place, piece in zip(places, pt_refs):
            blocks = piece.shape[0] // PTS
            window[place * PTS : (place + blocks) * PTS, :] = piece[...]
            for block in range(place, place + blocks):
                set_levels(block, window, level_row, level_col, 3.0 / width * LOG2E)
        if makes:
            n_ref, row_ref, col_ref = refs[:3]
            kept, *buffers = rest
            make_tiles(
                n_ref[stage],
                n_ref[stage + 1],
                row_ref,
                col_ref,
                window,
                level_row,
                level_col,
                kept,
                buffers,
            )

    return pl.pallas_call(
        kernel,
        out_shape=shapes,
        in_specs=[spec(SMEM)] * len(scalars) + [spec(VMEM)] * (len(pts) + len(state)),
        out_specs=[spec(VMEM)] * len(shapes),
        input_output_aliases={first + index: index for index in range(len(state))},
        scratch_shapes=[VMEM((PTS, PTS), jnp.float32)] * (2 if makes else 0),
        cost_estimate=cost(2**32 if stage == 2 else 2**20, 2**20),
        compiler_params=pltpu.CompilerParams(vmem_limit_bytes=6 * 2**20),
        name=name,
    )(*scalars, *pts, *state)


def products(entries, kinds, vecs, tiles, start, targets, height, folds):
    firsts = sorted(vecs)
    tall, held = vecs[firsts[0]].shape
    blocks_dev = held // PTS
    begun = list(start)
    source_low, source_high = firsts[0], firsts[-1] + blocks_dev
    low = min(first for ranges in targets for first, _ in ranges)
    high = max(last for ranges in targets for _, last in ranges)
    shapes = [
        jax.ShapeDtypeStruct((sum(last - first for first, last in ranges), height, PTS), jnp.float32)
        for ranges in targets
    ]

    def pieces(refs):
        for ranges, ref in zip(targets, refs):
            at = 0
            for first, last in ranges:
                yield ref, slice(at, at + last - first), slice(first - low, last - low)
                at += last - first

    def fold(value):
        out = value[:height]
        for index in range(1, folds):
            out = out + value[index * height : (index + 1) * height]
        return out

    def kernel(*refs):
        tile_ref, source_ref, target_ref, bounds = refs[:4]
        vec_refs = refs[4 : 4 + len(firsts)]
        kept = refs[4 + len(firsts)]
        start_refs = refs[5 + len(firsts) : 5 + len(firsts) + len(begun)]
        outs = refs[5 + len(firsts) + len(begun) : -2]
        u_win, acc = refs[-2:]
        for first, ref in zip(firsts, vec_refs):
            for block in range(blocks_dev):
                lanes = slice(block * PTS, (block + 1) * PTS)
                u_win[first - source_low + block] = ref[:, lanes]
        if begun:
            for ref, inside, places in pieces(start_refs):
                acc[places] = ref[inside]
        else:
            for place in range(high - low + 1):
                acc[place] = jnp.zeros((height, PTS), jnp.float32)

        spare = high - low
        unroll = 4

        def several(begin, end, transposed):
            def body(step, carry):
                done = []
                for lane in range(unroll):
                    index = begin + step * unroll + lane
                    valid = index < end
                    index = jnp.minimum(index, end - 1)
                    vec = u_win[source_ref[index] - source_low]
                    tile = kept[tile_ref[index]]
                    if transposed:
                        value = lax.dot_general(
                            vec,
                            tile,
                            (((1,), (1,)), ((), ())),
                            preferred_element_type=jnp.float32,
                        )
                    else:
                        value = jnp.dot(vec, tile, preferred_element_type=jnp.float32)
                    done.append((jnp.where(valid, target_ref[index] - low, spare), fold(value)))
                for target, value in done:
                    acc[target] += value
                return carry

            lax.fori_loop(0, lax.div(end - begin + unroll - 1, unroll), body, 0)

        for kind in kinds:
            several(bounds[2 * kind], bounds[2 * kind + 1], True)
            several(bounds[2 * kind + 1], bounds[2 * kind + 2], False)
        for out, inside, places in pieces(outs):
            out[inside] = acc[places]

    call = pl.pallas_call(
        kernel,
        out_shape=shapes,
        in_specs=[spec(SMEM)] * 4 + [spec(VMEM)] * (len(firsts) + 1 + len(begun)),
        out_specs=[spec(VMEM)] * len(shapes),
        scratch_shapes=[
            VMEM((source_high - source_low, tall, PTS), jnp.bfloat16),
            VMEM((high - low + 1, height, PTS), jnp.float32),
        ],
        cost_estimate=cost(2**31 if FROM_FAR in kinds else 2**20, 2**20),
        compiler_params=pltpu.CompilerParams(vmem_limit_bytes=10 * 2**20),
        name="products",
    )
    return list(call(*entries, *[vecs[first] for first in firsts], tiles, *begun))


def urgent_ranges(group, blocks_dev):
    messages = [
        [rel for rel in range(group) if rel & bit and rel % bit == 0] for bit in bits_of(group)
    ]
    return [
        [(rel * blocks_dev, (rel + 1) * blocks_dev) for rel in rels]
        for rels in messages + [[group]]
    ]


def send_urgent(results, later, group, blocks_dev):
    final = []
    *messages, far = results
    parts = {}
    behind = None
    for bit, message in zip(bits_of(group), messages):
        rels = [rel for rel in range(group) if rel & bit and rel % bit == 0]
        for index, rel in enumerate(rels):
            if rel in parts:
                held = message[index * blocks_dev : (index + 1) * blocks_dev]
                message = held + parts[rel] if len(rels) == 1 else message.at[
                    index * blocks_dev : (index + 1) * blocks_dev
                ].add(parts[rel])
        if bit > 1:
            message, *later = lax.optimization_barrier((message, *later))
        got = swap(message, "grp", bit)
        if behind is None:
            got, far = lax.optimization_barrier((got, far))
            behind = from_behind(far, "blk", 1)
        final.append(got)
        for index, rel in enumerate(rels):
            if rel ^ bit:
                piece = got[index * blocks_dev : (index + 1) * blocks_dev]
                parts[rel ^ bit] = parts[rel ^ bit] + piece if rel ^ bit in parts else piece
    if behind is None:
        behind = from_behind(far, "blk", 1)
    return [behind] + final, later


def finish_home(entries, vecs, tiles, start, blocks_dev, height, folds):
    return products(entries, (TO_OWN,), vecs, tiles, [start], [[(0, blocks_dev)]], height, folds)


def scaled_gram(parts, own, counts, degree, earlier):
    columns = own.shape[0] if degree is not None else own.shape[0] - EXTRA
    total = own.shape[1]
    first = degree is None
    shapes = [
        jax.ShapeDtypeStruct((columns, total), jnp.float32),
        jax.ShapeDtypeStruct((columns, columns * (1 if first else 2)), jnp.float32),
    ]
    if first:
        shapes.append(jax.ShapeDtypeStruct((2 * columns, total), jnp.bfloat16))
        shapes.append(jax.ShapeDtypeStruct((8, total), jnp.float32))
    operands = list(parts) + [own]
    operands += [] if first else [degree, earlier]

    def kernel(count_ref, *refs):
        ins = list(refs[: len(operands)])
        outs = list(refs[len(operands) :])
        part_refs = ins[: len(parts)]
        own_ref = ins[len(parts)]
        z_out, gram_out = outs[:2]
        gram = jnp.zeros((columns, columns), jnp.float32)
        for block in range(total // PTS):
            lanes = slice(block * PTS, (block + 1) * PTS)
            sums = part_refs[0][block]
            for part in part_refs[1:]:
                sums = sums + part[block]
            if first:
                level = 1.0 + sums[columns : columns + 1, :]
                outs[-1][:, lanes] = jnp.broadcast_to(level, (8, PTS))
            else:
                level = ins[len(parts) + 1][0:1, lanes]
            used = lax.broadcasted_iota(jnp.int32, (columns, PTS), 1) < count_ref[block]
            held = own_ref[0:columns, lanes].astype(jnp.float32)
            z = (held + jnp.where(used, sums[0:columns], 0.0)) / level
            z_out[:, lanes] = z
            if first:
                high = z.astype(jnp.bfloat16)
                outs[2][0:columns, lanes] = high
                rest = z - high.astype(jnp.float32)
                outs[2][columns : 2 * columns, lanes] = rest.astype(jnp.bfloat16)
            gram = gram + lax.dot_general(
                z, z, (((1,), (1,)), ((), ())), precision=HIGHEST, preferred_element_type=jnp.float32
            )
        if not first:
            gram = jnp.concatenate([ins[-1][...], gram], axis=1)
        gram_out[...] = gram

    return pl.pallas_call(
        kernel,
        out_shape=tuple(shapes),
        in_specs=[spec(SMEM)] + [spec(VMEM)] * len(operands),
        out_specs=(spec(VMEM),) * len(shapes),
        cost_estimate=cost(2**26, 2**21),
        compiler_params=pltpu.CompilerParams(vmem_limit_bytes=6 * 2**20),
        name="scaled_gram",
    )(counts, *operands)


def inverse_factor(gram):
    size = gram.shape[0]
    row_id = lax.broadcasted_iota(jnp.int32, (size, size), 0)
    col_id = lax.broadcasted_iota(jnp.int32, (size, size), 1)
    eye = jnp.where(row_id == col_id, 1.0, 0.0)
    whole = jnp.concatenate([gram, eye], axis=1)
    wide = 2 * size
    count = size // 8
    groups = [whole[8 * g : 8 * g + 8, :] for g in range(count)]
    within = lax.broadcasted_iota(jnp.int32, (8, wide), 0)

    def spread_row(value, row):
        return jnp.broadcast_to(value[row : row + 1, :], (8, wide))

    results = []
    for g in range(count):
        spread = [
            [
                jnp.broadcast_to(groups[other][:, 8 * g + k : 8 * g + k + 1], (8, wide))
                for other in range(g, count)
            ]
            for k in range(8)
        ]
        pivots = jnp.ones((8, wide), jnp.float32)
        for j in range(8):
            column = spread[j]
            pivot = spread_row(column[0], j)
            pivots = jnp.where(within == j, pivot, pivots)
            over = 1.0 / pivot
            below = jnp.where(within > j, column[0], 0.0)
            for k in range(j + 1, 8):
                share = spread_row(column[0], k) * over
                spread[k][0] = spread[k][0] - below * share
                for other in range(1, count - g):
                    spread[k][other] = spread[k][other] - column[other] * share
            top = spread_row(groups[g], j) * over
            groups[g] = groups[g] - below * top
            for other in range(1, count - g):
                groups[g + other] = groups[g + other] - column[other] * top
        results.append(groups[g] * lax.rsqrt(pivots))
    return jnp.concatenate(results, axis=0)[:, size:wide]


def exact_dot(left, right, contract):
    return lax.dot_general(
        left,
        right,
        (contract, ((), ())),
        precision=HIGHEST,
        preferred_element_type=jnp.float32,
    )


def factors_kernel(grams, both_out, first_out, sound_out):
    columns = grams.shape[0]
    plain = ((1,), (0,))
    turned = ((1,), (1,))
    second = grams[:, columns : 2 * columns]
    first_inverse = inverse_factor(grams[:, 0:columns])
    middle = exact_dot(exact_dot(first_inverse, second, plain), first_inverse, turned)
    both = exact_dot(inverse_factor(middle), first_inverse, plain)
    both_out[...] = both
    first_out[...] = first_inverse
    row_id = lax.broadcasted_iota(jnp.int32, (columns, columns), 0)
    col_id = lax.broadcasted_iota(jnp.int32, (columns, columns), 1)
    trace = jnp.sum(jnp.where(row_id == col_id, second, 0.0))
    spread = jnp.sum(both * both) * trace / (columns * columns)
    sound_out[0] = jnp.where(spread < 64.0, 1, 0)


def factors(grams):
    columns = grams.shape[0]
    square = jax.ShapeDtypeStruct((columns, columns), jnp.float32)
    return pl.pallas_call(
        factors_kernel,
        out_shape=(square, square, jax.ShapeDtypeStruct((1,), jnp.int32)),
        in_specs=[spec(VMEM)],
        out_specs=(spec(VMEM), spec(VMEM), spec(SMEM)),
        cost_estimate=cost(2**30, 2**16),
        compiler_params=pltpu.CompilerParams(vmem_limit_bytes=2 * 2**20),
        name="factors",
    )(grams)


def apply_kernel(factor, z, out, *gram):
    value = exact_dot(factor[...], z[...], ((1,), (0,)))
    out[...] = value
    if gram:
        gram[0][...] = exact_dot(value, value, ((1,), (1,)))


def applied(factor, z, with_gram):
    shapes = [jax.ShapeDtypeStruct(z.shape, jnp.float32)]
    if with_gram:
        shapes.append(jax.ShapeDtypeStruct(factor.shape, jnp.float32))
    return pl.pallas_call(
        apply_kernel,
        out_shape=shapes,
        in_specs=[spec(VMEM)] * 2,
        out_specs=[spec(VMEM)] * len(shapes),
        compiler_params=pltpu.CompilerParams(vmem_limit_bytes=4 * 2**20),
        name="applied",
    )(factor, z)


def second_kernel(gram, first, out):
    out[...] = exact_dot(inverse_factor(gram[...]), first[...], ((1,), (0,)))


def second_factor(gram, first):
    return pl.pallas_call(
        second_kernel,
        out_shape=jax.ShapeDtypeStruct(gram.shape, jnp.float32),
        in_specs=[spec(VMEM)] * 2,
        out_specs=spec(VMEM),
        compiler_params=pltpu.CompilerParams(vmem_limit_bytes=2 * 2**20),
        name="second_factor",
    )(gram, first)


def sum_stages():
    return bits_of(lax.axis_size("blk") * lax.axis_size("grp"))


def pairs_of(bits):
    return [bits[first : first + 2] for first in range(0, len(bits), 2)]


def all_sum(value, stages, beside=None):
    count = lax.axis_size("blk") * lax.axis_size("grp")
    for bits in stages:
        moves = [0]
        for bit in bits if isinstance(bits, list) else [bits]:
            moves += [move ^ bit for move in moves]
        terms = [value] + [
            lax.ppermute(value, ("blk", "grp"), [(source, source ^ move) for source in range(count)])
            for move in moves[1:]
        ]
        if beside is not None:
            terms[0], beside = lax.optimization_barrier((terms[0], beside))
        while len(terms) > 1:
            terms = [left + right for left, right in zip(terms[::2], terms[1::2])]
        value = terms[0]
    return value if beside is None else (value, beside)


def per_device(points, counts, pair_rows, pair_cols, pair_live, start):
    group = lax.axis_size("grp")
    blocks_dev = counts.shape[0]
    columns = start.shape[0]
    slots = pair_rows.shape[0]
    cap = max(-(-slots // group), blocks_dev * blocks_dev * group)
    half = (blocks_dev // 2) * PTS

    home = min(2, group) * blocks_dev

    rows, cols, n, *entries = listing(
        pair_rows, pair_cols, pair_live, group, cap, blocks_dev
    )
    mate = swap(points, "grp", 1)
    chunks = [points[:half], points[half:]]
    far = [from_behind(chunk, "blk", -1) for chunk in chunks]
    crossed = [gather_far_bits(chunk) for chunk in chunks]
    begin, mate = lax.optimization_barrier((start, mate))
    vec = opening(begin, counts)
    tied = lax.optimization_barrier((vec, n, rows, cols, far[0], *crossed[0].values()))
    vec, n, rows, cols, far[0] = tied[:5]
    crossed[0] = dict(zip(crossed[0], tied[5:]))
    cross_vec = gather_far_bits(vec)
    far_vec = from_behind(vec, "blk", -1)
    mate_vec = swap(vec, "grp", 1)

    def direct(index):
        offset = index * (blocks_dev // 2)
        found = {group * blocks_dev + offset: far[index]}
        for rel, value in crossed[index].items():
            found[rel * blocks_dev + offset] = value
        return found

    def passed_on(index):
        offset = index * (blocks_dev // 2)
        found = {}
        for rel, value in crossed[index].items():
            cut = value.shape[0] // (1 if index else 2)
            parts = [swap(value[at : at + cut], "grp", 1) for at in range(0, value.shape[0], cut)]
            found[(rel ^ 1) * blocks_dev + offset] = jnp.concatenate(parts, 0)
        return found

    def build(stage, fresh, state, name):
        return list(
            build_tiles(stage, fresh, n, rows, cols, state, group, blocks_dev, cap, name)
        )

    state = build(0, {0: points, blocks_dev: mate, **direct(0)}, (), "first_tiles")
    state = build(1, passed_on(0), state, "second_tiles")
    urgent = urgent_ranges(group, blocks_dev)
    ranges = [[(0, blocks_dev)]] + urgent
    height = columns + 8
    vecs_home = {0: vec, blocks_dev: mate_vec}
    begun = products(entries, (HOME_EARLY,), vecs_home, state[3], (), ranges, height, 1)
    tied = lax.optimization_barrier((far[1], begun[0], state[1], *crossed[1].values()))
    far[1], begun[0], state[1] = tied[:3]
    crossed[1] = dict(zip(crossed[1], tied[3:]))
    last = passed_on(1)
    *grown, kept = state
    state = build(None, direct(1), grown, "more_blocks") + [kept]
    state = build(2, last, state, "last_tiles")
    kept = state[-1]
    tied = lax.optimization_barrier((kept, *cross_vec.values()))
    kept = tied[0]
    cross_vec = dict(zip(cross_vec, tied[1:]))

    def window_of(own, mate, crossed, far):
        found = {0: own, blocks_dev: mate, group * blocks_dev: far}
        for rel, value in crossed.items():
            found[rel * blocks_dev] = value
            found[(rel ^ 1) * blocks_dev] = swap(value, "grp", 1)
        return found

    def beyond(vecs):
        return {place: value for place, value in vecs.items() if place >= home}

    vecs = window_of(vec, mate_vec, cross_vec, far_vec)
    at_home, *results = products(
        entries, (HOME_LAST,), vecs_home, kept, begun, ranges, height, 1
    )
    results = products(
        entries, (FROM_SLAB, FROM_FAR), beyond(vecs), kept, results, urgent, height, 1
    )
    sums, (at_home,) = send_urgent(results, (at_home,), group, blocks_dev)
    sums = finish_home(entries, beyond(vecs), kept, at_home, blocks_dev, height, 1) + sums
    z, gram, parts, degree = scaled_gram(sums, vec, counts, None, None)

    far_part = from_behind(parts, "blk", -1)
    crossed = gather_far_bits(parts)
    mate_part = swap(parts, "grp", 1)
    at_home, *results = products(
        entries,
        (HOME_EARLY, HOME_LAST),
        {0: parts, blocks_dev: mate_part},
        kept,
        (),
        ranges,
        columns,
        2,
    )
    at_home, *tied = lax.optimization_barrier((at_home, *crossed.values()))
    crossed = dict(zip(crossed, tied))
    vecs = beyond(window_of(parts, mate_part, crossed, far_part))
    results = products(
        entries, (FROM_SLAB, FROM_FAR), vecs, kept, results, urgent, columns, 2
    )
    sums, (at_home,) = send_urgent(results, (at_home,), group, blocks_dev)
    sums = finish_home(entries, vecs, kept, at_home, blocks_dev, columns, 2) + sums
    z, grams = scaled_gram(sums, z, counts, degree, gram)

    stages = sum_stages()
    stages = stages[:1] + pairs_of(stages[1:])
    both, first, sound = factors(all_sum(grams, stages))

    def at_once(both, first, z):
        return both

    def in_two(both, first, z):
        return second_factor(all_sum(applied(first, z, True)[1], stages), first)

    return applied(lax.cond(sound[0] == 1, at_once, in_two, both, first, z), z, False)[0]


def solution(mesh):
    in_specs = (
        P(("blk", "grp"), None),
        P(("blk", "grp")),
        P("blk"),
        P("blk"),
        P("blk"),
        P(None, ("blk", "grp")),
    )
    out_specs = P(None, ("blk", "grp"))
    return jax.shard_map(
        per_device, mesh=mesh, in_specs=in_specs, out_specs=out_specs, check_vma=False
    )
```

```python
import functools

import jax
import jax.numpy as jnp
from jax import lax
from jax.experimental import pallas as pl
from jax.experimental.pallas import tpu as pltpu
from jax.sharding import PartitionSpec as P

PTS = 512
LOG2E = 1.4426950408889634
DEAD = 65536.0
EXTRA = 16
HOME_EARLY, HOME_LAST, TO_OTHERS, TO_OWN = range(4)
KINDS = 4
VMEM = pltpu.VMEM
SMEM = pltpu.SMEM
HIGHEST = lax.Precision.HIGHEST


def cost(flops, moved):
    return pl.CostEstimate(flops=int(flops), bytes_accessed=int(moved), transcendentals=0)


def spec(space):
    return pl.BlockSpec(memory_space=space)


def swap(value, axis, bit):
    count = lax.axis_size(axis)
    return lax.ppermute(value, axis, [(source, source ^ bit) for source in range(count)])


def from_behind(value, axis, steps):
    count = lax.axis_size(axis)
    initial, last = (max(0, -steps), min(count, count - steps))
    return lax.ppermute(value, axis, [(source, source + steps) for source in range(initial, last)])


def bits_of(count):
    bits = []
    bit = 1
    while bit < count:
        bits.append(bit)
        bit *= 2
    return bits


def gather_near(value, axis):
    held = {0: value}
    for bit in reversed(bits_of(lax.axis_size(axis))):
        for rel in list(held):
            held[rel ^ bit] = swap(held[rel], axis, bit)
    return [held[rel] for rel in range(len(held))]


def gather_far_bits(value):
    held = {0: value}
    for bit in reversed(bits_of(lax.axis_size("grp"))[1:]):
        for rel in list(held):
            held[rel ^ bit] = swap(held[rel], "grp", bit)
    held.pop(0)
    return held


def opening_kernel(start, counts, out):
    columns, total = start.shape
    for block in range(total // PTS):
        lanes = slice(block * PTS, (block + 1) * PTS)
        used = lax.broadcasted_iota(jnp.int32, (columns, PTS), 1) < counts[block]
        out[0:columns, lanes] = jnp.where(used, start[:, lanes], 0.0).astype(jnp.bfloat16)
        which = lax.broadcasted_iota(jnp.int32, (EXTRA, PTS), 0)
        place_in = lax.broadcasted_iota(jnp.int32, (EXTRA, PTS), 1)
        ones = jnp.logical_and(which == 0, place_in < counts[block])
        out[columns : columns + EXTRA, lanes] = jnp.where(ones, 1.0, 0.0).astype(jnp.bfloat16)


def opening(start, counts):
    columns, total = start.shape
    return pl.pallas_call(
        opening_kernel,
        out_shape=jax.ShapeDtypeStruct((columns + EXTRA, total), jnp.bfloat16),
        in_specs=[spec(VMEM), spec(SMEM)],
        out_specs=spec(VMEM),
        cost_estimate=cost(2**20, 2**19),
        compiler_params=pltpu.CompilerParams(vmem_limit_bytes=2 * 2**20),
        name="opening",
    )(start, counts)


def stage_of(place, group, blocks_dev):
    piece = lax.div(place, blocks_dev)
    first_half = lax.rem(place, blocks_dev) < blocks_dev // 2
    later = jnp.where(first_half, jnp.where(lax.rem(piece, 2) == 0, 0, 1), 2)
    return jnp.where(piece < min(2, group), 0, later)


def listing_kernel(
    group,
    cap,
    blocks_dev,
    rows,
    cols,
    live,
    out_rows,
    out_cols,
    out_n,
    tiles,
    sources,
    targets,
    bounds,
    owners,
):
    slab = blocks_dev * group
    slots = rows.shape[0]
    member = lax.axis_index("grp")

    def local_near(block, device):
        return (lax.div(block, blocks_dev) ^ device) * blocks_dev + lax.rem(block, blocks_dev)

    def local_far(block):
        return slab + lax.rem(block - slab, blocks_dev)

    def count_far(slot, carry):
        col = cols[slot]
        far = jnp.logical_and(slot < live[0], col >= slab)
        owner = lax.div(col - slab, blocks_dev)
        owners[slot] = jnp.where(far, owner, -1)
        return tuple(
            old + jnp.where(jnp.logical_and(far, owner == device), 1, 0)
            for device, old in enumerate(carry)
        )

    loads = lax.fori_loop(0, slots, count_far, (jnp.int32(0),) * group)

    def give(slot, loads):
        row, col = rows[slot], cols[slot]
        near = jnp.logical_and(slot < live[0], col < slab)
        best = jnp.int32(2**30)
        owner = jnp.int32(0)
        for device in range(group):
            stage = jnp.maximum(
                stage_of(local_near(row, device), group, blocks_dev),
                stage_of(local_near(col, device), group, blocks_dev),
            )
            score = loads[device] + 64 * stage + jnp.where(loads[device] < cap, 0, 2**20)
            owner = jnp.where(score < best, device, owner)
            best = jnp.minimum(score, best)

        @pl.when(near)
        def _():
            owners[slot] = owner

        return tuple(
            load + jnp.where(jnp.logical_and(near, owner == device), 1, 0)
            for device, load in enumerate(loads)
        )

    lax.fori_loop(0, slots, give, loads)

    def place_those(wanted, filled):
        def place(slot, filled):
            row, col = rows[slot], cols[slot]
            row_place = local_near(row, member)
            col_place = jnp.where(col >= slab, local_far(col), local_near(col, member))
            stage = jnp.maximum(
                stage_of(row_place, group, blocks_dev), stage_of(col_place, group, blocks_dev)
            )
            mine = jnp.logical_and(owners[slot] == member, stage == wanted)

            @pl.when(mine)
            def _():
                out_rows[filled] = row_place
                out_cols[filled] = col_place

            return filled + jnp.where(mine, 1, 0)

        return lax.fori_loop(0, slots, place, filled)

    count = jnp.int32(0)
    out_n[0] = count
    for wanted in range(3):
        count = place_those(wanted, count)
        out_n[wanted + 1] = count

    home = min(2, group) * blocks_dev
    bounds[0] = jnp.int32(0)
    filled = jnp.int32(0)
    for kind in range(KINDS):
        for to_row in (True, False):

            def enter(index, filled):
                source = (out_cols if to_row else out_rows)[index]
                target = (out_rows if to_row else out_cols)[index]
                own_target = jnp.logical_and(source >= home, target < blocks_dev)
                other_target = jnp.logical_and(source >= home, target >= blocks_dev)
                if kind == HOME_EARLY:
                    wanted = jnp.logical_and(source < home, index < out_n[2])
                elif kind == HOME_LAST:
                    wanted = jnp.logical_and(source < home, index >= out_n[2])
                elif kind == TO_OTHERS:
                    wanted = other_target
                else:
                    wanted = own_target

                @pl.when(wanted)
                def _():
                    tiles[filled] = index
                    sources[filled] = source
                    targets[filled] = target

                return filled + jnp.where(wanted, 1, 0)

            filled = lax.fori_loop(0, count, enter, filled)
            bounds[2 * kind + (1 if to_row else 2)] = filled


def listing(rows, cols, live, group, cap, blocks_dev):
    return pl.pallas_call(
        functools.partial(listing_kernel, group, cap, blocks_dev),
        out_shape=(
            jax.ShapeDtypeStruct((cap,), jnp.int32),
            jax.ShapeDtypeStruct((cap,), jnp.int32),
            jax.ShapeDtypeStruct((4,), jnp.int32),
            jax.ShapeDtypeStruct((2 * cap,), jnp.int32),
            jax.ShapeDtypeStruct((2 * cap,), jnp.int32),
            jax.ShapeDtypeStruct((2 * cap,), jnp.int32),
            jax.ShapeDtypeStruct((2 * KINDS + 1,), jnp.int32),
        ),
        in_specs=[spec(SMEM)] * 3,
        out_specs=(spec(SMEM),) * 7,
        scratch_shapes=[SMEM((rows.shape[0],), jnp.int32)],
        cost_estimate=cost(2**20, 2**10),
        compiler_params=pltpu.CompilerParams(vmem_limit_bytes=2**20),
        name="listing",
    )(rows, cols, live)


def set_levels(place, window, level_row, level_col, scale):
    block = window[place * PTS : (place + 1) * PTS, :]
    width = block.shape[1]
    part = jnp.zeros((PTS, 128), jnp.float32)
    for lane in range(0, width, 128):
        wide = block[:, lane : lane + 128].astype(jnp.float32)
        part = part + wide * wide
    level_row[place] = scale * lax.dot_general(
        jnp.ones((8, 128), jnp.float32),
        part,
        (((1,), (1,)), ((), ())),
        precision=HIGHEST,
        preferred_element_type=jnp.float32,
    )
    if place < level_col.shape[0]:
        total = jnp.sum(part, axis=1, keepdims=True) * scale
        level_col[place] = jnp.broadcast_to(total, (PTS, 128))


def make_tiles(low, high, rows, cols, window, level_row, level_col, kept, buffers):
    width = window.shape[1]
    scale = 6.0 / width * LOG2E
    count = high - low
    spare = kept.shape[0] - 1

    def cross(tile, buffer):
        index = low + jnp.minimum(tile, count - 1)
        left = window[pl.ds(pl.multiple_of(rows[index] * PTS, PTS), PTS), :]
        right = window[pl.ds(pl.multiple_of(cols[index] * PTS, PTS), PTS), :]
        buffer[...] = lax.dot_general(
            left, right, (((1,), (1,)), ((), ())), preferred_element_type=jnp.float32
        )

    def finish(tile, buffer):
        valid = jnp.logical_and(tile >= 0, tile < count)
        index = low + jnp.clip(tile, 0, count - 1)
        row, col = rows[index], cols[index]
        right_level = level_row[col][0:1, :]
        left_level = jnp.concatenate([level_col[row]] * (PTS // 128), axis=1)
        value = jnp.exp2(buffer[...] * scale - left_level - right_level)
        kept[jnp.where(valid, index, spare)] = value.astype(jnp.bfloat16)

    def body(pair, carry):
        cross(2 * pair, buffers[0])
        finish(2 * pair - 1, buffers[1])
        cross(2 * pair + 1, buffers[1])
        finish(2 * pair, buffers[0])
        return carry

    @pl.when(count > 0)
    def _():
        buffers[1][...] = jnp.zeros((PTS, PTS), jnp.float32)

    lax.fori_loop(0, jnp.where(count > 0, lax.div(count, 2) + 1, 0), body, 0)


def build_tiles(stage, fresh, n, rows, cols, state, group, blocks_dev, cap, name):
    places = list(fresh)
    pts = list(fresh.values())
    width = pts[0].shape[1]
    total = (group + 1) * blocks_dev
    near = group * blocks_dev
    shapes = [
        jax.ShapeDtypeStruct((total * PTS, width), jnp.bfloat16),
        jax.ShapeDtypeStruct((total, 8, PTS), jnp.float32),
        jax.ShapeDtypeStruct((near, PTS, 128), jnp.float32),
    ]
    makes = stage is not None
    if makes:
        shapes.append(jax.ShapeDtypeStruct((cap + 1, PTS, PTS), jnp.bfloat16))
    state = state[: len(shapes)]
    scalars = (n, rows, cols) if makes else ()
    first = len(scalars) + len(pts)

    def kernel(*refs):
        pt_refs = refs[len(scalars) : first]
        window, level_row, level_col, *rest = refs[first + len(state) :]
        for place, piece in zip(places, pt_refs):
            blocks = piece.shape[0] // PTS
            window[place * PTS : (place + blocks) * PTS, :] = piece[...]
            for block in range(place, place + blocks):
                set_levels(block, window, level_row, level_col, 3.0 / width * LOG2E)
        if makes:
            n_ref, row_ref, col_ref = refs[:3]
            kept, *buffers = rest
            make_tiles(
                n_ref[stage],
                n_ref[stage + 1],
                row_ref,
                col_ref,
                window,
                level_row,
                level_col,
                kept,
                buffers,
            )

    return pl.pallas_call(
        kernel,
        out_shape=shapes,
        in_specs=[spec(SMEM)] * len(scalars) + [spec(VMEM)] * (len(pts) + len(state)),
        out_specs=[spec(VMEM)] * len(shapes),
        input_output_aliases={first + index: index for index in range(len(state))},
        scratch_shapes=[VMEM((PTS, PTS), jnp.float32)] * (2 if makes else 0),
        cost_estimate=cost(2**32 if stage == 2 else 2**20, 2**20),
        compiler_params=pltpu.CompilerParams(vmem_limit_bytes=6 * 2**20),
        name=name,
    )(*scalars, *pts, *state)


def products(entries, kinds, vecs, tiles, start, targets, height, folds):
    firsts = sorted(vecs)
    tall, held = vecs[firsts[0]].shape
    blocks_dev = held // PTS
    begun = list(start)
    source_low, source_high = firsts[0], firsts[-1] + blocks_dev
    low = min(first for ranges in targets for first, _ in ranges)
    high = max(last for ranges in targets for _, last in ranges)
    shapes = [
        jax.ShapeDtypeStruct((sum(last - first for first, last in ranges), height, PTS), jnp.float32)
        for ranges in targets
    ]

    def pieces(refs):
        for ranges, ref in zip(targets, refs):
            at = 0
            for first, last in ranges:
                yield ref, slice(at, at + last - first), slice(first - low, last - low)
                at += last - first

    def fold(value):
        out = value[:height]
        for index in range(1, folds):
            out = out + value[index * height : (index + 1) * height]
        return out

    def kernel(*refs):
        tile_ref, source_ref, target_ref, bounds = refs[:4]
        vec_refs = refs[4 : 4 + len(firsts)]
        kept = refs[4 + len(firsts)]
        start_refs = refs[5 + len(firsts) : 5 + len(firsts) + len(begun)]
        outs = refs[5 + len(firsts) + len(begun) : -2]
        u_win, acc = refs[-2:]
        for first, ref in zip(firsts, vec_refs):
            for block in range(blocks_dev):
                lanes = slice(block * PTS, (block + 1) * PTS)
                u_win[first - source_low + block] = ref[:, lanes]
        if begun:
            for ref, inside, places in pieces(start_refs):
                acc[places] = ref[inside]
        else:
            for place in range(high - low + 1):
                acc[place] = jnp.zeros((height, PTS), jnp.float32)

        spare = high - low
        unroll = 4

        def several(begin, end, transposed):
            def body(step, carry):
                done = []
                for lane in range(unroll):
                    index = begin + step * unroll + lane
                    valid = index < end
                    index = jnp.minimum(index, end - 1)
                    vec = u_win[source_ref[index] - source_low]
                    tile = kept[tile_ref[index]]
                    if transposed:
                        value = lax.dot_general(
                            vec,
                            tile,
                            (((1,), (1,)), ((), ())),
                            preferred_element_type=jnp.float32,
                        )
                    else:
                        value = jnp.dot(vec, tile, preferred_element_type=jnp.float32)
                    done.append((jnp.where(valid, target_ref[index] - low, spare), fold(value)))
                for target, value in done:
                    acc[target] += value
                return carry

            lax.fori_loop(0, lax.div(end - begin + unroll - 1, unroll), body, 0)

        for kind in kinds:
            several(bounds[2 * kind], bounds[2 * kind + 1], True)
            several(bounds[2 * kind + 1], bounds[2 * kind + 2], False)
        for out, inside, places in pieces(outs):
            out[inside] = acc[places]

    call = pl.pallas_call(
        kernel,
        out_shape=shapes,
        in_specs=[spec(SMEM)] * 4 + [spec(VMEM)] * (len(firsts) + 1 + len(begun)),
        out_specs=[spec(VMEM)] * len(shapes),
        scratch_shapes=[
            VMEM((source_high - source_low, tall, PTS), jnp.bfloat16),
            VMEM((high - low + 1, height, PTS), jnp.float32),
        ],
        cost_estimate=cost(2**31 if TO_OTHERS in kinds else 2**20, 2**20),
        compiler_params=pltpu.CompilerParams(vmem_limit_bytes=10 * 2**20),
        name="products",
    )
    return list(call(*entries, *[vecs[first] for first in firsts], tiles, *begun))


def urgent_ranges(group, blocks_dev):
    messages = [
        [rel for rel in range(group) if rel & bit and rel % bit == 0] for bit in bits_of(group)
    ]
    return [
        [(rel * blocks_dev, (rel + 1) * blocks_dev) for rel in rels]
        for rels in messages + [[group]]
    ]


def send_urgent(results, later, group, blocks_dev):
    final = []
    *messages, far = results
    parts = {}
    behind = None
    for bit, message in zip(bits_of(group), messages):
        rels = [rel for rel in range(group) if rel & bit and rel % bit == 0]
        for index, rel in enumerate(rels):
            if rel in parts:
                held = message[index * blocks_dev : (index + 1) * blocks_dev]
                message = held + parts[rel] if len(rels) == 1 else message.at[
                    index * blocks_dev : (index + 1) * blocks_dev
                ].add(parts[rel])
        if bit > 1:
            message, *later = lax.optimization_barrier((message, *later))
        got = swap(message, "grp", bit)
        if behind is None:
            got, far = lax.optimization_barrier((got, far))
            behind = from_behind(far, "blk", 1)
        final.append(got)
        for index, rel in enumerate(rels):
            if rel ^ bit:
                piece = got[index * blocks_dev : (index + 1) * blocks_dev]
                parts[rel ^ bit] = parts[rel ^ bit] + piece if rel ^ bit in parts else piece
    if behind is None:
        behind = from_behind(far, "blk", 1)
    return [behind] + final, later


def finish_home(entries, vecs, tiles, start, blocks_dev, height, folds):
    return products(entries, (TO_OWN,), vecs, tiles, [start], [[(0, blocks_dev)]], height, folds)


def scaled_gram(parts, own, counts, degree, earlier):
    columns = own.shape[0] if degree is not None else own.shape[0] - EXTRA
    total = own.shape[1]
    first = degree is None
    shapes = [
        jax.ShapeDtypeStruct((columns, total), jnp.float32),
        jax.ShapeDtypeStruct((columns, columns * (1 if first else 2)), jnp.float32),
    ]
    if first:
        shapes.append(jax.ShapeDtypeStruct((2 * columns, total), jnp.bfloat16))
        shapes.append(jax.ShapeDtypeStruct((8, total), jnp.float32))
    operands = list(parts) + [own]
    operands += [] if first else [degree, earlier]

    def kernel(count_ref, *refs):
        ins = list(refs[: len(operands)])
        outs = list(refs[len(operands) :])
        part_refs = ins[: len(parts)]
        own_ref = ins[len(parts)]
        z_out, gram_out = outs[:2]
        gram = jnp.zeros((columns, columns), jnp.float32)
        for block in range(total // PTS):
            lanes = slice(block * PTS, (block + 1) * PTS)
            sums = part_refs[0][block]
            for part in part_refs[1:]:
                sums = sums + part[block]
            if first:
                level = 1.0 + sums[columns : columns + 1, :]
                outs[-1][:, lanes] = jnp.broadcast_to(level, (8, PTS))
            else:
                level = ins[len(parts) + 1][0:1, lanes]
            used = lax.broadcasted_iota(jnp.int32, (columns, PTS), 1) < count_ref[block]
            held = own_ref[0:columns, lanes].astype(jnp.float32)
            z = (held + jnp.where(used, sums[0:columns], 0.0)) / level
            z_out[:, lanes] = z
            if first:
                high = z.astype(jnp.bfloat16)
                outs[2][0:columns, lanes] = high
                rest = z - high.astype(jnp.float32)
                outs[2][columns : 2 * columns, lanes] = rest.astype(jnp.bfloat16)
            gram = gram + lax.dot_general(
                z, z, (((1,), (1,)), ((), ())), precision=HIGHEST, preferred_element_type=jnp.float32
            )
        if not first:
            gram = jnp.concatenate([ins[-1][...], gram], axis=1)
        gram_out[...] = gram

    return pl.pallas_call(
        kernel,
        out_shape=tuple(shapes),
        in_specs=[spec(SMEM)] + [spec(VMEM)] * len(operands),
        out_specs=(spec(VMEM),) * len(shapes),
        cost_estimate=cost(2**26, 2**21),
        compiler_params=pltpu.CompilerParams(vmem_limit_bytes=6 * 2**20),
        name="scaled_gram",
    )(counts, *operands)


def inverse_factor(gram):
    size = gram.shape[0]
    row_id = lax.broadcasted_iota(jnp.int32, (size, size), 0)
    col_id = lax.broadcasted_iota(jnp.int32, (size, size), 1)
    eye = jnp.where(row_id == col_id, 1.0, 0.0)
    whole = jnp.concatenate([gram, eye], axis=1)
    wide = 2 * size
    count = size // 8
    groups = [whole[8 * g : 8 * g + 8, :] for g in range(count)]
    within = lax.broadcasted_iota(jnp.int32, (8, wide), 0)

    def spread_row(value, row):
        return jnp.broadcast_to(value[row : row + 1, :], (8, wide))

    results = []
    for g in range(count):
        spread = [
            [
                jnp.broadcast_to(groups[other][:, 8 * g + k : 8 * g + k + 1], (8, wide))
                for other in range(g, count)
            ]
            for k in range(8)
        ]
        pivots = jnp.ones((8, wide), jnp.float32)
        for j in range(8):
            column = spread[j]
            pivot = spread_row(column[0], j)
            pivots = jnp.where(within == j, pivot, pivots)
            over = 1.0 / pivot
            below = jnp.where(within > j, column[0], 0.0)
            for k in range(j + 1, 8):
                share = spread_row(column[0], k) * over
                spread[k][0] = spread[k][0] - below * share
                for other in range(1, count - g):
                    spread[k][other] = spread[k][other] - column[other] * share
            top = spread_row(groups[g], j) * over
            groups[g] = groups[g] - below * top
            for other in range(1, count - g):
                groups[g + other] = groups[g + other] - column[other] * top
        results.append(groups[g] * lax.rsqrt(pivots))
    return jnp.concatenate(results, axis=0)[:, size:wide]


def exact_dot(left, right, contract):
    return lax.dot_general(
        left,
        right,
        (contract, ((), ())),
        precision=HIGHEST,
        preferred_element_type=jnp.float32,
    )


def factors_kernel(grams, both_out, first_out, sound_out):
    columns = grams.shape[0]
    plain = ((1,), (0,))
    turned = ((1,), (1,))
    second = grams[:, columns : 2 * columns]
    first_inverse = inverse_factor(grams[:, 0:columns])
    middle = exact_dot(exact_dot(first_inverse, second, plain), first_inverse, turned)
    both = exact_dot(inverse_factor(middle), first_inverse, plain)
    both_out[...] = both
    first_out[...] = first_inverse
    row_id = lax.broadcasted_iota(jnp.int32, (columns, columns), 0)
    col_id = lax.broadcasted_iota(jnp.int32, (columns, columns), 1)
    trace = jnp.sum(jnp.where(row_id == col_id, second, 0.0))
    spread = jnp.sum(both * both) * trace / (columns * columns)
    sound_out[0] = jnp.where(spread < 64.0, 1, 0)


def factors(grams):
    columns = grams.shape[0]
    square = jax.ShapeDtypeStruct((columns, columns), jnp.float32)
    return pl.pallas_call(
        factors_kernel,
        out_shape=(square, square, jax.ShapeDtypeStruct((1,), jnp.int32)),
        in_specs=[spec(VMEM)],
        out_specs=(spec(VMEM), spec(VMEM), spec(SMEM)),
        cost_estimate=cost(2**30, 2**16),
        compiler_params=pltpu.CompilerParams(vmem_limit_bytes=2 * 2**20),
        name="factors",
    )(grams)


def apply_kernel(factor, z, out, *gram):
    value = exact_dot(factor[...], z[...], ((1,), (0,)))
    out[...] = value
    if gram:
        gram[0][...] = exact_dot(value, value, ((1,), (1,)))


def applied(factor, z, with_gram):
    shapes = [jax.ShapeDtypeStruct(z.shape, jnp.float32)]
    if with_gram:
        shapes.append(jax.ShapeDtypeStruct(factor.shape, jnp.float32))
    return pl.pallas_call(
        apply_kernel,
        out_shape=shapes,
        in_specs=[spec(VMEM)] * 2,
        out_specs=[spec(VMEM)] * len(shapes),
        compiler_params=pltpu.CompilerParams(vmem_limit_bytes=4 * 2**20),
        name="applied",
    )(factor, z)


def second_kernel(gram, first, out):
    out[...] = exact_dot(inverse_factor(gram[...]), first[...], ((1,), (0,)))


def second_factor(gram, first):
    return pl.pallas_call(
        second_kernel,
        out_shape=jax.ShapeDtypeStruct(gram.shape, jnp.float32),
        in_specs=[spec(VMEM)] * 2,
        out_specs=spec(VMEM),
        compiler_params=pltpu.CompilerParams(vmem_limit_bytes=2 * 2**20),
        name="second_factor",
    )(gram, first)


def sum_stages():
    return bits_of(lax.axis_size("blk") * lax.axis_size("grp"))


def pairs_of(bits):
    return [bits[first : first + 2] for first in range(0, len(bits), 2)]


def all_sum(value, stages, beside=None):
    count = lax.axis_size("blk") * lax.axis_size("grp")
    for bits in stages:
        moves = [0]
        for bit in bits if isinstance(bits, list) else [bits]:
            moves += [move ^ bit for move in moves]
        terms = [value] + [
            lax.ppermute(value, ("blk", "grp"), [(source, source ^ move) for source in range(count)])
            for move in moves[1:]
        ]
        if beside is not None:
            terms[0], beside = lax.optimization_barrier((terms[0], beside))
        while len(terms) > 1:
            terms = [left + right for left, right in zip(terms[::2], terms[1::2])]
        value = terms[0]
    return value if beside is None else (value, beside)


def per_device(points, counts, pair_rows, pair_cols, pair_live, start):
    group = lax.axis_size("grp")
    blocks_dev = counts.shape[0]
    columns = start.shape[0]
    slots = pair_rows.shape[0]
    cap = max(-(-slots // group), blocks_dev * blocks_dev * group)
    half = (blocks_dev // 2) * PTS

    home = min(2, group) * blocks_dev

    rows, cols, n, *entries = listing(
        pair_rows, pair_cols, pair_live, group, cap, blocks_dev
    )
    mate = swap(points, "grp", 1)
    chunks = [points[:half], points[half:]]
    far = [from_behind(chunk, "blk", -1) for chunk in chunks]
    crossed = [gather_far_bits(chunk) for chunk in chunks]
    begin, mate = lax.optimization_barrier((start, mate))
    vec = opening(begin, counts)
    tied = lax.optimization_barrier((vec, n, rows, cols, far[0], *crossed[0].values()))
    vec, n, rows, cols, far[0] = tied[:5]
    crossed[0] = dict(zip(crossed[0], tied[5:]))
    cross_vec = gather_far_bits(vec)
    far_vec = from_behind(vec, "blk", -1)
    mate_vec = swap(vec, "grp", 1)

    def direct(index):
        offset = index * (blocks_dev // 2)
        found = {group * blocks_dev + offset: far[index]}
        for rel, value in crossed[index].items():
            found[rel * blocks_dev + offset] = value
        return found

    def passed_on(index):
        offset = index * (blocks_dev // 2)
        found = {}
        for rel, value in crossed[index].items():
            cut = value.shape[0] // (1 if index else 2)
            parts = [swap(value[at : at + cut], "grp", 1) for at in range(0, value.shape[0], cut)]
            found[(rel ^ 1) * blocks_dev + offset] = jnp.concatenate(parts, 0)
        return found

    def build(stage, fresh, state, name):
        return list(
            build_tiles(stage, fresh, n, rows, cols, state, group, blocks_dev, cap, name)
        )

    state = build(0, {0: points, blocks_dev: mate, **direct(0)}, (), "first_tiles")
    state = build(1, passed_on(0), state, "second_tiles")
    urgent = urgent_ranges(group, blocks_dev)
    ranges = [[(0, blocks_dev)]] + urgent
    height = columns + 8
    vecs_home = {0: vec, blocks_dev: mate_vec}
    begun = products(entries, (HOME_EARLY,), vecs_home, state[3], (), ranges, height, 1)
    tied = lax.optimization_barrier((far[1], begun[0], state[1], *crossed[1].values()))
    far[1], begun[0], state[1] = tied[:3]
    crossed[1] = dict(zip(crossed[1], tied[3:]))
    last = passed_on(1)
    *grown, kept = state
    state = build(None, direct(1), grown, "more_blocks") + [kept]
    state = build(2, last, state, "last_tiles")
    kept = state[-1]
    tied = lax.optimization_barrier((kept, *cross_vec.values()))
    kept = tied[0]
    cross_vec = dict(zip(cross_vec, tied[1:]))

    def window_of(own, mate, crossed, far):
        found = {0: own, blocks_dev: mate, group * blocks_dev: far}
        for rel, value in crossed.items():
            found[rel * blocks_dev] = value
            found[(rel ^ 1) * blocks_dev] = swap(value, "grp", 1)
        return found

    def beyond(vecs):
        return {place: value for place, value in vecs.items() if place >= home}

    vecs = window_of(vec, mate_vec, cross_vec, far_vec)
    at_home, *results = products(
        entries, (HOME_LAST,), vecs_home, kept, begun, ranges, height, 1
    )
    results = products(entries, (TO_OTHERS,), beyond(vecs), kept, results, urgent, height, 1)
    sums, (at_home,) = send_urgent(results, (at_home,), group, blocks_dev)
    sums = finish_home(entries, beyond(vecs), kept, at_home, blocks_dev, height, 1) + sums
    z, gram, parts, degree = scaled_gram(sums, vec, counts, None, None)

    far_part = from_behind(parts, "blk", -1)
    crossed = gather_far_bits(parts)
    mate_part = swap(parts, "grp", 1)
    at_home, *results = products(
        entries,
        (HOME_EARLY, HOME_LAST),
        {0: parts, blocks_dev: mate_part},
        kept,
        (),
        ranges,
        columns,
        2,
    )
    at_home, *tied = lax.optimization_barrier((at_home, *crossed.values()))
    crossed = dict(zip(crossed, tied))
    vecs = beyond(window_of(parts, mate_part, crossed, far_part))
    results = products(entries, (TO_OTHERS,), vecs, kept, results, urgent, columns, 2)
    sums, (at_home,) = send_urgent(results, (at_home,), group, blocks_dev)
    sums = finish_home(entries, vecs, kept, at_home, blocks_dev, columns, 2) + sums
    z, grams = scaled_gram(sums, z, counts, degree, gram)

    stages = sum_stages()
    stages = stages[:1] + pairs_of(stages[1:])
    both, first, sound = factors(all_sum(grams, stages))

    def at_once(both, first, z):
        return both

    def in_two(both, first, z):
        return second_factor(all_sum(applied(first, z, True)[1], stages), first)

    return applied(lax.cond(sound[0] == 1, at_once, in_two, both, first, z), z, False)[0]


def solution(mesh):
    in_specs = (
        P(("blk", "grp"), None),
        P(("blk", "grp")),
        P("blk"),
        P("blk"),
        P("blk"),
        P(None, ("blk", "grp")),
    )
    out_specs = P(None, ("blk", "grp"))
    return jax.shard_map(
        per_device, mesh=mesh, in_specs=in_specs, out_specs=out_specs, check_vma=False
    )
```

```python
import functools

import jax
import jax.numpy as jnp
from jax import lax
from jax.experimental import pallas as pl
from jax.experimental.pallas import tpu as pltpu
from jax.sharding import PartitionSpec as P

PTS = 512
LOG2E = 1.4426950408889634
DEAD = 65536.0
EXTRA = 16
HOME_EARLY, HOME_LAST, TO_OTHERS, TO_OWN = range(4)
KINDS = 4
VMEM = pltpu.VMEM
SMEM = pltpu.SMEM
HIGHEST = lax.Precision.HIGHEST


def cost(flops, moved):
    return pl.CostEstimate(flops=int(flops), bytes_accessed=int(moved), transcendentals=0)


def spec(space):
    return pl.BlockSpec(memory_space=space)


def swap(value, axis, bit):
    count = lax.axis_size(axis)
    return lax.ppermute(value, axis, [(source, source ^ bit) for source in range(count)])


def from_behind(value, axis, steps):
    count = lax.axis_size(axis)
    initial, last = (max(0, -steps), min(count, count - steps))
    return lax.ppermute(value, axis, [(source, source + steps) for source in range(initial, last)])


def bits_of(count):
    bits = []
    bit = 1
    while bit < count:
        bits.append(bit)
        bit *= 2
    return bits


def gather_near(value, axis):
    held = {0: value}
    for bit in reversed(bits_of(lax.axis_size(axis))):
        for rel in list(held):
            held[rel ^ bit] = swap(held[rel], axis, bit)
    return [held[rel] for rel in range(len(held))]


def gather_far_bits(value):
    held = {0: value}
    for bit in reversed(bits_of(lax.axis_size("grp"))[1:]):
        for rel in list(held):
            held[rel ^ bit] = swap(held[rel], "grp", bit)
    held.pop(0)
    return held


def opening_kernel(start, counts, out):
    columns, total = start.shape
    for block in range(total // PTS):
        lanes = slice(block * PTS, (block + 1) * PTS)
        used = lax.broadcasted_iota(jnp.int32, (columns, PTS), 1) < counts[block]
        out[0:columns, lanes] = jnp.where(used, start[:, lanes], 0.0).astype(jnp.bfloat16)
        which = lax.broadcasted_iota(jnp.int32, (EXTRA, PTS), 0)
        place_in = lax.broadcasted_iota(jnp.int32, (EXTRA, PTS), 1)
        ones = jnp.logical_and(which == 0, place_in < counts[block])
        out[columns : columns + EXTRA, lanes] = jnp.where(ones, 1.0, 0.0).astype(jnp.bfloat16)


def opening(start, counts):
    columns, total = start.shape
    return pl.pallas_call(
        opening_kernel,
        out_shape=jax.ShapeDtypeStruct((columns + EXTRA, total), jnp.bfloat16),
        in_specs=[spec(VMEM), spec(SMEM)],
        out_specs=spec(VMEM),
        cost_estimate=cost(2**20, 2**19),
        compiler_params=pltpu.CompilerParams(vmem_limit_bytes=2 * 2**20),
        name="opening",
    )(start, counts)


def stage_of(place, group, blocks_dev):
    piece = lax.div(place, blocks_dev)
    first_half = lax.rem(place, blocks_dev) < blocks_dev // 2
    later = jnp.where(first_half, jnp.where(lax.rem(piece, 2) == 0, 0, 1), 2)
    return jnp.where(piece < min(2, group), 0, later)


def listing_kernel(
    group,
    cap,
    blocks_dev,
    rows,
    cols,
    live,
    out_rows,
    out_cols,
    out_n,
    tiles,
    sources,
    targets,
    bounds,
    owners,
):
    slab = blocks_dev * group
    slots = rows.shape[0]
    member = lax.axis_index("grp")

    def local_near(block, device):
        return (lax.div(block, blocks_dev) ^ device) * blocks_dev + lax.rem(block, blocks_dev)

    def local_far(block):
        return slab + lax.rem(block - slab, blocks_dev)

    def count_far(slot, carry):
        col = cols[slot]
        far = jnp.logical_and(slot < live[0], col >= slab)
        owner = lax.div(col - slab, blocks_dev)
        owners[slot] = jnp.where(far, owner, -1)
        return tuple(
            old + jnp.where(jnp.logical_and(far, owner == device), 1, 0)
            for device, old in enumerate(carry)
        )

    loads = lax.fori_loop(0, slots, count_far, (jnp.int32(0),) * group)

    def give(slot, loads):
        row, col = rows[slot], cols[slot]
        near = jnp.logical_and(slot < live[0], col < slab)
        best = jnp.int32(2**30)
        owner = jnp.int32(0)
        for device in range(group):
            stage = jnp.maximum(
                stage_of(local_near(row, device), group, blocks_dev),
                stage_of(local_near(col, device), group, blocks_dev),
            )
            score = loads[device] + 64 * stage + jnp.where(loads[device] < cap, 0, 2**20)
            owner = jnp.where(score < best, device, owner)
            best = jnp.minimum(score, best)

        @pl.when(near)
        def _():
            owners[slot] = owner

        return tuple(
            load + jnp.where(jnp.logical_and(near, owner == device), 1, 0)
            for device, load in enumerate(loads)
        )

    lax.fori_loop(0, slots, give, loads)

    def place_those(wanted, filled):
        def place(slot, filled):
            row, col = rows[slot], cols[slot]
            row_place = local_near(row, member)
            col_place = jnp.where(col >= slab, local_far(col), local_near(col, member))
            stage = jnp.maximum(
                stage_of(row_place, group, blocks_dev), stage_of(col_place, group, blocks_dev)
            )
            mine = jnp.logical_and(owners[slot] == member, stage == wanted)

            @pl.when(mine)
            def _():
                out_rows[filled] = row_place
                out_cols[filled] = col_place

            return filled + jnp.where(mine, 1, 0)

        return lax.fori_loop(0, slots, place, filled)

    count = jnp.int32(0)
    out_n[0] = count
    for wanted in range(3):
        count = place_those(wanted, count)
        out_n[wanted + 1] = count

    home = min(2, group) * blocks_dev
    bounds[0] = jnp.int32(0)
    filled = jnp.int32(0)
    for kind in range(KINDS):
        for to_row in (True, False):

            def enter(index, filled):
                source = (out_cols if to_row else out_rows)[index]
                target = (out_rows if to_row else out_cols)[index]
                own_target = jnp.logical_and(source >= home, target < blocks_dev)
                other_target = jnp.logical_and(source >= home, target >= blocks_dev)
                if kind == HOME_EARLY:
                    wanted = jnp.logical_and(source < home, index < out_n[2])
                elif kind == HOME_LAST:
                    wanted = jnp.logical_and(source < home, index >= out_n[2])
                elif kind == TO_OTHERS:
                    wanted = other_target
                else:
                    wanted = own_target

                @pl.when(wanted)
                def _():
                    tiles[filled] = index
                    sources[filled] = source
                    targets[filled] = target

                return filled + jnp.where(wanted, 1, 0)

            filled = lax.fori_loop(0, count, enter, filled)
            bounds[2 * kind + (1 if to_row else 2)] = filled


def listing(rows, cols, live, group, cap, blocks_dev):
    return pl.pallas_call(
        functools.partial(listing_kernel, group, cap, blocks_dev),
        out_shape=(
            jax.ShapeDtypeStruct((cap,), jnp.int32),
            jax.ShapeDtypeStruct((cap,), jnp.int32),
            jax.ShapeDtypeStruct((4,), jnp.int32),
            jax.ShapeDtypeStruct((2 * cap,), jnp.int32),
            jax.ShapeDtypeStruct((2 * cap,), jnp.int32),
            jax.ShapeDtypeStruct((2 * cap,), jnp.int32),
            jax.ShapeDtypeStruct((2 * KINDS + 1,), jnp.int32),
        ),
        in_specs=[spec(SMEM)] * 3,
        out_specs=(spec(SMEM),) * 7,
        scratch_shapes=[SMEM((rows.shape[0],), jnp.int32)],
        cost_estimate=cost(2**20, 2**10),
        compiler_params=pltpu.CompilerParams(vmem_limit_bytes=2**20),
        name="listing",
    )(rows, cols, live)


def set_levels(place, window, level_row, level_col, scale):
    block = window[place * PTS : (place + 1) * PTS, :]
    width = block.shape[1]
    part = jnp.zeros((PTS, 128), jnp.float32)
    for lane in range(0, width, 128):
        wide = block[:, lane : lane + 128].astype(jnp.float32)
        part = part + wide * wide
    level_row[place] = scale * lax.dot_general(
        jnp.ones((8, 128), jnp.float32),
        part,
        (((1,), (1,)), ((), ())),
        precision=HIGHEST,
        preferred_element_type=jnp.float32,
    )
    if place < level_col.shape[0]:
        total = jnp.sum(part, axis=1, keepdims=True) * scale
        level_col[place] = jnp.broadcast_to(total, (PTS, 128))


def make_tiles(low, high, rows, cols, window, level_row, level_col, kept, buffers):
    width = window.shape[1]
    scale = 6.0 / width * LOG2E
    count = high - low
    spare = kept.shape[0] - 1

    def cross(tile, buffer):
        index = low + jnp.minimum(tile, count - 1)
        left = window[pl.ds(pl.multiple_of(rows[index] * PTS, PTS), PTS), :]
        right = window[pl.ds(pl.multiple_of(cols[index] * PTS, PTS), PTS), :]
        buffer[...] = lax.dot_general(
            left, right, (((1,), (1,)), ((), ())), preferred_element_type=jnp.float32
        )

    def finish(tile, buffer):
        valid = jnp.logical_and(tile >= 0, tile < count)
        index = low + jnp.clip(tile, 0, count - 1)
        row, col = rows[index], cols[index]
        right_level = level_row[col][0:1, :]
        left_level = jnp.concatenate([level_col[row]] * (PTS // 128), axis=1)
        value = jnp.exp2(buffer[...] * scale - left_level - right_level)
        kept[jnp.where(valid, index, spare)] = value.astype(jnp.bfloat16)

    def body(pair, carry):
        cross(2 * pair, buffers[0])
        finish(2 * pair - 1, buffers[1])
        cross(2 * pair + 1, buffers[1])
        finish(2 * pair, buffers[0])
        return carry

    @pl.when(count > 0)
    def _():
        buffers[1][...] = jnp.zeros((PTS, PTS), jnp.float32)

    lax.fori_loop(0, jnp.where(count > 0, lax.div(count, 2) + 1, 0), body, 0)


def build_tiles(stage, fresh, n, rows, cols, state, group, blocks_dev, cap, name):
    places = list(fresh)
    pts = list(fresh.values())
    width = pts[0].shape[1]
    total = (group + 1) * blocks_dev
    near = group * blocks_dev
    shapes = [
        jax.ShapeDtypeStruct((total * PTS, width), jnp.bfloat16),
        jax.ShapeDtypeStruct((total, 8, PTS), jnp.float32),
        jax.ShapeDtypeStruct((near, PTS, 128), jnp.float32),
    ]
    makes = stage is not None
    if makes:
        shapes.append(jax.ShapeDtypeStruct((cap + 1, PTS, PTS), jnp.bfloat16))
    state = state[: len(shapes)]
    scalars = (n, rows, cols) if makes else ()
    first = len(scalars) + len(pts)

    def kernel(*refs):
        pt_refs = refs[len(scalars) : first]
        window, level_row, level_col, *rest = refs[first + len(state) :]
        for place, piece in zip(places, pt_refs):
            blocks = piece.shape[0] // PTS
            window[place * PTS : (place + blocks) * PTS, :] = piece[...]
            for block in range(place, place + blocks):
                set_levels(block, window, level_row, level_col, 3.0 / width * LOG2E)
        if makes:
            n_ref, row_ref, col_ref = refs[:3]
            kept, *buffers = rest
            make_tiles(
                n_ref[stage],
                n_ref[stage + 1],
                row_ref,
                col_ref,
                window,
                level_row,
                level_col,
                kept,
                buffers,
            )

    return pl.pallas_call(
        kernel,
        out_shape=shapes,
        in_specs=[spec(SMEM)] * len(scalars) + [spec(VMEM)] * (len(pts) + len(state)),
        out_specs=[spec(VMEM)] * len(shapes),
        input_output_aliases={first + index: index for index in range(len(state))},
        scratch_shapes=[VMEM((PTS, PTS), jnp.float32)] * (2 if makes else 0),
        cost_estimate=cost(2**32 if stage == 2 else 2**20, 2**20),
        compiler_params=pltpu.CompilerParams(vmem_limit_bytes=6 * 2**20),
        name=name,
    )(*scalars, *pts, *state)


def products(entries, kinds, vecs, tiles, start, targets, height, folds):
    firsts = sorted(vecs)
    tall, held = vecs[firsts[0]].shape
    blocks_dev = held // PTS
    begun = list(start)
    source_low, source_high = firsts[0], firsts[-1] + blocks_dev
    low = min(first for ranges in targets for first, _ in ranges)
    high = max(last for ranges in targets for _, last in ranges)
    shapes = [
        jax.ShapeDtypeStruct((sum(last - first for first, last in ranges), height, PTS), jnp.float32)
        for ranges in targets
    ]

    def pieces(refs):
        for ranges, ref in zip(targets, refs):
            at = 0
            for first, last in ranges:
                yield ref, slice(at, at + last - first), slice(first - low, last - low)
                at += last - first

    def fold(value):
        out = value[:height]
        for index in range(1, folds):
            out = out + value[index * height : (index + 1) * height]
        return out

    def kernel(*refs):
        tile_ref, source_ref, target_ref, bounds = refs[:4]
        vec_refs = refs[4 : 4 + len(firsts)]
        kept = refs[4 + len(firsts)]
        start_refs = refs[5 + len(firsts) : 5 + len(firsts) + len(begun)]
        outs = refs[5 + len(firsts) + len(begun) : -2]
        u_win, acc = refs[-2:]
        for first, ref in zip(firsts, vec_refs):
            for block in range(blocks_dev):
                lanes = slice(block * PTS, (block + 1) * PTS)
                u_win[first - source_low + block] = ref[:, lanes]
        if begun:
            for ref, inside, places in pieces(start_refs):
                acc[places] = ref[inside]
        else:
            for place in range(high - low + 1):
                acc[place] = jnp.zeros((height, PTS), jnp.float32)

        spare = high - low
        unroll = 4

        def several(begin, end, transposed):
            def body(step, carry):
                done = []
                for lane in range(unroll):
                    index = begin + step * unroll + lane
                    valid = index < end
                    index = jnp.minimum(index, end - 1)
                    vec = u_win[source_ref[index] - source_low]
                    tile = kept[tile_ref[index]]
                    if transposed:
                        value = lax.dot_general(
                            vec,
                            tile,
                            (((1,), (1,)), ((), ())),
                            preferred_element_type=jnp.float32,
                        )
                    else:
                        value = jnp.dot(vec, tile, preferred_element_type=jnp.float32)
                    done.append((jnp.where(valid, target_ref[index] - low, spare), fold(value)))
                for target, value in done:
                    acc[target] += value
                return carry

            lax.fori_loop(0, lax.div(end - begin + unroll - 1, unroll), body, 0)

        for kind in kinds:
            several(bounds[2 * kind], bounds[2 * kind + 1], True)
            several(bounds[2 * kind + 1], bounds[2 * kind + 2], False)
        for out, inside, places in pieces(outs):
            out[inside] = acc[places]

    call = pl.pallas_call(
        kernel,
        out_shape=shapes,
        in_specs=[spec(SMEM)] * 4 + [spec(VMEM)] * (len(firsts) + 1 + len(begun)),
        out_specs=[spec(VMEM)] * len(shapes),
        scratch_shapes=[
            VMEM((source_high - source_low, tall, PTS), jnp.bfloat16),
            VMEM((high - low + 1, height, PTS), jnp.float32),
        ],
        cost_estimate=cost(2**31 if TO_OTHERS in kinds else 2**20, 2**20),
        compiler_params=pltpu.CompilerParams(vmem_limit_bytes=10 * 2**20),
        name="products",
    )
    return list(call(*entries, *[vecs[first] for first in firsts], tiles, *begun))


def urgent_ranges(group, blocks_dev):
    messages = [
        [rel for rel in range(group) if rel & bit and rel % bit == 0] for bit in bits_of(group)
    ]
    return [
        [(rel * blocks_dev, (rel + 1) * blocks_dev) for rel in rels]
        for rels in messages + [[group]]
    ]


def send_urgent(results, later, group, blocks_dev):
    *messages, far = results
    final = [from_behind(far, "blk", 1)]
    parts = {}
    for bit, message in zip(bits_of(group), messages):
        rels = [rel for rel in range(group) if rel & bit and rel % bit == 0]
        for index, rel in enumerate(rels):
            if rel in parts:
                held = message[index * blocks_dev : (index + 1) * blocks_dev]
                message = held + parts[rel] if len(rels) == 1 else message.at[
                    index * blocks_dev : (index + 1) * blocks_dev
                ].add(parts[rel])
        if bit > 1:
            message, *later = lax.optimization_barrier((message, *later))
        got = swap(message, "grp", bit)
        final.append(got)
        for index, rel in enumerate(rels):
            if rel ^ bit:
                piece = got[index * blocks_dev : (index + 1) * blocks_dev]
                parts[rel ^ bit] = parts[rel ^ bit] + piece if rel ^ bit in parts else piece
    return final, later


def finish_home(entries, vecs, tiles, start, blocks_dev, height, folds):
    return products(entries, (TO_OWN,), vecs, tiles, [start], [[(0, blocks_dev)]], height, folds)


def scaled_gram(parts, own, counts, degree, earlier):
    columns = own.shape[0] if degree is not None else own.shape[0] - EXTRA
    total = own.shape[1]
    first = degree is None
    shapes = [
        jax.ShapeDtypeStruct((columns, total), jnp.float32),
        jax.ShapeDtypeStruct((columns, columns * (1 if first else 2)), jnp.float32),
    ]
    if first:
        shapes.append(jax.ShapeDtypeStruct((2 * columns, total), jnp.bfloat16))
        shapes.append(jax.ShapeDtypeStruct((8, total), jnp.float32))
    operands = list(parts) + [own]
    operands += [] if first else [degree, earlier]

    def kernel(count_ref, *refs):
        ins = list(refs[: len(operands)])
        outs = list(refs[len(operands) :])
        part_refs = ins[: len(parts)]
        own_ref = ins[len(parts)]
        z_out, gram_out = outs[:2]
        gram = jnp.zeros((columns, columns), jnp.float32)
        for block in range(total // PTS):
            lanes = slice(block * PTS, (block + 1) * PTS)
            sums = part_refs[0][block]
            for part in part_refs[1:]:
                sums = sums + part[block]
            if first:
                level = 1.0 + sums[columns : columns + 1, :]
                outs[-1][:, lanes] = jnp.broadcast_to(level, (8, PTS))
            else:
                level = ins[len(parts) + 1][0:1, lanes]
            used = lax.broadcasted_iota(jnp.int32, (columns, PTS), 1) < count_ref[block]
            held = own_ref[0:columns, lanes].astype(jnp.float32)
            z = (held + jnp.where(used, sums[0:columns], 0.0)) / level
            z_out[:, lanes] = z
            if first:
                high = z.astype(jnp.bfloat16)
                outs[2][0:columns, lanes] = high
                rest = z - high.astype(jnp.float32)
                outs[2][columns : 2 * columns, lanes] = rest.astype(jnp.bfloat16)
            gram = gram + lax.dot_general(
                z, z, (((1,), (1,)), ((), ())), precision=HIGHEST, preferred_element_type=jnp.float32
            )
        if not first:
            gram = jnp.concatenate([ins[-1][...], gram], axis=1)
        gram_out[...] = gram

    return pl.pallas_call(
        kernel,
        out_shape=tuple(shapes),
        in_specs=[spec(SMEM)] + [spec(VMEM)] * len(operands),
        out_specs=(spec(VMEM),) * len(shapes),
        cost_estimate=cost(2**26, 2**21),
        compiler_params=pltpu.CompilerParams(vmem_limit_bytes=6 * 2**20),
        name="scaled_gram",
    )(counts, *operands)


def inverse_factor(gram):
    size = gram.shape[0]
    row_id = lax.broadcasted_iota(jnp.int32, (size, size), 0)
    col_id = lax.broadcasted_iota(jnp.int32, (size, size), 1)
    eye = jnp.where(row_id == col_id, 1.0, 0.0)
    whole = jnp.concatenate([gram, eye], axis=1)
    wide = 2 * size
    count = size // 8
    groups = [whole[8 * g : 8 * g + 8, :] for g in range(count)]
    within = lax.broadcasted_iota(jnp.int32, (8, wide), 0)

    def spread_row(value, row):
        return jnp.broadcast_to(value[row : row + 1, :], (8, wide))

    results = []
    for g in range(count):
        spread = [
            [
                jnp.broadcast_to(groups[other][:, 8 * g + k : 8 * g + k + 1], (8, wide))
                for other in range(g, count)
            ]
            for k in range(8)
        ]
        pivots = jnp.ones((8, wide), jnp.float32)
        for j in range(8):
            column = spread[j]
            pivot = spread_row(column[0], j)
            pivots = jnp.where(within == j, pivot, pivots)
            over = 1.0 / pivot
            below = jnp.where(within > j, column[0], 0.0)
            for k in range(j + 1, 8):
                share = spread_row(column[0], k) * over
                spread[k][0] = spread[k][0] - below * share
                for other in range(1, count - g):
                    spread[k][other] = spread[k][other] - column[other] * share
            top = spread_row(groups[g], j) * over
            groups[g] = groups[g] - below * top
            for other in range(1, count - g):
                groups[g + other] = groups[g + other] - column[other] * top
        results.append(groups[g] * lax.rsqrt(pivots))
    return jnp.concatenate(results, axis=0)[:, size:wide]


def exact_dot(left, right, contract):
    return lax.dot_general(
        left,
        right,
        (contract, ((), ())),
        precision=HIGHEST,
        preferred_element_type=jnp.float32,
    )


def factors_kernel(grams, both_out, first_out, sound_out):
    columns = grams.shape[0]
    plain = ((1,), (0,))
    turned = ((1,), (1,))
    second = grams[:, columns : 2 * columns]
    first_inverse = inverse_factor(grams[:, 0:columns])
    middle = exact_dot(exact_dot(first_inverse, second, plain), first_inverse, turned)
    both = exact_dot(inverse_factor(middle), first_inverse, plain)
    both_out[...] = both
    first_out[...] = first_inverse
    row_id = lax.broadcasted_iota(jnp.int32, (columns, columns), 0)
    col_id = lax.broadcasted_iota(jnp.int32, (columns, columns), 1)
    trace = jnp.sum(jnp.where(row_id == col_id, second, 0.0))
    spread = jnp.sum(both * both) * trace / (columns * columns)
    sound_out[0] = jnp.where(spread < 64.0, 1, 0)


def factors(grams):
    columns = grams.shape[0]
    square = jax.ShapeDtypeStruct((columns, columns), jnp.float32)
    return pl.pallas_call(
        factors_kernel,
        out_shape=(square, square, jax.ShapeDtypeStruct((1,), jnp.int32)),
        in_specs=[spec(VMEM)],
        out_specs=(spec(VMEM), spec(VMEM), spec(SMEM)),
        cost_estimate=cost(2**30, 2**16),
        compiler_params=pltpu.CompilerParams(vmem_limit_bytes=2 * 2**20),
        name="factors",
    )(grams)


def apply_kernel(factor, z, out, *gram):
    value = exact_dot(factor[...], z[...], ((1,), (0,)))
    out[...] = value
    if gram:
        gram[0][...] = exact_dot(value, value, ((1,), (1,)))


def applied(factor, z, with_gram):
    shapes = [jax.ShapeDtypeStruct(z.shape, jnp.float32)]
    if with_gram:
        shapes.append(jax.ShapeDtypeStruct(factor.shape, jnp.float32))
    return pl.pallas_call(
        apply_kernel,
        out_shape=shapes,
        in_specs=[spec(VMEM)] * 2,
        out_specs=[spec(VMEM)] * len(shapes),
        compiler_params=pltpu.CompilerParams(vmem_limit_bytes=4 * 2**20),
        name="applied",
    )(factor, z)


def second_kernel(gram, first, out):
    out[...] = exact_dot(inverse_factor(gram[...]), first[...], ((1,), (0,)))


def second_factor(gram, first):
    return pl.pallas_call(
        second_kernel,
        out_shape=jax.ShapeDtypeStruct(gram.shape, jnp.float32),
        in_specs=[spec(VMEM)] * 2,
        out_specs=spec(VMEM),
        compiler_params=pltpu.CompilerParams(vmem_limit_bytes=2 * 2**20),
        name="second_factor",
    )(gram, first)


def sum_stages():
    return bits_of(lax.axis_size("blk") * lax.axis_size("grp"))


def pairs_of(bits):
    return [bits[first : first + 2] for first in range(0, len(bits), 2)]


def all_sum(value, stages, beside=None):
    count = lax.axis_size("blk") * lax.axis_size("grp")
    for bits in stages:
        moves = [0]
        for bit in bits if isinstance(bits, list) else [bits]:
            moves += [move ^ bit for move in moves]
        terms = [value] + [
            lax.ppermute(value, ("blk", "grp"), [(source, source ^ move) for source in range(count)])
            for move in moves[1:]
        ]
        if beside is not None:
            terms[0], beside = lax.optimization_barrier((terms[0], beside))
        while len(terms) > 1:
            terms = [left + right for left, right in zip(terms[::2], terms[1::2])]
        value = terms[0]
    return value if beside is None else (value, beside)


def per_device(points, counts, pair_rows, pair_cols, pair_live, start):
    group = lax.axis_size("grp")
    blocks_dev = counts.shape[0]
    columns = start.shape[0]
    slots = pair_rows.shape[0]
    cap = max(-(-slots // group), blocks_dev * blocks_dev * group)
    half = (blocks_dev // 2) * PTS

    home = min(2, group) * blocks_dev

    rows, cols, n, *entries = listing(
        pair_rows, pair_cols, pair_live, group, cap, blocks_dev
    )
    first_chunk = points[:half]
    rest, first_chunk = lax.optimization_barrier((points, first_chunk))
    mate = swap(rest, "grp", 1)
    chunks = [first_chunk, rest[half:]]
    far = [from_behind(chunk, "blk", -1) for chunk in chunks]
    crossed = [gather_far_bits(chunk) for chunk in chunks]
    begin, mate = lax.optimization_barrier((start, mate))
    vec = opening(begin, counts)
    tied = lax.optimization_barrier((vec, n, rows, cols, far[0], *crossed[0].values()))
    vec, n, rows, cols, far[0] = tied[:5]
    crossed[0] = dict(zip(crossed[0], tied[5:]))
    cross_vec = gather_far_bits(vec)
    far_vec = from_behind(vec, "blk", -1)
    mate_vec = swap(vec, "grp", 1)

    def direct(index):
        offset = index * (blocks_dev // 2)
        found = {group * blocks_dev + offset: far[index]}
        for rel, value in crossed[index].items():
            found[rel * blocks_dev + offset] = value
        return found

    def passed_on(index):
        offset = index * (blocks_dev // 2)
        found = {}
        for rel, value in crossed[index].items():
            cut = value.shape[0] // (1 if index else 2)
            parts = [swap(value[at : at + cut], "grp", 1) for at in range(0, value.shape[0], cut)]
            found[(rel ^ 1) * blocks_dev + offset] = jnp.concatenate(parts, 0)
        return found

    def build(stage, fresh, state, name):
        return list(
            build_tiles(stage, fresh, n, rows, cols, state, group, blocks_dev, cap, name)
        )

    state = build(0, {0: points, blocks_dev: mate, **direct(0)}, (), "first_tiles")
    state = build(1, passed_on(0), state, "second_tiles")
    urgent = urgent_ranges(group, blocks_dev)
    ranges = [[(0, blocks_dev)]] + urgent
    height = columns + 8
    vecs_home = {0: vec, blocks_dev: mate_vec}
    begun = products(entries, (HOME_EARLY,), vecs_home, state[3], (), ranges, height, 1)
    tied = lax.optimization_barrier((far[1], begun[0], state[1], *crossed[1].values()))
    far[1], begun[0], state[1] = tied[:3]
    crossed[1] = dict(zip(crossed[1], tied[3:]))
    last = passed_on(1)
    *grown, kept = state
    state = build(None, direct(1), grown, "more_blocks") + [kept]
    state = build(2, last, state, "last_tiles")
    kept = state[-1]
    tied = lax.optimization_barrier((kept, *cross_vec.values()))
    kept = tied[0]
    cross_vec = dict(zip(cross_vec, tied[1:]))

    def window_of(own, mate, crossed, far):
        found = {0: own, blocks_dev: mate, group * blocks_dev: far}
        for rel, value in crossed.items():
            found[rel * blocks_dev] = value
            found[(rel ^ 1) * blocks_dev] = swap(value, "grp", 1)
        return found

    def beyond(vecs):
        return {place: value for place, value in vecs.items() if place >= home}

    vecs = window_of(vec, mate_vec, cross_vec, far_vec)
    at_home, *results = products(
        entries, (HOME_LAST,), vecs_home, kept, begun, ranges, height, 1
    )
    results = products(entries, (TO_OTHERS,), beyond(vecs), kept, results, urgent, height, 1)
    sums, (at_home,) = send_urgent(results, (at_home,), group, blocks_dev)
    sums = finish_home(entries, beyond(vecs), kept, at_home, blocks_dev, height, 1) + sums
    z, gram, parts, degree = scaled_gram(sums, vec, counts, None, None)

    far_part = from_behind(parts, "blk", -1)
    crossed = gather_far_bits(parts)
    mate_part = swap(parts, "grp", 1)
    at_home, *results = products(
        entries,
        (HOME_EARLY, HOME_LAST),
        {0: parts, blocks_dev: mate_part},
        kept,
        (),
        ranges,
        columns,
        2,
    )
    at_home, *tied = lax.optimization_barrier((at_home, *crossed.values()))
    crossed = dict(zip(crossed, tied))
    vecs = beyond(window_of(parts, mate_part, crossed, far_part))
    results = products(entries, (TO_OTHERS,), vecs, kept, results, urgent, columns, 2)
    sums, (at_home,) = send_urgent(results, (at_home,), group, blocks_dev)
    sums = finish_home(entries, vecs, kept, at_home, blocks_dev, columns, 2) + sums
    z, grams = scaled_gram(sums, z, counts, degree, gram)

    stages = sum_stages()
    stages = stages[:1] + pairs_of(stages[1:])
    both, first, sound = factors(all_sum(grams, stages))

    def at_once(both, first, z):
        return both

    def in_two(both, first, z):
        return second_factor(all_sum(applied(first, z, True)[1], stages), first)

    return applied(lax.cond(sound[0] == 1, at_once, in_two, both, first, z), z, False)[0]


def solution(mesh):
    in_specs = (
        P(("blk", "grp"), None),
        P(("blk", "grp")),
        P("blk"),
        P("blk"),
        P("blk"),
        P(None, ("blk", "grp")),
    )
    out_specs = P(None, ("blk", "grp"))
    return jax.shard_map(
        per_device, mesh=mesh, in_specs=in_specs, out_specs=out_specs, check_vma=False
    )
```

```python
import functools

import jax
import jax.numpy as jnp
from jax import lax
from jax.experimental import pallas as pl
from jax.experimental.pallas import tpu as pltpu
from jax.sharding import PartitionSpec as P

PTS = 512
LOG2E = 1.4426950408889634
DEAD = 65536.0
EXTRA = 16
HOME_EARLY, HOME_LAST, TO_OTHERS, TO_OWN = range(4)
KINDS = 4
VMEM = pltpu.VMEM
SMEM = pltpu.SMEM
HIGHEST = lax.Precision.HIGHEST


def cost(flops, moved):
    return pl.CostEstimate(flops=int(flops), bytes_accessed=int(moved), transcendentals=0)


def spec(space):
    return pl.BlockSpec(memory_space=space)


def swap(value, axis, bit):
    count = lax.axis_size(axis)
    return lax.ppermute(value, axis, [(source, source ^ bit) for source in range(count)])


def from_behind(value, axis, steps):
    count = lax.axis_size(axis)
    initial, last = (max(0, -steps), min(count, count - steps))
    return lax.ppermute(value, axis, [(source, source + steps) for source in range(initial, last)])


def bits_of(count):
    bits = []
    bit = 1
    while bit < count:
        bits.append(bit)
        bit *= 2
    return bits


def gather_near(value, axis):
    held = {0: value}
    for bit in reversed(bits_of(lax.axis_size(axis))):
        for rel in list(held):
            held[rel ^ bit] = swap(held[rel], axis, bit)
    return [held[rel] for rel in range(len(held))]


def gather_far_bits(value):
    held = {0: value}
    for bit in reversed(bits_of(lax.axis_size("grp"))[1:]):
        for rel in list(held):
            held[rel ^ bit] = swap(held[rel], "grp", bit)
    held.pop(0)
    return held


def opening_kernel(start, counts, out):
    columns, total = start.shape
    for block in range(total // PTS):
        lanes = slice(block * PTS, (block + 1) * PTS)
        used = lax.broadcasted_iota(jnp.int32, (columns, PTS), 1) < counts[block]
        out[0:columns, lanes] = jnp.where(used, start[:, lanes], 0.0).astype(jnp.bfloat16)
        which = lax.broadcasted_iota(jnp.int32, (EXTRA, PTS), 0)
        place_in = lax.broadcasted_iota(jnp.int32, (EXTRA, PTS), 1)
        ones = jnp.logical_and(which == 0, place_in < counts[block])
        out[columns : columns + EXTRA, lanes] = jnp.where(ones, 1.0, 0.0).astype(jnp.bfloat16)


def opening(start, counts):
    columns, total = start.shape
    return pl.pallas_call(
        opening_kernel,
        out_shape=jax.ShapeDtypeStruct((columns + EXTRA, total), jnp.bfloat16),
        in_specs=[spec(VMEM), spec(SMEM)],
        out_specs=spec(VMEM),
        cost_estimate=cost(2**20, 2**19),
        compiler_params=pltpu.CompilerParams(vmem_limit_bytes=2 * 2**20),
        name="opening",
    )(start, counts)


def stage_of(place, group, blocks_dev):
    piece = lax.div(place, blocks_dev)
    first_half = lax.rem(place, blocks_dev) < blocks_dev // 2
    later = jnp.where(first_half, jnp.where(lax.rem(piece, 2) == 0, 0, 1), 2)
    return jnp.where(piece < min(2, group), 0, later)


def listing_kernel(
    group,
    cap,
    blocks_dev,
    rows,
    cols,
    live,
    out_rows,
    out_cols,
    out_n,
    tiles,
    sources,
    targets,
    bounds,
    owners,
):
    slab = blocks_dev * group
    slots = rows.shape[0]
    member = lax.axis_index("grp")

    def local_near(block, device):
        return (lax.div(block, blocks_dev) ^ device) * blocks_dev + lax.rem(block, blocks_dev)

    def local_far(block):
        return slab + lax.rem(block - slab, blocks_dev)

    def count_far(slot, carry):
        col = cols[slot]
        far = jnp.logical_and(slot < live[0], col >= slab)
        owner = lax.div(col - slab, blocks_dev)
        owners[slot] = jnp.where(far, owner, -1)
        return tuple(
            old + jnp.where(jnp.logical_and(far, owner == device), 1, 0)
            for device, old in enumerate(carry)
        )

    loads = lax.fori_loop(0, slots, count_far, (jnp.int32(0),) * group)

    def give(slot, loads):
        row, col = rows[slot], cols[slot]
        near = jnp.logical_and(slot < live[0], col < slab)
        best = jnp.int32(2**30)
        owner = jnp.int32(0)
        for device in range(group):
            stage = jnp.maximum(
                stage_of(local_near(row, device), group, blocks_dev),
                stage_of(local_near(col, device), group, blocks_dev),
            )
            score = loads[device] + 64 * stage + jnp.where(loads[device] < cap, 0, 2**20)
            owner = jnp.where(score < best, device, owner)
            best = jnp.minimum(score, best)

        @pl.when(near)
        def _():
            owners[slot] = owner

        return tuple(
            load + jnp.where(jnp.logical_and(near, owner == device), 1, 0)
            for device, load in enumerate(loads)
        )

    lax.fori_loop(0, slots, give, loads)

    def place_those(wanted, filled):
        def place(slot, filled):
            row, col = rows[slot], cols[slot]
            row_place = local_near(row, member)
            col_place = jnp.where(col >= slab, local_far(col), local_near(col, member))
            stage = jnp.maximum(
                stage_of(row_place, group, blocks_dev), stage_of(col_place, group, blocks_dev)
            )
            mine = jnp.logical_and(owners[slot] == member, stage == wanted)

            @pl.when(mine)
            def _():
                out_rows[filled] = row_place
                out_cols[filled] = col_place

            return filled + jnp.where(mine, 1, 0)

        return lax.fori_loop(0, slots, place, filled)

    count = jnp.int32(0)
    out_n[0] = count
    for wanted in range(3):
        count = place_those(wanted, count)
        out_n[wanted + 1] = count

    home = min(2, group) * blocks_dev
    bounds[0] = jnp.int32(0)
    filled = jnp.int32(0)
    for kind in range(KINDS):
        for to_row in (True, False):

            def enter(index, filled):
                source = (out_cols if to_row else out_rows)[index]
                target = (out_rows if to_row else out_cols)[index]
                own_target = jnp.logical_and(source >= home, target < blocks_dev)
                other_target = jnp.logical_and(source >= home, target >= blocks_dev)
                if kind == HOME_EARLY:
                    wanted = jnp.logical_and(source < home, index < out_n[2])
                elif kind == HOME_LAST:
                    wanted = jnp.logical_and(source < home, index >= out_n[2])
                elif kind == TO_OTHERS:
                    wanted = other_target
                else:
                    wanted = own_target

                @pl.when(wanted)
                def _():
                    tiles[filled] = index
                    sources[filled] = source
                    targets[filled] = target

                return filled + jnp.where(wanted, 1, 0)

            filled = lax.fori_loop(0, count, enter, filled)
            bounds[2 * kind + (1 if to_row else 2)] = filled


def listing(rows, cols, live, group, cap, blocks_dev):
    return pl.pallas_call(
        functools.partial(listing_kernel, group, cap, blocks_dev),
        out_shape=(
            jax.ShapeDtypeStruct((cap,), jnp.int32),
            jax.ShapeDtypeStruct((cap,), jnp.int32),
            jax.ShapeDtypeStruct((4,), jnp.int32),
            jax.ShapeDtypeStruct((2 * cap,), jnp.int32),
            jax.ShapeDtypeStruct((2 * cap,), jnp.int32),
            jax.ShapeDtypeStruct((2 * cap,), jnp.int32),
            jax.ShapeDtypeStruct((2 * KINDS + 1,), jnp.int32),
        ),
        in_specs=[spec(SMEM)] * 3,
        out_specs=(spec(SMEM),) * 7,
        scratch_shapes=[SMEM((rows.shape[0],), jnp.int32)],
        cost_estimate=cost(2**20, 2**10),
        compiler_params=pltpu.CompilerParams(vmem_limit_bytes=2**20),
        name="listing",
    )(rows, cols, live)


def set_levels(place, window, level_row, level_col, scale):
    block = window[place * PTS : (place + 1) * PTS, :]
    width = block.shape[1]
    part = jnp.zeros((PTS, 128), jnp.float32)
    for lane in range(0, width, 128):
        wide = block[:, lane : lane + 128].astype(jnp.float32)
        part = part + wide * wide
    level_row[place] = scale * lax.dot_general(
        jnp.ones((8, 128), jnp.float32),
        part,
        (((1,), (1,)), ((), ())),
        precision=HIGHEST,
        preferred_element_type=jnp.float32,
    )
    if place < level_col.shape[0]:
        total = jnp.sum(part, axis=1, keepdims=True) * scale
        level_col[place] = jnp.broadcast_to(total, (PTS, 128))


def make_tiles(low, high, rows, cols, window, level_row, level_col, kept, buffers):
    width = window.shape[1]
    scale = 6.0 / width * LOG2E
    count = high - low
    spare = kept.shape[0] - 1

    def cross(tile, buffer):
        index = low + jnp.minimum(tile, count - 1)
        left = window[pl.ds(pl.multiple_of(rows[index] * PTS, PTS), PTS), :]
        right = window[pl.ds(pl.multiple_of(cols[index] * PTS, PTS), PTS), :]
        buffer[...] = lax.dot_general(
            left, right, (((1,), (1,)), ((), ())), preferred_element_type=jnp.float32
        )

    def finish(tile, buffer):
        valid = jnp.logical_and(tile >= 0, tile < count)
        index = low + jnp.clip(tile, 0, count - 1)
        row, col = rows[index], cols[index]
        right_level = level_row[col][0:1, :]
        left_level = jnp.concatenate([level_col[row]] * (PTS // 128), axis=1)
        value = jnp.exp2(buffer[...] * scale - left_level - right_level)
        kept[jnp.where(valid, index, spare)] = value.astype(jnp.bfloat16)

    def body(pair, carry):
        cross(2 * pair, buffers[0])
        finish(2 * pair - 1, buffers[1])
        cross(2 * pair + 1, buffers[1])
        finish(2 * pair, buffers[0])
        return carry

    @pl.when(count > 0)
    def _():
        buffers[1][...] = jnp.zeros((PTS, PTS), jnp.float32)

    lax.fori_loop(0, jnp.where(count > 0, lax.div(count, 2) + 1, 0), body, 0)


def build_tiles(stage, fresh, n, rows, cols, state, group, blocks_dev, cap, name):
    places = list(fresh)
    pts = list(fresh.values())
    width = pts[0].shape[1]
    total = (group + 1) * blocks_dev
    near = group * blocks_dev
    shapes = [
        jax.ShapeDtypeStruct((total * PTS, width), jnp.bfloat16),
        jax.ShapeDtypeStruct((total, 8, PTS), jnp.float32),
        jax.ShapeDtypeStruct((near, PTS, 128), jnp.float32),
    ]
    makes = stage is not None
    if makes:
        shapes.append(jax.ShapeDtypeStruct((cap + 1, PTS, PTS), jnp.bfloat16))
    state = state[: len(shapes)]
    scalars = (n, rows, cols) if makes else ()
    first = len(scalars) + len(pts)

    def kernel(*refs):
        pt_refs = refs[len(scalars) : first]
        window, level_row, level_col, *rest = refs[first + len(state) :]
        for place, piece in zip(places, pt_refs):
            blocks = piece.shape[0] // PTS
            window[place * PTS : (place + blocks) * PTS, :] = piece[...]
            for block in range(place, place + blocks):
                set_levels(block, window, level_row, level_col, 3.0 / width * LOG2E)
        if makes:
            n_ref, row_ref, col_ref = refs[:3]
            kept, *buffers = rest
            make_tiles(
                n_ref[stage],
                n_ref[stage + 1],
                row_ref,
                col_ref,
                window,
                level_row,
                level_col,
                kept,
                buffers,
            )

    return pl.pallas_call(
        kernel,
        out_shape=shapes,
        in_specs=[spec(SMEM)] * len(scalars) + [spec(VMEM)] * (len(pts) + len(state)),
        out_specs=[spec(VMEM)] * len(shapes),
        input_output_aliases={first + index: index for index in range(len(state))},
        scratch_shapes=[VMEM((PTS, PTS), jnp.float32)] * (2 if makes else 0),
        cost_estimate=cost(2**32 if stage == 2 else 2**20, 2**20),
        compiler_params=pltpu.CompilerParams(vmem_limit_bytes=6 * 2**20),
        name=name,
    )(*scalars, *pts, *state)


def products(entries, kinds, vecs, tiles, start, targets, height, folds):
    firsts = sorted(vecs)
    tall, held = vecs[firsts[0]].shape
    blocks_dev = held // PTS
    begun = list(start)
    source_low, source_high = firsts[0], firsts[-1] + blocks_dev
    low = min(first for ranges in targets for first, _ in ranges)
    high = max(last for ranges in targets for _, last in ranges)
    shapes = [
        jax.ShapeDtypeStruct((sum(last - first for first, last in ranges), height, PTS), jnp.float32)
        for ranges in targets
    ]

    def pieces(refs):
        for ranges, ref in zip(targets, refs):
            at = 0
            for first, last in ranges:
                yield ref, slice(at, at + last - first), slice(first - low, last - low)
                at += last - first

    def fold(value):
        out = value[:height]
        for index in range(1, folds):
            out = out + value[index * height : (index + 1) * height]
        return out

    def kernel(*refs):
        tile_ref, source_ref, target_ref, bounds = refs[:4]
        vec_refs = refs[4 : 4 + len(firsts)]
        kept = refs[4 + len(firsts)]
        start_refs = refs[5 + len(firsts) : 5 + len(firsts) + len(begun)]
        outs = refs[5 + len(firsts) + len(begun) : -2]
        u_win, acc = refs[-2:]
        for first, ref in zip(firsts, vec_refs):
            for block in range(blocks_dev):
                lanes = slice(block * PTS, (block + 1) * PTS)
                u_win[first - source_low + block] = ref[:, lanes]
        if begun:
            for ref, inside, places in pieces(start_refs):
                acc[places] = ref[inside]
        else:
            for place in range(high - low + 1):
                acc[place] = jnp.zeros((height, PTS), jnp.float32)

        spare = high - low
        unroll = 4

        def several(begin, end, transposed):
            def body(step, carry):
                done = []
                for lane in range(unroll):
                    index = begin + step * unroll + lane
                    valid = index < end
                    index = jnp.minimum(index, end - 1)
                    vec = u_win[source_ref[index] - source_low]
                    tile = kept[tile_ref[index]]
                    if transposed:
                        value = lax.dot_general(
                            vec,
                            tile,
                            (((1,), (1,)), ((), ())),
                            preferred_element_type=jnp.float32,
                        )
                    else:
                        value = jnp.dot(vec, tile, preferred_element_type=jnp.float32)
                    done.append((jnp.where(valid, target_ref[index] - low, spare), fold(value)))
                for target, value in done:
                    acc[target] += value
                return carry

            lax.fori_loop(0, lax.div(end - begin + unroll - 1, unroll), body, 0)

        for kind in kinds:
            several(bounds[2 * kind], bounds[2 * kind + 1], True)
            several(bounds[2 * kind + 1], bounds[2 * kind + 2], False)
        for out, inside, places in pieces(outs):
            out[inside] = acc[places]

    call = pl.pallas_call(
        kernel,
        out_shape=shapes,
        in_specs=[spec(SMEM)] * 4 + [spec(VMEM)] * (len(firsts) + 1 + len(begun)),
        out_specs=[spec(VMEM)] * len(shapes),
        scratch_shapes=[
            VMEM((source_high - source_low, tall, PTS), jnp.bfloat16),
            VMEM((high - low + 1, height, PTS), jnp.float32),
        ],
        cost_estimate=cost(2**31 if TO_OTHERS in kinds else 2**20, 2**20),
        compiler_params=pltpu.CompilerParams(vmem_limit_bytes=10 * 2**20),
        name="products",
    )
    return list(call(*entries, *[vecs[first] for first in firsts], tiles, *begun))


def urgent_ranges(group, blocks_dev):
    messages = [
        [rel for rel in range(group) if rel & bit and rel % bit == 0] for bit in bits_of(group)
    ]
    return [
        [(rel * blocks_dev, (rel + 1) * blocks_dev) for rel in rels]
        for rels in messages + [[group]]
    ]


def send_urgent(results, later, group, blocks_dev):
    *messages, far = results
    final = [from_behind(far, "blk", 1)]
    parts = {}
    for bit, message in zip(bits_of(group), messages):
        rels = [rel for rel in range(group) if rel & bit and rel % bit == 0]
        for index, rel in enumerate(rels):
            if rel in parts:
                held = message[index * blocks_dev : (index + 1) * blocks_dev]
                message = held + parts[rel] if len(rels) == 1 else message.at[
                    index * blocks_dev : (index + 1) * blocks_dev
                ].add(parts[rel])
        if bit > 1:
            message, *later = lax.optimization_barrier((message, *later))
        got = swap(message, "grp", bit)
        final.append(got)
        for index, rel in enumerate(rels):
            if rel ^ bit:
                piece = got[index * blocks_dev : (index + 1) * blocks_dev]
                parts[rel ^ bit] = parts[rel ^ bit] + piece if rel ^ bit in parts else piece
    return final, later


def finish_home(entries, vecs, tiles, start, blocks_dev, height, folds):
    return products(entries, (TO_OWN,), vecs, tiles, [start], [[(0, blocks_dev)]], height, folds)


def scaled_gram(parts, own, counts, degree, earlier):
    columns = own.shape[0] if degree is not None else own.shape[0] - EXTRA
    total = own.shape[1]
    first = degree is None
    shapes = [
        jax.ShapeDtypeStruct((columns, total), jnp.float32),
        jax.ShapeDtypeStruct((columns, columns * (1 if first else 2)), jnp.float32),
    ]
    if first:
        shapes.append(jax.ShapeDtypeStruct((2 * columns, total), jnp.bfloat16))
        shapes.append(jax.ShapeDtypeStruct((8, total), jnp.float32))
    operands = list(parts) + [own]
    operands += [] if first else [degree, earlier]

    def kernel(count_ref, *refs):
        ins = list(refs[: len(operands)])
        outs = list(refs[len(operands) :])
        part_refs = ins[: len(parts)]
        own_ref = ins[len(parts)]
        z_out, gram_out = outs[:2]
        gram = jnp.zeros((columns, columns), jnp.float32)
        for block in range(total // PTS):
            lanes = slice(block * PTS, (block + 1) * PTS)
            sums = part_refs[0][block]
            for part in part_refs[1:]:
                sums = sums + part[block]
            if first:
                level = 1.0 + sums[columns : columns + 1, :]
                outs[-1][:, lanes] = jnp.broadcast_to(level, (8, PTS))
            else:
                level = ins[len(parts) + 1][0:1, lanes]
            used = lax.broadcasted_iota(jnp.int32, (columns, PTS), 1) < count_ref[block]
            held = own_ref[0:columns, lanes].astype(jnp.float32)
            z = (held + jnp.where(used, sums[0:columns], 0.0)) / level
            z_out[:, lanes] = z
            if first:
                high = z.astype(jnp.bfloat16)
                outs[2][0:columns, lanes] = high
                rest = z - high.astype(jnp.float32)
                outs[2][columns : 2 * columns, lanes] = rest.astype(jnp.bfloat16)
            gram = gram + lax.dot_general(
                z, z, (((1,), (1,)), ((), ())), precision=HIGHEST, preferred_element_type=jnp.float32
            )
        if not first:
            gram = jnp.concatenate([ins[-1][...], gram], axis=1)
        gram_out[...] = gram

    return pl.pallas_call(
        kernel,
        out_shape=tuple(shapes),
        in_specs=[spec(SMEM)] + [spec(VMEM)] * len(operands),
        out_specs=(spec(VMEM),) * len(shapes),
        cost_estimate=cost(2**26, 2**21),
        compiler_params=pltpu.CompilerParams(vmem_limit_bytes=6 * 2**20),
        name="scaled_gram",
    )(counts, *operands)


def inverse_factor(gram):
    size = gram.shape[0]
    row_id = lax.broadcasted_iota(jnp.int32, (size, size), 0)
    col_id = lax.broadcasted_iota(jnp.int32, (size, size), 1)
    eye = jnp.where(row_id == col_id, 1.0, 0.0)
    whole = jnp.concatenate([gram, eye], axis=1)
    wide = 2 * size
    count = size // 8
    groups = [whole[8 * g : 8 * g + 8, :] for g in range(count)]
    within = lax.broadcasted_iota(jnp.int32, (8, wide), 0)

    def spread_row(value, row):
        return jnp.broadcast_to(value[row : row + 1, :], (8, wide))

    results = []
    for g in range(count):
        spread = [
            [
                jnp.broadcast_to(groups[other][:, 8 * g + k : 8 * g + k + 1], (8, wide))
                for other in range(g, count)
            ]
            for k in range(8)
        ]
        pivots = jnp.ones((8, wide), jnp.float32)
        for j in range(8):
            column = spread[j]
            pivot = spread_row(column[0], j)
            pivots = jnp.where(within == j, pivot, pivots)
            over = 1.0 / pivot
            below = jnp.where(within > j, column[0], 0.0)
            for k in range(j + 1, 8):
                share = spread_row(column[0], k) * over
                spread[k][0] = spread[k][0] - below * share
                for other in range(1, count - g):
                    spread[k][other] = spread[k][other] - column[other] * share
            top = spread_row(groups[g], j) * over
            groups[g] = groups[g] - below * top
            for other in range(1, count - g):
                groups[g + other] = groups[g + other] - column[other] * top
        results.append(groups[g] * lax.rsqrt(pivots))
    return jnp.concatenate(results, axis=0)[:, size:wide]


def exact_dot(left, right, contract):
    return lax.dot_general(
        left,
        right,
        (contract, ((), ())),
        precision=HIGHEST,
        preferred_element_type=jnp.float32,
    )


def factors_kernel(grams, both_out, first_out, sound_out):
    columns = grams.shape[0]
    plain = ((1,), (0,))
    turned = ((1,), (1,))
    second = grams[:, columns : 2 * columns]
    first_inverse = inverse_factor(grams[:, 0:columns])
    middle = exact_dot(exact_dot(first_inverse, second, plain), first_inverse, turned)
    both = exact_dot(inverse_factor(middle), first_inverse, plain)
    both_out[...] = both
    first_out[...] = first_inverse
    row_id = lax.broadcasted_iota(jnp.int32, (columns, columns), 0)
    col_id = lax.broadcasted_iota(jnp.int32, (columns, columns), 1)
    trace = jnp.sum(jnp.where(row_id == col_id, second, 0.0))
    spread = jnp.sum(both * both) * trace / (columns * columns)
    sound_out[0] = jnp.where(spread < 64.0, 1, 0)


def factors(grams):
    columns = grams.shape[0]
    square = jax.ShapeDtypeStruct((columns, columns), jnp.float32)
    return pl.pallas_call(
        factors_kernel,
        out_shape=(square, square, jax.ShapeDtypeStruct((1,), jnp.int32)),
        in_specs=[spec(VMEM)],
        out_specs=(spec(VMEM), spec(VMEM), spec(SMEM)),
        cost_estimate=cost(2**30, 2**16),
        compiler_params=pltpu.CompilerParams(vmem_limit_bytes=2 * 2**20),
        name="factors",
    )(grams)


def apply_kernel(factor, z, out, *gram):
    value = exact_dot(factor[...], z[...], ((1,), (0,)))
    out[...] = value
    if gram:
        gram[0][...] = exact_dot(value, value, ((1,), (1,)))


def applied(factor, z, with_gram):
    shapes = [jax.ShapeDtypeStruct(z.shape, jnp.float32)]
    if with_gram:
        shapes.append(jax.ShapeDtypeStruct(factor.shape, jnp.float32))
    return pl.pallas_call(
        apply_kernel,
        out_shape=shapes,
        in_specs=[spec(VMEM)] * 2,
        out_specs=[spec(VMEM)] * len(shapes),
        compiler_params=pltpu.CompilerParams(vmem_limit_bytes=4 * 2**20),
        name="applied",
    )(factor, z)


def second_kernel(gram, first, out):
    out[...] = exact_dot(inverse_factor(gram[...]), first[...], ((1,), (0,)))


def second_factor(gram, first):
    return pl.pallas_call(
        second_kernel,
        out_shape=jax.ShapeDtypeStruct(gram.shape, jnp.float32),
        in_specs=[spec(VMEM)] * 2,
        out_specs=spec(VMEM),
        compiler_params=pltpu.CompilerParams(vmem_limit_bytes=2 * 2**20),
        name="second_factor",
    )(gram, first)


def sum_stages():
    return bits_of(lax.axis_size("blk") * lax.axis_size("grp"))


def pairs_of(bits):
    return [bits[first : first + 2] for first in range(0, len(bits), 2)]


def all_sum(value, stages, beside=None):
    count = lax.axis_size("blk") * lax.axis_size("grp")
    for bits in stages:
        moves = [0]
        for bit in bits if isinstance(bits, list) else [bits]:
            moves += [move ^ bit for move in moves]
        terms = [value] + [
            lax.ppermute(value, ("blk", "grp"), [(source, source ^ move) for source in range(count)])
            for move in moves[1:]
        ]
        if beside is not None:
            terms[0], beside = lax.optimization_barrier((terms[0], beside))
        while len(terms) > 1:
            terms = [left + right for left, right in zip(terms[::2], terms[1::2])]
        value = terms[0]
    return value if beside is None else (value, beside)


def per_device(points, counts, pair_rows, pair_cols, pair_live, start):
    group = lax.axis_size("grp")
    blocks_dev = counts.shape[0]
    columns = start.shape[0]
    slots = pair_rows.shape[0]
    cap = max(-(-slots // group), blocks_dev * blocks_dev * group)
    half = (blocks_dev // 2) * PTS

    home = min(2, group) * blocks_dev

    rows, cols, n, *entries = listing(
        pair_rows, pair_cols, pair_live, group, cap, blocks_dev
    )
    first_chunk = points[:half]
    rest, first_chunk = lax.optimization_barrier((points, first_chunk))
    mate = swap(rest, "grp", 1)
    chunks = [first_chunk, rest[half:]]
    far = [from_behind(chunk, "blk", -1) for chunk in chunks]
    crossed = [gather_far_bits(chunk) for chunk in chunks]
    vec = opening(start, counts)
    tied = lax.optimization_barrier((vec, n, rows, cols, far[0], *crossed[0].values()))
    vec, n, rows, cols, far[0] = tied[:5]
    crossed[0] = dict(zip(crossed[0], tied[5:]))
    cross_vec = gather_far_bits(vec)
    far_vec = from_behind(vec, "blk", -1)
    mate_vec = swap(vec, "grp", 1)

    def direct(index):
        offset = index * (blocks_dev // 2)
        found = {group * blocks_dev + offset: far[index]}
        for rel, value in crossed[index].items():
            found[rel * blocks_dev + offset] = value
        return found

    def passed_on(index):
        offset = index * (blocks_dev // 2)
        found = {}
        for rel, value in crossed[index].items():
            cut = value.shape[0] // (1 if index else 2)
            parts = [swap(value[at : at + cut], "grp", 1) for at in range(0, value.shape[0], cut)]
            found[(rel ^ 1) * blocks_dev + offset] = jnp.concatenate(parts, 0)
        return found

    def build(stage, fresh, state, name):
        return list(
            build_tiles(stage, fresh, n, rows, cols, state, group, blocks_dev, cap, name)
        )

    state = build(0, {0: points, blocks_dev: mate, **direct(0)}, (), "first_tiles")
    state = build(1, passed_on(0), state, "second_tiles")
    urgent = urgent_ranges(group, blocks_dev)
    ranges = [[(0, blocks_dev)]] + urgent
    height = columns + 8
    vecs_home = {0: vec, blocks_dev: mate_vec}
    begun = products(entries, (HOME_EARLY,), vecs_home, state[3], (), ranges, height, 1)
    tied = lax.optimization_barrier((far[1], begun[0], state[1], *crossed[1].values()))
    far[1], begun[0], state[1] = tied[:3]
    crossed[1] = dict(zip(crossed[1], tied[3:]))
    last = passed_on(1)
    *grown, kept = state
    state = build(None, direct(1), grown, "more_blocks") + [kept]
    state = build(2, last, state, "last_tiles")
    kept = state[-1]
    tied = lax.optimization_barrier((kept, *cross_vec.values()))
    kept = tied[0]
    cross_vec = dict(zip(cross_vec, tied[1:]))

    def window_of(own, mate, crossed, far):
        found = {0: own, blocks_dev: mate, group * blocks_dev: far}
        for rel, value in crossed.items():
            found[rel * blocks_dev] = value
            found[(rel ^ 1) * blocks_dev] = swap(value, "grp", 1)
        return found

    def beyond(vecs):
        return {place: value for place, value in vecs.items() if place >= home}

    vecs = window_of(vec, mate_vec, cross_vec, far_vec)
    at_home, *results = products(
        entries, (HOME_LAST,), vecs_home, kept, begun, ranges, height, 1
    )
    results = products(entries, (TO_OTHERS,), beyond(vecs), kept, results, urgent, height, 1)
    sums, (at_home,) = send_urgent(results, (at_home,), group, blocks_dev)
    sums = finish_home(entries, beyond(vecs), kept, at_home, blocks_dev, height, 1) + sums
    z, gram, parts, degree = scaled_gram(sums, vec, counts, None, None)

    far_part = from_behind(parts, "blk", -1)
    crossed = gather_far_bits(parts)
    mate_part = swap(parts, "grp", 1)
    at_home, *results = products(
        entries,
        (HOME_EARLY, HOME_LAST),
        {0: parts, blocks_dev: mate_part},
        kept,
        (),
        ranges,
        columns,
        2,
    )
    at_home, *tied = lax.optimization_barrier((at_home, *crossed.values()))
    crossed = dict(zip(crossed, tied))
    vecs = beyond(window_of(parts, mate_part, crossed, far_part))
    results = products(entries, (TO_OTHERS,), vecs, kept, results, urgent, columns, 2)
    sums, (at_home,) = send_urgent(results, (at_home,), group, blocks_dev)
    sums = finish_home(entries, vecs, kept, at_home, blocks_dev, columns, 2) + sums
    z, grams = scaled_gram(sums, z, counts, degree, gram)

    stages = sum_stages()
    stages = stages[:1] + pairs_of(stages[1:])
    both, first, sound = factors(all_sum(grams, stages))

    def at_once(both, first, z):
        return both

    def in_two(both, first, z):
        return second_factor(all_sum(applied(first, z, True)[1], stages), first)

    return applied(lax.cond(sound[0] == 1, at_once, in_two, both, first, z), z, False)[0]


def solution(mesh):
    in_specs = (
        P(("blk", "grp"), None),
        P(("blk", "grp")),
        P("blk"),
        P("blk"),
        P("blk"),
        P(None, ("blk", "grp")),
    )
    out_specs = P(None, ("blk", "grp"))
    return jax.shard_map(
        per_device, mesh=mesh, in_specs=in_specs, out_specs=out_specs, check_vma=False
    )
```

```python
import functools

import jax
import jax.numpy as jnp
from jax import lax
from jax.experimental import pallas as pl
from jax.experimental.pallas import tpu as pltpu
from jax.sharding import PartitionSpec as P

PTS = 512
LOG2E = 1.4426950408889634
DEAD = 65536.0
EXTRA = 16
HOME_EARLY, HOME_LAST, TO_OTHERS, TO_OWN = range(4)
KINDS = 4
VMEM = pltpu.VMEM
SMEM = pltpu.SMEM
HIGHEST = lax.Precision.HIGHEST


def cost(flops, moved):
    return pl.CostEstimate(flops=int(flops), bytes_accessed=int(moved), transcendentals=0)


def spec(space):
    return pl.BlockSpec(memory_space=space)


def swap(value, axis, bit):
    count = lax.axis_size(axis)
    return lax.ppermute(value, axis, [(source, source ^ bit) for source in range(count)])


def from_behind(value, axis, steps):
    count = lax.axis_size(axis)
    initial, last = (max(0, -steps), min(count, count - steps))
    return lax.ppermute(value, axis, [(source, source + steps) for source in range(initial, last)])


def bits_of(count):
    bits = []
    bit = 1
    while bit < count:
        bits.append(bit)
        bit *= 2
    return bits


def gather_near(value, axis):
    held = {0: value}
    for bit in reversed(bits_of(lax.axis_size(axis))):
        for rel in list(held):
            held[rel ^ bit] = swap(held[rel], axis, bit)
    return [held[rel] for rel in range(len(held))]


def gather_far_bits(value):
    held = {0: value}
    for bit in reversed(bits_of(lax.axis_size("grp"))[1:]):
        for rel in list(held):
            held[rel ^ bit] = swap(held[rel], "grp", bit)
    held.pop(0)
    return held


def opening_kernel(start, counts, out):
    columns, total = start.shape
    for block in range(total // PTS):
        lanes = slice(block * PTS, (block + 1) * PTS)
        used = lax.broadcasted_iota(jnp.int32, (columns, PTS), 1) < counts[block]
        out[0:columns, lanes] = jnp.where(used, start[:, lanes], 0.0).astype(jnp.bfloat16)
        which = lax.broadcasted_iota(jnp.int32, (EXTRA, PTS), 0)
        place_in = lax.broadcasted_iota(jnp.int32, (EXTRA, PTS), 1)
        ones = jnp.logical_and(which == 0, place_in < counts[block])
        out[columns : columns + EXTRA, lanes] = jnp.where(ones, 1.0, 0.0).astype(jnp.bfloat16)


def opening(start, counts):
    columns, total = start.shape
    return pl.pallas_call(
        opening_kernel,
        out_shape=jax.ShapeDtypeStruct((columns + EXTRA, total), jnp.bfloat16),
        in_specs=[spec(VMEM), spec(SMEM)],
        out_specs=spec(VMEM),
        cost_estimate=cost(2**20, 2**19),
        compiler_params=pltpu.CompilerParams(vmem_limit_bytes=2 * 2**20),
        name="opening",
    )(start, counts)


def stage_of(place, group, blocks_dev):
    piece = lax.div(place, blocks_dev)
    first_half = lax.rem(place, blocks_dev) < blocks_dev // 2
    later = jnp.where(first_half, jnp.where(lax.rem(piece, 2) == 0, 0, 1), 2)
    return jnp.where(piece < min(2, group), 0, later)


def listing_kernel(
    group,
    cap,
    blocks_dev,
    rows,
    cols,
    live,
    out_rows,
    out_cols,
    out_n,
    tiles,
    sources,
    targets,
    bounds,
    owners,
    row_places,
    col_places,
):
    slab = blocks_dev * group
    member = lax.axis_index("grp")

    def local_near(block, device):
        return (lax.div(block, blocks_dev) ^ device) * blocks_dev + lax.rem(block, blocks_dev)

    def local_far(block):
        return slab + lax.rem(block - slab, blocks_dev)

    def far_of(col):
        return col >= slab

    def count_far(slot, carry):
        col = cols[slot]
        far = far_of(col)
        owner = lax.div(col - slab, blocks_dev)
        owners[slot] = jnp.where(far, owner, -1)
        return tuple(
            old + jnp.where(jnp.logical_and(far, owner == device), 1, 0)
            for device, old in enumerate(carry)
        )

    loads = lax.fori_loop(0, live[0], count_far, (jnp.int32(0),) * group)

    def give(slot, loads):
        row, col = rows[slot], cols[slot]
        near = jnp.logical_not(far_of(col))
        best = jnp.int32(2**30)
        owner = jnp.int32(0)
        for device in range(group):
            stage = jnp.maximum(
                stage_of(local_near(row, device), group, blocks_dev),
                stage_of(local_near(col, device), group, blocks_dev),
            )
            score = loads[device] + 64 * stage + jnp.where(loads[device] < cap, 0, 2**20)
            owner = jnp.where(score < best, device, owner)
            best = jnp.minimum(score, best)

        row_place = local_near(row, member)
        col_place = jnp.where(far_of(col), local_far(col), local_near(col, member))
        stage = jnp.maximum(
            stage_of(row_place, group, blocks_dev), stage_of(col_place, group, blocks_dev)
        )
        mine = jnp.where(near, owner, owners[slot]) == member
        row_places[slot] = row_place
        col_places[slot] = col_place
        owners[slot] = jnp.where(mine, stage, -1)
        return tuple(
            load + jnp.where(jnp.logical_and(near, owner == device), 1, 0)
            for device, load in enumerate(loads)
        )

    lax.fori_loop(0, live[0], give, loads)

    def place_those(wanted, filled):
        def place(slot, filled):
            mine = owners[slot] == wanted

            @pl.when(mine)
            def _():
                out_rows[filled] = row_places[slot]
                out_cols[filled] = col_places[slot]

            return filled + jnp.where(mine, 1, 0)

        return lax.fori_loop(0, live[0], place, filled)

    count = jnp.int32(0)
    out_n[0] = count
    for wanted in range(3):
        count = place_those(wanted, count)
        out_n[wanted + 1] = count

    home = min(2, group) * blocks_dev
    bounds[0] = jnp.int32(0)
    filled = jnp.int32(0)
    for kind in range(KINDS):
        for to_row in (True, False):

            def enter(index, filled):
                source = (out_cols if to_row else out_rows)[index]
                target = (out_rows if to_row else out_cols)[index]
                own_target = jnp.logical_and(source >= home, target < blocks_dev)
                other_target = jnp.logical_and(source >= home, target >= blocks_dev)
                if kind == HOME_EARLY:
                    wanted = jnp.logical_and(source < home, index < out_n[2])
                elif kind == HOME_LAST:
                    wanted = jnp.logical_and(source < home, index >= out_n[2])
                elif kind == TO_OTHERS:
                    wanted = other_target
                else:
                    wanted = own_target

                @pl.when(wanted)
                def _():
                    tiles[filled] = index
                    sources[filled] = source
                    targets[filled] = target

                return filled + jnp.where(wanted, 1, 0)

            filled = lax.fori_loop(0, count, enter, filled)
            bounds[2 * kind + (1 if to_row else 2)] = filled


def listing(rows, cols, live, group, cap, blocks_dev):
    return pl.pallas_call(
        functools.partial(listing_kernel, group, cap, blocks_dev),
        out_shape=(
            jax.ShapeDtypeStruct((cap,), jnp.int32),
            jax.ShapeDtypeStruct((cap,), jnp.int32),
            jax.ShapeDtypeStruct((4,), jnp.int32),
            jax.ShapeDtypeStruct((2 * cap,), jnp.int32),
            jax.ShapeDtypeStruct((2 * cap,), jnp.int32),
            jax.ShapeDtypeStruct((2 * cap,), jnp.int32),
            jax.ShapeDtypeStruct((2 * KINDS + 1,), jnp.int32),
        ),
        in_specs=[spec(SMEM)] * 3,
        out_specs=(spec(SMEM),) * 7,
        scratch_shapes=[SMEM((rows.shape[0],), jnp.int32)] * 3,
        cost_estimate=cost(2**20, 2**10),
        compiler_params=pltpu.CompilerParams(vmem_limit_bytes=2**20),
        name="listing",
    )(rows, cols, live)


def set_levels(place, window, level_row, level_col, scale):
    block = window[place * PTS : (place + 1) * PTS, :]
    width = block.shape[1]
    part = jnp.zeros((PTS, 128), jnp.float32)
    for lane in range(0, width, 128):
        wide = block[:, lane : lane + 128].astype(jnp.float32)
        part = part + wide * wide
    level_row[place] = scale * lax.dot_general(
        jnp.ones((8, 128), jnp.float32),
        part,
        (((1,), (1,)), ((), ())),
        precision=HIGHEST,
        preferred_element_type=jnp.float32,
    )
    if place < level_col.shape[0]:
        total = jnp.sum(part, axis=1, keepdims=True) * scale
        level_col[place] = jnp.broadcast_to(total, (PTS, 128))


def make_tiles(low, high, rows, cols, window, level_row, level_col, kept, buffers):
    width = window.shape[1]
    scale = 6.0 / width * LOG2E
    count = high - low
    spare = kept.shape[0] - 1

    def cross(tile, buffer):
        index = low + jnp.minimum(tile, count - 1)
        left = window[pl.ds(pl.multiple_of(rows[index] * PTS, PTS), PTS), :]
        right = window[pl.ds(pl.multiple_of(cols[index] * PTS, PTS), PTS), :]
        buffer[...] = lax.dot_general(
            left, right, (((1,), (1,)), ((), ())), preferred_element_type=jnp.float32
        )

    def finish(tile, buffer):
        valid = jnp.logical_and(tile >= 0, tile < count)
        index = low + jnp.clip(tile, 0, count - 1)
        row, col = rows[index], cols[index]
        right_level = level_row[col][0:1, :]
        left_level = jnp.concatenate([level_col[row]] * (PTS // 128), axis=1)
        value = jnp.exp2(buffer[...] * scale - left_level - right_level)
        kept[jnp.where(valid, index, spare)] = value.astype(jnp.bfloat16)

    def body(pair, carry):
        cross(2 * pair, buffers[0])
        finish(2 * pair - 1, buffers[1])
        cross(2 * pair + 1, buffers[1])
        finish(2 * pair, buffers[0])
        return carry

    @pl.when(count > 0)
    def _():
        buffers[1][...] = jnp.zeros((PTS, PTS), jnp.float32)

    lax.fori_loop(0, jnp.where(count > 0, lax.div(count, 2) + 1, 0), body, 0)


def build_tiles(stage, fresh, n, rows, cols, state, group, blocks_dev, cap, name):
    places = list(fresh)
    pts = list(fresh.values())
    width = pts[0].shape[1]
    total = (group + 1) * blocks_dev
    near = group * blocks_dev
    shapes = [
        jax.ShapeDtypeStruct((total * PTS, width), jnp.bfloat16),
        jax.ShapeDtypeStruct((total, 8, PTS), jnp.float32),
        jax.ShapeDtypeStruct((near, PTS, 128), jnp.float32),
    ]
    makes = stage is not None
    if makes:
        shapes.append(jax.ShapeDtypeStruct((cap + 1, PTS, PTS), jnp.bfloat16))
    state = state[: len(shapes)]
    scalars = (n, rows, cols) if makes else ()
    first = len(scalars) + len(pts)

    def kernel(*refs):
        pt_refs = refs[len(scalars) : first]
        window, level_row, level_col, *rest = refs[first + len(state) :]
        for place, piece in zip(places, pt_refs):
            blocks = piece.shape[0] // PTS
            window[place * PTS : (place + blocks) * PTS, :] = piece[...]
            for block in range(place, place + blocks):
                set_levels(block, window, level_row, level_col, 3.0 / width * LOG2E)
        if makes:
            n_ref, row_ref, col_ref = refs[:3]
            kept, *buffers = rest
            make_tiles(
                n_ref[stage],
                n_ref[stage + 1],
                row_ref,
                col_ref,
                window,
                level_row,
                level_col,
                kept,
                buffers,
            )

    return pl.pallas_call(
        kernel,
        out_shape=shapes,
        in_specs=[spec(SMEM)] * len(scalars) + [spec(VMEM)] * (len(pts) + len(state)),
        out_specs=[spec(VMEM)] * len(shapes),
        input_output_aliases={first + index: index for index in range(len(state))},
        scratch_shapes=[VMEM((PTS, PTS), jnp.float32)] * (2 if makes else 0),
        cost_estimate=cost(2**32 if stage == 2 else 2**20, 2**20),
        compiler_params=pltpu.CompilerParams(vmem_limit_bytes=6 * 2**20),
        name=name,
    )(*scalars, *pts, *state)


def products(entries, kinds, vecs, tiles, start, targets, height, folds):
    firsts = sorted(vecs)
    tall, held = vecs[firsts[0]].shape
    blocks_dev = held // PTS
    begun = list(start)
    source_low, source_high = firsts[0], firsts[-1] + blocks_dev
    low = min(first for ranges in targets for first, _ in ranges)
    high = max(last for ranges in targets for _, last in ranges)
    shapes = [
        jax.ShapeDtypeStruct((sum(last - first for first, last in ranges), height, PTS), jnp.float32)
        for ranges in targets
    ]

    def pieces(refs):
        for ranges, ref in zip(targets, refs):
            at = 0
            for first, last in ranges:
                yield ref, slice(at, at + last - first), slice(first - low, last - low)
                at += last - first

    def fold(value):
        out = value[:height]
        for index in range(1, folds):
            out = out + value[index * height : (index + 1) * height]
        return out

    def kernel(*refs):
        tile_ref, source_ref, target_ref, bounds = refs[:4]
        vec_refs = refs[4 : 4 + len(firsts)]
        kept = refs[4 + len(firsts)]
        start_refs = refs[5 + len(firsts) : 5 + len(firsts) + len(begun)]
        outs = refs[5 + len(firsts) + len(begun) : -2]
        u_win, acc = refs[-2:]
        for first, ref in zip(firsts, vec_refs):
            for block in range(blocks_dev):
                lanes = slice(block * PTS, (block + 1) * PTS)
                u_win[first - source_low + block] = ref[:, lanes]
        if begun:
            for ref, inside, places in pieces(start_refs):
                acc[places] = ref[inside]
        else:
            for place in range(high - low + 1):
                acc[place] = jnp.zeros((height, PTS), jnp.float32)

        spare = high - low
        unroll = 4

        def several(begin, end, transposed):
            def body(step, carry):
                done = []
                for lane in range(unroll):
                    index = begin + step * unroll + lane
                    valid = index < end
                    index = jnp.minimum(index, end - 1)
                    vec = u_win[source_ref[index] - source_low]
                    tile = kept[tile_ref[index]]
                    if transposed:
                        value = lax.dot_general(
                            vec,
                            tile,
                            (((1,), (1,)), ((), ())),
                            preferred_element_type=jnp.float32,
                        )
                    else:
                        value = jnp.dot(vec, tile, preferred_element_type=jnp.float32)
                    done.append((jnp.where(valid, target_ref[index] - low, spare), fold(value)))
                for target, value in done:
                    acc[target] += value
                return carry

            lax.fori_loop(0, lax.div(end - begin + unroll - 1, unroll), body, 0)

        for kind in kinds:
            several(bounds[2 * kind], bounds[2 * kind + 1], True)
            several(bounds[2 * kind + 1], bounds[2 * kind + 2], False)
        for out, inside, places in pieces(outs):
            out[inside] = acc[places]

    call = pl.pallas_call(
        kernel,
        out_shape=shapes,
        in_specs=[spec(SMEM)] * 4 + [spec(VMEM)] * (len(firsts) + 1 + len(begun)),
        out_specs=[spec(VMEM)] * len(shapes),
        scratch_shapes=[
            VMEM((source_high - source_low, tall, PTS), jnp.bfloat16),
            VMEM((high - low + 1, height, PTS), jnp.float32),
        ],
        cost_estimate=cost(2**31 if TO_OTHERS in kinds else 2**20, 2**20),
        compiler_params=pltpu.CompilerParams(vmem_limit_bytes=10 * 2**20),
        name="products",
    )
    return list(call(*entries, *[vecs[first] for first in firsts], tiles, *begun))


def urgent_ranges(group, blocks_dev):
    messages = [
        [rel for rel in range(group) if rel & bit and rel % bit == 0] for bit in bits_of(group)
    ]
    return [
        [(rel * blocks_dev, (rel + 1) * blocks_dev) for rel in rels]
        for rels in messages + [[group]]
    ]


def send_urgent(results, later, group, blocks_dev):
    *messages, far = results
    final = [from_behind(far, "blk", 1)]
    parts = {}
    for bit, message in zip(bits_of(group), messages):
        rels = [rel for rel in range(group) if rel & bit and rel % bit == 0]
        for index, rel in enumerate(rels):
            if rel in parts:
                held = message[index * blocks_dev : (index + 1) * blocks_dev]
                message = held + parts[rel] if len(rels) == 1 else message.at[
                    index * blocks_dev : (index + 1) * blocks_dev
                ].add(parts[rel])
        if bit > 1:
            message, *later = lax.optimization_barrier((message, *later))
        got = swap(message, "grp", bit)
        final.append(got)
        for index, rel in enumerate(rels):
            if rel ^ bit:
                piece = got[index * blocks_dev : (index + 1) * blocks_dev]
                parts[rel ^ bit] = parts[rel ^ bit] + piece if rel ^ bit in parts else piece
    return final, later


def finish_home(entries, vecs, tiles, start, blocks_dev, height, folds):
    return products(entries, (TO_OWN,), vecs, tiles, [start], [[(0, blocks_dev)]], height, folds)


def scaled_gram(parts, own, counts, degree, earlier):
    columns = own.shape[0] if degree is not None else own.shape[0] - EXTRA
    total = own.shape[1]
    first = degree is None
    shapes = [
        jax.ShapeDtypeStruct((columns, total), jnp.float32),
        jax.ShapeDtypeStruct((columns, columns * (1 if first else 2)), jnp.float32),
    ]
    if first:
        shapes.append(jax.ShapeDtypeStruct((2 * columns, total), jnp.bfloat16))
        shapes.append(jax.ShapeDtypeStruct((8, total), jnp.float32))
    operands = list(parts) + [own]
    operands += [] if first else [degree, earlier]

    def kernel(count_ref, *refs):
        ins = list(refs[: len(operands)])
        outs = list(refs[len(operands) :])
        part_refs = ins[: len(parts)]
        own_ref = ins[len(parts)]
        z_out, gram_out = outs[:2]
        gram = jnp.zeros((columns, columns), jnp.float32)
        for block in range(total // PTS):
            lanes = slice(block * PTS, (block + 1) * PTS)
            sums = part_refs[0][block]
            for part in part_refs[1:]:
                sums = sums + part[block]
            if first:
                level = 1.0 + sums[columns : columns + 1, :]
                outs[-1][:, lanes] = jnp.broadcast_to(level, (8, PTS))
            else:
                level = ins[len(parts) + 1][0:1, lanes]
            used = lax.broadcasted_iota(jnp.int32, (columns, PTS), 1) < count_ref[block]
            held = own_ref[0:columns, lanes].astype(jnp.float32)
            z = (held + jnp.where(used, sums[0:columns], 0.0)) / level
            z_out[:, lanes] = z
            if first:
                high = z.astype(jnp.bfloat16)
                outs[2][0:columns, lanes] = high
                rest = z - high.astype(jnp.float32)
                outs[2][columns : 2 * columns, lanes] = rest.astype(jnp.bfloat16)
            gram = gram + lax.dot_general(
                z, z, (((1,), (1,)), ((), ())), precision=HIGHEST, preferred_element_type=jnp.float32
            )
        if not first:
            gram = jnp.concatenate([ins[-1][...], gram], axis=1)
        gram_out[...] = gram

    return pl.pallas_call(
        kernel,
        out_shape=tuple(shapes),
        in_specs=[spec(SMEM)] + [spec(VMEM)] * len(operands),
        out_specs=(spec(VMEM),) * len(shapes),
        cost_estimate=cost(2**26, 2**21),
        compiler_params=pltpu.CompilerParams(vmem_limit_bytes=6 * 2**20),
        name="scaled_gram",
    )(counts, *operands)


def inverse_factor(gram):
    size = gram.shape[0]
    row_id = lax.broadcasted_iota(jnp.int32, (size, size), 0)
    col_id = lax.broadcasted_iota(jnp.int32, (size, size), 1)
    eye = jnp.where(row_id == col_id, 1.0, 0.0)
    whole = jnp.concatenate([gram, eye], axis=1)
    wide = 2 * size
    count = size // 8
    groups = [whole[8 * g : 8 * g + 8, :] for g in range(count)]
    within = lax.broadcasted_iota(jnp.int32, (8, wide), 0)

    def spread_row(value, row):
        return jnp.broadcast_to(value[row : row + 1, :], (8, wide))

    results = []
    for g in range(count):
        spread = [
            [
                jnp.broadcast_to(groups[other][:, 8 * g + k : 8 * g + k + 1], (8, wide))
                for other in range(g, count)
            ]
            for k in range(8)
        ]
        pivots = jnp.ones((8, wide), jnp.float32)
        for j in range(8):
            column = spread[j]
            pivot = spread_row(column[0], j)
            pivots = jnp.where(within == j, pivot, pivots)
            over = 1.0 / pivot
            below = jnp.where(within > j, column[0], 0.0)
            for k in range(j + 1, 8):
                share = spread_row(column[0], k) * over
                spread[k][0] = spread[k][0] - below * share
                for other in range(1, count - g):
                    spread[k][other] = spread[k][other] - column[other] * share
            top = spread_row(groups[g], j) * over
            groups[g] = groups[g] - below * top
            for other in range(1, count - g):
                groups[g + other] = groups[g + other] - column[other] * top
        results.append(groups[g] * lax.rsqrt(pivots))
    return jnp.concatenate(results, axis=0)[:, size:wide]


def exact_dot(left, right, contract):
    return lax.dot_general(
        left,
        right,
        (contract, ((), ())),
        precision=HIGHEST,
        preferred_element_type=jnp.float32,
    )


def factors_kernel(grams, both_out, first_out, sound_out):
    columns = grams.shape[0]
    plain = ((1,), (0,))
    turned = ((1,), (1,))
    second = grams[:, columns : 2 * columns]
    first_inverse = inverse_factor(grams[:, 0:columns])
    middle = exact_dot(exact_dot(first_inverse, second, plain), first_inverse, turned)
    both = exact_dot(inverse_factor(middle), first_inverse, plain)
    both_out[...] = both
    first_out[...] = first_inverse
    row_id = lax.broadcasted_iota(jnp.int32, (columns, columns), 0)
    col_id = lax.broadcasted_iota(jnp.int32, (columns, columns), 1)
    trace = jnp.sum(jnp.where(row_id == col_id, second, 0.0))
    spread = jnp.sum(both * both) * trace / (columns * columns)
    sound_out[0] = jnp.where(spread < 64.0, 1, 0)


def factors(grams):
    columns = grams.shape[0]
    square = jax.ShapeDtypeStruct((columns, columns), jnp.float32)
    return pl.pallas_call(
        factors_kernel,
        out_shape=(square, square, jax.ShapeDtypeStruct((1,), jnp.int32)),
        in_specs=[spec(VMEM)],
        out_specs=(spec(VMEM), spec(VMEM), spec(SMEM)),
        cost_estimate=cost(2**30, 2**16),
        compiler_params=pltpu.CompilerParams(vmem_limit_bytes=2 * 2**20),
        name="factors",
    )(grams)


def apply_kernel(factor, z, out, *gram):
    value = exact_dot(factor[...], z[...], ((1,), (0,)))
    out[...] = value
    if gram:
        gram[0][...] = exact_dot(value, value, ((1,), (1,)))


def applied(factor, z, with_gram):
    shapes = [jax.ShapeDtypeStruct(z.shape, jnp.float32)]
    if with_gram:
        shapes.append(jax.ShapeDtypeStruct(factor.shape, jnp.float32))
    return pl.pallas_call(
        apply_kernel,
        out_shape=shapes,
        in_specs=[spec(VMEM)] * 2,
        out_specs=[spec(VMEM)] * len(shapes),
        compiler_params=pltpu.CompilerParams(vmem_limit_bytes=4 * 2**20),
        name="applied",
    )(factor, z)


def second_kernel(gram, first, out):
    out[...] = exact_dot(inverse_factor(gram[...]), first[...], ((1,), (0,)))


def second_factor(gram, first):
    return pl.pallas_call(
        second_kernel,
        out_shape=jax.ShapeDtypeStruct(gram.shape, jnp.float32),
        in_specs=[spec(VMEM)] * 2,
        out_specs=spec(VMEM),
        compiler_params=pltpu.CompilerParams(vmem_limit_bytes=2 * 2**20),
        name="second_factor",
    )(gram, first)


def sum_stages():
    return bits_of(lax.axis_size("blk") * lax.axis_size("grp"))


def pairs_of(bits):
    return [bits[first : first + 2] for first in range(0, len(bits), 2)]


def all_sum(value, stages, beside=None):
    count = lax.axis_size("blk") * lax.axis_size("grp")
    for bits in stages:
        moves = [0]
        for bit in bits if isinstance(bits, list) else [bits]:
            moves += [move ^ bit for move in moves]
        terms = [value] + [
            lax.ppermute(value, ("blk", "grp"), [(source, source ^ move) for source in range(count)])
            for move in moves[1:]
        ]
        if beside is not None:
            terms[0], beside = lax.optimization_barrier((terms[0], beside))
        while len(terms) > 1:
            terms = [left + right for left, right in zip(terms[::2], terms[1::2])]
        value = terms[0]
    return value if beside is None else (value, beside)


def per_device(points, counts, pair_rows, pair_cols, pair_live, start):
    group = lax.axis_size("grp")
    blocks_dev = counts.shape[0]
    columns = start.shape[0]
    slots = pair_rows.shape[0]
    cap = max(-(-slots // group), blocks_dev * blocks_dev * group)
    half = (blocks_dev // 2) * PTS

    home = min(2, group) * blocks_dev

    rows, cols, n, *entries = listing(
        pair_rows, pair_cols, pair_live, group, cap, blocks_dev
    )
    first_chunk = points[:half]
    rest, first_chunk = lax.optimization_barrier((points, first_chunk))
    mate = swap(rest, "grp", 1)
    chunks = [first_chunk, rest[half:]]
    far = [from_behind(chunk, "blk", -1) for chunk in chunks]
    crossed = [gather_far_bits(chunk) for chunk in chunks]
    vec = opening(start, counts)
    tied = lax.optimization_barrier((vec, n, rows, cols, far[0], *crossed[0].values()))
    vec, n, rows, cols, far[0] = tied[:5]
    crossed[0] = dict(zip(crossed[0], tied[5:]))
    cross_vec = gather_far_bits(vec)
    far_vec = from_behind(vec, "blk", -1)
    mate_vec = swap(vec, "grp", 1)

    def direct(index):
        offset = index * (blocks_dev // 2)
        found = {group * blocks_dev + offset: far[index]}
        for rel, value in crossed[index].items():
            found[rel * blocks_dev + offset] = value
        return found

    def passed_on(index):
        offset = index * (blocks_dev // 2)
        found = {}
        for rel, value in crossed[index].items():
            cut = value.shape[0] // (1 if index else 2)
            parts = [swap(value[at : at + cut], "grp", 1) for at in range(0, value.shape[0], cut)]
            found[(rel ^ 1) * blocks_dev + offset] = jnp.concatenate(parts, 0)
        return found

    def build(stage, fresh, state, name):
        return list(
            build_tiles(stage, fresh, n, rows, cols, state, group, blocks_dev, cap, name)
        )

    state = build(0, {0: points, blocks_dev: mate, **direct(0)}, (), "first_tiles")
    state = build(1, passed_on(0), state, "second_tiles")
    urgent = urgent_ranges(group, blocks_dev)
    ranges = [[(0, blocks_dev)]] + urgent
    height = columns + 8
    vecs_home = {0: vec, blocks_dev: mate_vec}
    begun = products(entries, (HOME_EARLY,), vecs_home, state[3], (), ranges, height, 1)
    tied = lax.optimization_barrier((far[1], begun[0], state[1], *crossed[1].values()))
    far[1], begun[0], state[1] = tied[:3]
    crossed[1] = dict(zip(crossed[1], tied[3:]))
    last = passed_on(1)
    *grown, kept = state
    state = build(None, direct(1), grown, "more_blocks") + [kept]
    state = build(2, last, state, "last_tiles")
    kept = state[-1]
    tied = lax.optimization_barrier((kept, *cross_vec.values()))
    kept = tied[0]
    cross_vec = dict(zip(cross_vec, tied[1:]))

    def window_of(own, mate, crossed, far):
        found = {0: own, blocks_dev: mate, group * blocks_dev: far}
        for rel, value in crossed.items():
            found[rel * blocks_dev] = value
            found[(rel ^ 1) * blocks_dev] = swap(value, "grp", 1)
        return found

    def beyond(vecs):
        return {place: value for place, value in vecs.items() if place >= home}

    vecs = window_of(vec, mate_vec, cross_vec, far_vec)
    at_home, *results = products(
        entries, (HOME_LAST,), vecs_home, kept, begun, ranges, height, 1
    )
    results = products(entries, (TO_OTHERS,), beyond(vecs), kept, results, urgent, height, 1)
    sums, (at_home,) = send_urgent(results, (at_home,), group, blocks_dev)
    sums = finish_home(entries, beyond(vecs), kept, at_home, blocks_dev, height, 1) + sums
    z, gram, parts, degree = scaled_gram(sums, vec, counts, None, None)

    far_part = from_behind(parts, "blk", -1)
    crossed = gather_far_bits(parts)
    mate_part = swap(parts, "grp", 1)
    at_home, *results = products(
        entries,
        (HOME_EARLY, HOME_LAST),
        {0: parts, blocks_dev: mate_part},
        kept,
        (),
        ranges,
        columns,
        2,
    )
    at_home, *tied = lax.optimization_barrier((at_home, *crossed.values()))
    crossed = dict(zip(crossed, tied))
    vecs = beyond(window_of(parts, mate_part, crossed, far_part))
    results = products(entries, (TO_OTHERS,), vecs, kept, results, urgent, columns, 2)
    sums, (at_home,) = send_urgent(results, (at_home,), group, blocks_dev)
    sums = finish_home(entries, vecs, kept, at_home, blocks_dev, columns, 2) + sums
    z, grams = scaled_gram(sums, z, counts, degree, gram)

    stages = sum_stages()
    stages = stages[:1] + pairs_of(stages[1:])
    both, first, sound = factors(all_sum(grams, stages))

    def at_once(both, first, z):
        return both

    def in_two(both, first, z):
        return second_factor(all_sum(applied(first, z, True)[1], stages), first)

    return applied(lax.cond(sound[0] == 1, at_once, in_two, both, first, z), z, False)[0]


def solution(mesh):
    in_specs = (
        P(("blk", "grp"), None),
        P(("blk", "grp")),
        P("blk"),
        P("blk"),
        P("blk"),
        P(None, ("blk", "grp")),
    )
    out_specs = P(None, ("blk", "grp"))
    return jax.shard_map(
        per_device, mesh=mesh, in_specs=in_specs, out_specs=out_specs, check_vma=False
    )
```

```python
import functools

import jax
import jax.numpy as jnp
from jax import lax
from jax.experimental import pallas as pl
from jax.experimental.pallas import tpu as pltpu
from jax.sharding import PartitionSpec as P

PTS = 512
LOG2E = 1.4426950408889634
DEAD = 65536.0
EXTRA = 16
HOME_EARLY, HOME_LAST, TO_OTHERS, TO_OWN = range(4)
KINDS = 4
VMEM = pltpu.VMEM
SMEM = pltpu.SMEM
HIGHEST = lax.Precision.HIGHEST


def cost(flops, moved):
    return pl.CostEstimate(flops=int(flops), bytes_accessed=int(moved), transcendentals=0)


def spec(space):
    return pl.BlockSpec(memory_space=space)


def swap(value, axis, bit):
    count = lax.axis_size(axis)
    return lax.ppermute(value, axis, [(source, source ^ bit) for source in range(count)])


def from_behind(value, axis, steps):
    count = lax.axis_size(axis)
    initial, last = (max(0, -steps), min(count, count - steps))
    return lax.ppermute(value, axis, [(source, source + steps) for source in range(initial, last)])


def bits_of(count):
    bits = []
    bit = 1
    while bit < count:
        bits.append(bit)
        bit *= 2
    return bits


def gather_near(value, axis):
    held = {0: value}
    for bit in reversed(bits_of(lax.axis_size(axis))):
        for rel in list(held):
            held[rel ^ bit] = swap(held[rel], axis, bit)
    return [held[rel] for rel in range(len(held))]


def gather_far_bits(value):
    held = {0: value}
    for bit in reversed(bits_of(lax.axis_size("grp"))[1:]):
        for rel in list(held):
            held[rel ^ bit] = swap(held[rel], "grp", bit)
    held.pop(0)
    return held


def opening_kernel(start, counts, out):
    columns, total = start.shape
    for block in range(total // PTS):
        lanes = slice(block * PTS, (block + 1) * PTS)
        used = lax.broadcasted_iota(jnp.int32, (columns, PTS), 1) < counts[block]
        out[0:columns, lanes] = jnp.where(used, start[:, lanes], 0.0).astype(jnp.bfloat16)
        which = lax.broadcasted_iota(jnp.int32, (EXTRA, PTS), 0)
        place_in = lax.broadcasted_iota(jnp.int32, (EXTRA, PTS), 1)
        ones = jnp.logical_and(which == 0, place_in < counts[block])
        out[columns : columns + EXTRA, lanes] = jnp.where(ones, 1.0, 0.0).astype(jnp.bfloat16)


def opening(start, counts):
    columns, total = start.shape
    return pl.pallas_call(
        opening_kernel,
        out_shape=jax.ShapeDtypeStruct((columns + EXTRA, total), jnp.bfloat16),
        in_specs=[spec(VMEM), spec(SMEM)],
        out_specs=spec(VMEM),
        cost_estimate=cost(2**20, 2**19),
        compiler_params=pltpu.CompilerParams(vmem_limit_bytes=2 * 2**20),
        name="opening",
    )(start, counts)


def stage_of(place, group, blocks_dev):
    piece = lax.div(place, blocks_dev)
    first_half = lax.rem(place, blocks_dev) < blocks_dev // 2
    later = jnp.where(first_half, jnp.where(lax.rem(piece, 2) == 0, 0, 1), 2)
    return jnp.where(piece < min(2, group), 0, later)


def listing_kernel(
    group,
    cap,
    blocks_dev,
    rows,
    cols,
    live,
    out_rows,
    out_cols,
    out_n,
    tiles,
    sources,
    targets,
    bounds,
    owners,
    row_places,
    col_places,
):
    slab = blocks_dev * group
    member = lax.axis_index("grp")

    def local_near(block, device):
        return (lax.div(block, blocks_dev) ^ device) * blocks_dev + lax.rem(block, blocks_dev)

    def local_far(block):
        return slab + lax.rem(block - slab, blocks_dev)

    def far_of(col):
        return col >= slab

    def count_far(slot, carry):
        col = cols[slot]
        far = far_of(col)
        owner = lax.div(col - slab, blocks_dev)
        owners[slot] = jnp.where(far, owner, -1)
        return tuple(
            old + jnp.where(jnp.logical_and(far, owner == device), 1, 0)
            for device, old in enumerate(carry)
        )

    loads = lax.fori_loop(0, live[0], count_far, (jnp.int32(0),) * group)

    def give(slot, loads):
        row, col = rows[slot], cols[slot]
        near = jnp.logical_not(far_of(col))
        best = jnp.int32(2**30)
        owner = jnp.int32(0)
        for device in range(group):
            stage = jnp.maximum(
                stage_of(local_near(row, device), group, blocks_dev),
                stage_of(local_near(col, device), group, blocks_dev),
            )
            score = loads[device] + 64 * stage + jnp.where(loads[device] < cap, 0, 2**20)
            owner = jnp.where(score < best, device, owner)
            best = jnp.minimum(score, best)

        row_place = local_near(row, member)
        col_place = jnp.where(far_of(col), local_far(col), local_near(col, member))
        stage = jnp.maximum(
            stage_of(row_place, group, blocks_dev), stage_of(col_place, group, blocks_dev)
        )
        mine = jnp.where(near, owner, owners[slot]) == member
        row_places[slot] = row_place
        col_places[slot] = col_place
        owners[slot] = jnp.where(mine, stage, -1)
        return tuple(
            load + jnp.where(jnp.logical_and(near, owner == device), 1, 0)
            for device, load in enumerate(loads)
        )

    lax.fori_loop(0, live[0], give, loads)

    def place_those(wanted, filled):
        def place(slot, filled):
            mine = owners[slot] == wanted

            @pl.when(mine)
            def _():
                out_rows[filled] = row_places[slot]
                out_cols[filled] = col_places[slot]

            return filled + jnp.where(mine, 1, 0)

        return lax.fori_loop(0, live[0], place, filled)

    count = jnp.int32(0)
    out_n[0] = count
    for wanted in range(3):
        count = place_those(wanted, count)
        out_n[wanted + 1] = count

    home = min(2, group) * blocks_dev
    bounds[0] = jnp.int32(0)
    filled = jnp.int32(0)
    for kind in range(KINDS):
        for to_row in (True, False):

            def enter(index, filled):
                source = (out_cols if to_row else out_rows)[index]
                target = (out_rows if to_row else out_cols)[index]
                own_target = jnp.logical_and(source >= home, target < blocks_dev)
                other_target = jnp.logical_and(source >= home, target >= blocks_dev)
                if kind == HOME_EARLY:
                    wanted = jnp.logical_and(source < home, index < out_n[2])
                elif kind == HOME_LAST:
                    wanted = jnp.logical_and(source < home, index >= out_n[2])
                elif kind == TO_OTHERS:
                    wanted = other_target
                else:
                    wanted = own_target

                @pl.when(wanted)
                def _():
                    tiles[filled] = index
                    sources[filled] = source
                    targets[filled] = target

                return filled + jnp.where(wanted, 1, 0)

            filled = lax.fori_loop(0, count, enter, filled)
            bounds[2 * kind + (1 if to_row else 2)] = filled


def listing(rows, cols, live, group, cap, blocks_dev):
    return pl.pallas_call(
        functools.partial(listing_kernel, group, cap, blocks_dev),
        out_shape=(
            jax.ShapeDtypeStruct((cap,), jnp.int32),
            jax.ShapeDtypeStruct((cap,), jnp.int32),
            jax.ShapeDtypeStruct((4,), jnp.int32),
            jax.ShapeDtypeStruct((2 * cap,), jnp.int32),
            jax.ShapeDtypeStruct((2 * cap,), jnp.int32),
            jax.ShapeDtypeStruct((2 * cap,), jnp.int32),
            jax.ShapeDtypeStruct((2 * KINDS + 1,), jnp.int32),
        ),
        in_specs=[spec(SMEM)] * 3,
        out_specs=(spec(SMEM),) * 7,
        scratch_shapes=[SMEM((rows.shape[0],), jnp.int32)] * 3,
        cost_estimate=cost(2**20, 2**10),
        compiler_params=pltpu.CompilerParams(vmem_limit_bytes=2**20),
        name="listing",
    )(rows, cols, live)


def set_levels(place, window, level_row, level_col, scale):
    block = window[place * PTS : (place + 1) * PTS, :]
    width = block.shape[1]
    part = jnp.zeros((PTS, 128), jnp.float32)
    for lane in range(0, width, 128):
        wide = block[:, lane : lane + 128].astype(jnp.float32)
        part = part + wide * wide
    level_row[place] = scale * lax.dot_general(
        jnp.ones((8, 128), jnp.float32),
        part,
        (((1,), (1,)), ((), ())),
        precision=HIGHEST,
        preferred_element_type=jnp.float32,
    )
    if place < level_col.shape[0]:
        total = jnp.sum(part, axis=1, keepdims=True) * scale
        level_col[place] = jnp.broadcast_to(total, (PTS, 128))


def make_tiles(low, high, rows, cols, window, level_row, level_col, kept, buffers):
    width = window.shape[1]
    scale = 6.0 / width * LOG2E
    count = high - low
    spare = kept.shape[0] - 1

    def cross(tile, buffer):
        index = low + jnp.minimum(tile, count - 1)
        left = window[pl.ds(pl.multiple_of(rows[index] * PTS, PTS), PTS), :]
        right = window[pl.ds(pl.multiple_of(cols[index] * PTS, PTS), PTS), :]
        buffer[...] = lax.dot_general(
            left, right, (((1,), (1,)), ((), ())), preferred_element_type=jnp.float32
        )

    def finish(tile, buffer):
        valid = jnp.logical_and(tile >= 0, tile < count)
        index = low + jnp.clip(tile, 0, count - 1)
        row, col = rows[index], cols[index]
        right_level = level_row[col][0:1, :]
        left_level = jnp.concatenate([level_col[row]] * (PTS // 128), axis=1)
        value = jnp.exp2(buffer[...] * scale - left_level - right_level)
        kept[jnp.where(valid, index, spare)] = value.astype(jnp.bfloat16)

    def body(pair, carry):
        cross(2 * pair, buffers[0])
        finish(2 * pair - 1, buffers[1])
        cross(2 * pair + 1, buffers[1])
        finish(2 * pair, buffers[0])
        return carry

    @pl.when(count > 0)
    def _():
        buffers[1][...] = jnp.zeros((PTS, PTS), jnp.float32)

    lax.fori_loop(0, lax.div(count + 1, 2), body, 0)

    @pl.when(jnp.logical_and(count > 0, lax.rem(count, 2) == 0))
    def _():
        finish(count - 1, buffers[1])


def build_tiles(stage, fresh, n, rows, cols, state, group, blocks_dev, cap, name):
    places = list(fresh)
    pts = list(fresh.values())
    width = pts[0].shape[1]
    total = (group + 1) * blocks_dev
    near = group * blocks_dev
    shapes = [
        jax.ShapeDtypeStruct((total * PTS, width), jnp.bfloat16),
        jax.ShapeDtypeStruct((total, 8, PTS), jnp.float32),
        jax.ShapeDtypeStruct((near, PTS, 128), jnp.float32),
    ]
    makes = stage is not None
    if makes:
        shapes.append(jax.ShapeDtypeStruct((cap + 1, PTS, PTS), jnp.bfloat16))
    state = state[: len(shapes)]
    scalars = (n, rows, cols) if makes else ()
    first = len(scalars) + len(pts)

    def kernel(*refs):
        pt_refs = refs[len(scalars) : first]
        window, level_row, level_col, *rest = refs[first + len(state) :]
        for place, piece in zip(places, pt_refs):
            blocks = piece.shape[0] // PTS
            window[place * PTS : (place + blocks) * PTS, :] = piece[...]
            for block in range(place, place + blocks):
                set_levels(block, window, level_row, level_col, 3.0 / width * LOG2E)
        if makes:
            n_ref, row_ref, col_ref = refs[:3]
            kept, *buffers = rest
            make_tiles(
                n_ref[stage],
                n_ref[stage + 1],
                row_ref,
                col_ref,
                window,
                level_row,
                level_col,
                kept,
                buffers,
            )

    return pl.pallas_call(
        kernel,
        out_shape=shapes,
        in_specs=[spec(SMEM)] * len(scalars) + [spec(VMEM)] * (len(pts) + len(state)),
        out_specs=[spec(VMEM)] * len(shapes),
        input_output_aliases={first + index: index for index in range(len(state))},
        scratch_shapes=[VMEM((PTS, PTS), jnp.float32)] * (2 if makes else 0),
        cost_estimate=cost(2**32 if stage == 2 else 2**20, 2**20),
        compiler_params=pltpu.CompilerParams(vmem_limit_bytes=6 * 2**20),
        name=name,
    )(*scalars, *pts, *state)


def products(entries, kinds, vecs, tiles, start, targets, height, folds):
    firsts = sorted(vecs)
    tall, held = vecs[firsts[0]].shape
    blocks_dev = held // PTS
    begun = list(start)
    source_low, source_high = firsts[0], firsts[-1] + blocks_dev
    low = min(first for ranges in targets for first, _ in ranges)
    high = max(last for ranges in targets for _, last in ranges)
    shapes = [
        jax.ShapeDtypeStruct((sum(last - first for first, last in ranges), height, PTS), jnp.float32)
        for ranges in targets
    ]

    def pieces(refs):
        for ranges, ref in zip(targets, refs):
            at = 0
            for first, last in ranges:
                yield ref, slice(at, at + last - first), slice(first - low, last - low)
                at += last - first

    def fold(value):
        out = value[:height]
        for index in range(1, folds):
            out = out + value[index * height : (index + 1) * height]
        return out

    def kernel(*refs):
        tile_ref, source_ref, target_ref, bounds = refs[:4]
        vec_refs = refs[4 : 4 + len(firsts)]
        kept = refs[4 + len(firsts)]
        start_refs = refs[5 + len(firsts) : 5 + len(firsts) + len(begun)]
        outs = refs[5 + len(firsts) + len(begun) : -2]
        u_win, acc = refs[-2:]
        for first, ref in zip(firsts, vec_refs):
            for block in range(blocks_dev):
                lanes = slice(block * PTS, (block + 1) * PTS)
                u_win[first - source_low + block] = ref[:, lanes]
        if begun:
            for ref, inside, places in pieces(start_refs):
                acc[places] = ref[inside]
        else:
            for place in range(high - low + 1):
                acc[place] = jnp.zeros((height, PTS), jnp.float32)

        spare = high - low
        unroll = 4

        def several(begin, end, transposed):
            def body(step, carry):
                done = []
                for lane in range(unroll):
                    index = begin + step * unroll + lane
                    valid = index < end
                    index = jnp.minimum(index, end - 1)
                    vec = u_win[source_ref[index] - source_low]
                    tile = kept[tile_ref[index]]
                    if transposed:
                        value = lax.dot_general(
                            vec,
                            tile,
                            (((1,), (1,)), ((), ())),
                            preferred_element_type=jnp.float32,
                        )
                    else:
                        value = jnp.dot(vec, tile, preferred_element_type=jnp.float32)
                    done.append((jnp.where(valid, target_ref[index] - low, spare), fold(value)))
                for target, value in done:
                    acc[target] += value
                return carry

            lax.fori_loop(0, lax.div(end - begin + unroll - 1, unroll), body, 0)

        for kind in kinds:
            several(bounds[2 * kind], bounds[2 * kind + 1], True)
            several(bounds[2 * kind + 1], bounds[2 * kind + 2], False)
        for out, inside, places in pieces(outs):
            out[inside] = acc[places]

    call = pl.pallas_call(
        kernel,
        out_shape=shapes,
        in_specs=[spec(SMEM)] * 4 + [spec(VMEM)] * (len(firsts) + 1 + len(begun)),
        out_specs=[spec(VMEM)] * len(shapes),
        scratch_shapes=[
            VMEM((source_high - source_low, tall, PTS), jnp.bfloat16),
            VMEM((high - low + 1, height, PTS), jnp.float32),
        ],
        cost_estimate=cost(2**31 if TO_OTHERS in kinds else 2**20, 2**20),
        compiler_params=pltpu.CompilerParams(vmem_limit_bytes=10 * 2**20),
        name="products",
    )
    return list(call(*entries, *[vecs[first] for first in firsts], tiles, *begun))


def urgent_ranges(group, blocks_dev):
    messages = [
        [rel for rel in range(group) if rel & bit and rel % bit == 0] for bit in bits_of(group)
    ]
    return [
        [(rel * blocks_dev, (rel + 1) * blocks_dev) for rel in rels]
        for rels in messages + [[group]]
    ]


def send_urgent(results, later, group, blocks_dev):
    *messages, far = results
    final = [from_behind(far, "blk", 1)]
    parts = {}
    for bit, message in zip(bits_of(group), messages):
        rels = [rel for rel in range(group) if rel & bit and rel % bit == 0]
        for index, rel in enumerate(rels):
            if rel in parts:
                held = message[index * blocks_dev : (index + 1) * blocks_dev]
                message = held + parts[rel] if len(rels) == 1 else message.at[
                    index * blocks_dev : (index + 1) * blocks_dev
                ].add(parts[rel])
        if bit > 1:
            message, *later = lax.optimization_barrier((message, *later))
        got = swap(message, "grp", bit)
        final.append(got)
        for index, rel in enumerate(rels):
            if rel ^ bit:
                piece = got[index * blocks_dev : (index + 1) * blocks_dev]
                parts[rel ^ bit] = parts[rel ^ bit] + piece if rel ^ bit in parts else piece
    return final, later


def finish_home(entries, vecs, tiles, start, blocks_dev, height, folds):
    return products(entries, (TO_OWN,), vecs, tiles, [start], [[(0, blocks_dev)]], height, folds)


def scaled_gram(parts, own, counts, degree, earlier):
    columns = own.shape[0] if degree is not None else own.shape[0] - EXTRA
    total = own.shape[1]
    first = degree is None
    shapes = [
        jax.ShapeDtypeStruct((columns, total), jnp.float32),
        jax.ShapeDtypeStruct((columns, columns * (1 if first else 2)), jnp.float32),
    ]
    if first:
        shapes.append(jax.ShapeDtypeStruct((2 * columns, total), jnp.bfloat16))
        shapes.append(jax.ShapeDtypeStruct((8, total), jnp.float32))
    operands = list(parts) + [own]
    operands += [] if first else [degree, earlier]

    def kernel(count_ref, *refs):
        ins = list(refs[: len(operands)])
        outs = list(refs[len(operands) :])
        part_refs = ins[: len(parts)]
        own_ref = ins[len(parts)]
        z_out, gram_out = outs[:2]
        gram = jnp.zeros((columns, columns), jnp.float32)
        for block in range(total // PTS):
            lanes = slice(block * PTS, (block + 1) * PTS)
            sums = part_refs[0][block]
            for part in part_refs[1:]:
                sums = sums + part[block]
            if first:
                level = 1.0 + sums[columns : columns + 1, :]
                outs[-1][:, lanes] = jnp.broadcast_to(level, (8, PTS))
            else:
                level = ins[len(parts) + 1][0:1, lanes]
            used = lax.broadcasted_iota(jnp.int32, (columns, PTS), 1) < count_ref[block]
            held = own_ref[0:columns, lanes].astype(jnp.float32)
            z = (held + jnp.where(used, sums[0:columns], 0.0)) / level
            z_out[:, lanes] = z
            if first:
                high = z.astype(jnp.bfloat16)
                outs[2][0:columns, lanes] = high
                rest = z - high.astype(jnp.float32)
                outs[2][columns : 2 * columns, lanes] = rest.astype(jnp.bfloat16)
            gram = gram + lax.dot_general(
                z, z, (((1,), (1,)), ((), ())), precision=HIGHEST, preferred_element_type=jnp.float32
            )
        if not first:
            gram = jnp.concatenate([ins[-1][...], gram], axis=1)
        gram_out[...] = gram

    return pl.pallas_call(
        kernel,
        out_shape=tuple(shapes),
        in_specs=[spec(SMEM)] + [spec(VMEM)] * len(operands),
        out_specs=(spec(VMEM),) * len(shapes),
        cost_estimate=cost(2**26, 2**21),
        compiler_params=pltpu.CompilerParams(vmem_limit_bytes=6 * 2**20),
        name="scaled_gram",
    )(counts, *operands)


def inverse_factor(gram):
    size = gram.shape[0]
    row_id = lax.broadcasted_iota(jnp.int32, (size, size), 0)
    col_id = lax.broadcasted_iota(jnp.int32, (size, size), 1)
    eye = jnp.where(row_id == col_id, 1.0, 0.0)
    whole = jnp.concatenate([gram, eye], axis=1)
    wide = 2 * size
    count = size // 8
    groups = [whole[8 * g : 8 * g + 8, :] for g in range(count)]
    within = lax.broadcasted_iota(jnp.int32, (8, wide), 0)

    def spread_row(value, row):
        return jnp.broadcast_to(value[row : row + 1, :], (8, wide))

    results = []
    for g in range(count):
        spread = [
            [
                jnp.broadcast_to(groups[other][:, 8 * g + k : 8 * g + k + 1], (8, wide))
                for other in range(g, count)
            ]
            for k in range(8)
        ]
        pivots = jnp.ones((8, wide), jnp.float32)
        for j in range(8):
            column = spread[j]
            pivot = spread_row(column[0], j)
            pivots = jnp.where(within == j, pivot, pivots)
            over = 1.0 / pivot
            below = jnp.where(within > j, column[0], 0.0)
            for k in range(j + 1, 8):
                share = spread_row(column[0], k) * over
                spread[k][0] = spread[k][0] - below * share
                for other in range(1, count - g):
                    spread[k][other] = spread[k][other] - column[other] * share
            top = spread_row(groups[g], j) * over
            groups[g] = groups[g] - below * top
            for other in range(1, count - g):
                groups[g + other] = groups[g + other] - column[other] * top
        results.append(groups[g] * lax.rsqrt(pivots))
    return jnp.concatenate(results, axis=0)[:, size:wide]


def exact_dot(left, right, contract):
    return lax.dot_general(
        left,
        right,
        (contract, ((), ())),
        precision=HIGHEST,
        preferred_element_type=jnp.float32,
    )


def factors_kernel(grams, both_out, first_out, sound_out):
    columns = grams.shape[0]
    plain = ((1,), (0,))
    turned = ((1,), (1,))
    second = grams[:, columns : 2 * columns]
    first_inverse = inverse_factor(grams[:, 0:columns])
    middle = exact_dot(exact_dot(first_inverse, second, plain), first_inverse, turned)
    both = exact_dot(inverse_factor(middle), first_inverse, plain)
    both_out[...] = both
    first_out[...] = first_inverse
    row_id = lax.broadcasted_iota(jnp.int32, (columns, columns), 0)
    col_id = lax.broadcasted_iota(jnp.int32, (columns, columns), 1)
    trace = jnp.sum(jnp.where(row_id == col_id, second, 0.0))
    spread = jnp.sum(both * both) * trace / (columns * columns)
    sound_out[0] = jnp.where(spread < 64.0, 1, 0)


def factors(grams):
    columns = grams.shape[0]
    square = jax.ShapeDtypeStruct((columns, columns), jnp.float32)
    return pl.pallas_call(
        factors_kernel,
        out_shape=(square, square, jax.ShapeDtypeStruct((1,), jnp.int32)),
        in_specs=[spec(VMEM)],
        out_specs=(spec(VMEM), spec(VMEM), spec(SMEM)),
        cost_estimate=cost(2**30, 2**16),
        compiler_params=pltpu.CompilerParams(vmem_limit_bytes=2 * 2**20),
        name="factors",
    )(grams)


def apply_kernel(factor, z, out, *gram):
    value = exact_dot(factor[...], z[...], ((1,), (0,)))
    out[...] = value
    if gram:
        gram[0][...] = exact_dot(value, value, ((1,), (1,)))


def applied(factor, z, with_gram):
    shapes = [jax.ShapeDtypeStruct(z.shape, jnp.float32)]
    if with_gram:
        shapes.append(jax.ShapeDtypeStruct(factor.shape, jnp.float32))
    return pl.pallas_call(
        apply_kernel,
        out_shape=shapes,
        in_specs=[spec(VMEM)] * 2,
        out_specs=[spec(VMEM)] * len(shapes),
        compiler_params=pltpu.CompilerParams(vmem_limit_bytes=4 * 2**20),
        name="applied",
    )(factor, z)


def second_kernel(gram, first, out):
    out[...] = exact_dot(inverse_factor(gram[...]), first[...], ((1,), (0,)))


def second_factor(gram, first):
    return pl.pallas_call(
        second_kernel,
        out_shape=jax.ShapeDtypeStruct(gram.shape, jnp.float32),
        in_specs=[spec(VMEM)] * 2,
        out_specs=spec(VMEM),
        compiler_params=pltpu.CompilerParams(vmem_limit_bytes=2 * 2**20),
        name="second_factor",
    )(gram, first)


def sum_stages():
    return bits_of(lax.axis_size("blk") * lax.axis_size("grp"))


def pairs_of(bits):
    return [bits[first : first + 2] for first in range(0, len(bits), 2)]


def all_sum(value, stages, beside=None):
    count = lax.axis_size("blk") * lax.axis_size("grp")
    for bits in stages:
        moves = [0]
        for bit in bits if isinstance(bits, list) else [bits]:
            moves += [move ^ bit for move in moves]
        terms = [value] + [
            lax.ppermute(value, ("blk", "grp"), [(source, source ^ move) for source in range(count)])
            for move in moves[1:]
        ]
        if beside is not None:
            terms[0], beside = lax.optimization_barrier((terms[0], beside))
        while len(terms) > 1:
            terms = [left + right for left, right in zip(terms[::2], terms[1::2])]
        value = terms[0]
    return value if beside is None else (value, beside)


def per_device(points, counts, pair_rows, pair_cols, pair_live, start):
    group = lax.axis_size("grp")
    blocks_dev = counts.shape[0]
    columns = start.shape[0]
    slots = pair_rows.shape[0]
    cap = max(-(-slots // group), blocks_dev * blocks_dev * group)
    half = (blocks_dev // 2) * PTS

    home = min(2, group) * blocks_dev

    rows, cols, n, *entries = listing(
        pair_rows, pair_cols, pair_live, group, cap, blocks_dev
    )
    first_chunk = points[:half]
    rest, first_chunk = lax.optimization_barrier((points, first_chunk))
    mate = swap(rest, "grp", 1)
    chunks = [first_chunk, rest[half:]]
    far = [from_behind(chunk, "blk", -1) for chunk in chunks]
    crossed = [gather_far_bits(chunk) for chunk in chunks]
    vec = opening(start, counts)
    tied = lax.optimization_barrier((vec, n, rows, cols, far[0], *crossed[0].values()))
    vec, n, rows, cols, far[0] = tied[:5]
    crossed[0] = dict(zip(crossed[0], tied[5:]))
    cross_vec = gather_far_bits(vec)
    far_vec = from_behind(vec, "blk", -1)
    mate_vec = swap(vec, "grp", 1)

    def direct(index):
        offset = index * (blocks_dev // 2)
        found = {group * blocks_dev + offset: far[index]}
        for rel, value in crossed[index].items():
            found[rel * blocks_dev + offset] = value
        return found

    def passed_on(index):
        offset = index * (blocks_dev // 2)
        found = {}
        for rel, value in crossed[index].items():
            cut = value.shape[0] // (1 if index else 2)
            parts = [swap(value[at : at + cut], "grp", 1) for at in range(0, value.shape[0], cut)]
            found[(rel ^ 1) * blocks_dev + offset] = jnp.concatenate(parts, 0)
        return found

    def build(stage, fresh, state, name):
        return list(
            build_tiles(stage, fresh, n, rows, cols, state, group, blocks_dev, cap, name)
        )

    state = build(0, {0: points, blocks_dev: mate, **direct(0)}, (), "first_tiles")
    state = build(1, passed_on(0), state, "second_tiles")
    urgent = urgent_ranges(group, blocks_dev)
    ranges = [[(0, blocks_dev)]] + urgent
    height = columns + 8
    vecs_home = {0: vec, blocks_dev: mate_vec}
    begun = products(entries, (HOME_EARLY,), vecs_home, state[3], (), ranges, height, 1)
    tied = lax.optimization_barrier((far[1], begun[0], state[1], *crossed[1].values()))
    far[1], begun[0], state[1] = tied[:3]
    crossed[1] = dict(zip(crossed[1], tied[3:]))
    last = passed_on(1)
    *grown, kept = state
    state = build(None, direct(1), grown, "more_blocks") + [kept]
    state = build(2, last, state, "last_tiles")
    kept = state[-1]
    tied = lax.optimization_barrier((kept, *cross_vec.values()))
    kept = tied[0]
    cross_vec = dict(zip(cross_vec, tied[1:]))

    def window_of(own, mate, crossed, far):
        found = {0: own, blocks_dev: mate, group * blocks_dev: far}
        for rel, value in crossed.items():
            found[rel * blocks_dev] = value
            found[(rel ^ 1) * blocks_dev] = swap(value, "grp", 1)
        return found

    def beyond(vecs):
        return {place: value for place, value in vecs.items() if place >= home}

    vecs = window_of(vec, mate_vec, cross_vec, far_vec)
    at_home, *results = products(
        entries, (HOME_LAST,), vecs_home, kept, begun, ranges, height, 1
    )
    results = products(entries, (TO_OTHERS,), beyond(vecs), kept, results, urgent, height, 1)
    sums, (at_home,) = send_urgent(results, (at_home,), group, blocks_dev)
    sums = finish_home(entries, beyond(vecs), kept, at_home, blocks_dev, height, 1) + sums
    z, gram, parts, degree = scaled_gram(sums, vec, counts, None, None)

    far_part = from_behind(parts, "blk", -1)
    crossed = gather_far_bits(parts)
    mate_part = swap(parts, "grp", 1)
    at_home, *results = products(
        entries,
        (HOME_EARLY, HOME_LAST),
        {0: parts, blocks_dev: mate_part},
        kept,
        (),
        ranges,
        columns,
        2,
    )
    at_home, *tied = lax.optimization_barrier((at_home, *crossed.values()))
    crossed = dict(zip(crossed, tied))
    vecs = beyond(window_of(parts, mate_part, crossed, far_part))
    results = products(entries, (TO_OTHERS,), vecs, kept, results, urgent, columns, 2)
    sums, (at_home,) = send_urgent(results, (at_home,), group, blocks_dev)
    sums = finish_home(entries, vecs, kept, at_home, blocks_dev, columns, 2) + sums
    z, grams = scaled_gram(sums, z, counts, degree, gram)

    stages = sum_stages()
    stages = stages[:1] + pairs_of(stages[1:])
    both, first, sound = factors(all_sum(grams, stages))

    def at_once(both, first, z):
        return both

    def in_two(both, first, z):
        return second_factor(all_sum(applied(first, z, True)[1], stages), first)

    return applied(lax.cond(sound[0] == 1, at_once, in_two, both, first, z), z, False)[0]


def solution(mesh):
    in_specs = (
        P(("blk", "grp"), None),
        P(("blk", "grp")),
        P("blk"),
        P("blk"),
        P("blk"),
        P(None, ("blk", "grp")),
    )
    out_specs = P(None, ("blk", "grp"))
    return jax.shard_map(
        per_device, mesh=mesh, in_specs=in_specs, out_specs=out_specs, check_vma=False
    )
```

```python
import functools

import jax
import jax.numpy as jnp
from jax import lax
from jax.experimental import pallas as pl
from jax.experimental.pallas import tpu as pltpu
from jax.sharding import PartitionSpec as P

PTS = 512
LOG2E = 1.4426950408889634
DEAD = 65536.0
EXTRA = 16
HOME_EARLY, HOME_LAST, TO_OTHERS, TO_OWN = range(4)
KINDS = 4
VMEM = pltpu.VMEM
SMEM = pltpu.SMEM
HIGHEST = lax.Precision.HIGHEST


def cost(flops, moved):
    return pl.CostEstimate(flops=int(flops), bytes_accessed=int(moved), transcendentals=0)


def spec(space):
    return pl.BlockSpec(memory_space=space)


def swap(value, axis, bit):
    count = lax.axis_size(axis)
    return lax.ppermute(value, axis, [(source, source ^ bit) for source in range(count)])


def from_behind(value, axis, steps):
    count = lax.axis_size(axis)
    initial, last = (max(0, -steps), min(count, count - steps))
    return lax.ppermute(value, axis, [(source, source + steps) for source in range(initial, last)])


def bits_of(count):
    bits = []
    bit = 1
    while bit < count:
        bits.append(bit)
        bit *= 2
    return bits


def gather_near(value, axis):
    held = {0: value}
    for bit in reversed(bits_of(lax.axis_size(axis))):
        for rel in list(held):
            held[rel ^ bit] = swap(held[rel], axis, bit)
    return [held[rel] for rel in range(len(held))]


def gather_far_bits(value):
    held = {0: value}
    for bit in reversed(bits_of(lax.axis_size("grp"))[1:]):
        for rel in list(held):
            held[rel ^ bit] = swap(held[rel], "grp", bit)
    held.pop(0)
    return held


def opening_kernel(start, counts, out):
    columns, total = start.shape
    for block in range(total // PTS):
        lanes = slice(block * PTS, (block + 1) * PTS)
        used = lax.broadcasted_iota(jnp.int32, (columns, PTS), 1) < counts[block]
        out[0:columns, lanes] = jnp.where(used, start[:, lanes], 0.0).astype(jnp.bfloat16)
        which = lax.broadcasted_iota(jnp.int32, (EXTRA, PTS), 0)
        place_in = lax.broadcasted_iota(jnp.int32, (EXTRA, PTS), 1)
        ones = jnp.logical_and(which == 0, place_in < counts[block])
        out[columns : columns + EXTRA, lanes] = jnp.where(ones, 1.0, 0.0).astype(jnp.bfloat16)


def opening(start, counts):
    columns, total = start.shape
    return pl.pallas_call(
        opening_kernel,
        out_shape=jax.ShapeDtypeStruct((columns + EXTRA, total), jnp.bfloat16),
        in_specs=[spec(VMEM), spec(SMEM)],
        out_specs=spec(VMEM),
        cost_estimate=cost(2**20, 2**19),
        compiler_params=pltpu.CompilerParams(vmem_limit_bytes=2 * 2**20),
        name="opening",
    )(start, counts)


def stage_of(place, group, blocks_dev):
    piece = lax.div(place, blocks_dev)
    first_half = lax.rem(place, blocks_dev) < blocks_dev // 2
    later = jnp.where(first_half, jnp.where(lax.rem(piece, 2) == 0, 0, 1), 2)
    return jnp.where(piece < min(2, group), 0, later)


def listing_kernel(
    group,
    cap,
    blocks_dev,
    rows,
    cols,
    live,
    out_rows,
    out_cols,
    out_n,
    tiles,
    sources,
    targets,
    bounds,
    owners,
    row_places,
    col_places,
):
    slab = blocks_dev * group
    member = lax.axis_index("grp")

    def local_near(block, device):
        return (lax.div(block, blocks_dev) ^ device) * blocks_dev + lax.rem(block, blocks_dev)

    def local_far(block):
        return slab + lax.rem(block - slab, blocks_dev)

    def far_of(col):
        return col >= slab

    def count_far(slot, carry):
        col = cols[slot]
        far = far_of(col)
        owner = lax.div(col - slab, blocks_dev)
        owners[slot] = jnp.where(far, owner, -1)
        return tuple(
            old + jnp.where(jnp.logical_and(far, owner == device), 1, 0)
            for device, old in enumerate(carry)
        )

    loads = lax.fori_loop(0, live[0], count_far, (jnp.int32(0),) * group)

    def give(slot, loads):
        row, col = rows[slot], cols[slot]
        near = jnp.logical_not(far_of(col))
        best = jnp.int32(2**30)
        owner = jnp.int32(0)
        for device in range(group):
            stage = jnp.maximum(
                stage_of(local_near(row, device), group, blocks_dev),
                stage_of(local_near(col, device), group, blocks_dev),
            )
            score = loads[device] + 64 * stage + jnp.where(loads[device] < cap, 0, 2**20)
            owner = jnp.where(score < best, device, owner)
            best = jnp.minimum(score, best)

        row_place = local_near(row, member)
        col_place = jnp.where(far_of(col), local_far(col), local_near(col, member))
        stage = jnp.maximum(
            stage_of(row_place, group, blocks_dev), stage_of(col_place, group, blocks_dev)
        )
        mine = jnp.where(near, owner, owners[slot]) == member
        row_places[slot] = row_place
        col_places[slot] = col_place
        owners[slot] = jnp.where(mine, stage, -1)
        return tuple(
            load + jnp.where(jnp.logical_and(near, owner == device), 1, 0)
            for device, load in enumerate(loads)
        )

    lax.fori_loop(0, live[0], give, loads)

    def place_those(wanted, filled):
        def place(slot, filled):
            mine = owners[slot] == wanted

            @pl.when(mine)
            def _():
                out_rows[filled] = row_places[slot]
                out_cols[filled] = col_places[slot]

            return filled + jnp.where(mine, 1, 0)

        return lax.fori_loop(0, live[0], place, filled)

    count = jnp.int32(0)
    out_n[0] = count
    for wanted in range(3):
        count = place_those(wanted, count)
        out_n[wanted + 1] = count

    home = min(2, group) * blocks_dev
    bounds[0] = jnp.int32(0)
    filled = jnp.int32(0)
    for kind in range(KINDS):
        for to_row in (True, False):

            def enter(index, filled):
                source = (out_cols if to_row else out_rows)[index]
                target = (out_rows if to_row else out_cols)[index]
                own_target = jnp.logical_and(source >= home, target < blocks_dev)
                other_target = jnp.logical_and(source >= home, target >= blocks_dev)
                if kind == HOME_EARLY:
                    wanted = jnp.logical_and(source < home, index < out_n[2])
                elif kind == HOME_LAST:
                    wanted = jnp.logical_and(source < home, index >= out_n[2])
                elif kind == TO_OTHERS:
                    wanted = other_target
                else:
                    wanted = own_target

                @pl.when(wanted)
                def _():
                    tiles[filled] = index
                    sources[filled] = source
                    targets[filled] = target

                return filled + jnp.where(wanted, 1, 0)

            filled = lax.fori_loop(0, count, enter, filled)
            bounds[2 * kind + (1 if to_row else 2)] = filled


def listing(rows, cols, live, group, cap, blocks_dev):
    return pl.pallas_call(
        functools.partial(listing_kernel, group, cap, blocks_dev),
        out_shape=(
            jax.ShapeDtypeStruct((cap,), jnp.int32),
            jax.ShapeDtypeStruct((cap,), jnp.int32),
            jax.ShapeDtypeStruct((4,), jnp.int32),
            jax.ShapeDtypeStruct((2 * cap,), jnp.int32),
            jax.ShapeDtypeStruct((2 * cap,), jnp.int32),
            jax.ShapeDtypeStruct((2 * cap,), jnp.int32),
            jax.ShapeDtypeStruct((2 * KINDS + 1,), jnp.int32),
        ),
        in_specs=[spec(SMEM)] * 3,
        out_specs=(spec(SMEM),) * 7,
        scratch_shapes=[SMEM((rows.shape[0],), jnp.int32)] * 3,
        cost_estimate=cost(2**20, 2**10),
        compiler_params=pltpu.CompilerParams(vmem_limit_bytes=2**20),
        name="listing",
    )(rows, cols, live)


def set_levels(place, window, level_row, level_col, scale):
    block = window[place * PTS : (place + 1) * PTS, :]
    width = block.shape[1]
    part = jnp.zeros((PTS, 128), jnp.float32)
    for lane in range(0, width, 128):
        wide = block[:, lane : lane + 128].astype(jnp.float32)
        part = part + wide * wide
    level_row[place] = scale * lax.dot_general(
        jnp.ones((8, 128), jnp.float32),
        part,
        (((1,), (1,)), ((), ())),
        precision=HIGHEST,
        preferred_element_type=jnp.float32,
    )
    if place < level_col.shape[0]:
        total = jnp.sum(part, axis=1, keepdims=True) * scale
        level_col[place] = jnp.broadcast_to(total, (PTS, 128))


def make_tiles(low, high, rows, cols, window, level_row, level_col, kept, buffers):
    width = window.shape[1]
    scale = 6.0 / width * LOG2E
    count = high - low
    spare = kept.shape[0] - 1

    def cross(tile, buffer):
        index = low + jnp.minimum(tile, count - 1)
        left = window[pl.ds(pl.multiple_of(rows[index] * PTS, PTS), PTS), :]
        right = window[pl.ds(pl.multiple_of(cols[index] * PTS, PTS), PTS), :]
        buffer[...] = lax.dot_general(
            left, right, (((1,), (1,)), ((), ())), preferred_element_type=jnp.float32
        )

    def finish(tile, buffer):
        valid = jnp.logical_and(tile >= 0, tile < count)
        index = low + jnp.clip(tile, 0, count - 1)
        row, col = rows[index], cols[index]
        right_level = level_row[col][0:1, :]
        left_level = jnp.concatenate([level_col[row]] * (PTS // 128), axis=1)
        value = jnp.exp2(buffer[...] * scale - left_level - right_level)
        kept[jnp.where(valid, index, spare)] = value.astype(jnp.bfloat16)

    def body(pair, carry):
        cross(2 * pair, buffers[0])
        finish(2 * pair - 1, buffers[1])
        cross(2 * pair + 1, buffers[1])
        finish(2 * pair, buffers[0])
        return carry

    @pl.when(count > 0)
    def _():
        buffers[1][...] = jnp.zeros((PTS, PTS), jnp.float32)

    lax.fori_loop(0, lax.div(count + 1, 2), body, 0)

    @pl.when(jnp.logical_and(count > 0, lax.rem(count, 2) == 0))
    def _():
        finish(count - 1, buffers[1])


def build_tiles(stage, fresh, n, rows, cols, state, group, blocks_dev, cap, name):
    places = list(fresh)
    pts = list(fresh.values())
    width = pts[0].shape[1]
    total = (group + 1) * blocks_dev
    near = group * blocks_dev
    shapes = [
        jax.ShapeDtypeStruct((total * PTS, width), jnp.bfloat16),
        jax.ShapeDtypeStruct((total, 8, PTS), jnp.float32),
        jax.ShapeDtypeStruct((near, PTS, 128), jnp.float32),
    ]
    makes = stage is not None
    if makes:
        shapes.append(jax.ShapeDtypeStruct((cap + 1, PTS, PTS), jnp.bfloat16))
    state = state[: len(shapes)]
    scalars = (n, rows, cols) if makes else ()
    first = len(scalars) + len(pts)

    def kernel(*refs):
        pt_refs = refs[len(scalars) : first]
        window, level_row, level_col, *rest = refs[first + len(state) :]
        for place, piece in zip(places, pt_refs):
            blocks = piece.shape[0] // PTS
            window[place * PTS : (place + blocks) * PTS, :] = piece[...]
            for block in range(place, place + blocks):
                set_levels(block, window, level_row, level_col, 3.0 / width * LOG2E)
        if makes:
            n_ref, row_ref, col_ref = refs[:3]
            kept, *buffers = rest
            make_tiles(
                n_ref[stage],
                n_ref[stage + 1],
                row_ref,
                col_ref,
                window,
                level_row,
                level_col,
                kept,
                buffers,
            )

    return pl.pallas_call(
        kernel,
        out_shape=shapes,
        in_specs=[spec(SMEM)] * len(scalars) + [spec(VMEM)] * (len(pts) + len(state)),
        out_specs=[spec(VMEM)] * len(shapes),
        input_output_aliases={first + index: index for index in range(len(state))},
        scratch_shapes=[VMEM((PTS, PTS), jnp.float32)] * (2 if makes else 0),
        cost_estimate=cost(2**32 if stage == 2 else 2**20, 2**20),
        compiler_params=pltpu.CompilerParams(vmem_limit_bytes=6 * 2**20),
        name=name,
    )(*scalars, *pts, *state)


def products(entries, kinds, vecs, tiles, start, targets, height, folds):
    firsts = sorted(vecs)
    tall, held = vecs[firsts[0]].shape
    blocks_dev = held // PTS
    begun = list(start)
    source_low, source_high = firsts[0], firsts[-1] + blocks_dev
    low = min(first for ranges in targets for first, _ in ranges)
    high = max(last for ranges in targets for _, last in ranges)
    shapes = [
        jax.ShapeDtypeStruct((sum(last - first for first, last in ranges), height, PTS), jnp.float32)
        for ranges in targets
    ]

    def pieces(refs):
        for ranges, ref in zip(targets, refs):
            at = 0
            for first, last in ranges:
                yield ref, slice(at, at + last - first), slice(first - low, last - low)
                at += last - first

    def fold(value):
        out = value[:height]
        for index in range(1, folds):
            out = out + value[index * height : (index + 1) * height]
        return out

    def kernel(*refs):
        tile_ref, source_ref, target_ref, bounds = refs[:4]
        vec_refs = refs[4 : 4 + len(firsts)]
        kept = refs[4 + len(firsts)]
        start_refs = refs[5 + len(firsts) : 5 + len(firsts) + len(begun)]
        outs = refs[5 + len(firsts) + len(begun) : -2]
        u_win, acc = refs[-2:]
        for first, ref in zip(firsts, vec_refs):
            for block in range(blocks_dev):
                lanes = slice(block * PTS, (block + 1) * PTS)
                u_win[first - source_low + block] = ref[:, lanes]
        if begun:
            for ref, inside, places in pieces(start_refs):
                acc[places] = ref[inside]
        else:
            for place in range(high - low + 1):
                acc[place] = jnp.zeros((height, PTS), jnp.float32)

        spare = high - low
        unroll = 4

        def several(begin, end, transposed):
            def body(step, carry):
                done = []
                for lane in range(unroll):
                    index = begin + step * unroll + lane
                    valid = index < end
                    index = jnp.minimum(index, end - 1)
                    vec = u_win[source_ref[index] - source_low]
                    tile = kept[tile_ref[index]]
                    if transposed:
                        value = lax.dot_general(
                            vec,
                            tile,
                            (((1,), (1,)), ((), ())),
                            preferred_element_type=jnp.float32,
                        )
                    else:
                        value = jnp.dot(vec, tile, preferred_element_type=jnp.float32)
                    done.append((jnp.where(valid, target_ref[index] - low, spare), fold(value)))
                for target, value in done:
                    acc[target] += value
                return carry

            lax.fori_loop(0, lax.div(end - begin + unroll - 1, unroll), body, 0)

        for kind in kinds:
            several(bounds[2 * kind], bounds[2 * kind + 1], True)
            several(bounds[2 * kind + 1], bounds[2 * kind + 2], False)
        for out, inside, places in pieces(outs):
            out[inside] = acc[places]

    call = pl.pallas_call(
        kernel,
        out_shape=shapes,
        in_specs=[spec(SMEM)] * 4 + [spec(VMEM)] * (len(firsts) + 1 + len(begun)),
        out_specs=[spec(VMEM)] * len(shapes),
        scratch_shapes=[
            VMEM((source_high - source_low, tall, PTS), jnp.bfloat16),
            VMEM((high - low + 1, height, PTS), jnp.float32),
        ],
        cost_estimate=cost(2**31 if TO_OTHERS in kinds else 2**20, 2**20),
        compiler_params=pltpu.CompilerParams(vmem_limit_bytes=10 * 2**20),
        name="products",
    )
    return list(call(*entries, *[vecs[first] for first in firsts], tiles, *begun))


def urgent_ranges(group, blocks_dev):
    messages = [
        [rel for rel in range(group) if rel & bit and rel % bit == 0] for bit in bits_of(group)
    ]
    return [
        [(rel * blocks_dev, (rel + 1) * blocks_dev) for rel in rels]
        for rels in messages + [[group]]
    ]


def send_urgent(results, later, group, blocks_dev):
    *messages, far = results
    final = [from_behind(far, "blk", 1)]
    parts = {}
    for bit, message in zip(bits_of(group), messages):
        rels = [rel for rel in range(group) if rel & bit and rel % bit == 0]
        for index, rel in enumerate(rels):
            if rel in parts:
                held = message[index * blocks_dev : (index + 1) * blocks_dev]
                message = held + parts[rel] if len(rels) == 1 else message.at[
                    index * blocks_dev : (index + 1) * blocks_dev
                ].add(parts[rel])
        if bit > 1:
            message, *later = lax.optimization_barrier((message, *later))
        got = swap(message, "grp", bit)
        final.append(got)
        for index, rel in enumerate(rels):
            if rel ^ bit:
                piece = got[index * blocks_dev : (index + 1) * blocks_dev]
                parts[rel ^ bit] = parts[rel ^ bit] + piece if rel ^ bit in parts else piece
    return final, later


def finish_home(entries, vecs, tiles, start, blocks_dev, height, folds):
    return products(entries, (TO_OWN,), vecs, tiles, [start], [[(0, blocks_dev)]], height, folds)


def scaled_gram(parts, own, counts, degree, earlier):
    columns = own.shape[0] if degree is not None else own.shape[0] - EXTRA
    total = own.shape[1]
    first = degree is None
    shapes = [
        jax.ShapeDtypeStruct((columns, total), jnp.float32),
        jax.ShapeDtypeStruct((columns, columns * (1 if first else 2)), jnp.float32),
    ]
    if first:
        shapes.append(jax.ShapeDtypeStruct((2 * columns, total), jnp.bfloat16))
        shapes.append(jax.ShapeDtypeStruct((8, total), jnp.float32))
    operands = list(parts) + [own]
    operands += [] if first else [degree, earlier]

    def kernel(count_ref, *refs):
        ins = list(refs[: len(operands)])
        outs = list(refs[len(operands) :])
        part_refs = ins[: len(parts)]
        own_ref = ins[len(parts)]
        z_out, gram_out = outs[:2]
        gram = jnp.zeros((columns, columns), jnp.float32)
        for block in range(total // PTS):
            lanes = slice(block * PTS, (block + 1) * PTS)
            sums = part_refs[0][block]
            for part in part_refs[1:]:
                sums = sums + part[block]
            if first:
                level = 1.0 + sums[columns : columns + 1, :]
                outs[-1][:, lanes] = jnp.broadcast_to(level, (8, PTS))
            else:
                level = ins[len(parts) + 1][0:1, lanes]
            used = lax.broadcasted_iota(jnp.int32, (columns, PTS), 1) < count_ref[block]
            held = own_ref[0:columns, lanes].astype(jnp.float32)
            z = (held + jnp.where(used, sums[0:columns], 0.0)) / level
            z_out[:, lanes] = z
            if first:
                high = z.astype(jnp.bfloat16)
                outs[2][0:columns, lanes] = high
                rest = z - high.astype(jnp.float32)
                outs[2][columns : 2 * columns, lanes] = rest.astype(jnp.bfloat16)
            gram = gram + lax.dot_general(
                z, z, (((1,), (1,)), ((), ())), precision=HIGHEST, preferred_element_type=jnp.float32
            )
        if not first:
            gram = jnp.concatenate([ins[-1][...], gram], axis=1)
        gram_out[...] = gram

    return pl.pallas_call(
        kernel,
        out_shape=tuple(shapes),
        in_specs=[spec(SMEM)] + [spec(VMEM)] * len(operands),
        out_specs=(spec(VMEM),) * len(shapes),
        cost_estimate=cost(2**26, 2**21),
        compiler_params=pltpu.CompilerParams(vmem_limit_bytes=6 * 2**20),
        name="scaled_gram",
    )(counts, *operands)


def inverse_factor(gram):
    size = gram.shape[0]
    row_id = lax.broadcasted_iota(jnp.int32, (size, size), 0)
    col_id = lax.broadcasted_iota(jnp.int32, (size, size), 1)
    eye = jnp.where(row_id == col_id, 1.0, 0.0)
    whole = jnp.concatenate([gram, eye], axis=1)
    wide = 2 * size
    count = size // 8
    groups = [whole[8 * g : 8 * g + 8, :] for g in range(count)]
    within = lax.broadcasted_iota(jnp.int32, (8, wide), 0)

    def spread_row(value, row):
        return jnp.broadcast_to(value[row : row + 1, :], (8, wide))

    results = []
    for g in range(count):
        spread = [
            [
                jnp.broadcast_to(groups[other][:, 8 * g + k : 8 * g + k + 1], (8, wide))
                for other in range(g, count)
            ]
            for k in range(8)
        ]
        pivots = jnp.ones((8, wide), jnp.float32)
        for j in range(8):
            column = spread[j]
            pivot = spread_row(column[0], j)
            pivots = jnp.where(within == j, pivot, pivots)
            over = 1.0 / pivot
            below = jnp.where(within > j, column[0], 0.0)
            for k in range(j + 1, 8):
                share = spread_row(column[0], k) * over
                spread[k][0] = spread[k][0] - below * share
                for other in range(1, count - g):
                    spread[k][other] = spread[k][other] - column[other] * share
            top = spread_row(groups[g], j) * over
            groups[g] = groups[g] - below * top
            for other in range(1, count - g):
                groups[g + other] = groups[g + other] - column[other] * top
        results.append(groups[g] * lax.rsqrt(pivots))
    return jnp.concatenate(results, axis=0)[:, size:wide]


def exact_dot(left, right, contract):
    return lax.dot_general(
        left,
        right,
        (contract, ((), ())),
        precision=HIGHEST,
        preferred_element_type=jnp.float32,
    )


def factors_kernel(grams, both_out, first_out, sound_out):
    columns = grams.shape[0]
    plain = ((1,), (0,))
    turned = ((1,), (1,))
    second = grams[:, columns : 2 * columns]
    first_inverse = inverse_factor(grams[:, 0:columns])
    middle = exact_dot(exact_dot(first_inverse, second, plain), first_inverse, turned)
    both = exact_dot(inverse_factor(middle), first_inverse, plain)
    both_out[...] = both
    first_out[...] = first_inverse
    row_id = lax.broadcasted_iota(jnp.int32, (columns, columns), 0)
    col_id = lax.broadcasted_iota(jnp.int32, (columns, columns), 1)
    trace = jnp.sum(jnp.where(row_id == col_id, second, 0.0))
    spread = jnp.sum(both * both) * trace / (columns * columns)
    sound_out[0] = jnp.where(spread < 64.0, 1, 0)


def factors(grams):
    columns = grams.shape[0]
    square = jax.ShapeDtypeStruct((columns, columns), jnp.float32)
    return pl.pallas_call(
        factors_kernel,
        out_shape=(square, square, jax.ShapeDtypeStruct((1,), jnp.int32)),
        in_specs=[spec(VMEM)],
        out_specs=(spec(VMEM), spec(VMEM), spec(SMEM)),
        cost_estimate=cost(2**30, 2**16),
        compiler_params=pltpu.CompilerParams(vmem_limit_bytes=2 * 2**20),
        name="factors",
    )(grams)


def apply_kernel(factor, z, out, *gram):
    value = exact_dot(factor[...], z[...], ((1,), (0,)))
    out[...] = value
    if gram:
        gram[0][...] = exact_dot(value, value, ((1,), (1,)))


def applied(factor, z, with_gram):
    shapes = [jax.ShapeDtypeStruct(z.shape, jnp.float32)]
    if with_gram:
        shapes.append(jax.ShapeDtypeStruct(factor.shape, jnp.float32))
    return pl.pallas_call(
        apply_kernel,
        out_shape=shapes,
        in_specs=[spec(VMEM)] * 2,
        out_specs=[spec(VMEM)] * len(shapes),
        compiler_params=pltpu.CompilerParams(vmem_limit_bytes=4 * 2**20),
        name="applied",
    )(factor, z)


def second_kernel(gram, first, out):
    out[...] = exact_dot(inverse_factor(gram[...]), first[...], ((1,), (0,)))


def second_factor(gram, first):
    return pl.pallas_call(
        second_kernel,
        out_shape=jax.ShapeDtypeStruct(gram.shape, jnp.float32),
        in_specs=[spec(VMEM)] * 2,
        out_specs=spec(VMEM),
        compiler_params=pltpu.CompilerParams(vmem_limit_bytes=2 * 2**20),
        name="second_factor",
    )(gram, first)


def sum_stages():
    return bits_of(lax.axis_size("blk") * lax.axis_size("grp"))


def pairs_of(bits):
    return [bits[first : first + 2] for first in range(0, len(bits), 2)]


def all_sum(value, stages, beside=None):
    count = lax.axis_size("blk") * lax.axis_size("grp")
    for bits in stages:
        moves = [0]
        for bit in bits if isinstance(bits, list) else [bits]:
            moves += [move ^ bit for move in moves]
        terms = [value] + [
            lax.ppermute(value, ("blk", "grp"), [(source, source ^ move) for source in range(count)])
            for move in moves[1:]
        ]
        if beside is not None:
            terms[0], beside = lax.optimization_barrier((terms[0], beside))
        while len(terms) > 1:
            terms = [left + right for left, right in zip(terms[::2], terms[1::2])]
        value = terms[0]
    return value if beside is None else (value, beside)


def per_device(points, counts, pair_rows, pair_cols, pair_live, start):
    group = lax.axis_size("grp")
    blocks_dev = counts.shape[0]
    columns = start.shape[0]
    slots = pair_rows.shape[0]
    cap = max(-(-slots // group), blocks_dev * blocks_dev * group)
    half = (blocks_dev // 2) * PTS

    home = min(2, group) * blocks_dev

    rows, cols, n, *entries = listing(
        pair_rows, pair_cols, pair_live, group, cap, blocks_dev
    )
    first_chunk = points[:half]
    rest, first_chunk = lax.optimization_barrier((points, first_chunk))
    mate = swap(rest, "grp", 1)
    chunks = [first_chunk, rest[half:]]
    far = [from_behind(chunk, "blk", -1) for chunk in chunks]
    crossed = [gather_far_bits(chunk) for chunk in chunks]
    vec = opening(start, counts)
    tied = lax.optimization_barrier((vec, n, rows, cols, far[0], *crossed[0].values()))
    vec, n, rows, cols, far[0] = tied[:5]
    crossed[0] = dict(zip(crossed[0], tied[5:]))
    far_vec = from_behind(vec, "blk", -1)
    cross_vec = gather_far_bits(vec)
    mate_vec = swap(vec, "grp", 1)

    def direct(index):
        offset = index * (blocks_dev // 2)
        found = {group * blocks_dev + offset: far[index]}
        for rel, value in crossed[index].items():
            found[rel * blocks_dev + offset] = value
        return found

    def passed_on(index):
        offset = index * (blocks_dev // 2)
        found = {}
        for rel, value in crossed[index].items():
            cut = value.shape[0] // (1 if index else 2)
            parts = [swap(value[at : at + cut], "grp", 1) for at in range(0, value.shape[0], cut)]
            found[(rel ^ 1) * blocks_dev + offset] = jnp.concatenate(parts, 0)
        return found

    def build(stage, fresh, state, name):
        return list(
            build_tiles(stage, fresh, n, rows, cols, state, group, blocks_dev, cap, name)
        )

    state = build(0, {0: points, blocks_dev: mate, **direct(0)}, (), "first_tiles")
    state = build(1, passed_on(0), state, "second_tiles")
    urgent = urgent_ranges(group, blocks_dev)
    ranges = [[(0, blocks_dev)]] + urgent
    height = columns + 8
    vecs_home = {0: vec, blocks_dev: mate_vec}
    begun = products(entries, (HOME_EARLY,), vecs_home, state[3], (), ranges, height, 1)
    tied = lax.optimization_barrier((far[1], begun[0], state[1], *crossed[1].values()))
    far[1], begun[0], state[1] = tied[:3]
    crossed[1] = dict(zip(crossed[1], tied[3:]))
    last = passed_on(1)
    *grown, kept = state
    state = build(None, direct(1), grown, "more_blocks") + [kept]
    state = build(2, last, state, "last_tiles")
    kept = state[-1]
    tied = lax.optimization_barrier((kept, far_vec, *cross_vec.values()))
    kept, far_vec = tied[:2]
    cross_vec = dict(zip(cross_vec, tied[2:]))

    def window_of(own, mate, crossed, far):
        found = {0: own, blocks_dev: mate, group * blocks_dev: far}
        for rel, value in crossed.items():
            found[rel * blocks_dev] = value
            found[(rel ^ 1) * blocks_dev] = swap(value, "grp", 1)
        return found

    def beyond(vecs):
        return {place: value for place, value in vecs.items() if place >= home}

    vecs = window_of(vec, mate_vec, cross_vec, far_vec)
    at_home, *results = products(
        entries, (HOME_LAST,), vecs_home, kept, begun, ranges, height, 1
    )
    results = products(entries, (TO_OTHERS,), beyond(vecs), kept, results, urgent, height, 1)
    sums, (at_home,) = send_urgent(results, (at_home,), group, blocks_dev)
    sums = finish_home(entries, beyond(vecs), kept, at_home, blocks_dev, height, 1) + sums
    z, gram, parts, degree = scaled_gram(sums, vec, counts, None, None)

    far_part = from_behind(parts, "blk", -1)
    crossed = gather_far_bits(parts)
    mate_part = swap(parts, "grp", 1)
    at_home, *results = products(
        entries,
        (HOME_EARLY, HOME_LAST),
        {0: parts, blocks_dev: mate_part},
        kept,
        (),
        ranges,
        columns,
        2,
    )
    at_home, *tied = lax.optimization_barrier((at_home, *crossed.values()))
    crossed = dict(zip(crossed, tied))
    vecs = beyond(window_of(parts, mate_part, crossed, far_part))
    results = products(entries, (TO_OTHERS,), vecs, kept, results, urgent, columns, 2)
    sums, (at_home,) = send_urgent(results, (at_home,), group, blocks_dev)
    sums = finish_home(entries, vecs, kept, at_home, blocks_dev, columns, 2) + sums
    z, grams = scaled_gram(sums, z, counts, degree, gram)

    stages = sum_stages()
    stages = stages[:1] + pairs_of(stages[1:])
    both, first, sound = factors(all_sum(grams, stages))

    def at_once(both, first, z):
        return both

    def in_two(both, first, z):
        return second_factor(all_sum(applied(first, z, True)[1], stages), first)

    return applied(lax.cond(sound[0] == 1, at_once, in_two, both, first, z), z, False)[0]


def solution(mesh):
    in_specs = (
        P(("blk", "grp"), None),
        P(("blk", "grp")),
        P("blk"),
        P("blk"),
        P("blk"),
        P(None, ("blk", "grp")),
    )
    out_specs = P(None, ("blk", "grp"))
    return jax.shard_map(
        per_device, mesh=mesh, in_specs=in_specs, out_specs=out_specs, check_vma=False
    )
```

```python
import functools

import jax
import jax.numpy as jnp
from jax import lax
from jax.experimental import pallas as pl
from jax.experimental.pallas import tpu as pltpu
from jax.sharding import PartitionSpec as P

PTS = 512
LOG2E = 1.4426950408889634
DEAD = 65536.0
EXTRA = 16
HOME_EARLY, HOME_LAST, TO_OTHERS, TO_OWN = range(4)
KINDS = 4
VMEM = pltpu.VMEM
SMEM = pltpu.SMEM
HIGHEST = lax.Precision.HIGHEST


def cost(flops, moved):
    return pl.CostEstimate(flops=int(flops), bytes_accessed=int(moved), transcendentals=0)


def spec(space):
    return pl.BlockSpec(memory_space=space)


def swap(value, axis, bit):
    count = lax.axis_size(axis)
    return lax.ppermute(value, axis, [(source, source ^ bit) for source in range(count)])


def from_behind(value, axis, steps):
    count = lax.axis_size(axis)
    initial, last = (max(0, -steps), min(count, count - steps))
    return lax.ppermute(value, axis, [(source, source + steps) for source in range(initial, last)])


def bits_of(count):
    bits = []
    bit = 1
    while bit < count:
        bits.append(bit)
        bit *= 2
    return bits


def gather_near(value, axis):
    held = {0: value}
    for bit in reversed(bits_of(lax.axis_size(axis))):
        for rel in list(held):
            held[rel ^ bit] = swap(held[rel], axis, bit)
    return [held[rel] for rel in range(len(held))]


def gather_far_bits(value):
    held = {0: value}
    for bit in reversed(bits_of(lax.axis_size("grp"))[1:]):
        for rel in list(held):
            held[rel ^ bit] = swap(held[rel], "grp", bit)
    held.pop(0)
    return held


def opening_kernel(start, counts, out):
    columns, total = start.shape
    for block in range(total // PTS):
        lanes = slice(block * PTS, (block + 1) * PTS)
        used = lax.broadcasted_iota(jnp.int32, (columns, PTS), 1) < counts[block]
        out[0:columns, lanes] = jnp.where(used, start[:, lanes], 0.0).astype(jnp.bfloat16)
        which = lax.broadcasted_iota(jnp.int32, (EXTRA, PTS), 0)
        place_in = lax.broadcasted_iota(jnp.int32, (EXTRA, PTS), 1)
        ones = jnp.logical_and(which == 0, place_in < counts[block])
        out[columns : columns + EXTRA, lanes] = jnp.where(ones, 1.0, 0.0).astype(jnp.bfloat16)


def opening(start, counts):
    columns, total = start.shape
    return pl.pallas_call(
        opening_kernel,
        out_shape=jax.ShapeDtypeStruct((columns + EXTRA, total), jnp.bfloat16),
        in_specs=[spec(VMEM), spec(SMEM)],
        out_specs=spec(VMEM),
        cost_estimate=cost(2**20, 2**19),
        compiler_params=pltpu.CompilerParams(vmem_limit_bytes=2 * 2**20),
        name="opening",
    )(start, counts)


def stage_of(place, group, blocks_dev):
    piece = lax.div(place, blocks_dev)
    first_half = lax.rem(place, blocks_dev) < blocks_dev // 2
    later = jnp.where(first_half, jnp.where(lax.rem(piece, 2) == 0, 0, 1), 2)
    return jnp.where(piece < min(2, group), 0, later)


def listing_kernel(
    group,
    cap,
    blocks_dev,
    rows,
    cols,
    live,
    out_rows,
    out_cols,
    out_n,
    tiles,
    sources,
    targets,
    bounds,
    owners,
    row_places,
    col_places,
):
    slab = blocks_dev * group
    member = lax.axis_index("grp")

    def local_near(block, device):
        return (lax.div(block, blocks_dev) ^ device) * blocks_dev + lax.rem(block, blocks_dev)

    def local_far(block):
        return slab + lax.rem(block - slab, blocks_dev)

    def far_of(col):
        return col >= slab

    def count_far(slot, carry):
        col = cols[slot]
        far = far_of(col)
        owner = lax.div(col - slab, blocks_dev)
        owners[slot] = jnp.where(far, owner, -1)
        return tuple(
            old + jnp.where(jnp.logical_and(far, owner == device), 1, 0)
            for device, old in enumerate(carry)
        )

    loads = lax.fori_loop(0, live[0], count_far, (jnp.int32(0),) * group)

    def give(slot, loads):
        row, col = rows[slot], cols[slot]
        near = jnp.logical_not(far_of(col))
        best = jnp.int32(2**30)
        owner = jnp.int32(0)
        for device in range(group):
            stage = jnp.maximum(
                stage_of(local_near(row, device), group, blocks_dev),
                stage_of(local_near(col, device), group, blocks_dev),
            )
            score = loads[device] + 64 * stage + jnp.where(loads[device] < cap, 0, 2**20)
            owner = jnp.where(score < best, device, owner)
            best = jnp.minimum(score, best)

        row_place = local_near(row, member)
        col_place = jnp.where(far_of(col), local_far(col), local_near(col, member))
        stage = jnp.maximum(
            stage_of(row_place, group, blocks_dev), stage_of(col_place, group, blocks_dev)
        )
        mine = jnp.where(near, owner, owners[slot]) == member
        row_places[slot] = row_place
        col_places[slot] = col_place
        owners[slot] = jnp.where(mine, stage, -1)
        return tuple(
            load + jnp.where(jnp.logical_and(near, owner == device), 1, 0)
            for device, load in enumerate(loads)
        )

    lax.fori_loop(0, live[0], give, loads)

    def place_those(wanted, filled):
        def place(slot, filled):
            mine = owners[slot] == wanted

            @pl.when(mine)
            def _():
                out_rows[filled] = row_places[slot]
                out_cols[filled] = col_places[slot]

            return filled + jnp.where(mine, 1, 0)

        return lax.fori_loop(0, live[0], place, filled)

    count = jnp.int32(0)
    out_n[0] = count
    for wanted in range(3):
        count = place_those(wanted, count)
        out_n[wanted + 1] = count

    home = min(2, group) * blocks_dev
    bounds[0] = jnp.int32(0)
    filled = jnp.int32(0)
    for kind in range(KINDS):
        for to_row in (True, False):

            def enter(index, filled):
                source = (out_cols if to_row else out_rows)[index]
                target = (out_rows if to_row else out_cols)[index]
                own_target = jnp.logical_and(source >= home, target < blocks_dev)
                other_target = jnp.logical_and(source >= home, target >= blocks_dev)
                if kind == HOME_EARLY:
                    wanted = jnp.logical_and(source < home, index < out_n[2])
                elif kind == HOME_LAST:
                    wanted = jnp.logical_and(source < home, index >= out_n[2])
                elif kind == TO_OTHERS:
                    wanted = other_target
                else:
                    wanted = own_target

                @pl.when(wanted)
                def _():
                    tiles[filled] = index
                    sources[filled] = source
                    targets[filled] = target

                return filled + jnp.where(wanted, 1, 0)

            filled = lax.fori_loop(0, count, enter, filled)
            bounds[2 * kind + (1 if to_row else 2)] = filled


def listing(rows, cols, live, group, cap, blocks_dev):
    return pl.pallas_call(
        functools.partial(listing_kernel, group, cap, blocks_dev),
        out_shape=(
            jax.ShapeDtypeStruct((cap,), jnp.int32),
            jax.ShapeDtypeStruct((cap,), jnp.int32),
            jax.ShapeDtypeStruct((4,), jnp.int32),
            jax.ShapeDtypeStruct((2 * cap,), jnp.int32),
            jax.ShapeDtypeStruct((2 * cap,), jnp.int32),
            jax.ShapeDtypeStruct((2 * cap,), jnp.int32),
            jax.ShapeDtypeStruct((2 * KINDS + 1,), jnp.int32),
        ),
        in_specs=[spec(SMEM)] * 3,
        out_specs=(spec(SMEM),) * 7,
        scratch_shapes=[SMEM((rows.shape[0],), jnp.int32)] * 3,
        cost_estimate=cost(2**20, 2**10),
        compiler_params=pltpu.CompilerParams(vmem_limit_bytes=2**20),
        name="listing",
    )(rows, cols, live)


def set_levels(place, window, level_row, level_col, scale):
    block = window[place * PTS : (place + 1) * PTS, :]
    width = block.shape[1]
    part = jnp.zeros((PTS, 128), jnp.float32)
    for lane in range(0, width, 128):
        wide = block[:, lane : lane + 128].astype(jnp.float32)
        part = part + wide * wide
    level_row[place] = scale * lax.dot_general(
        jnp.ones((8, 128), jnp.float32),
        part,
        (((1,), (1,)), ((), ())),
        precision=HIGHEST,
        preferred_element_type=jnp.float32,
    )
    if place < level_col.shape[0]:
        total = jnp.sum(part, axis=1, keepdims=True) * scale
        level_col[place] = jnp.broadcast_to(total, (PTS, 128))


def make_tiles(low, high, rows, cols, window, level_row, level_col, kept, buffers):
    width = window.shape[1]
    scale = 6.0 / width * LOG2E
    count = high - low
    spare = kept.shape[0] - 1

    def cross(tile, buffer):
        index = low + jnp.minimum(tile, count - 1)
        left = window[pl.ds(pl.multiple_of(rows[index] * PTS, PTS), PTS), :]
        right = window[pl.ds(pl.multiple_of(cols[index] * PTS, PTS), PTS), :]
        buffer[...] = lax.dot_general(
            left, right, (((1,), (1,)), ((), ())), preferred_element_type=jnp.float32
        )

    def finish(tile, buffer):
        valid = jnp.logical_and(tile >= 0, tile < count)
        index = low + jnp.clip(tile, 0, count - 1)
        row, col = rows[index], cols[index]
        right_level = level_row[col][0:1, :]
        left_level = jnp.concatenate([level_col[row]] * (PTS // 128), axis=1)
        value = jnp.exp2(buffer[...] * scale - left_level - right_level)
        kept[jnp.where(valid, index, spare)] = value.astype(jnp.bfloat16)

    def body(pair, carry):
        cross(2 * pair, buffers[0])
        finish(2 * pair - 1, buffers[1])
        cross(2 * pair + 1, buffers[1])
        finish(2 * pair, buffers[0])
        return carry

    @pl.when(count > 0)
    def _():
        buffers[1][...] = jnp.zeros((PTS, PTS), jnp.float32)

    lax.fori_loop(0, lax.div(count + 1, 2), body, 0)

    @pl.when(jnp.logical_and(count > 0, lax.rem(count, 2) == 0))
    def _():
        finish(count - 1, buffers[1])


def build_tiles(stage, fresh, n, rows, cols, state, group, blocks_dev, cap, name):
    places = list(fresh)
    pts = list(fresh.values())
    width = pts[0].shape[1]
    total = (group + 1) * blocks_dev
    near = group * blocks_dev
    shapes = [
        jax.ShapeDtypeStruct((total * PTS, width), jnp.bfloat16),
        jax.ShapeDtypeStruct((total, 8, PTS), jnp.float32),
        jax.ShapeDtypeStruct((near, PTS, 128), jnp.float32),
    ]
    makes = stage is not None
    if makes:
        shapes.append(jax.ShapeDtypeStruct((cap + 1, PTS, PTS), jnp.bfloat16))
    state = state[: len(shapes)]
    scalars = (n, rows, cols) if makes else ()
    first = len(scalars) + len(pts)

    def kernel(*refs):
        pt_refs = refs[len(scalars) : first]
        window, level_row, level_col, *rest = refs[first + len(state) :]
        for place, piece in zip(places, pt_refs):
            blocks = piece.shape[0] // PTS
            window[place * PTS : (place + blocks) * PTS, :] = piece[...]
            for block in range(place, place + blocks):
                set_levels(block, window, level_row, level_col, 3.0 / width * LOG2E)
        if makes:
            n_ref, row_ref, col_ref = refs[:3]
            kept, *buffers = rest
            make_tiles(
                n_ref[stage],
                n_ref[stage + 1],
                row_ref,
                col_ref,
                window,
                level_row,
                level_col,
                kept,
                buffers,
            )

    return pl.pallas_call(
        kernel,
        out_shape=shapes,
        in_specs=[spec(SMEM)] * len(scalars) + [spec(VMEM)] * (len(pts) + len(state)),
        out_specs=[spec(VMEM)] * len(shapes),
        input_output_aliases={first + index: index for index in range(len(state))},
        scratch_shapes=[VMEM((PTS, PTS), jnp.float32)] * (2 if makes else 0),
        cost_estimate=cost(2**32 if stage == 2 else 2**20, 2**20),
        compiler_params=pltpu.CompilerParams(vmem_limit_bytes=6 * 2**20),
        name=name,
    )(*scalars, *pts, *state)


def products(entries, kinds, vecs, tiles, start, targets, height, folds):
    firsts = sorted(vecs)
    tall, held = vecs[firsts[0]].shape
    blocks_dev = held // PTS
    begun = list(start)
    source_low, source_high = firsts[0], firsts[-1] + blocks_dev
    low = min(first for ranges in targets for first, _ in ranges)
    high = max(last for ranges in targets for _, last in ranges)
    shapes = [
        jax.ShapeDtypeStruct((sum(last - first for first, last in ranges), height, PTS), jnp.float32)
        for ranges in targets
    ]

    def pieces(refs):
        for ranges, ref in zip(targets, refs):
            at = 0
            for first, last in ranges:
                yield ref, slice(at, at + last - first), slice(first - low, last - low)
                at += last - first

    def fold(value):
        out = value[:height]
        for index in range(1, folds):
            out = out + value[index * height : (index + 1) * height]
        return out

    def kernel(*refs):
        tile_ref, source_ref, target_ref, bounds = refs[:4]
        vec_refs = refs[4 : 4 + len(firsts)]
        kept = refs[4 + len(firsts)]
        start_refs = refs[5 + len(firsts) : 5 + len(firsts) + len(begun)]
        outs = refs[5 + len(firsts) + len(begun) : -2]
        u_win, acc = refs[-2:]
        for first, ref in zip(firsts, vec_refs):
            for block in range(blocks_dev):
                lanes = slice(block * PTS, (block + 1) * PTS)
                u_win[first - source_low + block] = ref[:, lanes]
        if begun:
            for ref, inside, places in pieces(start_refs):
                acc[places] = ref[inside]
        else:
            for place in range(high - low + 1):
                acc[place] = jnp.zeros((height, PTS), jnp.float32)

        spare = high - low
        unroll = 4

        def several(begin, end, transposed):
            def body(step, carry):
                done = []
                for lane in range(unroll):
                    index = begin + step * unroll + lane
                    valid = index < end
                    index = jnp.minimum(index, end - 1)
                    vec = u_win[source_ref[index] - source_low]
                    tile = kept[tile_ref[index]]
                    if transposed:
                        value = lax.dot_general(
                            vec,
                            tile,
                            (((1,), (1,)), ((), ())),
                            preferred_element_type=jnp.float32,
                        )
                    else:
                        value = jnp.dot(vec, tile, preferred_element_type=jnp.float32)
                    done.append((jnp.where(valid, target_ref[index] - low, spare), fold(value)))
                for target, value in done:
                    acc[target] += value
                return carry

            lax.fori_loop(0, lax.div(end - begin + unroll - 1, unroll), body, 0)

        for kind in kinds:
            several(bounds[2 * kind], bounds[2 * kind + 1], True)
            several(bounds[2 * kind + 1], bounds[2 * kind + 2], False)
        for out, inside, places in pieces(outs):
            out[inside] = acc[places]

    call = pl.pallas_call(
        kernel,
        out_shape=shapes,
        in_specs=[spec(SMEM)] * 4 + [spec(VMEM)] * (len(firsts) + 1 + len(begun)),
        out_specs=[spec(VMEM)] * len(shapes),
        scratch_shapes=[
            VMEM((source_high - source_low, tall, PTS), jnp.bfloat16),
            VMEM((high - low + 1, height, PTS), jnp.float32),
        ],
        cost_estimate=cost(2**31 if TO_OTHERS in kinds else 2**20, 2**20),
        compiler_params=pltpu.CompilerParams(vmem_limit_bytes=10 * 2**20),
        name="products",
    )
    return list(call(*entries, *[vecs[first] for first in firsts], tiles, *begun))


def urgent_ranges(group, blocks_dev):
    messages = [
        [rel for rel in range(group) if rel & bit and rel % bit == 0] for bit in bits_of(group)
    ]
    return [
        [(rel * blocks_dev, (rel + 1) * blocks_dev) for rel in rels]
        for rels in messages + [[group]]
    ]


def send_urgent(results, later, group, blocks_dev):
    *messages, far = results
    final = [from_behind(far, "blk", 1)]
    parts = {}
    for bit, message in zip(bits_of(group), messages):
        rels = [rel for rel in range(group) if rel & bit and rel % bit == 0]
        for index, rel in enumerate(rels):
            if rel in parts:
                held = message[index * blocks_dev : (index + 1) * blocks_dev]
                message = held + parts[rel] if len(rels) == 1 else message.at[
                    index * blocks_dev : (index + 1) * blocks_dev
                ].add(parts[rel])
        if bit > 1:
            message, *later = lax.optimization_barrier((message, *later))
        got = swap(message, "grp", bit)
        final.append(got)
        for index, rel in enumerate(rels):
            if rel ^ bit:
                piece = got[index * blocks_dev : (index + 1) * blocks_dev]
                parts[rel ^ bit] = parts[rel ^ bit] + piece if rel ^ bit in parts else piece
    return final, later


def finish_home(entries, vecs, tiles, start, blocks_dev, height, folds):
    return products(entries, (TO_OWN,), vecs, tiles, [start], [[(0, blocks_dev)]], height, folds)


def scaled_gram(parts, own, counts, degree, earlier):
    columns = own.shape[0] if degree is not None else own.shape[0] - EXTRA
    total = own.shape[1]
    first = degree is None
    shapes = [
        jax.ShapeDtypeStruct((columns, total), jnp.float32),
        jax.ShapeDtypeStruct((columns, columns * (1 if first else 2)), jnp.float32),
    ]
    if first:
        shapes.append(jax.ShapeDtypeStruct((2 * columns, total), jnp.bfloat16))
        shapes.append(jax.ShapeDtypeStruct((8, total), jnp.float32))
    operands = list(parts) + [own]
    operands += [] if first else [degree, earlier]

    def kernel(count_ref, *refs):
        ins = list(refs[: len(operands)])
        outs = list(refs[len(operands) :])
        part_refs = ins[: len(parts)]
        own_ref = ins[len(parts)]
        z_out, gram_out = outs[:2]
        gram = jnp.zeros((columns, columns), jnp.float32)
        for block in range(total // PTS):
            lanes = slice(block * PTS, (block + 1) * PTS)
            sums = part_refs[0][block]
            for part in part_refs[1:]:
                sums = sums + part[block]
            if first:
                level = 1.0 + sums[columns : columns + 1, :]
                outs[-1][:, lanes] = jnp.broadcast_to(level, (8, PTS))
            else:
                level = ins[len(parts) + 1][0:1, lanes]
            used = lax.broadcasted_iota(jnp.int32, (columns, PTS), 1) < count_ref[block]
            held = own_ref[0:columns, lanes].astype(jnp.float32)
            z = (held + jnp.where(used, sums[0:columns], 0.0)) / level
            z_out[:, lanes] = z
            if first:
                high = z.astype(jnp.bfloat16)
                outs[2][0:columns, lanes] = high
                rest = z - high.astype(jnp.float32)
                outs[2][columns : 2 * columns, lanes] = rest.astype(jnp.bfloat16)
            gram = gram + lax.dot_general(
                z, z, (((1,), (1,)), ((), ())), precision=HIGHEST, preferred_element_type=jnp.float32
            )
        if not first:
            gram = jnp.concatenate([ins[-1][...], gram], axis=1)
        gram_out[...] = gram

    return pl.pallas_call(
        kernel,
        out_shape=tuple(shapes),
        in_specs=[spec(SMEM)] + [spec(VMEM)] * len(operands),
        out_specs=(spec(VMEM),) * len(shapes),
        cost_estimate=cost(2**26, 2**21),
        compiler_params=pltpu.CompilerParams(vmem_limit_bytes=6 * 2**20),
        name="scaled_gram",
    )(counts, *operands)


def inverse_factor(gram):
    size = gram.shape[0]
    row_id = lax.broadcasted_iota(jnp.int32, (size, size), 0)
    col_id = lax.broadcasted_iota(jnp.int32, (size, size), 1)
    eye = jnp.where(row_id == col_id, 1.0, 0.0)
    whole = jnp.concatenate([gram, eye], axis=1)
    wide = 2 * size
    count = size // 8
    groups = [whole[8 * g : 8 * g + 8, :] for g in range(count)]
    within = lax.broadcasted_iota(jnp.int32, (8, wide), 0)

    def spread_row(value, row):
        return jnp.broadcast_to(value[row : row + 1, :], (8, wide))

    results = []
    for g in range(count):
        spread = [
            [
                jnp.broadcast_to(groups[other][:, 8 * g + k : 8 * g + k + 1], (8, wide))
                for other in range(g, count)
            ]
            for k in range(8)
        ]
        pivots = jnp.ones((8, wide), jnp.float32)
        for j in range(8):
            column = spread[j]
            pivot = spread_row(column[0], j)
            pivots = jnp.where(within == j, pivot, pivots)
            over = 1.0 / pivot
            below = jnp.where(within > j, column[0], 0.0)
            for k in range(j + 1, 8):
                share = spread_row(column[0], k) * over
                spread[k][0] = spread[k][0] - below * share
                for other in range(1, count - g):
                    spread[k][other] = spread[k][other] - column[other] * share
            top = spread_row(groups[g], j) * over
            groups[g] = groups[g] - below * top
            for other in range(1, count - g):
                groups[g + other] = groups[g + other] - column[other] * top
        results.append(groups[g] * lax.rsqrt(pivots))
    return jnp.concatenate(results, axis=0)[:, size:wide]


def exact_dot(left, right, contract):
    return lax.dot_general(
        left,
        right,
        (contract, ((), ())),
        precision=HIGHEST,
        preferred_element_type=jnp.float32,
    )


def factors_kernel(grams, both_out, first_out, sound_out):
    columns = grams.shape[0]
    plain = ((1,), (0,))
    turned = ((1,), (1,))
    second = grams[:, columns : 2 * columns]
    first_inverse = inverse_factor(grams[:, 0:columns])
    middle = exact_dot(exact_dot(first_inverse, second, plain), first_inverse, turned)
    both = exact_dot(inverse_factor(middle), first_inverse, plain)
    both_out[...] = both
    first_out[...] = first_inverse
    row_id = lax.broadcasted_iota(jnp.int32, (columns, columns), 0)
    col_id = lax.broadcasted_iota(jnp.int32, (columns, columns), 1)
    trace = jnp.sum(jnp.where(row_id == col_id, second, 0.0))
    spread = jnp.sum(both * both) * trace / (columns * columns)
    sound_out[0] = jnp.where(spread < 64.0, 1, 0)


def factors(grams):
    columns = grams.shape[0]
    square = jax.ShapeDtypeStruct((columns, columns), jnp.float32)
    return pl.pallas_call(
        factors_kernel,
        out_shape=(square, square, jax.ShapeDtypeStruct((1,), jnp.int32)),
        in_specs=[spec(VMEM)],
        out_specs=(spec(VMEM), spec(VMEM), spec(SMEM)),
        cost_estimate=cost(2**30, 2**16),
        compiler_params=pltpu.CompilerParams(vmem_limit_bytes=2 * 2**20),
        name="factors",
    )(grams)


def apply_kernel(factor, z, out, *gram):
    value = exact_dot(factor[...], z[...], ((1,), (0,)))
    out[...] = value
    if gram:
        gram[0][...] = exact_dot(value, value, ((1,), (1,)))


def applied(factor, z, with_gram):
    shapes = [jax.ShapeDtypeStruct(z.shape, jnp.float32)]
    if with_gram:
        shapes.append(jax.ShapeDtypeStruct(factor.shape, jnp.float32))
    return pl.pallas_call(
        apply_kernel,
        out_shape=shapes,
        in_specs=[spec(VMEM)] * 2,
        out_specs=[spec(VMEM)] * len(shapes),
        compiler_params=pltpu.CompilerParams(vmem_limit_bytes=4 * 2**20),
        name="applied",
    )(factor, z)


def second_kernel(gram, first, out):
    out[...] = exact_dot(inverse_factor(gram[...]), first[...], ((1,), (0,)))


def second_factor(gram, first):
    return pl.pallas_call(
        second_kernel,
        out_shape=jax.ShapeDtypeStruct(gram.shape, jnp.float32),
        in_specs=[spec(VMEM)] * 2,
        out_specs=spec(VMEM),
        compiler_params=pltpu.CompilerParams(vmem_limit_bytes=2 * 2**20),
        name="second_factor",
    )(gram, first)


def sum_stages():
    return bits_of(lax.axis_size("blk") * lax.axis_size("grp"))


def pairs_of(bits):
    return [bits[first : first + 2] for first in range(0, len(bits), 2)]


def all_sum(value, stages, beside=None):
    count = lax.axis_size("blk") * lax.axis_size("grp")
    for bits in stages:
        moves = [0]
        for bit in bits if isinstance(bits, list) else [bits]:
            moves += [move ^ bit for move in moves]
        terms = [value] + [
            lax.ppermute(value, ("blk", "grp"), [(source, source ^ move) for source in range(count)])
            for move in moves[1:]
        ]
        if beside is not None:
            terms[0], beside = lax.optimization_barrier((terms[0], beside))
        while len(terms) > 1:
            terms = [left + right for left, right in zip(terms[::2], terms[1::2])]
        value = terms[0]
    return value if beside is None else (value, beside)


def per_device(points, counts, pair_rows, pair_cols, pair_live, start):
    group = lax.axis_size("grp")
    blocks_dev = counts.shape[0]
    columns = start.shape[0]
    slots = pair_rows.shape[0]
    cap = max(-(-slots // group), blocks_dev * blocks_dev * group)
    half = (blocks_dev // 2) * PTS

    home = min(2, group) * blocks_dev

    rows, cols, n, *entries = listing(
        pair_rows, pair_cols, pair_live, group, cap, blocks_dev
    )
    first_chunk = points[:half]
    rest, first_chunk = lax.optimization_barrier((points, first_chunk))
    mate = swap(rest, "grp", 1)
    chunks = [first_chunk, rest[half:]]
    far = [from_behind(chunk, "blk", -1) for chunk in chunks]
    crossed = [gather_far_bits(chunk) for chunk in chunks]
    vec = opening(start, counts)
    tied = lax.optimization_barrier((vec, n, rows, cols, far[0], *crossed[0].values()))
    vec, n, rows, cols, far[0] = tied[:5]
    crossed[0] = dict(zip(crossed[0], tied[5:]))
    cross_vec = gather_far_bits(vec)
    far_vec = from_behind(vec, "blk", -1)
    mate_vec = swap(vec, "grp", 1)

    def direct(index):
        offset = index * (blocks_dev // 2)
        found = {group * blocks_dev + offset: far[index]}
        for rel, value in crossed[index].items():
            found[rel * blocks_dev + offset] = value
        return found

    def passed_on(index):
        offset = index * (blocks_dev // 2)
        found = {}
        for rel, value in crossed[index].items():
            cut = value.shape[0] // (1 if index else 2)
            parts = [swap(value[at : at + cut], "grp", 1) for at in range(0, value.shape[0], cut)]
            found[(rel ^ 1) * blocks_dev + offset] = jnp.concatenate(parts, 0)
        return found

    def build(stage, fresh, state, name):
        return list(
            build_tiles(stage, fresh, n, rows, cols, state, group, blocks_dev, cap, name)
        )

    state = build(0, {0: points, blocks_dev: mate, **direct(0)}, (), "first_tiles")
    state = build(1, passed_on(0), state, "second_tiles")
    urgent = urgent_ranges(group, blocks_dev)
    ranges = [[(0, blocks_dev)]] + urgent
    height = columns + 8
    vecs_home = {0: vec, blocks_dev: mate_vec}
    begun = products(entries, (HOME_EARLY,), vecs_home, state[3], (), ranges, height, 1)
    tied = lax.optimization_barrier((far[1], begun[0], state[1], *crossed[1].values()))
    far[1], begun[0], state[1] = tied[:3]
    crossed[1] = dict(zip(crossed[1], tied[3:]))
    last = passed_on(1)
    *grown, kept = state
    state = build(None, direct(1), grown, "more_blocks") + [kept]
    state = build(2, last, state, "last_tiles")
    kept = state[-1]
    tied = lax.optimization_barrier((kept, *cross_vec.values()))
    kept = tied[0]
    cross_vec = dict(zip(cross_vec, tied[1:]))

    def window_of(own, mate, crossed, far):
        found = {0: own, blocks_dev: mate, group * blocks_dev: far}
        for rel, value in crossed.items():
            found[rel * blocks_dev] = value
            found[(rel ^ 1) * blocks_dev] = swap(value, "grp", 1)
        return found

    def beyond(vecs):
        return {place: value for place, value in vecs.items() if place >= home}

    vecs = window_of(vec, mate_vec, cross_vec, far_vec)
    at_home, *results = products(
        entries, (HOME_LAST,), vecs_home, kept, begun, ranges, height, 1
    )
    results = products(entries, (TO_OTHERS,), beyond(vecs), kept, results, urgent, height, 1)
    sums, (at_home,) = send_urgent(results, (at_home,), group, blocks_dev)
    sums = finish_home(entries, beyond(vecs), kept, at_home, blocks_dev, height, 1) + sums
    z, gram, parts, degree = scaled_gram(sums, vec, counts, None, None)

    far_part = from_behind(parts, "blk", -1)
    crossed = gather_far_bits(parts)
    mate_part = swap(parts, "grp", 1)
    at_home, *results = products(
        entries,
        (HOME_EARLY, HOME_LAST),
        {0: parts, blocks_dev: mate_part},
        kept,
        (),
        ranges,
        columns,
        2,
    )
    at_home, far_part, *tied = lax.optimization_barrier((at_home, far_part, *crossed.values()))
    crossed = dict(zip(crossed, tied))
    vecs = beyond(window_of(parts, mate_part, crossed, far_part))
    results = products(entries, (TO_OTHERS,), vecs, kept, results, urgent, columns, 2)
    sums, (at_home,) = send_urgent(results, (at_home,), group, blocks_dev)
    sums = finish_home(entries, vecs, kept, at_home, blocks_dev, columns, 2) + sums
    z, grams = scaled_gram(sums, z, counts, degree, gram)

    stages = sum_stages()
    stages = stages[:1] + pairs_of(stages[1:])
    both, first, sound = factors(all_sum(grams, stages))

    def at_once(both, first, z):
        return both

    def in_two(both, first, z):
        return second_factor(all_sum(applied(first, z, True)[1], stages), first)

    return applied(lax.cond(sound[0] == 1, at_once, in_two, both, first, z), z, False)[0]


def solution(mesh):
    in_specs = (
        P(("blk", "grp"), None),
        P(("blk", "grp")),
        P("blk"),
        P("blk"),
        P("blk"),
        P(None, ("blk", "grp")),
    )
    out_specs = P(None, ("blk", "grp"))
    return jax.shard_map(
        per_device, mesh=mesh, in_specs=in_specs, out_specs=out_specs, check_vma=False
    )
```
